32 devices in a mesh: img: 4 (over y, core), row: 8 (over z, x).
Axes of the slice: x: 2, y: 2, z: 4, core: 2. Of those that a mesh axis runs over, the one named last changes fastest.
Arguments:
- images: bfloat16 [4, 64, 64, 512], P('img', 'row'), may hold values from -6 to 6
- timesteps: int32 [4], P('img'), may hold values from 0 to 999
- clip_embed: bfloat16 [4, 2048], P('img'), may hold values from -6 to 6
- context: bfloat16 [4, 132, 2048], P('img'), may hold values from -6 to 6
- out_cotangent: bfloat16 [4, 64, 64, 512], P('img', 'row'), may hold values from -6 to 6
- item_weight: int32 [4], P('img'), may hold values from 1 to 8
- first_gain: float32 [512], replicated, may hold values from 0.1 to 1.9
- first_bias: float32 [512], replicated, may hold values from -3 to 3
- first_kernel: bfloat16 [3, 3, 512, 512], replicated, may hold values from -0.09375 to 0.09375
- first_offset: float32 [512], replicated, may hold values from -3 to 3
- embed_weight: bfloat16 [2048, 1024], replicated, may hold values from -0.125 to 0.125
- embed_bias: float32 [1024], replicated, may hold values from -3 to 3
- second_gain: float32 [512], replicated, may hold values from 0.1 to 1.9
- second_bias: float32 [512], replicated, may hold values from -3 to 3
- second_kernel: bfloat16 [3, 3, 512, 512], replicated, may hold values from -0.09375 to 0.09375
- second_offset: float32 [512], replicated, may hold values from -3 to 3
- third_gain: float32 [512], replicated, may hold values from 0.1 to 1.9
- third_bias: float32 [512], replicated, may hold values from -0.6 to 0.6
- project_in: bfloat16 [512, 1536], replicated, may hold values from -0.25 to 0.25
- context_weight: bfloat16 [2048, 1024], replicated, may hold values from -0.125 to 0.125
- project_out: bfloat16 [512, 512], replicated, may hold values from -3 to 3
- output_bias: float32 [512], replicated, may hold values from -3 to 3
Outputs:
- result_image: bfloat16 [4, 64, 64, 512], P('img', 'row')
- image_grad: float32 [4, 64, 64, 512], P('img', 'row')
- first_gain_grad: float32 [512], P('row')
- first_bias_grad: float32 [512], P('row')
- first_kernel_grad: float32 [3, 3, 512, 512], P(None, None, 'row')
- first_offset_grad: float32 [512], P('row')
- embed_weight_grad: float32 [2048, 1024], P('row')
- embed_bias_grad: float32 [1024], P('row')
- second_gain_grad: float32 [512], P('row')
- second_bias_grad: float32 [512], P('row')
- second_kernel_grad: float32 [3, 3, 512, 512], P(None, None, 'row')
- second_offset_grad: float32 [512], P('row')
- third_gain_grad: float32 [512], P('row')
- third_bias_grad: float32 [512], P('row')
- project_in_grad: float32 [512, 1536], P('row')
- context_weight_grad: float32 [2048, 1024], P('row')
- project_out_grad: float32 [512, 512], P('row')
- output_bias_grad: float32 [512], P('row')
The draws below stay inside these ranges and needn't reach their ends.
All inputs are finite; a program needn't handle non-finite values.
Results may differ from the reference program's by a relative error of at most 0.019.
Values may be sent and summed in bfloat16 or wider, within the bound.
A program may use at most 128 MiB of HBM per device.

```python
import math
import jax
import jax.numpy as jnp
from jax import lax

C = 512
HEADS = 8
EMB = 2048
TXT = 2048
GROUPS = 32
H = 64
W = 64
HD = 64
CTX = 132
BATCH = 4


def set_ends(result, own_key, least, top_value):
    spot = [jax.random.randint(jax.random.fold_in(own_key, axis), (), 0, length) for axis, length in enumerate(result.shape)]
    longest = result.shape.index(max(result.shape))
    next_to = spot[:longest] + [(spot[longest] + 1) % result.shape[longest]] + spot[longest + 1:]
    return result.at[tuple(spot)].set(least).at[tuple(next_to)].set(top_value)


def shard_levels(own_key, shape, pieces, low, top_value):
    factor_of = 1.0
    for axis_at, blocks in pieces:
        heights = jax.random.uniform(jax.random.fold_in(jax.random.fold_in(own_key, 6), axis_at), (blocks,), jnp.float32, low / len(pieces), top_value / len(pieces))
        factor_of = factor_of * jnp.repeat(jnp.exp(heights), shape[axis_at] // blocks).reshape((-1,) + (1,) * (len(shape) - 1 - axis_at))
    return factor_of


def scatter_about(rng, extent, scale, most, split=(), kind=jnp.bfloat16):
    array = jax.random.normal(rng, extent, jnp.float32) * scale
    if len(split) > 0:
        array = shard_levels(rng, extent, split, -0.22, 0.18) * array
    return jnp.clip(array, min=-most, max=most).astype(kind)


def setup_inputs(seed: int = 0) -> dict:
    key_of = jax.random.split(jax.random.key(seed), 23)
    images = scatter_about(key_of[0], (BATCH, H, W, C), 1.0, 6.0, ((0, 4), (1, 8)))
    timesteps = set_ends(jax.random.randint(key_of[1], (BATCH,), 0, 1000), jax.random.fold_in(key_of[1], 1), 0, 999).astype(jnp.int32)
    clip_embed = scatter_about(key_of[2], (BATCH, EMB), 1.0, 6.0, ((0, 4),))
    context = scatter_about(key_of[3], (BATCH, CTX, TXT), 1.0, 6.0, ((0, 4),))
    out_cotangent = scatter_about(key_of[4], (BATCH, H, W, C), 1.0, 6.0, ((0, 4), (1, 8)))
    item_weight = set_ends(jax.random.randint(key_of[5], (BATCH,), 1, 9), jax.random.fold_in(key_of[5], 1), 1, 8).astype(jnp.int32)
    first_gain = jnp.clip(1.0 + 0.18 * jax.random.normal(key_of[6], (C,), jnp.float32), 0.1, 1.9)
    first_bias = scatter_about(key_of[7], (C,), 0.5, 3.0, (), jnp.float32)
    first_kernel = scatter_about(key_of[8], (3, 3, C, C), (9 * C) ** -0.5, 0.09375)
    first_offset = scatter_about(key_of[9], (C,), 0.5, 3.0, (), jnp.float32)
    embed_weight = scatter_about(key_of[10], (EMB, 2 * C), EMB ** -0.5, 0.125)
    embed_bias = scatter_about(key_of[11], (2 * C,), 0.5, 3.0, (), jnp.float32)
    second_gain = jnp.clip(1.0 + 0.18 * jax.random.normal(key_of[12], (C,), jnp.float32), 0.1, 1.9)
    second_bias = scatter_about(key_of[13], (C,), 0.5, 3.0, (), jnp.float32)
    second_kernel = scatter_about(key_of[14], (3, 3, C, C), (9 * C) ** -0.5, 0.09375)
    second_offset = scatter_about(key_of[15], (C,), 0.5, 3.0, (), jnp.float32)
    third_gain = jnp.clip(1.0 + 0.18 * jax.random.normal(key_of[16], (C,), jnp.float32), 0.1, 1.9)
    third_bias = scatter_about(key_of[17], (C,), 0.1, 0.6, (), jnp.float32)
    project_in = scatter_about(key_of[18], (C, 3 * C), C ** -0.5, 0.25)
    context_weight = scatter_about(key_of[19], (TXT, 2 * C), TXT ** -0.5, 0.125)
    project_out = scatter_about(key_of[20], (C, C), 4 ** -0.5, 3.0)
    output_bias = scatter_about(key_of[21], (C,), 0.5, 3.0, (), jnp.float32)
    return {"images": images, "timesteps": timesteps, "clip_embed": clip_embed, "context": context, "out_cotangent": out_cotangent, "item_weight": item_weight, "first_gain": first_gain, "first_bias": first_bias, "first_kernel": first_kernel, "first_offset": first_offset, "embed_weight": embed_weight, "embed_bias": embed_bias, "second_gain": second_gain, "second_bias": second_bias, "second_kernel": second_kernel, "second_offset": second_offset, "third_gain": third_gain, "third_bias": third_bias, "project_in": project_in, "context_weight": context_weight, "project_out": project_out, "output_bias": output_bias}


@jax.custom_vjp
def low(v):
    return lax.optimization_barrier(v.astype(jnp.bfloat16)).astype(jnp.float32)

@jax.custom_vjp
def low_back(v):
    return v

def low_keep(v):
    return (low(v), None)

def low_pass(kept, grad):
    return (grad,)

def back_keep(v):
    return (v, None)

def back_low(kept, grad):
    return (low(grad),)
low.defvjp(low_keep, low_pass)
low_back.defvjp(back_keep, back_low)
HIGHEST = lax.Precision.HIGHEST
EPSILON = 1e-05

def sinusoid(steps, width):
    half_width = width // 2
    frequency = jnp.exp(-math.log(10000.0) * jnp.arange(half_width, dtype=jnp.float32) / half_width)
    angles = steps.astype(jnp.float32)[:, None] * frequency[None, :]
    return jnp.concatenate([jnp.cos(angles), jnp.sin(angles)], axis=1)

def convolve(values, kernel):
    return lax.conv_general_dilated(values, kernel, (1, 1), ((1, 1), (1, 1)), dimension_numbers=('NHWC', 'HWIO', 'NHWC'), precision=HIGHEST)

def group_norm(values, gain, bias):
    shape_all = values.shape
    grouped = values.reshape(shape_all[0], shape_all[1], shape_all[2], GROUPS, shape_all[3] // GROUPS)
    center = lax.optimization_barrier(jnp.mean(grouped, axis=(1, 2, 4), keepdims=True))
    spread = lax.optimization_barrier(jnp.mean(grouped * grouped, axis=(1, 2, 4), keepdims=True)) - center * center
    normed = ((grouped - center) * lax.rsqrt(spread + EPSILON)).reshape(shape_all)
    return normed * gain + bias

def score_block(query_blk, keys_img, vals_img):
    scores = jnp.einsum('qhd,khd->hqk', query_blk, keys_img, precision=HIGHEST) * 0.125
    scores = low_back(scores)
    weights = jax.nn.softmax(scores, axis=-1)
    return jnp.einsum('hqk,khd->qhd', low(weights), vals_img, precision=HIGHEST)

def attend_image(packed):
    query_img, keys_img, vals_img = packed
    count_q = query_img.shape[0]
    block_rows = min(512, count_q)
    blocks = query_img.reshape(count_q // block_rows, block_rows, HEADS, HD)
    step_fn = jax.checkpoint(score_block)
    outs_blk = lax.map(lambda blk: step_fn(blk, keys_img, vals_img), blocks)
    return outs_blk.reshape(count_q, HEADS, HD)

def forward(image_f, first_gain, first_bias, first_kernel, first_offset, embed_weight, embed_bias, second_gain, second_bias, second_kernel, second_offset, third_gain, third_bias, project_in, context_weight, project_out, output_bias, embedding, context_f):
    batch_n = image_f.shape[0]
    norm_one = group_norm(image_f, first_gain, first_bias)
    act_one = low(jax.nn.silu(norm_one))
    hidden_one = low_back(convolve(act_one, first_kernel)) + first_offset
    scale_shift = jnp.dot(low(jax.nn.silu(embedding)), embed_weight, precision=HIGHEST) + embed_bias
    scale_part = scale_shift[:, None, None, :C]
    shift_part = scale_shift[:, None, None, C:]
    norm_two = group_norm(hidden_one, second_gain, second_bias) * (1.0 + scale_part) + shift_part
    act_two = low(jax.nn.silu(norm_two))
    middle = image_f + low_back(convolve(act_two, second_kernel)) + second_offset
    act_three = low(group_norm(middle, third_gain, third_bias))
    triple = low_back(low(jnp.einsum('bhwc,ck->bhwk', act_three, project_in, precision=HIGHEST)))
    triple = triple.reshape(batch_n, H * W, 3, HEADS, HD)
    enc_pair = low(jnp.einsum('bct,tk->bck', context_f, context_weight, precision=HIGHEST))
    enc_pair = enc_pair.reshape(batch_n, CTX, 2, HEADS, HD)
    keys_all = jnp.concatenate([enc_pair[:, :, 0], triple[:, :, 1]], axis=1)
    vals_all = jnp.concatenate([enc_pair[:, :, 1], triple[:, :, 2]], axis=1)
    attended = lax.map(attend_image, (triple[:, :, 0], keys_all, vals_all))
    attended = low_back(low(attended)).reshape(batch_n, H, W, C)
    branch = low_back(jnp.einsum('bhwc,cd->bhwd', attended, project_out, precision=HIGHEST))
    return middle + branch + output_bias

def reference(images, timesteps, clip_embed, context, out_cotangent, item_weight, first_gain, first_bias, first_kernel, first_offset, embed_weight, embed_bias, second_gain, second_bias, second_kernel, second_offset, third_gain, third_bias, project_in, context_weight, project_out, output_bias):
    f32 = jnp.float32
    embedding = sinusoid(timesteps, EMB) + clip_embed.astype(f32)
    context_f = context.astype(f32)

    def wrapped(image_f, g_one, b_one, k_one, o_one, e_w, e_b, g_two, b_two, k_two, o_two, g_three, b_three, p_in, c_w, p_out, o_b):
        return forward(image_f, g_one, b_one, k_one, o_one, e_w, e_b, g_two, b_two, k_two, o_two, g_three, b_three, p_in, c_w, p_out, o_b, embedding, context_f)
    output, pullback = jax.vjp(wrapped, images.astype(f32), first_gain.astype(f32), first_bias.astype(f32), first_kernel.astype(f32), first_offset.astype(f32), embed_weight.astype(f32), embed_bias.astype(f32), second_gain.astype(f32), second_bias.astype(f32), second_kernel.astype(f32), second_offset.astype(f32), third_gain.astype(f32), third_bias.astype(f32), project_in.astype(f32), context_weight.astype(f32), project_out.astype(f32), output_bias.astype(f32))
    weight_scale = item_weight.astype(f32) * 0.25
    cotangent = out_cotangent.astype(f32) * weight_scale[:, None, None, None]
    grads = pullback(cotangent)
    return (output.astype(jnp.bfloat16), grads[0], grads[1], grads[2], grads[3], grads[4], grads[5], grads[6], grads[7], grads[8], grads[9], grads[10], grads[11], grads[12], grads[13], grads[14], grads[15], grads[16])
```

```python
import functools
import math

import jax
import jax.numpy as jnp
from jax import lax
from jax.experimental import pallas as pl
from jax.experimental.pallas import tpu as pltpu
from jax.sharding import PartitionSpec as P

HEADS = 8
GROUPS = 32
EPSILON = 1e-05
f32 = jnp.float32
bf16 = jnp.bfloat16
MESH = pl.DeviceIdType.MESH
LOG2E=math.log2(math.e)

def nt(a,b):
    return lax.dot_general(a,b,(((1,),(1,)),((),())),preferred_element_type=f32)
def nn(a,b):
    return jnp.dot(a,b,preferred_element_type=f32)

def attn_kernel(cfg, *refs):
    if cfg[0]:
        q_ref, ctx_ref, g_ref, out_ref, dq_ref, dctx_ref = refs[:6]
        kv_ref, dkv_ref = q_ref, dq_ref
        at_kv = cfg[-1]
    else:
        q_ref, kv_ref, ctx_ref, g_ref, out_ref, dq_ref, dkv_ref, dctx_ref = refs[:8]
        at_kv = 0
    (kx, vx, kt, vt, sbuf, pbuf, acc) = refs[-7:]
    joined, nqs, nsrc, width, bq, kc, nctx, padc, hd = cfg
    npix = nsrc*width
    nk = npix + padc
    ones_rows = jnp.where(lax.broadcasted_iota(jnp.int32,(hd,width),0)<2,1.0,0.0).astype(bf16)
    def fill(pair, at, w):
        k = pair[:hd].astype(f32)*(LOG2E*0.125)
        hi = k.astype(bf16)
        lo = (k-hi.astype(f32)).astype(bf16)
        kx[pl.ds(at,w),:] = jnp.concatenate([hi,lo],axis=0).T
        vfull = jnp.concatenate([pair[hd:], ones_rows[:, :w]],axis=0)
        vx[pl.ds(at,w),:] = vfull.T
        return vfull
    for s in range(nsrc):
        pair = kv_ref[s, at_kv:]
        vfull = fill(pair, s*width, width)
        kt[:, s*width:(s+1)*width] = pair[:hd]
        vt[:, s*width:(s+1)*width] = vfull[:hd+16]
    cpair = ctx_ref[...]
    vfull = fill(cpair, npix, padc)
    kt[:, npix:npix+padc] = cpair[:hd]
    vt[:, npix:npix+padc] = vfull[:hd+16]
    acc[...] = jnp.zeros_like(acc)

    nfull = npix//kc
    per = width//bq
    def block(j, _):
        s = j//per
        off = pl.multiple_of((j%per)*bq, bq)
        qt = q_ref[s,:hd,pl.ds(off,bq)]
        gt = g_ref[s,:,pl.ds(off,bq)]
        q2 = jnp.concatenate([qt,qt],axis=0)
        sc = nn(kx[pl.ds(npix,padc),:], q2)
        sc = jnp.where(lax.broadcasted_iota(jnp.int32,(padc,bq),0)<nctx, sc, -jnp.inf)
        sbuf[pl.ds(npix,padc),:] = sc
        m8 = jnp.max(sc.reshape(padc//8,8,bq),axis=0)
        def phase_a(c, m8):
            at = pl.multiple_of(c*kc,kc)
            sv = nn(kx[pl.ds(at,kc),:], q2)
            sbuf[pl.ds(at,kc),:] = sv
            return jnp.maximum(m8, jnp.max(sv.reshape(kc//8,8,bq),axis=0))
        m8 = lax.fori_loop(0,nfull,phase_a,m8,unroll=True)
        m = jnp.max(m8,axis=0,keepdims=True)
        pc = jnp.exp2(sbuf[pl.ds(npix,padc),:]-m).astype(bf16)
        pbuf[pl.ds(npix,padc),:] = pc
        o = nn(vt[:,npix:npix+padc], pc)
        def phase_b(c, o):
            at = pl.multiple_of(c*kc,kc)
            p = jnp.exp2(sbuf[pl.ds(at,kc),:]-m).astype(bf16)
            pbuf[pl.ds(at,kc),:] = p
            return o + nn(vt[:,pl.ds(at,kc)], p)
        o = lax.fori_loop(0,nfull,phase_b,o,unroll=True)
        inv = 1.0/o[hd:hd+1]
        att = o[:hd]*inv
        out_ref[s,:,pl.ds(off,bq)] = att.astype(bf16)
        gf = gt.astype(f32)
        delta = jnp.sum(gf*att,axis=0,keepdims=True)*inv
        gl = (gf*inv).astype(bf16)
        dhi = (-delta).astype(bf16)
        dlo = (-delta-dhi.astype(f32)).astype(bf16)
        gx = jnp.concatenate([gl,dhi,dlo,jnp.zeros((hd-2,bq),bf16)],axis=0)
        zero = jnp.zeros((hd,bq),bf16)
        rq = jnp.concatenate([qt,zero],axis=0).T
        rg = jnp.concatenate([zero,gl],axis=0).T
        rr = jnp.concatenate([rq,rg],axis=0)
        def piece(at, w, dq):
            p = pbuf[pl.ds(at,w),:]
            dp = nn(vx[pl.ds(at,w),:], gx)
            ds = (p.astype(f32)*dp).astype(bf16)
            acc[pl.ds(at,w),:] += nn(jnp.concatenate([ds,p],axis=1), rr)
            return dq + nn(kt[:,pl.ds(at,w)], ds)
        dq = piece(npix, padc, jnp.zeros((hd,bq),f32))
        def phase_d(c, dq):
            return piece(pl.multiple_of(c*kc,kc), kc, dq)
        dq = lax.fori_loop(0,nfull,phase_d,dq,unroll=True)
        dq_ref[s,:hd,pl.ds(off,bq)] = (dq*0.125).astype(bf16)
        return 0
    lax.fori_loop(0, nqs*per, block, 0)
    scale = jnp.where(lax.broadcasted_iota(jnp.int32,(1,2*hd),1)<hd,0.125,1.0)
    for s in range(nsrc):
        dkv_ref[s, at_kv:] = (acc[s*width:(s+1)*width,:]*scale).astype(bf16).T
    dctx_ref[...] = (acc[npix:npix+padc,:]*scale).astype(bf16)

def attention(q, kv, ctx, g, nctx, bq=512, kc=512):
    joined = kv is None
    nqs, _, width = q.shape
    hd = g.shape[1]
    nsrc = nqs if joined else kv.shape[0]
    padc = ctx.shape[1]
    nk = nsrc*width+padc
    cfg=(joined,nqs,nsrc,width,bq,kc,nctx,padc,hd)
    V=pl.BlockSpec(memory_space=pltpu.VMEM)
    S=jax.ShapeDtypeStruct
    grads=(S((nqs,3*hd,width),bf16),) if joined else (S((nqs,hd,width),bf16),S((nsrc,2*hd,width),bf16))
    args=(q,ctx,g) if joined else (q,kv,ctx,g)
    return pl.pallas_call(
        functools.partial(attn_kernel,cfg),
        out_shape=(S((nqs,hd,width),bf16),)+grads+(S((padc,2*hd),bf16),),
        in_specs=[V]*len(args), out_specs=(V,)*(2+len(grads)),
        scratch_shapes=[pltpu.VMEM((nk,2*hd),bf16),pltpu.VMEM((nk,2*hd),bf16),
                        pltpu.VMEM((hd,nk),bf16),pltpu.VMEM((hd+16,nk),bf16),
                        pltpu.VMEM((nk,bq),f32),pltpu.VMEM((nk,bq),bf16),
                        pltpu.VMEM((nk,2*hd),f32)],
        compiler_params=pltpu.CompilerParams(vmem_limit_bytes=48*2**20),
        cost_estimate=pl.CostEstimate(flops=6*2*64*4096*4228,bytes_accessed=8*2**20,transcendentals=4096*4228),
        name="attend",
    )(*args)

def exchange_kernel(axis, n, x_ref, out_ref, send_sem, recv_sem):
    me = lax.axis_index(axis)
    barrier = pltpu.get_barrier_semaphore()
    for k in range(1, n):
        pl.semaphore_signal(
            barrier, inc=1, device_id={axis: lax.rem(me + k, n)}, device_id_type=MESH
        )
    out_ref[me] = x_ref[...]
    pl.semaphore_wait(barrier, n - 1)
    copies = []
    for k in range(1, n):
        copy = pltpu.make_async_remote_copy(
            src_ref=x_ref,
            dst_ref=out_ref.at[me],
            send_sem=send_sem.at[k - 1],
            recv_sem=recv_sem.at[k - 1],
            device_id={axis: lax.rem(me + k, n)},
            device_id_type=MESH,
        )
        copy.start()
        copies.append(copy)
    for copy in copies:
        copy.wait()


def exchange(x, axis, cid):
    n = lax.axis_size(axis)
    V = pl.BlockSpec(memory_space=pltpu.VMEM)
    return pl.pallas_call(
        functools.partial(exchange_kernel, axis, n),
        out_shape=jax.ShapeDtypeStruct((n,) + x.shape, x.dtype),
        in_specs=[V],
        out_specs=V,
        scratch_shapes=[
            pltpu.SemaphoreType.DMA((n - 1,)),
            pltpu.SemaphoreType.DMA((n - 1,)),
        ],
        compiler_params=pltpu.CompilerParams(collective_id=cid, has_side_effects=True),
        name="exchange_" + axis,
    )(x)


def row_sum(rows):
    x = jnp.concatenate(
        [jnp.stack(rows), jnp.zeros((8 - len(rows), rows[0].shape[0]), f32)], axis=0
    )
    return jnp.sum(exchange(x, "row", 1), axis=0)


def sinusoid(steps, width):
    half_width = width // 2
    frequency = jnp.exp(-math.log(10000.0) * jnp.arange(half_width, dtype=f32) / half_width)
    angles = steps.astype(f32)[:, None] * frequency[None, :]
    return jnp.concatenate([jnp.cos(angles), jnp.sin(angles)], axis=1)


def swish_slope(values):
    sig_v = jax.nn.sigmoid(values)
    return sig_v * (1.0 + values * (1.0 - sig_v))


def per_group(vec, members):
    n = vec.shape[-1]
    g = jnp.sum(vec.reshape(vec.shape[0], GROUPS, n // GROUPS), axis=2) / members
    return jnp.repeat(g, n // GROUPS, axis=1)


def norm_stats(values, members):
    sums = row_sum([jnp.sum(values, axis=0), jnp.sum(values * values, axis=0)])
    means = per_group(sums[:2], members)
    return (means[0], lax.rsqrt(means[1] - means[0] * means[0] + EPSILON))


def halo(x):
    devices = lax.axis_size("row")
    up = [(i, i + 1) for i in range(devices - 1)]
    down = [(i + 1, i) for i in range(devices - 1)]
    before = lax.ppermute(x[-1:], "row", up)
    after = lax.ppermute(x[:1], "row", down)
    return jnp.concatenate([before, x, after], axis=0)


def conv(padded, kernel):
    x = jnp.pad(padded, ((0, 0), (1, 1), (0, 0)))[None]
    return lax.conv_general_dilated(
        x,
        kernel,
        (1, 1),
        "VALID",
        dimension_numbers=("NHWC", "HWIO", "NHWC"),
        preferred_element_type=f32,
    )[0]


def flip_kernel(kernel):
    return jnp.flip(kernel, (0, 1)).transpose(0, 1, 3, 2)


def tn(left, right):
    return lax.dot_general(left, right, (((0,), (0,)), ((), ())), preferred_element_type=f32)


def split_cols(x, n):
    rows, cols = x.shape
    return x.reshape(rows, n, cols // n).transpose(1, 0, 2)


def kernel_grad(acts, grad_padded, tall):
    n = lax.axis_size("img")
    rows, wide, ch = grad_padded.shape
    part = ch // n
    g = lax.all_to_all(
        split_cols(grad_padded.reshape(rows * wide, ch), n),
        "img",
        split_axis=0,
        concat_axis=0,
        tiled=True,
    ).reshape(n, rows, wide, part)
    g = jnp.pad(g, ((0, 0), (0, 0), (1, 1), (0, 0)))
    lines = []
    for ky in range(3):
        for kx in range(3):
            lines.append(
                g[:, 2 - ky : 2 - ky + tall, 2 - kx : 2 - kx + wide].reshape(-1, part)
            )
    return tn(acts, jnp.concatenate(lines, axis=1))


def local(
    images,
    timesteps,
    clip_embed,
    context,
    out_cotangent,
    item_weight,
    first_gain,
    first_bias,
    first_kernel,
    first_offset,
    embed_weight,
    embed_bias,
    second_gain,
    second_bias,
    second_kernel,
    second_offset,
    third_gain,
    third_bias,
    project_in,
    context_weight,
    project_out,
    output_bias,
):
    _, tall, wide, ch = images.shape
    pixels = tall * wide
    hd = ch // HEADS
    nrow = lax.axis_size("row")
    nimg = lax.axis_size("img")
    me_row = lax.axis_index("row")
    gq = nrow // HEADS
    head = me_row // gq
    text = context.shape[2]
    nctx = context.shape[1]
    members = float(nrow * pixels * (ch // GROUPS))

    def gather_img(x):
        return lax.all_gather(x, "img", axis=0, tiled=True)

    grad_out = out_cotangent.reshape(pixels, ch).astype(f32) * (item_weight.astype(f32) * 0.25)
    grad_low = grad_out.astype(bf16)
    attended_grad = (
        lax.dot_general(project_out, grad_low, (((1,), (1,)), ((), ())), preferred_element_type=f32)
        .astype(bf16)
        .reshape(HEADS, hd, pixels)
    )

    def queries_out(x):
        x = x.reshape(HEADS, hd, gq, pixels // gq).transpose(0, 2, 1, 3)
        x = x.reshape(nrow, hd, pixels // gq)
        return x

    def a2a(x):
        return lax.all_to_all(x, "row", split_axis=0, concat_axis=0, tiled=True)

    grad_heads = a2a(queries_out(attended_grad))

    image_f = images.reshape(pixels, ch).astype(f32)
    embedding = sinusoid(timesteps, clip_embed.shape[1]) + clip_embed.astype(f32)
    embed_act = jax.nn.silu(embedding).astype(bf16)
    scale_shift = (jnp.dot(embed_act, embed_weight, preferred_element_type=f32) + embed_bias)[0]
    scale1 = 1.0 + scale_shift[:ch]
    shift = scale_shift[ch:]
    pair_at = (head // 2) * (2 * hd)
    cw_k = lax.dynamic_slice_in_dim(context_weight, pair_at, 2 * hd, 1)
    cw_v = lax.dynamic_slice_in_dim(context_weight, ch + pair_at, 2 * hd, 1)
    cw = jnp.concatenate([cw_k, cw_v], axis=1)
    enc = lax.dot_general(
        cw, context[0], (((0,), (1,)), ((), ())), preferred_element_type=f32
    ).astype(bf16)
    enc = enc.reshape(2, 2, hd, nctx)
    enc = jnp.where(head % 2 == 0, enc[:, 0], enc[:, 1]).reshape(2 * hd, nctx)
    padc = -(-nctx // 16) * 16
    enc = jnp.pad(enc, ((0, 0), (0, padc - nctx)))

    mean1, rstd1 = norm_stats(image_f, members)
    normed1 = (image_f - mean1) * rstd1
    norm_one = normed1 * first_gain + first_bias
    act_one = jax.nn.silu(norm_one).astype(bf16)
    hidden = conv(halo(act_one.reshape(tall, wide, ch)), first_kernel).reshape(pixels, ch)
    hidden = hidden + first_offset
    acts_one = gather_img(act_one)
    mean2, rstd2 = norm_stats(hidden, members)
    normed2 = (hidden - mean2) * rstd2
    affine_two = normed2 * second_gain + second_bias
    norm_two = affine_two * scale1 + shift
    act_two = jax.nn.silu(norm_two).astype(bf16)
    acts_two = gather_img(act_two)
    middle = (
        image_f
        + conv(halo(act_two.reshape(tall, wide, ch)), second_kernel).reshape(pixels, ch)
        + second_offset
    )
    mean3, rstd3 = norm_stats(middle, members)
    normed3 = (middle - mean3) * rstd3
    act_three = (normed3 * third_gain + third_bias).astype(bf16)
    acts_three = gather_img(act_three)
    triple = (
        lax.dot_general(project_in, act_three, (((0,), (1,)), ((), ())), preferred_element_type=f32)
        .astype(bf16)
        .reshape(3, HEADS, hd, pixels)
    )
    if gq == 1:
        recv = a2a(triple.transpose(1, 0, 2, 3).reshape(nrow, 3 * hd, pixels))
        q_h, kv_h = recv[:, :hd], recv[:, hd:]
        grad_h = grad_heads
    else:
        pair = triple[1:].transpose(1, 0, 2, 3).reshape(HEADS, 1, 2 * hd, pixels)
        pair = jnp.broadcast_to(pair, (HEADS, gq, 2 * hd, pixels)).reshape(nrow, 2 * hd, pixels)
        q_h, kv_h = a2a(queries_out(triple[0])), a2a(pair)

        def regroup(x, rows):
            x = x.transpose(1, 0, 2).reshape(rows, -1, 512)
            return x.transpose(1, 0, 2)

        q_h, kv_h, grad_h = regroup(q_h, hd), regroup(kv_h, 2 * hd), regroup(grad_heads, hd)
    att_h, dq_h, dkv_h, dctx = attention(q_h, kv_h, enc, grad_h, nctx)
    if gq == 1:
        attended = a2a(att_h).reshape(ch, pixels)
        back = a2a(jnp.concatenate([dq_h, dkv_h], axis=1)).reshape(HEADS, 3, hd, pixels)
        back = back.transpose(1, 0, 2, 3).reshape(3 * ch, pixels)
    else:

        def ungroup(x, part):
            rows = x.shape[1]
            x = x.transpose(1, 0, 2).reshape(rows, nrow, part)
            return x.transpose(1, 0, 2)

        def from_queries(x):
            x = x.reshape(HEADS, gq, hd, pixels // gq).transpose(0, 2, 1, 3)
            return x.reshape(ch, pixels)

        attended = from_queries(a2a(ungroup(att_h, pixels // gq)))
        dq = from_queries(a2a(ungroup(dq_h, pixels // gq)))
        dkv = a2a(ungroup(dkv_h, pixels)).reshape(HEADS, gq, 2, hd, pixels)
        dkv = jnp.sum(dkv.astype(f32), axis=1).astype(bf16)
        dkv = dkv.transpose(1, 0, 2, 3).reshape(2 * ch, pixels)
        back = jnp.concatenate([dq, dkv], axis=0)
    branch = tn(attended, project_out)
    result_image = (middle + branch + output_bias).astype(bf16)

    part_text = text // nrow
    enc_all = lax.all_gather(dctx[:nctx].astype(bf16), ("img", "row"), axis=0)
    enc_all = enc_all.reshape(nimg, HEADS, gq, nctx, 2, hd)
    if gq > 1:
        enc_all = jnp.sum(enc_all.astype(f32), axis=2, keepdims=True).astype(bf16)
    enc_all = enc_all[:, :, 0].transpose(0, 2, 3, 1, 4).reshape(nimg * nctx, 2 * ch)
    ctx_rows = lax.dynamic_slice_in_dim(context[0], me_row * part_text, part_text, 1)
    ctx_rows = gather_img(ctx_rows)
    context_weight_grad = tn(ctx_rows, enc_all)

    triple_grad = back.T
    act_three_grad = lax.dot_general(
        triple_grad, project_in, (((1,), (1,)), ((), ())), preferred_element_type=f32
    )
    sums3 = row_sum(
        [
            jnp.sum(act_three_grad * normed3, axis=0),
            jnp.sum(act_three_grad, axis=0),
            jnp.sum(grad_out, axis=0),
        ]
    )

    def norm_back(u, normed, rstd, gain, gain_sum, bias_sum):
        means = per_group(jnp.stack([gain * bias_sum, gain * gain_sum]), members)
        return rstd * (u * gain - means[0] - normed * means[1])

    middle_grad = grad_out + norm_back(
        act_three_grad, normed3, rstd3, third_gain, sums3[0], sums3[1]
    )
    middle_low = halo(middle_grad.astype(bf16).reshape(tall, wide, ch))
    act_two_grad = conv(middle_low, flip_kernel(second_kernel)).reshape(pixels, ch)
    norm_two_grad = act_two_grad * swish_slope(norm_two)
    sums2 = row_sum(
        [
            jnp.sum(norm_two_grad * normed2, axis=0),
            jnp.sum(norm_two_grad, axis=0),
            jnp.sum(middle_grad, axis=0),
        ]
    )
    scale_grad = second_gain * sums2[0] + second_bias * sums2[1]
    shift_grad = sums2[1]
    gain2_sum, bias2_sum = scale1 * sums2[0], scale1 * sums2[1]
    hidden_grad = norm_back(
        norm_two_grad * scale1, normed2, rstd2, second_gain, gain2_sum, bias2_sum
    )
    hidden_low = halo(hidden_grad.astype(bf16).reshape(tall, wide, ch))
    act_one_grad = conv(hidden_low, flip_kernel(first_kernel)).reshape(pixels, ch)
    norm_one_grad = act_one_grad * swish_slope(norm_one)
    sums1 = row_sum(
        [
            jnp.sum(norm_one_grad * normed1, axis=0),
            jnp.sum(norm_one_grad, axis=0),
            jnp.sum(hidden_grad, axis=0),
        ]
    )
    image_grad = middle_grad + norm_back(
        norm_one_grad, normed1, rstd1, first_gain, sums1[0], sums1[1]
    )

    def swap_img(x):
        x = split_cols(x, nimg)
        x = lax.all_to_all(x, "img", split_axis=0, concat_axis=0, tiled=True)
        return x.reshape(-1, x.shape[2])

    kg2 = kernel_grad(acts_two, middle_low, tall)
    kg1 = kernel_grad(acts_one, hidden_low, tall)
    pin = tn(acts_three, swap_img(triple_grad))
    pout = tn(gather_img(attended.T), swap_img(grad_low))

    def finish(x):
        x = lax.psum_scatter(x.astype(bf16), "row", scatter_dimension=0, tiled=True)
        return lax.all_gather(x, "img", axis=0).astype(f32)

    c2 = finish(kg2)
    c1 = finish(kg1)
    c3 = finish(jnp.concatenate([pin, pout], axis=1))
    part = ch // nrow
    cols = ch // nimg

    def conv_out(x):
        return x.reshape(nimg, part, 3, 3, cols).transpose(2, 3, 1, 0, 4).reshape(3, 3, part, ch)

    wide_in = 3 * ch // nimg
    pin_out = c3[:, :, :wide_in].transpose(1, 0, 2).reshape(part, 3 * ch)
    pout_out = c3[:, :, wide_in:].transpose(1, 0, 2).reshape(part, ch)

    rows = jnp.stack(
        [
            sums1[0],
            sums1[1],
            sums1[2],
            gain2_sum,
            bias2_sum,
            sums2[2],
            sums3[0],
            sums3[1],
            sums3[2],
            scale_grad,
            shift_grad,
        ]
        + [jnp.zeros((ch,), f32)] * 5
    )
    every = exchange(rows, "img", 2)
    acts_embed = gather_img(embed_act)
    part_emb = embed_act.shape[1] // nrow
    acts_embed = lax.dynamic_slice_in_dim(acts_embed, me_row * part_emb, part_emb, 1).astype(f32)
    shift_scale = every[:, 9:11].reshape(nimg, 2 * ch)
    embed_weight_grad = jnp.sum(acts_embed[:, :, None] * shift_scale[:, None, :], axis=0)
    part_bias = 2 * ch // nrow
    embed_bias_grad = lax.dynamic_slice_in_dim(
        jnp.sum(shift_scale, axis=0), me_row * part_bias, part_bias, 0
    )
    vecs = lax.dynamic_slice_in_dim(jnp.sum(every[:, :9], axis=0), me_row * part, part, 1)
    return (
        result_image.reshape(images.shape),
        image_grad.reshape(images.shape),
        vecs[0],
        vecs[1],
        conv_out(c1),
        vecs[2],
        embed_weight_grad,
        embed_bias_grad,
        vecs[3],
        vecs[4],
        conv_out(c2),
        vecs[5],
        vecs[6],
        vecs[7],
        pin_out,
        context_weight_grad,
        pout_out,
        vecs[8],
    )


def nt_dot(a, b):
    return lax.dot_general(a, b, (((1,), (1,)), ((), ())), preferred_element_type=f32)


def group_total(x):
    per = x.shape[1] // GROUPS
    lane = lax.broadcasted_iota(jnp.int32, x.shape, 1)
    n = x.shape[1]
    step = 1
    while step < per:
        upper = (lane // step) % 2 == 1
        x = x + jnp.where(upper, pltpu.roll(x, step, 1), pltpu.roll(x, n - step, 1))
        step *= 2
    return x


def total(v):
    return jnp.sum(v, axis=0, keepdims=True)


def put_shifts(buf, at, v, wide):
    n, ch = v.shape
    col = lax.rem(lax.broadcasted_iota(jnp.int32, (n, 1), 0), wide)
    buf[pl.ds(at, n), pl.ds(ch, ch)] = v.astype(bf16)
    left = jnp.where(col == 0, 0.0, pltpu.roll(v, 1, 0))
    buf[pl.ds(at, n), pl.ds(0, ch)] = left.astype(bf16)
    right = jnp.where(col == wide - 1, 0.0, pltpu.roll(v, n - 1, 0))
    buf[pl.ds(at, n), pl.ds(2 * ch, ch)] = right.astype(bf16)


class Links:
    def __init__(self, nrow, nimg):
        self.nrow, self.nimg = nrow, nimg
        self.row, self.img = lax.axis_index("row"), lax.axis_index("img")

    def peer(self, axis, k):
        if axis == "row":
            return lax.rem(self.row + k, self.nrow)
        return lax.rem(self.img + k, self.nimg)

    def greet(self):
        barrier = pltpu.get_barrier_semaphore()
        for axis, n in (("row", self.nrow), ("img", self.nimg)):
            for k in range(1, n):
                pl.semaphore_signal(
                    barrier, inc=1, device_id={axis: self.peer(axis, k)}, device_id_type=MESH
                )

    def greeted(self):
        pl.semaphore_wait(pltpu.get_barrier_semaphore(), self.nrow + self.nimg - 2)

    def to(self, axis, at, src, dst, send, recv):
        return pltpu.make_async_remote_copy(
            src_ref=src,
            dst_ref=dst,
            send_sem=send,
            recv_sem=recv,
            device_id={axis: at},
            device_id_type=MESH,
        )

    def copy(self, axis, k, src, dst, send, recv):
        return self.to(axis, self.peer(axis, k), src, dst, send, recv)


class Stats:
    def __init__(self, links, src, dst, send, recv):
        self.links, self.src, self.dst, self.send, self.recv = links, src, dst, send, recv

    def start(self, stage, rows):
        links = self.links
        ch = rows[0].shape[1]
        blocks = [r[:, i * 128 : (i + 1) * 128] for r in rows for i in range(ch // 128)]
        height = self.src.shape[1]
        blocks = blocks + [jnp.zeros((1, 128), f32)] * (height - len(blocks))
        packed = jnp.concatenate(blocks, axis=0)
        self.src[stage] = packed
        self.dst[stage, links.row] = packed
        self.rows, self.per = len(rows), ch // 128
        self.copies = []
        for k in range(1, links.nrow):
            c = links.copy(
                "row",
                k,
                self.src.at[stage],
                self.dst.at[stage, links.row],
                self.send.at[stage, k - 1],
                self.recv.at[stage, k - 1],
            )
            c.start()
            self.copies.append(c)

    def finish(self, stage):
        for c in self.copies:
            c.wait()
        s = jnp.sum(self.dst[stage], axis=0)
        per = self.per
        rows = [
            jnp.concatenate([s[r * per + i : r * per + i + 1] for i in range(per)], axis=1)
            for r in range(self.rows)
        ]
        return jnp.concatenate(rows + [jnp.zeros((8 - self.rows, per * 128), f32)], axis=0)


class Halo:
    def __init__(self, links, out, land, send, recv, wide):
        self.links, self.out, self.land, self.wide = links, out, land, wide
        self.send, self.recv = send, recv

    def copies(self, stage):
        links, out, land = self.links, self.out, self.land
        down = links.copy(
            "row", links.nrow - 1, out.at[stage, 0], land.at[stage, 1],
            self.send.at[stage, 0], self.recv.at[stage, 1],
        )
        up = links.copy(
            "row", 1, out.at[stage, 1], land.at[stage, 0],
            self.send.at[stage, 1], self.recv.at[stage, 0],
        )
        return down, up

    def start(self, stage, first, last):
        links = self.links
        self.out[stage, 0] = first
        self.out[stage, 1] = last
        down, up = self.copies(stage)

        @pl.when(links.row > 0)
        def _():
            down.start()

        @pl.when(links.row < links.nrow - 1)
        def _():
            up.start()

        @pl.when(links.row == 0)
        def _():
            self.land[stage, 0] = jnp.zeros(first.shape, bf16)

        @pl.when(links.row == links.nrow - 1)
        def _():
            self.land[stage, 1] = jnp.zeros(first.shape, bf16)

    def finish(self, stage, buf):
        links = self.links
        down, up = self.copies(stage)

        @pl.when(links.row > 0)
        def _():
            down.wait_send()
            up.wait_recv()

        @pl.when(links.row < links.nrow - 1)
        def _():
            up.wait_send()
            down.wait_recv()

        wide = self.wide
        put_shifts(buf, 0, self.land[stage, 0].astype(f32), wide)
        put_shifts(buf, buf.shape[0] - wide, self.land[stage, 1].astype(f32), wide)


FRONT = (
    ("img", "oc", "pout", "par", "cxt", "emb", "w1h", "w2h", "winh", "cwh", "ewh")
    + ("hidden", "middle", "stats", "ss", "wt", "a3")
    + ("a1h", "a2h", "ctxh", "embh", "tgh", "atth", "ench")
    + ("w1", "w2", "win", "cw", "ctx", "ew", "buf", "at", "gs", "ts", "qkv", "g")
    + ("kx", "vx", "kt", "vt", "sb", "pb", "acc", "atb", "dqb", "dcb")
    + ("st_src", "st_dst", "h_out", "h_land")
    + ("wsem", "st_send", "st_recv", "h_send", "h_recv", "i_send", "i_recv", "r_send", "r_recv")
    + ("osem",)
)


def front_kernel(cfg, *refs):
    nrow, nimg, wide, ch, hd, kc = cfg
    R = dict(zip(FRONT, refs))
    px = R["img"].shape[0]
    members = float(nrow * px * (ch // GROUPS))
    links = Links(nrow, nimg)
    links.greet()
    head = links.row
    me = links.row

    def pair_at(at):
        return pl.ds(pl.multiple_of(at + (head // 2) * (2 * hd), 128), 2 * hd)

    loads = {
        "w1": (R["w1h"], R["w1"]),
        "ew": (R["ewh"], R["ew"]),
        "win": (R["winh"], R["win"]),
        "w2": (R["w2h"], R["w2"]),
        "ck": (R["cwh"].at[:, pair_at(0)], R["cw"].at[:, : 2 * hd]),
        "cv": (R["cwh"].at[:, pair_at(ch)], R["cw"].at[:, 2 * hd :]),
    }
    loads = {
        n: pltpu.make_async_copy(a, b, R["wsem"].at[i]) for i, (n, (a, b)) in enumerate(loads.items())
    }
    for c in loads.values():
        c.start()
    stats = Stats(links, R["st_src"], R["st_dst"], R["st_send"], R["st_recv"])
    halo = Halo(links, R["h_out"], R["h_land"], R["h_send"], R["h_recv"], wide)
    pending = []

    def par(i):
        return R["par"][i : i + 1, :]

    def share(slot, src, dst):
        copies = [pltpu.make_async_copy(src(links.img), dst(links.img), R["osem"].at[slot])]
        for k in range(1, nimg):
            copies.append(
                links.copy(
                    "img", k, src(links.peer("img", k)), dst(links.img),
                    R["i_send"].at[slot, k - 1], R["i_recv"].at[slot, k - 1],
                )
            )
        for c in copies:
            c.start()
        pending.extend(copies)

    def scatter(slot, src, dst):
        copies = []
        for k in range(1, nrow):
            copies.append(
                links.copy(
                    "row", k, src(links.peer("row", k)), dst(me),
                    R["r_send"].at[slot, k - 1], R["r_recv"].at[slot, k - 1],
                )
            )
        for c in copies:
            c.start()
        return copies

    def lanes(img):
        return pl.ds(pl.multiple_of(img * px, 128), px)

    def moments(v):
        return [total(v), total(v * v)]

    def center(stage, sums):
        means = group_total(sums) * (1.0 / members)
        mean = means[0:1]
        rstd = lax.rsqrt(means[1:2] - mean * mean + EPSILON)
        R["stats"][2 * stage : 2 * stage + 1, :] = mean
        R["stats"][2 * stage + 1 : 2 * stage + 2, :] = rstd
        return mean, rstd

    R["stats"][...] = jnp.zeros_like(R["stats"])
    rows = moments(R["img"][...].astype(f32))
    links.greeted()
    stats.start(0, rows)
    loads["ew"].wait()
    ss = nn(R["emb"][...].astype(bf16), R["ew"][...])[0:1]
    scale1 = 1.0 + (ss[:, :ch] + par(12))
    shift = ss[:, ch:] + par(13)
    R["ss"][...] = jnp.concatenate([scale1, shift, jnp.zeros((6, ch), f32)], axis=0)
    mean, rstd = center(0, stats.finish(0))

    def conv_stage(stage, act, weights):
        low = act.astype(bf16)
        buf = R["buf"]
        halo.start(stage, low[:wide], low[px - wide :])
        put_shifts(buf, wide, act, wide)
        acc = nn(buf[pl.ds(wide, px), :], weights[1])
        R["at"][stage] = low.T
        halo.finish(stage, buf)
        acc = acc + nn(buf[pl.ds(0, px), :], weights[0])
        return acc + nn(buf[pl.ds(2 * wide, px), :], weights[2])

    act = jax.nn.silu((R["img"][...].astype(f32) - mean) * rstd * par(0) + par(1))
    loads["w1"].wait()
    hidden = conv_stage(0, act, R["w1"]) + par(2)
    R["hidden"][...] = hidden
    stats.start(1, moments(hidden))
    loads["win"].wait()
    turned = R["win"][...].T
    for h in range(HEADS):
        for j in range(3):
            R["wt"][(3 * h + j) * hd : (3 * h + j + 1) * hd, :] = turned[
                j * ch + h * hd : j * ch + (h + 1) * hd
            ]
    low = (R["oc"][...].astype(f32) * par(10)).astype(bf16)
    R["gs"][...] = nt_dot(R["pout"][...], low).astype(bf16).reshape(R["gs"].shape)
    mean, rstd = center(1, stats.finish(1))
    affine = (R["hidden"][...] - mean) * rstd * par(3) + par(4)
    act = jax.nn.silu(affine * R["ss"][0:1] + R["ss"][1:2])
    loads["w2"].wait()
    middle = R["img"][...].astype(f32) + conv_stage(1, act, R["w2"]) + par(7)
    R["middle"][...] = middle
    stats.start(2, moments(middle))
    nctx, text = R["cxt"].shape
    padc = R["ctx"].shape[0]
    R["ctx"][...] = jnp.concatenate(
        [R["cxt"][...], jnp.zeros((padc - nctx, text), bf16)], axis=0
    )
    loads["ck"].wait()
    loads["cv"].wait()
    enc = nn(R["ctx"][...], R["cw"][...]).T.astype(bf16)
    first = lax.rem(head, 2) == 0
    enc = jnp.concatenate(
        [
            jnp.where(first, enc[2 * j * hd : (2 * j + 1) * hd], enc[(2 * j + 1) * hd : (2 * j + 2) * hd])
            for j in range(2)
        ],
        axis=0,
    )
    mean, rstd = center(2, stats.finish(2))
    act3 = ((R["middle"][...] - mean) * rstd * par(8) + par(9)).astype(bf16)
    R["a3"][...] = act3.T
    ts, qkv, gs, g = R["ts"], R["qkv"], R["gs"], R["g"]
    ts[...] = nn(R["wt"][...], R["a3"][...]).astype(bf16).reshape(ts.shape)
    c_kv = scatter(0, lambda r: ts.at[r, pl.ds(hd, 2 * hd)], lambda r: qkv.at[r, pl.ds(hd, 2 * hd)])
    c_q = scatter(1, lambda r: ts.at[r, pl.ds(0, hd)], lambda r: qkv.at[r, pl.ds(0, hd)])
    c_g = scatter(2, lambda r: gs.at[r], lambda r: g.at[r])
    for i in range(2):
        share(i, lambda p, i=i: R["at"].at[i], lambda p, i=i: R[("a1h", "a2h")[i]].at[:, lanes(p)])
    mine = text // nrow
    text_at = pl.ds(pl.multiple_of(me * mine, 128), mine)
    share(2, lambda p: R["ctx"].at[:, text_at], lambda p: R["ctxh"].at[p])
    wide_emb = R["emb"].shape[1] // nrow
    emb_at = pl.ds(pl.multiple_of(me * wide_emb, 128), wide_emb)
    share(3, lambda p: R["emb"].at[:, emb_at], lambda p: R["embh"].at[p])

    npix = nrow * px
    ones_rows = jnp.where(lax.broadcasted_iota(jnp.int32, (hd, px), 0) < 2, 1.0, 0.0).astype(bf16)
    kx, vx, kt, vt, sb, pb, acc = (R[n] for n in ("kx", "vx", "kt", "vt", "sb", "pb", "acc"))

    def fill(pair, at, w):
        k = pair[:hd].astype(f32) * (LOG2E * 0.125)
        hi = k.astype(bf16)
        lo = (k - hi.astype(f32)).astype(bf16)
        kx[pl.ds(at, w), :] = jnp.concatenate([hi, lo], axis=0).T
        vfull = jnp.concatenate([pair[hd:], ones_rows[:, :w]], axis=0)
        vx[pl.ds(at, w), :] = vfull.T
        kt[:, pl.ds(at, w)] = pair[:hd]
        vt[:, pl.ds(at, w)] = vfull[: hd + 16]

    fill(enc, npix, padc)
    qkv[me] = ts[me]
    g[me] = gs[me]
    acc[...] = jnp.zeros_like(acc)

    def own(r):
        return pl.multiple_of(r * px, 128)

    fill(ts[me, hd:], own(me), px)
    for k in range(1, nrow):
        c_kv[k - 1].wait()
        frm = lax.rem(me + nrow - k, nrow)
        fill(qkv[frm, hd:], own(frm), px)

    bq = px
    nfull = npix // kc

    def out_copies(i):
        at = lax.rem(me + nrow - i, nrow)
        a = links.to(
            "row", at, R["atb"].at[at], R["atth"].at[me],
            R["r_send"].at[3, i - 1], R["r_recv"].at[3, i - 1],
        )
        d = links.to(
            "row", at, R["dqb"].at[at, pl.ds(0, hd)], R["tgh"].at[me, pl.ds(0, hd)],
            R["r_send"].at[4, i - 1], R["r_recv"].at[4, i - 1],
        )
        return a, d

    def block(i, _):
        s = lax.rem(me + nrow - i, nrow)

        @pl.when(i > 0)
        def _():
            links.to(
                "row", s, ts.at[s, pl.ds(0, hd)], qkv.at[s, pl.ds(0, hd)],
                R["r_send"].at[1, i - 1], R["r_recv"].at[1, i - 1],
            ).wait_recv()
            links.to(
                "row", s, gs.at[s], g.at[s], R["r_send"].at[2, i - 1], R["r_recv"].at[2, i - 1]
            ).wait_recv()

        qt = qkv[s, :hd]
        gt = g[s]
        q2 = jnp.concatenate([qt, qt], axis=0)
        sc = nn(kx[pl.ds(npix, padc), :], q2)
        sc = jnp.where(lax.broadcasted_iota(jnp.int32, (padc, bq), 0) < nctx, sc, -jnp.inf)
        sb[pl.ds(npix, padc), :] = sc
        m8 = jnp.max(sc.reshape(padc // 8, 8, bq), axis=0)

        def phase_a(c, m8):
            at = pl.multiple_of(c * kc, kc)
            sv = nn(kx[pl.ds(at, kc), :], q2)
            sb[pl.ds(at, kc), :] = sv
            return jnp.maximum(m8, jnp.max(sv.reshape(kc // 8, 8, bq), axis=0))

        m8 = lax.fori_loop(0, nfull, phase_a, m8, unroll=True)
        m = jnp.max(m8, axis=0, keepdims=True)
        pc = jnp.exp2(sb[pl.ds(npix, padc), :] - m).astype(bf16)
        pb[pl.ds(npix, padc), :] = pc
        o = nn(vt[:, npix : npix + padc], pc)

        def phase_b(c, o):
            at = pl.multiple_of(c * kc, kc)
            p = jnp.exp2(sb[pl.ds(at, kc), :] - m).astype(bf16)
            pb[pl.ds(at, kc), :] = p
            return o + nn(vt[:, pl.ds(at, kc)], p)

        o = lax.fori_loop(0, nfull, phase_b, o, unroll=True)
        inv = 1.0 / o[hd : hd + 1]
        att = o[:hd] * inv
        R["atb"][s] = att.astype(bf16)
        gf = gt.astype(f32)
        delta = total(gf * att) * inv
        gl = (gf * inv).astype(bf16)
        dhi = (-delta).astype(bf16)
        dlo = (-delta - dhi.astype(f32)).astype(bf16)
        gx = jnp.concatenate([gl, dhi, dlo, jnp.zeros((hd - 2, bq), bf16)], axis=0)
        zero = jnp.zeros((hd, bq), bf16)
        rq = jnp.concatenate([qt, zero], axis=0).T
        rg = jnp.concatenate([zero, gl], axis=0).T
        rr = jnp.concatenate([rq, rg], axis=0)

        def piece(at, w, dq):
            p = pb[pl.ds(at, w), :]
            dp = nn(vx[pl.ds(at, w), :], gx)
            ds = (p.astype(f32) * dp).astype(bf16)
            acc[pl.ds(at, w), :] += nn(jnp.concatenate([ds, p], axis=1), rr)
            return dq + nn(kt[:, pl.ds(at, w)], ds)

        dq = piece(npix, padc, jnp.zeros((hd, bq), f32))

        def phase_d(c, dq):
            return piece(pl.multiple_of(c * kc, kc), kc, dq)

        dq = lax.fori_loop(0, nfull, phase_d, dq, unroll=True)
        R["dqb"][s, :hd] = (dq * 0.125).astype(bf16)

        @pl.when(i > 0)
        def _():
            for c in out_copies(i):
                c.start()

        return 0

    lax.fori_loop(0, nrow, block, 0)
    scale = jnp.where(lax.broadcasted_iota(jnp.int32, (1, 2 * hd), 1) < hd, 0.125, 1.0)
    copies = []
    for k in range(1, nrow):
        s = links.peer("row", k)
        R["dqb"][s, hd:] = (acc[pl.ds(own(s), px), :] * scale).astype(bf16).T
        c = links.copy(
            "row", k, R["dqb"].at[s, pl.ds(hd, 2 * hd)], R["tgh"].at[me, pl.ds(hd, 2 * hd)],
            R["r_send"].at[5, k - 1], R["r_recv"].at[5, k - 1],
        )
        c.start()
        copies.append(c)
    R["dcb"][...] = (acc[npix : npix + padc, :] * scale).astype(bf16)
    copies += scatter(6, lambda r: R["dcb"], lambda r: R["ench"].at[r])
    R["dqb"][me, hd:] = (acc[pl.ds(own(me), px), :] * scale).astype(bf16).T
    for i, (a, b) in enumerate(
        (
            (R["dqb"].at[me], R["tgh"].at[me]),
            (R["atb"].at[me], R["atth"].at[me]),
            (R["dcb"], R["ench"].at[me]),
        )
    ):
        c = pltpu.make_async_copy(a, b, R["osem"].at[4 + i])
        c.start()
        copies.append(c)
    for c in c_q + c_g:
        c.wait_send()
    for k in range(1, nrow):
        for c in out_copies(k):
            c.wait()
    for c in copies + pending:
        c.wait()


def front(images, out_cot, project_out, par, context, emb, w1, w2, win, cw, ew, nrow, nimg, wide):
    px, ch = images.shape
    hd = ch // HEADS
    padc = -(-context.shape[0] // 16) * 16
    cfg = (nrow, nimg, wide, ch, hd, 512)
    nk = nrow * px + padc
    V = pl.BlockSpec(memory_space=pltpu.VMEM)
    A = pl.BlockSpec(memory_space=pl.ANY)
    S = jax.ShapeDtypeStruct
    M = pltpu.VMEM
    dma = pltpu.SemaphoreType.DMA
    return pl.pallas_call(
        functools.partial(front_kernel, cfg),
        out_shape=(
            S((px, ch), f32),
            S((px, ch), f32),
            S((8, ch), f32),
            S((8, ch), f32),
            S((3 * ch, ch), bf16),
            S((ch, px), bf16),
            S((ch, nimg * px), bf16),
            S((ch, nimg * px), bf16),
            S((nimg, padc, context.shape[1] // nrow), bf16),
            S((nimg, 8, emb.shape[1] // nrow), f32),
            S((nrow, 3 * hd, px), bf16),
            S((nrow, hd, px), bf16),
            S((nrow, padc, 2 * hd), bf16),
        ),
        in_specs=[V] * 6 + [A] * 5,
        out_specs=(V,) * 6 + (A,) * 7,
        scratch_shapes=[
            M(w1.shape, bf16),
            M(w2.shape, bf16),
            M(win.shape, bf16),
            M((cw.shape[0], 4 * hd), bf16),
            M((padc, cw.shape[0]), bf16),
            M(ew.shape, bf16),
            M((px + 2 * wide, 3 * ch), bf16),
            M((2, ch, px), bf16),
            M((nrow, hd, px), bf16),
            M((nrow, 3 * hd, px), bf16),
            M((nrow, 3 * hd, px), bf16),
            M((nrow, hd, px), bf16),
            M((nk, 2 * hd), bf16),
            M((nk, 2 * hd), bf16),
            M((hd, nk), bf16),
            M((hd + 16, nk), bf16),
            M((nk, px), f32),
            M((nk, px), bf16),
            M((nk, 2 * hd), f32),
            M((nrow, hd, px), bf16),
            M((nrow, 3 * hd, px), bf16),
            M((padc, 2 * hd), bf16),
            M((3, 8, 128), f32),
            M((3, nrow, 8, 128), f32),
            M((2, 2, wide, ch), bf16),
            M((2, 2, wide, ch), bf16),
            dma((6,)),
            dma((3, nrow - 1)),
            dma((3, nrow - 1)),
            dma((2, 2)),
            dma((2, 2)),
            dma((4, nimg - 1)),
            dma((4, nimg - 1)),
            dma((7, nrow - 1)),
            dma((7, nrow - 1)),
            dma((8,)),
        ],
        compiler_params=pltpu.CompilerParams(
            collective_id=3, has_side_effects=True, vmem_limit_bytes=62 * 2**20
        ),
        name="front",
    )(images, out_cot, project_out, par, context, emb, w1, w2, win, cw, ew)
def slope(values):
    sig = jax.nn.sigmoid(values)
    return sig * (1.0 + values * (1.0 - sig))


BACK = (
    ("img", "oc", "par", "ss", "stats", "hidden", "middle", "a3", "tg", "att", "wt")
    + ("w2h", "w1h", "a2h", "a1h", "ench", "ctxh")
    + ("igrad", "kq", "oq", "cr", "every")
    + ("w2", "w1", "a2", "a1", "enc", "ctx")
    + ("mg", "ntg", "buf", "gq", "gs", "ks", "kx", "km", "kz", "kf")
    + ("os", "ox", "oy", "oz", "of", "encq", "cq", "vsrc")
    + ("st_src", "st_dst", "h_out", "h_land")
    + ("lsem", "st_send", "st_recv", "h_send", "h_recv", "i_send", "i_recv", "r_send", "r_recv")
    + ("x_send", "x_recv", "z_send", "z_recv", "osem")
)


def back_kernel(cfg, *refs):
    nrow, nimg, wide, ch, hd, padc = cfg
    R = dict(zip(BACK, refs))
    px = R["img"].shape[0]
    part = ch // nimg
    rows = ch // nrow
    deep = nrow // 2
    members = float(nrow * px * (ch // GROUPS))
    links = Links(nrow, nimg)
    links.greet()
    loads = {}
    for i, n in enumerate(("w2", "a2", "w1", "a1", "enc", "ctx")):
        loads[n] = pltpu.make_async_copy(R[n + "h"], R[n], R["lsem"].at[i])
        loads[n].start()
    stats = Stats(links, R["st_src"], R["st_dst"], R["st_send"], R["st_recv"])
    halo = Halo(links, R["h_out"], R["h_land"], R["h_send"], R["h_recv"], wide)
    row_z, row_x = links.row // 2, lax.rem(links.row, 2)
    img_y, img_c = links.img // 2, lax.rem(links.img, 2)

    def par(i):
        return R["par"][i : i + 1, :]

    def stat(i):
        return R["stats"][i : i + 1, :]

    scale1, shift = R["ss"][0:1], R["ss"][1:2]

    def share(slot, src, dst):
        copies = [pltpu.make_async_copy(src(links.img), dst(links.img), R["osem"].at[slot])]
        for k in range(1, nimg):
            copies.append(
                links.copy(
                    "img", k, src(links.peer("img", k)), dst(links.img),
                    R["i_send"].at[slot, k - 1], R["i_recv"].at[slot, k - 1],
                )
            )
        for c in copies:
            c.start()
        return copies

    def wait(copies):
        for c in copies:
            c.wait()

    def columns(at, img):
        return pl.ds(pl.multiple_of(at + img * part, 128), part)

    def row_x_start(slot, src, land):
        c = links.to(
            "row", links.row + 1 - 2 * row_x, src.at[:, 1 - row_x], land,
            R["x_send"].at[slot], R["x_recv"].at[slot],
        )
        c.start()
        return c

    def row_z_start(slot, c, src, land, mid, last):
        c.wait()
        mid[...] = (src[:, row_x].astype(f32) + land[...].astype(f32)).astype(bf16)
        copies = []
        for k in range(1, deep):
            z = lax.rem(row_z + k, deep)
            copies.append(
                links.to(
                    "row", 2 * z + row_x, mid.at[z], last.at[k - 1],
                    R["z_send"].at[slot, k - 1], R["z_recv"].at[slot, k - 1],
                )
            )
        for d in copies:
            d.start()
        return copies

    def row_end(copies, mid, last):
        wait(copies)
        s = mid[row_z].astype(f32)
        for k in range(1, deep):
            s = s + last[k - 1].astype(f32)
        return s.astype(bf16)

    def norm_back(u, normed, rstd, gain, gain_sum, bias_sum):
        both = jnp.concatenate([gain * bias_sum, gain * gain_sum, jnp.zeros((6, ch), f32)], axis=0)
        means = group_total(both) * (1.0 / members)
        return rstd * (u * gain - means[0:1] - normed * means[1:2])

    def conv_back(stage, grad, weights):
        low = grad.astype(bf16)
        buf = R["buf"].at[stage]
        halo.start(stage, low[:wide], low[px - wide :])
        put_shifts(buf, wide, grad, wide)

        def taps(ky, acc):
            for kx in range(3):
                g = buf[pl.ds(ky * wide, px), pl.ds(kx * ch, ch)]
                w = weights[2 - ky, pl.ds((2 - kx) * ch, ch), :]
                d = nt_dot(g, w)
                acc = d if acc is None else acc + d
            return acc

        acc = taps(1, None)
        halo.finish(stage, buf)
        copies = share(
            stage, lambda i: buf.at[:, columns(ch, i)], lambda i: R["gq"].at[stage, i]
        )
        acc = taps(0, acc)
        return taps(2, acc), copies

    def kernel_grads(stage, acts, copies):
        wait(copies)
        for b in range(nimg):
            put_shifts(R["gs"].at[b], 0, R["gq"][stage, b].astype(f32), wide)
        sent = []
        for ky in range(3):
            tot = None
            for b in range(nimg):
                d = nn(acts[:, b * px : (b + 1) * px], R["gs"][b, ky * wide : ky * wide + px, :])
                tot = d if tot is None else tot + d
            R["ks"][stage, ky] = tot.astype(bf16).reshape(deep, 2, rows, 3 * part)
            sent.append(row_x_start(3 * stage + ky, R["ks"].at[stage, ky], R["kx"].at[stage, ky]))
        return sent

    def kernel_mid(stage, sent):
        return [
            row_z_start(
                3 * stage + ky, sent[ky], R["ks"].at[stage, ky], R["kx"].at[stage, ky],
                R["km"].at[stage, ky], R["kz"].at[stage, ky],
            )
            for ky in range(3)
        ]

    def kernel_end(stage, copies):
        out = []
        for ky in range(3):
            R["kf"][stage, ky] = row_end(copies[ky], R["km"].at[stage, ky], R["kz"].at[stage, ky])
            out += share(
                2 + 3 * stage + ky,
                lambda i, ky=ky: R["kf"].at[stage, ky],
                lambda i, ky=ky: R["kq"].at[stage, ky, i],
            )
        return out

    tgt = R["tg"][...].reshape(3 * ch, px)
    u3 = nn(tgt.T, R["wt"][...])
    normed3 = (R["middle"][...] - stat(4)) * stat(5)
    grad_out = R["oc"][...].astype(f32) * par(10)
    R["mg"][...] = u3
    sums = [total(u3 * normed3), total(u3), total(grad_out)]
    links.greeted()
    stats.start(0, sums)
    loads["enc"].wait()
    c_encq = share(8, lambda i: R["enc"].at[pl.ds(2 * i, 2)], lambda i: R["encq"].at[i])
    a3 = R["a3"][...]
    low = (R["oc"][...].astype(f32) * par(10)).astype(bf16)
    pout = nn(R["att"][...].reshape(ch, px), low).astype(bf16)
    for q in range(nimg):
        pin = nt_dot(a3, R["tg"][2 * q : 2 * q + 2].reshape(6 * hd, px)).astype(bf16)
        R["os"][q // 2, q % 2] = jnp.concatenate(
            [pin, pout[:, q * part : (q + 1) * part]], axis=1
        )
    c_ox = links.to(
        "img", links.img + 1 - 2 * img_c, R["os"].at[:, 1 - img_c], R["ox"],
        R["i_send"].at[9, 0], R["i_recv"].at[9, 0],
    )
    c_ox.start()
    sums3 = stats.finish(0)
    normed3 = (R["middle"][...] - stat(4)) * stat(5)
    grad_out = R["oc"][...].astype(f32) * par(10)
    middle_grad = grad_out + norm_back(
        R["mg"][...], normed3, stat(5), par(8), sums3[0:1], sums3[1:2]
    )
    R["mg"][...] = middle_grad
    loads["w2"].wait()
    act_grad, c_g2 = conv_back(0, middle_grad, R["w2"])
    normed2 = (R["hidden"][...] - stat(2)) * stat(3)
    ntg = act_grad * slope((normed2 * par(3) + par(4)) * scale1 + shift)
    R["ntg"][...] = ntg
    stats.start(1, [total(ntg * normed2), total(ntg)])
    middle_sum = total(R["mg"][...])
    loads["a2"].wait()
    c_k2 = kernel_grads(0, R["a2"], c_g2)
    c_ox.wait()
    R["os"][:, 0] = (
        R["os"][:, img_c].astype(f32) + R["ox"][...].astype(f32)
    ).astype(bf16)
    c_oy = links.to(
        "img", lax.rem(links.img + 2, nimg), R["os"].at[1 - img_y, 0], R["oy"],
        R["i_send"].at[9, 1], R["i_recv"].at[9, 1],
    )
    c_oy.start()
    sums2 = stats.finish(1)
    normed2 = (R["hidden"][...] - stat(2)) * stat(3)
    hidden_grad = norm_back(
        R["ntg"][...] * scale1, normed2, stat(3), par(3), scale1 * sums2[0:1], scale1 * sums2[1:2]
    )
    hidden_sum = total(hidden_grad)
    loads["w1"].wait()
    act_grad, c_g1 = conv_back(1, hidden_grad, R["w1"])
    normed1 = (R["img"][...].astype(f32) - stat(0)) * stat(1)
    n1g = act_grad * slope(normed1 * par(0) + par(1))
    R["ntg"][...] = n1g
    stats.start(2, [total(n1g * normed1), total(n1g), hidden_sum, middle_sum])
    c_k2 = kernel_mid(0, c_k2)
    loads["a1"].wait()
    c_k1 = kernel_grads(1, R["a1"], c_g1)
    c_oy.wait()
    both = R["os"][img_y, 0].astype(f32) + R["oy"][...].astype(f32)
    R["of"][...] = both.astype(bf16).reshape(deep, 2, rows, 6 * hd + part)
    c_o = row_x_start(6, R["of"], R["oz"].at[0])
    sums1 = stats.finish(2)
    scale_grad = par(3) * sums2[0:1] + par(4) * sums2[1:2]
    R["vsrc"][...] = jnp.concatenate(
        [
            sums1[0:3],
            scale1 * sums2[0:1],
            scale1 * sums2[1:2],
            sums1[3:4],
            sums3[0:3],
            scale_grad,
            sums2[1:2],
            jnp.zeros((5, ch), f32),
        ],
        axis=0,
    )
    out = share(10, lambda i: R["vsrc"], lambda i: R["every"].at[i])
    c_k1 = kernel_mid(1, c_k1)
    normed1 = (R["img"][...].astype(f32) - stat(0)) * stat(1)
    R["igrad"][...] = R["mg"][...] + norm_back(
        R["ntg"][...], normed1, stat(1), par(0), sums1[0:1], sums1[1:2]
    )
    c_o = row_z_start(6, c_o, R["of"], R["oz"].at[0], R["oz"].at[1], R["oz"].at[2, pl.ds(0, deep - 1)])
    out += kernel_end(0, c_k2)
    wait(c_encq)
    loads["ctx"].wait()
    turned = R["ctx"][...].reshape(nimg * padc, -1).T
    pairs = jnp.concatenate([R["encq"][:, 0], R["encq"][:, 1]], axis=2)
    R["cq"][...] = nn(turned, pairs.reshape(nimg * padc, 4 * hd)).astype(bf16)
    out += share(11, lambda i: R["cq"], lambda i: R["cr"].at[i])
    out += kernel_end(1, c_k1)
    R["oy"][:rows] = row_end(c_o, R["oz"].at[1], R["oz"].at[2])
    out += share(12, lambda i: R["oy"].at[pl.ds(0, rows)], lambda i: R["oq"].at[i])
    wait(out)


def backward(nrow, nimg, wide, *args):
    px, ch = args[0].shape
    hd = ch // HEADS
    ctx, enc = args[16], args[15]
    padc = enc.shape[1]
    cfg = (nrow, nimg, wide, ch, hd, padc)
    part, rows, deep = ch // nimg, ch // nrow, nrow // 2
    proj = 6 * hd + part
    V = pl.BlockSpec(memory_space=pltpu.VMEM)
    A = pl.BlockSpec(memory_space=pl.ANY)
    S = jax.ShapeDtypeStruct
    dma = pltpu.SemaphoreType.DMA
    M = pltpu.VMEM
    text = ctx.shape[2]
    return pl.pallas_call(
        functools.partial(back_kernel, cfg),
        out_shape=(
            S((px, ch), f32),
            S((2, 3, nimg, rows, 3 * part), bf16),
            S((nimg, rows, proj), bf16),
            S((nimg, text, 4 * hd), bf16),
            S((nimg, 16, ch), f32),
        ),
        in_specs=[V] * 11 + [A] * 6,
        out_specs=(V,) + (A,) * 4,
        scratch_shapes=[
            M((3, 3 * ch, ch), bf16),
            M((3, 3 * ch, ch), bf16),
            M((ch, nimg * px), bf16),
            M((ch, nimg * px), bf16),
            M(enc.shape, bf16),
            M(ctx.shape, bf16),
            M((px, ch), f32),
            M((px, ch), f32),
            M((2, px + 2 * wide, 3 * ch), bf16),
            M((2, nimg, px + 2 * wide, part), bf16),
            M((nimg, px + 2 * wide, 3 * part), bf16),
            M((2, 3, deep, 2, rows, 3 * part), bf16),
            M((2, 3, deep, rows, 3 * part), bf16),
            M((2, 3, deep, rows, 3 * part), bf16),
            M((2, 3, deep - 1, rows, 3 * part), bf16),
            M((2, 3, rows, 3 * part), bf16),
            M((2, 2, ch, proj), bf16),
            M((2, ch, proj), bf16),
            M((ch, proj), bf16),
            M((3, deep, rows, proj), bf16),
            M((deep, 2, rows, proj), bf16),
            M((nimg, 2, padc, 2 * hd), bf16),
            M((text, 4 * hd), bf16),
            M((16, ch), f32),
            M((3, 16, 128), f32),
            M((3, nrow, 16, 128), f32),
            M((2, 2, wide, ch), bf16),
            M((2, 2, wide, ch), bf16),
            dma((6,)),
            dma((3, nrow - 1)),
            dma((3, nrow - 1)),
            dma((2, 2)),
            dma((2, 2)),
            dma((13, nimg - 1)),
            dma((13, nimg - 1)),
            dma((1, nrow - 1)),
            dma((1, nrow - 1)),
            dma((7,)),
            dma((7,)),
            dma((7, deep - 1)),
            dma((7, deep - 1)),
            dma((13,)),
        ],
        compiler_params=pltpu.CompilerParams(
            collective_id=4, has_side_effects=True, vmem_limit_bytes=60 * 2**20
        ),
        name="back",
    )(*args)


def finish_kernel(cfg, *refs):
    nrow, nimg, ch, hd, row_of = cfg
    (igrad, kq, oq, cr, every, emb, middle, att, pout, par) = refs[:10]
    (res, ig, k1g, k2g, ing, outg, ctxg, embg, vecs) = refs[10:]
    px = igrad.shape[0]
    part = ch // nimg
    ig[...] = igrad[...]
    attended = att[...].reshape(ch, px).T
    branch = nn(attended, pout[...])
    res[...] = (middle[...] + branch + par[11:12, :]).astype(bf16)
    for stage, out in ((0, k2g), (1, k1g)):
        for ky in range(3):
            for b in range(nimg):
                v = kq[stage, ky, b].astype(f32)
                for kx in range(3):
                    out[2 - ky, 2 - kx, :, b * part : (b + 1) * part] = v[
                        :, kx * part : (kx + 1) * part
                    ]
    for b in range(nimg):
        v = oq[b].astype(f32)
        for j in range(3):
            ing[:, j * ch + b * 2 * hd : j * ch + (b + 1) * 2 * hd] = jnp.concatenate(
                [v[:, j * hd : (j + 1) * hd], v[:, (3 + j) * hd : (4 + j) * hd]], axis=1
            )
        outg[:, b * part : (b + 1) * part] = v[:, 6 * hd :]
        v = cr[b].astype(f32)
        p = [v[:, j * hd : (j + 1) * hd] for j in range(4)]
        ctxg[:, b * 2 * hd : (b + 1) * 2 * hd] = jnp.concatenate([p[0], p[2]], axis=1)
        ctxg[:, ch + b * 2 * hd : ch + (b + 1) * 2 * hd] = jnp.concatenate([p[1], p[3]], axis=1)
    acts = emb[:, 0, :].T
    for j in range(2):
        d = None
        for b in range(nimg):
            t = acts[:, b : b + 1] * every[b, 9 + j : 10 + j]
            d = t if d is None else d + t
        embg[:, j * ch : (j + 1) * ch] = d
    vecs[...] = jnp.sum(every[...], axis=0)


def finish(nrow, nimg, *args):
    px, ch = args[0].shape
    hd = ch // HEADS
    cr, emb = args[3], args[5]
    rows = ch // nrow
    V = pl.BlockSpec(memory_space=pltpu.VMEM)
    S = jax.ShapeDtypeStruct
    return pl.pallas_call(
        functools.partial(finish_kernel, (nrow, nimg, ch, hd, 0)),
        out_shape=(
            S((px, ch), bf16),
            S((px, ch), f32),
            S((3, 3, rows, ch), f32),
            S((3, 3, rows, ch), f32),
            S((rows, 3 * ch), f32),
            S((rows, ch), f32),
            S((cr.shape[1], 2 * ch), f32),
            S((emb.shape[2], 2 * ch), f32),
            S((16, ch), f32),
        ),
        in_specs=[V] * 10,
        out_specs=(V,) * 9,
        compiler_params=pltpu.CompilerParams(vmem_limit_bytes=40 * 2**20),
        name="finish",
    )(*args)


def local_fast(
    images,
    timesteps,
    clip_embed,
    context,
    out_cotangent,
    item_weight,
    first_gain,
    first_bias,
    first_kernel,
    first_offset,
    embed_weight,
    embed_bias,
    second_gain,
    second_bias,
    second_kernel,
    second_offset,
    third_gain,
    third_bias,
    project_in,
    context_weight,
    project_out,
    output_bias,
):
    _, tall, wide, ch = images.shape
    pixels = tall * wide
    nrow = lax.axis_size("row")
    nimg = lax.axis_size("img")
    me_row = lax.axis_index("row")
    nctx = context.shape[1]
    image = images.reshape(pixels, ch)
    cotangent = out_cotangent.reshape(pixels, ch)
    weight = item_weight.astype(f32) * 0.25
    embedding = sinusoid(timesteps, clip_embed.shape[1]) + clip_embed.astype(f32)
    embed_act = jax.nn.silu(embedding).astype(bf16)
    zero = jnp.zeros((ch,), f32)
    par = jnp.stack(
        [
            first_gain,
            first_bias,
            first_offset,
            second_gain,
            second_bias,
            zero,
            zero,
            second_offset,
            third_gain,
            third_bias,
            jnp.broadcast_to(weight, (ch,)),
            output_bias,
            embed_bias[:ch],
            embed_bias[ch:],
            zero,
            zero,
        ]
    )
    emb = jnp.broadcast_to(embed_act.astype(f32), (8, embed_act.shape[1]))
    w1 = first_kernel.reshape(3, 3 * ch, ch)
    w2 = second_kernel.reshape(3, 3 * ch, ch)
    (
        hidden, middle, stats, ss, turned_in, act_three,
        acts_one, acts_two, ctx_parts, emb_parts, grads, attended, enc_grads,
    ) = front(
        image, cotangent, project_out, par, context[0], emb, w1, w2, project_in, context_weight,
        embed_weight, nrow, nimg, wide,
    )
    image_grad, kq, oq, cr, every = backward(
        nrow, nimg, wide,
        image, cotangent, par, ss, stats, hidden, middle, act_three, grads, attended, turned_in,
        w2, w1, acts_two, acts_one, enc_grads, ctx_parts,
    )
    result, image_grad, k1g, k2g, ing, outg, ctxg, embg, sums = finish(
        nrow, nimg, image_grad, kq, oq, cr, every, emb_parts, middle, attended, project_out, par
    )
    part = ch // nrow
    vecs = lax.dynamic_slice_in_dim(sums, me_row * part, part, 1)
    part_bias = 2 * ch // nrow
    bias = lax.dynamic_slice_in_dim(sums[9:11].reshape(2 * ch), me_row * part_bias, part_bias, 0)
    return (
        result.reshape(images.shape),
        image_grad.reshape(images.shape),
        vecs[0],
        vecs[1],
        k1g,
        vecs[2],
        embg,
        bias,
        vecs[3],
        vecs[4],
        k2g,
        vecs[5],
        vecs[6],
        vecs[7],
        ing,
        ctxg,
        outg,
        vecs[8],
    )


def solution(mesh):
    every = P()
    image = P("img", "row", None, None)
    placed = (image, P("img"), P("img", None), P("img", None, None), image, P("img")) + (every,) * 16
    vec = P("row")
    matrix = P("row", None)
    taps = P(None, None, "row", None)
    nimg, nrow = mesh.shape["img"], mesh.shape["row"]
    quick = nrow == HEADS and nimg == 4
    return jax.shard_map(
        local_fast if quick else local,
        mesh=mesh,
        in_specs=placed,
        out_specs=(
            image,
            image,
            vec,
            vec,
            taps,
            vec,
            matrix,
            vec,
            vec,
            vec,
            taps,
            vec,
            vec,
            vec,
            matrix,
            matrix,
            matrix,
            vec,
        ),
        check_vma=False,
    )
```

```python
import functools
import math

import jax
import jax.numpy as jnp
from jax import lax
from jax.experimental import pallas as pl
from jax.experimental.pallas import tpu as pltpu
from jax.sharding import PartitionSpec as P

HEADS = 8
GROUPS = 32
EPSILON = 1e-05
f32 = jnp.float32
bf16 = jnp.bfloat16
MESH = pl.DeviceIdType.MESH
LOG2E=math.log2(math.e)

def nt(a,b):
    return lax.dot_general(a,b,(((1,),(1,)),((),())),preferred_element_type=f32)
def nn(a,b):
    return jnp.dot(a,b,preferred_element_type=f32)

def attn_kernel(cfg, *refs):
    if cfg[0]:
        q_ref, ctx_ref, g_ref, out_ref, dq_ref, dctx_ref = refs[:6]
        kv_ref, dkv_ref = q_ref, dq_ref
        at_kv = cfg[-1]
    else:
        q_ref, kv_ref, ctx_ref, g_ref, out_ref, dq_ref, dkv_ref, dctx_ref = refs[:8]
        at_kv = 0
    (kx, vx, kt, vt, sbuf, pbuf, acc) = refs[-7:]
    joined, nqs, nsrc, width, bq, kc, nctx, padc, hd = cfg
    npix = nsrc*width
    nk = npix + padc
    ones_rows = jnp.where(lax.broadcasted_iota(jnp.int32,(hd,width),0)<2,1.0,0.0).astype(bf16)
    def fill(pair, at, w):
        k = pair[:hd].astype(f32)*(LOG2E*0.125)
        hi = k.astype(bf16)
        lo = (k-hi.astype(f32)).astype(bf16)
        kx[pl.ds(at,w),:] = jnp.concatenate([hi,lo],axis=0).T
        vfull = jnp.concatenate([pair[hd:], ones_rows[:, :w]],axis=0)
        vx[pl.ds(at,w),:] = vfull.T
        return vfull
    for s in range(nsrc):
        pair = kv_ref[s, at_kv:]
        vfull = fill(pair, s*width, width)
        kt[:, s*width:(s+1)*width] = pair[:hd]
        vt[:, s*width:(s+1)*width] = vfull[:hd+16]
    cpair = ctx_ref[...]
    vfull = fill(cpair, npix, padc)
    kt[:, npix:npix+padc] = cpair[:hd]
    vt[:, npix:npix+padc] = vfull[:hd+16]
    acc[...] = jnp.zeros_like(acc)

    nfull = npix//kc
    per = width//bq
    def block(j, _):
        s = j//per
        off = pl.multiple_of((j%per)*bq, bq)
        qt = q_ref[s,:hd,pl.ds(off,bq)]
        gt = g_ref[s,:,pl.ds(off,bq)]
        q2 = jnp.concatenate([qt,qt],axis=0)
        sc = nn(kx[pl.ds(npix,padc),:], q2)
        sc = jnp.where(lax.broadcasted_iota(jnp.int32,(padc,bq),0)<nctx, sc, -jnp.inf)
        sbuf[pl.ds(npix,padc),:] = sc
        m8 = jnp.max(sc.reshape(padc//8,8,bq),axis=0)
        def phase_a(c, m8):
            at = pl.multiple_of(c*kc,kc)
            sv = nn(kx[pl.ds(at,kc),:], q2)
            sbuf[pl.ds(at,kc),:] = sv
            return jnp.maximum(m8, jnp.max(sv.reshape(kc//8,8,bq),axis=0))
        m8 = lax.fori_loop(0,nfull,phase_a,m8,unroll=True)
        m = jnp.max(m8,axis=0,keepdims=True)
        pc = jnp.exp2(sbuf[pl.ds(npix,padc),:]-m).astype(bf16)
        pbuf[pl.ds(npix,padc),:] = pc
        o = nn(vt[:,npix:npix+padc], pc)
        def phase_b(c, o):
            at = pl.multiple_of(c*kc,kc)
            p = jnp.exp2(sbuf[pl.ds(at,kc),:]-m).astype(bf16)
            pbuf[pl.ds(at,kc),:] = p
            return o + nn(vt[:,pl.ds(at,kc)], p)
        o = lax.fori_loop(0,nfull,phase_b,o,unroll=True)
        inv = 1.0/o[hd:hd+1]
        att = o[:hd]*inv
        out_ref[s,:,pl.ds(off,bq)] = att.astype(bf16)
        gf = gt.astype(f32)
        delta = jnp.sum(gf*att,axis=0,keepdims=True)*inv
        gl = (gf*inv).astype(bf16)
        dhi = (-delta).astype(bf16)
        dlo = (-delta-dhi.astype(f32)).astype(bf16)
        gx = jnp.concatenate([gl,dhi,dlo,jnp.zeros((hd-2,bq),bf16)],axis=0)
        zero = jnp.zeros((hd,bq),bf16)
        rq = jnp.concatenate([qt,zero],axis=0).T
        rg = jnp.concatenate([zero,gl],axis=0).T
        rr = jnp.concatenate([rq,rg],axis=0)
        def piece(at, w, dq):
            p = pbuf[pl.ds(at,w),:]
            dp = nn(vx[pl.ds(at,w),:], gx)
            ds = (p.astype(f32)*dp).astype(bf16)
            acc[pl.ds(at,w),:] += nn(jnp.concatenate([ds,p],axis=1), rr)
            return dq + nn(kt[:,pl.ds(at,w)], ds)
        dq = piece(npix, padc, jnp.zeros((hd,bq),f32))
        def phase_d(c, dq):
            return piece(pl.multiple_of(c*kc,kc), kc, dq)
        dq = lax.fori_loop(0,nfull,phase_d,dq,unroll=True)
        dq_ref[s,:hd,pl.ds(off,bq)] = (dq*0.125).astype(bf16)
        return 0
    lax.fori_loop(0, nqs*per, block, 0)
    scale = jnp.where(lax.broadcasted_iota(jnp.int32,(1,2*hd),1)<hd,0.125,1.0)
    for s in range(nsrc):
        dkv_ref[s, at_kv:] = (acc[s*width:(s+1)*width,:]*scale).astype(bf16).T
    dctx_ref[...] = (acc[npix:npix+padc,:]*scale).astype(bf16)

def attention(q, kv, ctx, g, nctx, bq=512, kc=512):
    joined = kv is None
    nqs, _, width = q.shape
    hd = g.shape[1]
    nsrc = nqs if joined else kv.shape[0]
    padc = ctx.shape[1]
    nk = nsrc*width+padc
    cfg=(joined,nqs,nsrc,width,bq,kc,nctx,padc,hd)
    V=pl.BlockSpec(memory_space=pltpu.VMEM)
    S=jax.ShapeDtypeStruct
    grads=(S((nqs,3*hd,width),bf16),) if joined else (S((nqs,hd,width),bf16),S((nsrc,2*hd,width),bf16))
    args=(q,ctx,g) if joined else (q,kv,ctx,g)
    return pl.pallas_call(
        functools.partial(attn_kernel,cfg),
        out_shape=(S((nqs,hd,width),bf16),)+grads+(S((padc,2*hd),bf16),),
        in_specs=[V]*len(args), out_specs=(V,)*(2+len(grads)),
        scratch_shapes=[pltpu.VMEM((nk,2*hd),bf16),pltpu.VMEM((nk,2*hd),bf16),
                        pltpu.VMEM((hd,nk),bf16),pltpu.VMEM((hd+16,nk),bf16),
                        pltpu.VMEM((nk,bq),f32),pltpu.VMEM((nk,bq),bf16),
                        pltpu.VMEM((nk,2*hd),f32)],
        compiler_params=pltpu.CompilerParams(vmem_limit_bytes=48*2**20),
        cost_estimate=pl.CostEstimate(flops=6*2*64*4096*4228,bytes_accessed=8*2**20,transcendentals=4096*4228),
        name="attend",
    )(*args)

def exchange_kernel(axis, n, x_ref, out_ref, send_sem, recv_sem):
    me = lax.axis_index(axis)
    barrier = pltpu.get_barrier_semaphore()
    for k in range(1, n):
        pl.semaphore_signal(
            barrier, inc=1, device_id={axis: lax.rem(me + k, n)}, device_id_type=MESH
        )
    out_ref[me] = x_ref[...]
    pl.semaphore_wait(barrier, n - 1)
    copies = []
    for k in range(1, n):
        copy = pltpu.make_async_remote_copy(
            src_ref=x_ref,
            dst_ref=out_ref.at[me],
            send_sem=send_sem.at[k - 1],
            recv_sem=recv_sem.at[k - 1],
            device_id={axis: lax.rem(me + k, n)},
            device_id_type=MESH,
        )
        copy.start()
        copies.append(copy)
    for copy in copies:
        copy.wait()


def exchange(x, axis, cid):
    n = lax.axis_size(axis)
    V = pl.BlockSpec(memory_space=pltpu.VMEM)
    return pl.pallas_call(
        functools.partial(exchange_kernel, axis, n),
        out_shape=jax.ShapeDtypeStruct((n,) + x.shape, x.dtype),
        in_specs=[V],
        out_specs=V,
        scratch_shapes=[
            pltpu.SemaphoreType.DMA((n - 1,)),
            pltpu.SemaphoreType.DMA((n - 1,)),
        ],
        compiler_params=pltpu.CompilerParams(collective_id=cid, has_side_effects=True),
        name="exchange_" + axis,
    )(x)


def row_sum(rows):
    x = jnp.concatenate(
        [jnp.stack(rows), jnp.zeros((8 - len(rows), rows[0].shape[0]), f32)], axis=0
    )
    return jnp.sum(exchange(x, "row", 1), axis=0)


def sinusoid(steps, width):
    half_width = width // 2
    frequency = jnp.exp(-math.log(10000.0) * jnp.arange(half_width, dtype=f32) / half_width)
    angles = steps.astype(f32)[:, None] * frequency[None, :]
    return jnp.concatenate([jnp.cos(angles), jnp.sin(angles)], axis=1)


def swish_slope(values):
    sig_v = jax.nn.sigmoid(values)
    return sig_v * (1.0 + values * (1.0 - sig_v))


def per_group(vec, members):
    n = vec.shape[-1]
    g = jnp.sum(vec.reshape(vec.shape[0], GROUPS, n // GROUPS), axis=2) / members
    return jnp.repeat(g, n // GROUPS, axis=1)


def norm_stats(values, members):
    sums = row_sum([jnp.sum(values, axis=0), jnp.sum(values * values, axis=0)])
    means = per_group(sums[:2], members)
    return (means[0], lax.rsqrt(means[1] - means[0] * means[0] + EPSILON))


def halo(x):
    devices = lax.axis_size("row")
    up = [(i, i + 1) for i in range(devices - 1)]
    down = [(i + 1, i) for i in range(devices - 1)]
    before = lax.ppermute(x[-1:], "row", up)
    after = lax.ppermute(x[:1], "row", down)
    return jnp.concatenate([before, x, after], axis=0)


def conv(padded, kernel):
    x = jnp.pad(padded, ((0, 0), (1, 1), (0, 0)))[None]
    return lax.conv_general_dilated(
        x,
        kernel,
        (1, 1),
        "VALID",
        dimension_numbers=("NHWC", "HWIO", "NHWC"),
        preferred_element_type=f32,
    )[0]


def flip_kernel(kernel):
    return jnp.flip(kernel, (0, 1)).transpose(0, 1, 3, 2)


def tn(left, right):
    return lax.dot_general(left, right, (((0,), (0,)), ((), ())), preferred_element_type=f32)


def split_cols(x, n):
    rows, cols = x.shape
    return x.reshape(rows, n, cols // n).transpose(1, 0, 2)


def kernel_grad(acts, grad_padded, tall):
    n = lax.axis_size("img")
    rows, wide, ch = grad_padded.shape
    part = ch // n
    g = lax.all_to_all(
        split_cols(grad_padded.reshape(rows * wide, ch), n),
        "img",
        split_axis=0,
        concat_axis=0,
        tiled=True,
    ).reshape(n, rows, wide, part)
    g = jnp.pad(g, ((0, 0), (0, 0), (1, 1), (0, 0)))
    lines = []
    for ky in range(3):
        for kx in range(3):
            lines.append(
                g[:, 2 - ky : 2 - ky + tall, 2 - kx : 2 - kx + wide].reshape(-1, part)
            )
    return tn(acts, jnp.concatenate(lines, axis=1))


def local(
    images,
    timesteps,
    clip_embed,
    context,
    out_cotangent,
    item_weight,
    first_gain,
    first_bias,
    first_kernel,
    first_offset,
    embed_weight,
    embed_bias,
    second_gain,
    second_bias,
    second_kernel,
    second_offset,
    third_gain,
    third_bias,
    project_in,
    context_weight,
    project_out,
    output_bias,
):
    _, tall, wide, ch = images.shape
    pixels = tall * wide
    hd = ch // HEADS
    nrow = lax.axis_size("row")
    nimg = lax.axis_size("img")
    me_row = lax.axis_index("row")
    gq = nrow // HEADS
    head = me_row // gq
    text = context.shape[2]
    nctx = context.shape[1]
    members = float(nrow * pixels * (ch // GROUPS))

    def gather_img(x):
        return lax.all_gather(x, "img", axis=0, tiled=True)

    grad_out = out_cotangent.reshape(pixels, ch).astype(f32) * (item_weight.astype(f32) * 0.25)
    grad_low = grad_out.astype(bf16)
    attended_grad = (
        lax.dot_general(project_out, grad_low, (((1,), (1,)), ((), ())), preferred_element_type=f32)
        .astype(bf16)
        .reshape(HEADS, hd, pixels)
    )

    def queries_out(x):
        x = x.reshape(HEADS, hd, gq, pixels // gq).transpose(0, 2, 1, 3)
        x = x.reshape(nrow, hd, pixels // gq)
        return x

    def a2a(x):
        return lax.all_to_all(x, "row", split_axis=0, concat_axis=0, tiled=True)

    grad_heads = a2a(queries_out(attended_grad))

    image_f = images.reshape(pixels, ch).astype(f32)
    embedding = sinusoid(timesteps, clip_embed.shape[1]) + clip_embed.astype(f32)
    embed_act = jax.nn.silu(embedding).astype(bf16)
    scale_shift = (jnp.dot(embed_act, embed_weight, preferred_element_type=f32) + embed_bias)[0]
    scale1 = 1.0 + scale_shift[:ch]
    shift = scale_shift[ch:]
    pair_at = (head // 2) * (2 * hd)
    cw_k = lax.dynamic_slice_in_dim(context_weight, pair_at, 2 * hd, 1)
    cw_v = lax.dynamic_slice_in_dim(context_weight, ch + pair_at, 2 * hd, 1)
    cw = jnp.concatenate([cw_k, cw_v], axis=1)
    enc = lax.dot_general(
        cw, context[0], (((0,), (1,)), ((), ())), preferred_element_type=f32
    ).astype(bf16)
    enc = enc.reshape(2, 2, hd, nctx)
    enc = jnp.where(head % 2 == 0, enc[:, 0], enc[:, 1]).reshape(2 * hd, nctx)
    padc = -(-nctx // 16) * 16
    enc = jnp.pad(enc, ((0, 0), (0, padc - nctx)))

    mean1, rstd1 = norm_stats(image_f, members)
    normed1 = (image_f - mean1) * rstd1
    norm_one = normed1 * first_gain + first_bias
    act_one = jax.nn.silu(norm_one).astype(bf16)
    hidden = conv(halo(act_one.reshape(tall, wide, ch)), first_kernel).reshape(pixels, ch)
    hidden = hidden + first_offset
    acts_one = gather_img(act_one)
    mean2, rstd2 = norm_stats(hidden, members)
    normed2 = (hidden - mean2) * rstd2
    affine_two = normed2 * second_gain + second_bias
    norm_two = affine_two * scale1 + shift
    act_two = jax.nn.silu(norm_two).astype(bf16)
    acts_two = gather_img(act_two)
    middle = (
        image_f
        + conv(halo(act_two.reshape(tall, wide, ch)), second_kernel).reshape(pixels, ch)
        + second_offset
    )
    mean3, rstd3 = norm_stats(middle, members)
    normed3 = (middle - mean3) * rstd3
    act_three = (normed3 * third_gain + third_bias).astype(bf16)
    acts_three = gather_img(act_three)
    triple = (
        lax.dot_general(project_in, act_three, (((0,), (1,)), ((), ())), preferred_element_type=f32)
        .astype(bf16)
        .reshape(3, HEADS, hd, pixels)
    )
    if gq == 1:
        recv = a2a(triple.transpose(1, 0, 2, 3).reshape(nrow, 3 * hd, pixels))
        q_h, kv_h = recv[:, :hd], recv[:, hd:]
        grad_h = grad_heads
    else:
        pair = triple[1:].transpose(1, 0, 2, 3).reshape(HEADS, 1, 2 * hd, pixels)
        pair = jnp.broadcast_to(pair, (HEADS, gq, 2 * hd, pixels)).reshape(nrow, 2 * hd, pixels)
        q_h, kv_h = a2a(queries_out(triple[0])), a2a(pair)

        def regroup(x, rows):
            x = x.transpose(1, 0, 2).reshape(rows, -1, 512)
            return x.transpose(1, 0, 2)

        q_h, kv_h, grad_h = regroup(q_h, hd), regroup(kv_h, 2 * hd), regroup(grad_heads, hd)
    att_h, dq_h, dkv_h, dctx = attention(q_h, kv_h, enc, grad_h, nctx)
    if gq == 1:
        attended = a2a(att_h).reshape(ch, pixels)
        back = a2a(jnp.concatenate([dq_h, dkv_h], axis=1)).reshape(HEADS, 3, hd, pixels)
        back = back.transpose(1, 0, 2, 3).reshape(3 * ch, pixels)
    else:

        def ungroup(x, part):
            rows = x.shape[1]
            x = x.transpose(1, 0, 2).reshape(rows, nrow, part)
            return x.transpose(1, 0, 2)

        def from_queries(x):
            x = x.reshape(HEADS, gq, hd, pixels // gq).transpose(0, 2, 1, 3)
            return x.reshape(ch, pixels)

        attended = from_queries(a2a(ungroup(att_h, pixels // gq)))
        dq = from_queries(a2a(ungroup(dq_h, pixels // gq)))
        dkv = a2a(ungroup(dkv_h, pixels)).reshape(HEADS, gq, 2, hd, pixels)
        dkv = jnp.sum(dkv.astype(f32), axis=1).astype(bf16)
        dkv = dkv.transpose(1, 0, 2, 3).reshape(2 * ch, pixels)
        back = jnp.concatenate([dq, dkv], axis=0)
    branch = tn(attended, project_out)
    result_image = (middle + branch + output_bias).astype(bf16)

    part_text = text // nrow
    enc_all = lax.all_gather(dctx[:nctx].astype(bf16), ("img", "row"), axis=0)
    enc_all = enc_all.reshape(nimg, HEADS, gq, nctx, 2, hd)
    if gq > 1:
        enc_all = jnp.sum(enc_all.astype(f32), axis=2, keepdims=True).astype(bf16)
    enc_all = enc_all[:, :, 0].transpose(0, 2, 3, 1, 4).reshape(nimg * nctx, 2 * ch)
    ctx_rows = lax.dynamic_slice_in_dim(context[0], me_row * part_text, part_text, 1)
    ctx_rows = gather_img(ctx_rows)
    context_weight_grad = tn(ctx_rows, enc_all)

    triple_grad = back.T
    act_three_grad = lax.dot_general(
        triple_grad, project_in, (((1,), (1,)), ((), ())), preferred_element_type=f32
    )
    sums3 = row_sum(
        [
            jnp.sum(act_three_grad * normed3, axis=0),
            jnp.sum(act_three_grad, axis=0),
            jnp.sum(grad_out, axis=0),
        ]
    )

    def norm_back(u, normed, rstd, gain, gain_sum, bias_sum):
        means = per_group(jnp.stack([gain * bias_sum, gain * gain_sum]), members)
        return rstd * (u * gain - means[0] - normed * means[1])

    middle_grad = grad_out + norm_back(
        act_three_grad, normed3, rstd3, third_gain, sums3[0], sums3[1]
    )
    middle_low = halo(middle_grad.astype(bf16).reshape(tall, wide, ch))
    act_two_grad = conv(middle_low, flip_kernel(second_kernel)).reshape(pixels, ch)
    norm_two_grad = act_two_grad * swish_slope(norm_two)
    sums2 = row_sum(
        [
            jnp.sum(norm_two_grad * normed2, axis=0),
            jnp.sum(norm_two_grad, axis=0),
            jnp.sum(middle_grad, axis=0),
        ]
    )
    scale_grad = second_gain * sums2[0] + second_bias * sums2[1]
    shift_grad = sums2[1]
    gain2_sum, bias2_sum = scale1 * sums2[0], scale1 * sums2[1]
    hidden_grad = norm_back(
        norm_two_grad * scale1, normed2, rstd2, second_gain, gain2_sum, bias2_sum
    )
    hidden_low = halo(hidden_grad.astype(bf16).reshape(tall, wide, ch))
    act_one_grad = conv(hidden_low, flip_kernel(first_kernel)).reshape(pixels, ch)
    norm_one_grad = act_one_grad * swish_slope(norm_one)
    sums1 = row_sum(
        [
            jnp.sum(norm_one_grad * normed1, axis=0),
            jnp.sum(norm_one_grad, axis=0),
            jnp.sum(hidden_grad, axis=0),
        ]
    )
    image_grad = middle_grad + norm_back(
        norm_one_grad, normed1, rstd1, first_gain, sums1[0], sums1[1]
    )

    def swap_img(x):
        x = split_cols(x, nimg)
        x = lax.all_to_all(x, "img", split_axis=0, concat_axis=0, tiled=True)
        return x.reshape(-1, x.shape[2])

    kg2 = kernel_grad(acts_two, middle_low, tall)
    kg1 = kernel_grad(acts_one, hidden_low, tall)
    pin = tn(acts_three, swap_img(triple_grad))
    pout = tn(gather_img(attended.T), swap_img(grad_low))

    def finish(x):
        x = lax.psum_scatter(x.astype(bf16), "row", scatter_dimension=0, tiled=True)
        return lax.all_gather(x, "img", axis=0).astype(f32)

    c2 = finish(kg2)
    c1 = finish(kg1)
    c3 = finish(jnp.concatenate([pin, pout], axis=1))
    part = ch // nrow
    cols = ch // nimg

    def conv_out(x):
        return x.reshape(nimg, part, 3, 3, cols).transpose(2, 3, 1, 0, 4).reshape(3, 3, part, ch)

    wide_in = 3 * ch // nimg
    pin_out = c3[:, :, :wide_in].transpose(1, 0, 2).reshape(part, 3 * ch)
    pout_out = c3[:, :, wide_in:].transpose(1, 0, 2).reshape(part, ch)

    rows = jnp.stack(
        [
            sums1[0],
            sums1[1],
            sums1[2],
            gain2_sum,
            bias2_sum,
            sums2[2],
            sums3[0],
            sums3[1],
            sums3[2],
            scale_grad,
            shift_grad,
        ]
        + [jnp.zeros((ch,), f32)] * 5
    )
    every = exchange(rows, "img", 2)
    acts_embed = gather_img(embed_act)
    part_emb = embed_act.shape[1] // nrow
    acts_embed = lax.dynamic_slice_in_dim(acts_embed, me_row * part_emb, part_emb, 1).astype(f32)
    shift_scale = every[:, 9:11].reshape(nimg, 2 * ch)
    embed_weight_grad = jnp.sum(acts_embed[:, :, None] * shift_scale[:, None, :], axis=0)
    part_bias = 2 * ch // nrow
    embed_bias_grad = lax.dynamic_slice_in_dim(
        jnp.sum(shift_scale, axis=0), me_row * part_bias, part_bias, 0
    )
    vecs = lax.dynamic_slice_in_dim(jnp.sum(every[:, :9], axis=0), me_row * part, part, 1)
    return (
        result_image.reshape(images.shape),
        image_grad.reshape(images.shape),
        vecs[0],
        vecs[1],
        conv_out(c1),
        vecs[2],
        embed_weight_grad,
        embed_bias_grad,
        vecs[3],
        vecs[4],
        conv_out(c2),
        vecs[5],
        vecs[6],
        vecs[7],
        pin_out,
        context_weight_grad,
        pout_out,
        vecs[8],
    )


def nt_dot(a, b):
    return lax.dot_general(a, b, (((1,), (1,)), ((), ())), preferred_element_type=f32)


def group_total(x):
    per = x.shape[1] // GROUPS
    lane = lax.broadcasted_iota(jnp.int32, x.shape, 1)
    n = x.shape[1]
    step = 1
    while step < per:
        upper = (lane // step) % 2 == 1
        x = x + jnp.where(upper, pltpu.roll(x, step, 1), pltpu.roll(x, n - step, 1))
        step *= 2
    return x


def total(v):
    return jnp.sum(v, axis=0, keepdims=True)


def put_shifts(buf, at, v, wide):
    n, ch = v.shape
    col = lax.rem(lax.broadcasted_iota(jnp.int32, (n, 1), 0), wide)
    buf[pl.ds(at, n), pl.ds(ch, ch)] = v.astype(bf16)
    left = jnp.where(col == 0, 0.0, pltpu.roll(v, 1, 0))
    buf[pl.ds(at, n), pl.ds(0, ch)] = left.astype(bf16)
    right = jnp.where(col == wide - 1, 0.0, pltpu.roll(v, n - 1, 0))
    buf[pl.ds(at, n), pl.ds(2 * ch, ch)] = right.astype(bf16)


class Links:
    def __init__(self, nrow, nimg):
        self.nrow, self.nimg = nrow, nimg
        self.row, self.img = lax.axis_index("row"), lax.axis_index("img")

    def peer(self, axis, k):
        if axis == "row":
            return lax.rem(self.row + k, self.nrow)
        return lax.rem(self.img + k, self.nimg)

    def greet(self):
        barrier = pltpu.get_barrier_semaphore()
        for axis, n in (("row", self.nrow), ("img", self.nimg)):
            for k in range(1, n):
                pl.semaphore_signal(
                    barrier, inc=1, device_id={axis: self.peer(axis, k)}, device_id_type=MESH
                )

    def greeted(self):
        pl.semaphore_wait(pltpu.get_barrier_semaphore(), self.nrow + self.nimg - 2)

    def to(self, axis, at, src, dst, send, recv):
        return pltpu.make_async_remote_copy(
            src_ref=src,
            dst_ref=dst,
            send_sem=send,
            recv_sem=recv,
            device_id={axis: at},
            device_id_type=MESH,
        )

    def copy(self, axis, k, src, dst, send, recv):
        return self.to(axis, self.peer(axis, k), src, dst, send, recv)


class Stats:
    def __init__(self, links, src, dst, send, recv):
        self.links, self.src, self.dst, self.send, self.recv = links, src, dst, send, recv

    def start(self, stage, rows):
        links = self.links
        ch = rows[0].shape[1]
        blocks = [r[:, i * 128 : (i + 1) * 128] for r in rows for i in range(ch // 128)]
        height = self.src.shape[1]
        blocks = blocks + [jnp.zeros((1, 128), f32)] * (height - len(blocks))
        packed = jnp.concatenate(blocks, axis=0)
        self.src[stage] = packed
        self.dst[stage, links.row] = packed
        self.rows, self.per = len(rows), ch // 128
        self.copies = []
        for k in range(1, links.nrow):
            c = links.copy(
                "row",
                k,
                self.src.at[stage],
                self.dst.at[stage, links.row],
                self.send.at[stage, k - 1],
                self.recv.at[stage, k - 1],
            )
            c.start()
            self.copies.append(c)

    def finish(self, stage):
        for c in self.copies:
            c.wait()
        s = jnp.sum(self.dst[stage], axis=0)
        per = self.per
        rows = [
            jnp.concatenate([s[r * per + i : r * per + i + 1] for i in range(per)], axis=1)
            for r in range(self.rows)
        ]
        return jnp.concatenate(rows + [jnp.zeros((8 - self.rows, per * 128), f32)], axis=0)


class Halo:
    def __init__(self, links, send, recv):
        self.links, self.send, self.recv = links, send, recv

    def copies(self, slot, first, last, land):
        links = self.links
        down = links.copy(
            "row", links.nrow - 1, first, land.at[1],
            self.send.at[slot, 0], self.recv.at[slot, 1],
        )
        up = links.copy(
            "row", 1, last, land.at[0],
            self.send.at[slot, 1], self.recv.at[slot, 0],
        )
        return down, up

    def start(self, slot, first, last, land):
        links = self.links
        down, up = self.copies(slot, first, last, land)

        @pl.when(links.row > 0)
        def _():
            down.start()

        @pl.when(links.row < links.nrow - 1)
        def _():
            up.start()

        @pl.when(links.row == 0)
        def _():
            land[0] = jnp.zeros(land.shape[1:], land.dtype)

        @pl.when(links.row == links.nrow - 1)
        def _():
            land[1] = jnp.zeros(land.shape[1:], land.dtype)

        return down, up

    def finish(self, pair):
        links = self.links
        down, up = pair

        @pl.when(links.row > 0)
        def _():
            down.wait_send()
            up.wait_recv()

        @pl.when(links.row < links.nrow - 1)
        def _():
            up.wait_send()
            down.wait_recv()


def put_block(links, buf, mid, before, after, wide):
    put_shifts(buf, wide, mid, wide)
    put_shifts(buf, 0, jnp.where(links.row > 0, before, 0.0), wide)
    put_shifts(buf, buf.shape[0] - wide, jnp.where(links.row < links.nrow - 1, after, 0.0), wide)


def front_kernel(
    cfg,
    *refs,
):
    nvec = cfg[-1]
    _front(cfg[:-1], *refs[:6], refs[6 : 6 + nvec], *refs[6 + nvec :])


def _front(
    cfg,
    r_img,
    r_oc,
    r_pout,
    r_cxt,
    r_embv,
    r_weight,
    r_vecs,
    r_w1h,
    r_w2h,
    r_winh,
    r_cwh,
    r_ewh,
    r_par,
    r_hidden,
    r_middle,
    r_stats,
    r_ss,
    r_wt,
    r_a3,
    r_hoc,
    r_hhid,
    r_hmid,
    r_a1h,
    r_a2h,
    r_ctxh,
    r_embh,
    r_tgh,
    r_atth,
    r_ench,
    r_emb,
    r_himg,
    r_w1,
    r_w2,
    r_win,
    r_cw,
    r_ctx,
    r_ew,
    r_buf,
    r_at,
    r_gs,
    r_ts,
    r_qkv,
    r_g,
    r_kx,
    r_vx,
    r_kt,
    r_vt,
    r_sb,
    r_pb,
    r_acc,
    r_atb,
    r_dqb,
    r_dcb,
    r_st_src,
    r_st_dst,
    r_wsem,
    r_vsem,
    r_st_send,
    r_st_recv,
    r_h_send,
    r_h_recv,
    r_i_send,
    r_i_recv,
    r_r_send,
    r_r_recv,
    r_osem,
):
    nrow, nimg, wide, ch, hd, kc = cfg
    px = r_img.shape[0]
    members = float(nrow * px * (ch // GROUPS))
    links = Links(nrow, nimg)
    links.greet()
    head = links.row
    me = links.row

    def pair_at(at):
        return pl.ds(pl.multiple_of(at + (head // 2) * (2 * hd), 128), 2 * hd)

    pairs = (
        (r_w1h, r_w1),
        (r_ewh, r_ew),
        (r_winh, r_win),
        (r_w2h, r_w2),
        (r_cwh.at[:, pair_at(0)], r_cw.at[:, : 2 * hd]),
        (r_cwh.at[:, pair_at(ch)], r_cw.at[:, 2 * hd :]),
    )
    loads = [pltpu.make_async_copy(a, b, r_wsem.at[i]) for i, (a, b) in enumerate(pairs)]
    for c in loads:
        c.start()
    load_w1, load_ew, load_win, load_w2, load_ck, load_cv = loads
    places = (0, 1, 2, 3, 4, 7, 8, 9, 11, 12, 13)
    flat = [v for v in r_vecs[:-1]] + [r_vecs[-1].at[:, :ch], r_vecs[-1].at[:, ch:]]
    vec_loads = [
        pltpu.make_async_copy(v, r_par.at[pl.ds(at, 1)], r_vsem.at[i])
        for i, (v, at) in enumerate(zip(flat, places))
    ]
    for c in vec_loads:
        c.start()
    weight = r_weight[0].astype(f32) * 0.25
    for at in (5, 6, 14, 15):
        r_par[at : at + 1, :] = jnp.zeros((1, ch), f32)
    r_par[10:11, :] = jnp.full((1, ch), 1.0, f32) * weight
    stats = Stats(links, r_st_src, r_st_dst, r_st_send, r_st_recv)
    halo = Halo(links, r_h_send, r_h_recv)
    ends = (pl.ds(0, wide), pl.ds(px - wide, wide))

    def edges(slot, block, land):
        return halo.start(slot, block.at[ends[0]], block.at[ends[1]], land)

    pending = []

    def par(i):
        return r_par[i : i + 1, :]

    def share(slot, src, dst):
        copies = [pltpu.make_async_copy(src(links.img), dst(links.img), r_osem.at[slot])]
        for k in range(1, nimg):
            copies.append(
                links.copy(
                    "img", k, src(links.peer("img", k)), dst(links.img),
                    r_i_send.at[slot, k - 1], r_i_recv.at[slot, k - 1],
                )
            )
        for c in copies:
            c.start()
        pending.extend(copies)

    def scatter(slot, src, dst):
        copies = []
        for k in range(1, nrow):
            copies.append(
                links.copy(
                    "row", k, src(links.peer("row", k)), dst(me),
                    r_r_send.at[slot, k - 1], r_r_recv.at[slot, k - 1],
                )
            )
        for c in copies:
            c.start()
        return copies

    def lanes(img):
        return pl.ds(pl.multiple_of(img * px, 128), px)

    def moments(v):
        return [total(v), total(v * v)]

    def center(stage, sums):
        means = group_total(sums) * (1.0 / members)
        mean = means[0:1]
        rstd = lax.rsqrt(means[1:2] - mean * mean + EPSILON)
        r_stats[2 * stage : 2 * stage + 1, :] = mean
        r_stats[2 * stage + 1 : 2 * stage + 2, :] = rstd
        return mean, rstd

    r_stats[...] = jnp.zeros_like(r_stats)
    rows = moments(r_img[...].astype(f32))
    low = (r_oc[...].astype(f32) * weight).astype(bf16)
    r_gs[...] = nt_dot(r_pout[...], low).astype(bf16).reshape(r_gs.shape)
    r_emb[...] = jnp.broadcast_to(r_embv[...].astype(bf16).astype(f32), r_emb.shape)
    links.greeted()
    stats.start(0, rows)
    c_img = edges(0, r_img, r_himg)
    c_g = scatter(2, lambda r: r_gs.at[r], lambda r: r_g.at[r])
    for c in vec_loads:
        c.wait()
    load_ew.wait()
    ss = nn(r_emb[...].astype(bf16), r_ew[...])[0:1]
    scale1 = 1.0 + (ss[:, :ch] + par(12))
    shift = ss[:, ch:] + par(13)
    r_ss[...] = jnp.concatenate([scale1, shift, jnp.zeros((6, ch), f32)], axis=0)
    mean, rstd = center(0, stats.finish(0))

    def conv_stage(stage, act, before, after, weights):
        buf = r_buf
        put_block(links, buf, act, before, after, wide)
        acc = nn(buf[pl.ds(wide, px), :], weights[1])
        r_at[stage] = act.astype(bf16).T
        acc = acc + nn(buf[pl.ds(0, px), :], weights[0])
        return acc + nn(buf[pl.ds(2 * wide, px), :], weights[2])


    def act_one(v):
        return jax.nn.silu((v.astype(f32) - mean) * rstd * par(0) + par(1))

    halo.finish(c_img)
    load_w1.wait()
    hidden = conv_stage(
        0, act_one(r_img[...]), act_one(r_himg[0]), act_one(r_himg[1]), r_w1
    ) + par(2)
    r_hidden[...] = hidden
    stats.start(1, moments(hidden))
    c_hid = edges(1, r_hidden, r_hhid)
    load_win.wait()
    turned = r_win[...].T
    for h in range(HEADS):
        for j in range(3):
            r_wt[(3 * h + j) * hd : (3 * h + j + 1) * hd, :] = turned[
                j * ch + h * hd : j * ch + (h + 1) * hd
            ]
    mean_two, rstd_two = center(1, stats.finish(1))

    def act_two(v):
        affine = (v - mean_two) * rstd_two * par(3) + par(4)
        return jax.nn.silu(affine * r_ss[0:1] + r_ss[1:2])

    halo.finish(c_hid)
    load_w2.wait()
    middle = conv_stage(1, act_two(r_hidden[...]), act_two(r_hhid[0]), act_two(r_hhid[1]), r_w2)
    middle = r_img[...].astype(f32) + middle + par(7)
    r_middle[...] = middle
    stats.start(2, moments(middle))
    c_mid = edges(2, r_middle, r_hmid)
    c_oc = edges(3, r_oc, r_hoc)
    nctx, text = r_cxt.shape
    padc = r_ctx.shape[0]
    r_ctx[...] = jnp.concatenate(
        [r_cxt[...], jnp.zeros((padc - nctx, text), bf16)], axis=0
    )
    load_ck.wait()
    load_cv.wait()
    enc = nn(r_ctx[...], r_cw[...]).T.astype(bf16)
    first = lax.rem(head, 2) == 0
    enc = jnp.concatenate(
        [
            jnp.where(first, enc[2 * j * hd : (2 * j + 1) * hd], enc[(2 * j + 1) * hd : (2 * j + 2) * hd])
            for j in range(2)
        ],
        axis=0,
    )
    mean, rstd = center(2, stats.finish(2))
    act3 = ((r_middle[...] - mean) * rstd * par(8) + par(9)).astype(bf16)
    r_a3[...] = act3.T
    ts, qkv, gs, g = r_ts, r_qkv, r_gs, r_g
    ts[...] = nn(r_wt[...], r_a3[...]).astype(bf16).reshape(ts.shape)
    c_kv = scatter(0, lambda r: ts.at[r, pl.ds(hd, 2 * hd)], lambda r: qkv.at[r, pl.ds(hd, 2 * hd)])
    npix = nrow * px
    ones_rows = jnp.where(lax.broadcasted_iota(jnp.int32, (hd, px), 0) < 2, 1.0, 0.0).astype(bf16)
    kx, vx, kt, vt, sb, pb, acc = (r_kx, r_vx, r_kt, r_vt, r_sb, r_pb, r_acc)

    def fill(pair, at, w):
        k = pair[:hd].astype(f32) * (LOG2E * 0.125)
        hi = k.astype(bf16)
        lo = (k - hi.astype(f32)).astype(bf16)
        kx[pl.ds(at, w), :] = jnp.concatenate([hi, lo], axis=0).T
        vfull = jnp.concatenate([pair[hd:], ones_rows[:, :w]], axis=0)
        vx[pl.ds(at, w), :] = vfull.T
        kt[:, pl.ds(at, w)] = pair[:hd]
        vt[:, pl.ds(at, w)] = vfull[: hd + 16]

    fill(enc, npix, padc)
    qkv[me] = ts[me]
    g[me] = gs[me]
    acc[...] = jnp.zeros_like(acc)

    def own(r):
        return pl.multiple_of(r * px, 128)

    fill(ts[me, hd:], own(me), px)
    for k in range(1, nrow):
        c_kv[k - 1].wait()
        frm = lax.rem(me + nrow - k, nrow)
        fill(qkv[frm, hd:], own(frm), px)


    def q_copy(k):
        to = lax.rem(me + k, nrow)
        return links.to(
            "row", to, ts.at[to, pl.ds(0, hd)], qkv.at[me, pl.ds(0, hd)],
            r_r_send.at[1, k - 1], r_r_recv.at[1, k - 1],
        )

    ahead = 3
    for k in range(1, ahead):
        q_copy(k).start()
    for i in range(2):
        share(i, lambda p, i=i: r_at.at[i], lambda p, i=i: (r_a1h, r_a2h)[i].at[:, lanes(p)])
    mine = text // nrow
    text_at = pl.ds(pl.multiple_of(me * mine, 128), mine)
    share(2, lambda p: r_ctx.at[:, text_at], lambda p: r_ctxh.at[p])
    wide_emb = r_emb.shape[1] // nrow
    emb_at = pl.ds(pl.multiple_of(me * wide_emb, 128), wide_emb)
    share(3, lambda p: r_emb.at[:, emb_at], lambda p: r_embh.at[p])
    halo.finish(c_mid)
    halo.finish(c_oc)

    bq = px
    nfull = npix // kc

    def out_copies(i):
        at = lax.rem(me + nrow - i, nrow)
        a = links.to(
            "row", at, r_atb.at[at], r_atth.at[me],
            r_r_send.at[3, i - 1], r_r_recv.at[3, i - 1],
        )
        d = links.to(
            "row", at, r_dqb.at[at, pl.ds(0, hd)], r_tgh.at[me, pl.ds(0, hd)],
            r_r_send.at[4, i - 1], r_r_recv.at[4, i - 1],
        )
        return a, d

    def block(i, _):
        s = lax.rem(me + nrow - i, nrow)

        @pl.when(i + ahead < nrow)
        def _():
            q_copy(i + ahead).start()

        @pl.when(i > 0)
        def _():
            links.to(
                "row", s, ts.at[s, pl.ds(0, hd)], qkv.at[s, pl.ds(0, hd)],
                r_r_send.at[1, i - 1], r_r_recv.at[1, i - 1],
            ).wait_recv()
            links.to(
                "row", s, gs.at[s], g.at[s], r_r_send.at[2, i - 1], r_r_recv.at[2, i - 1]
            ).wait_recv()

        qt = qkv[s, :hd]
        gt = g[s]
        q2 = jnp.concatenate([qt, qt], axis=0)
        sc = nn(kx[pl.ds(npix, padc), :], q2)
        sc = jnp.where(lax.broadcasted_iota(jnp.int32, (padc, bq), 0) < nctx, sc, -jnp.inf)
        sb[pl.ds(npix, padc), :] = sc
        m8 = jnp.max(sc.reshape(padc // 8, 8, bq), axis=0)

        def phase_a(c, m8):
            at = pl.multiple_of(c * kc, kc)
            sv = nn(kx[pl.ds(at, kc), :], q2)
            sb[pl.ds(at, kc), :] = sv
            return jnp.maximum(m8, jnp.max(sv.reshape(kc // 8, 8, bq), axis=0))

        m8 = lax.fori_loop(0, nfull, phase_a, m8, unroll=True)
        m = jnp.max(m8, axis=0, keepdims=True)
        pc = jnp.exp2(sb[pl.ds(npix, padc), :] - m).astype(bf16)
        pb[pl.ds(npix, padc), :] = pc
        o = nn(vt[:, npix : npix + padc], pc)

        def phase_b(c, o):
            at = pl.multiple_of(c * kc, kc)
            p = jnp.exp2(sb[pl.ds(at, kc), :] - m).astype(bf16)
            pb[pl.ds(at, kc), :] = p
            return o + nn(vt[:, pl.ds(at, kc)], p)

        o = lax.fori_loop(0, nfull, phase_b, o, unroll=True)
        inv = 1.0 / o[hd : hd + 1]
        att = o[:hd] * inv
        r_atb[s] = att.astype(bf16)
        gf = gt.astype(f32)
        delta = total(gf * att) * inv
        gl = (gf * inv).astype(bf16)
        dhi = (-delta).astype(bf16)
        dlo = (-delta - dhi.astype(f32)).astype(bf16)
        gx = jnp.concatenate([gl, dhi, dlo, jnp.zeros((hd - 2, bq), bf16)], axis=0)

        def piece(at, w, dq):
            p = pb[pl.ds(at, w), :]
            dp = nn(vx[pl.ds(at, w), :], gx)
            ds = (p.astype(f32) * dp).astype(bf16)
            acc[:hd, pl.ds(at, w)] += nt_dot(qt, ds)
            acc[hd:, pl.ds(at, w)] += nt_dot(gl, p)
            return dq + nn(kt[:, pl.ds(at, w)], ds)

        dq = piece(npix, padc, jnp.zeros((hd, bq), f32))

        def phase_d(c, dq):
            return piece(pl.multiple_of(c * kc, kc), kc, dq)

        dq = lax.fori_loop(0, nfull, phase_d, dq, unroll=True)
        r_dqb[s, :hd] = (dq * 0.125).astype(bf16)

        @pl.when(i > 0)
        def _():
            for c in out_copies(i):
                c.start()

        return 0

    lax.fori_loop(0, nrow, block, 0)
    scale = jnp.where(lax.broadcasted_iota(jnp.int32, (2 * hd, 1), 0) < hd, 0.125, 1.0)
    copies = []
    for k in range(1, nrow):
        s = links.peer("row", k)
        r_dqb[s, hd:] = (acc[:, pl.ds(own(s), px)] * scale).astype(bf16)
        c = links.copy(
            "row", k, r_dqb.at[s, pl.ds(hd, 2 * hd)], r_tgh.at[me, pl.ds(hd, 2 * hd)],
            r_r_send.at[5, k - 1], r_r_recv.at[5, k - 1],
        )
        c.start()
        copies.append(c)
    r_dcb[...] = (acc[:, npix : npix + padc] * scale).astype(bf16).T
    copies += scatter(6, lambda r: r_dcb, lambda r: r_ench.at[r])
    r_dqb[me, hd:] = (acc[:, pl.ds(own(me), px)] * scale).astype(bf16)
    for i, (a, b) in enumerate(
        (
            (r_dqb.at[me], r_tgh.at[me]),
            (r_atb.at[me], r_atth.at[me]),
            (r_dcb, r_ench.at[me]),
        )
    ):
        c = pltpu.make_async_copy(a, b, r_osem.at[4 + i])
        c.start()
        copies.append(c)
    for k in range(1, nrow):
        q_copy(k).wait_send()
    for c in c_g:
        c.wait_send()
    for k in range(1, nrow):
        for c in out_copies(k):
            c.wait()
    for c in copies + pending:
        c.wait()


def front(
    images, out_cot, project_out, context, emb, weight, vectors, w1, w2, win, cw, ew, nrow, nimg, wide
):
    px, ch = images.shape
    hd = ch // HEADS
    padc = -(-context.shape[0] // 16) * 16
    cfg = (nrow, nimg, wide, ch, hd, 1024, len(vectors))
    nk = nrow * px + padc
    V = pl.BlockSpec(memory_space=pltpu.VMEM)
    A = pl.BlockSpec(memory_space=pl.ANY)
    S = jax.ShapeDtypeStruct
    M = pltpu.VMEM
    dma = pltpu.SemaphoreType.DMA
    return pl.pallas_call(
        functools.partial(front_kernel, cfg),
        out_shape=(
            S((16, ch), f32),
            S((px, ch), f32),
            S((px, ch), f32),
            S((8, ch), f32),
            S((8, ch), f32),
            S((3 * ch, ch), bf16),
            S((ch, px), bf16),
            S((2, wide, ch), bf16),
            S((2, wide, ch), f32),
            S((2, wide, ch), f32),
            S((ch, nimg * px), bf16),
            S((ch, nimg * px), bf16),
            S((nimg, padc, context.shape[1] // nrow), bf16),
            S((nimg, 8, emb.shape[1] // nrow), f32),
            S((nrow, 3 * hd, px), bf16),
            S((nrow, hd, px), bf16),
            S((nrow, padc, 2 * hd), bf16),
        ),
        in_specs=[V] * 5
        + [pl.BlockSpec(memory_space=pltpu.SMEM)]
        + [A] * (len(vectors) + 5),
        out_specs=(V,) * 10 + (A,) * 7,
        scratch_shapes=[
            M((8, emb.shape[1]), f32),
            M((2, wide, ch), bf16),
            M(w1.shape, bf16),
            M(w2.shape, bf16),
            M(win.shape, bf16),
            M((cw.shape[0], 4 * hd), bf16),
            M((padc, cw.shape[0]), bf16),
            M(ew.shape, bf16),
            M((px + 2 * wide, 3 * ch), bf16),
            M((2, ch, px), bf16),
            M((nrow, hd, px), bf16),
            M((nrow, 3 * hd, px), bf16),
            M((nrow, 3 * hd, px), bf16),
            M((nrow, hd, px), bf16),
            M((nk, 2 * hd), bf16),
            M((nk, 2 * hd), bf16),
            M((hd, nk), bf16),
            M((hd + 16, nk), bf16),
            M((nk, px), f32),
            M((nk, px), bf16),
            M((2 * hd, nk), f32),
            M((nrow, hd, px), bf16),
            M((nrow, 3 * hd, px), bf16),
            M((padc, 2 * hd), bf16),
            M((3, 8, 128), f32),
            M((3, nrow, 8, 128), f32),
            dma((6,)),
            dma((11,)),
            dma((3, nrow - 1)),
            dma((3, nrow - 1)),
            dma((4, 2)),
            dma((4, 2)),
            dma((4, nimg - 1)),
            dma((4, nimg - 1)),
            dma((7, nrow - 1)),
            dma((7, nrow - 1)),
            dma((8,)),
        ],
        compiler_params=pltpu.CompilerParams(
            collective_id=3, has_side_effects=True, vmem_limit_bytes=62 * 2**20
        ),
        name="front",
    )(images, out_cot, project_out, context, emb, weight, *vectors, w1, w2, win, cw, ew)
def slope(values):
    sig = jax.nn.sigmoid(values)
    return sig * (1.0 + values * (1.0 - sig))


def back_kernel(
    cfg,
    r_img,
    r_oc,
    r_par,
    r_ss,
    r_stats,
    r_hidden,
    r_middle,
    r_hoc,
    r_hhid,
    r_hmid,
    r_a3,
    r_tg,
    r_att,
    r_wt,
    r_w2h,
    r_w1h,
    r_a2h,
    r_a1h,
    r_ench,
    r_ctxh,
    r_igrad,
    r_kq,
    r_oq,
    r_cr,
    r_every,
    r_w2,
    r_w1,
    r_a2,
    r_a1,
    r_enc,
    r_ctx,
    r_mg,
    r_ntg,
    r_buf,
    r_gq,
    r_gs,
    r_ks,
    r_kx,
    r_km,
    r_kz,
    r_kf,
    r_os,
    r_ox,
    r_oy,
    r_oz,
    r_of,
    r_encq,
    r_cq,
    r_vsrc,
    r_st_src,
    r_st_dst,
    r_hu,
    r_kacc,
    r_lsem,
    r_st_send,
    r_st_recv,
    r_h_send,
    r_h_recv,
    r_i_send,
    r_i_recv,
    r_r_send,
    r_r_recv,
    r_x_send,
    r_x_recv,
    r_z_send,
    r_z_recv,
    r_osem,
):
    nrow, nimg, wide, ch, hd, padc = cfg
    px = r_img.shape[0]
    part = ch // nimg
    rows = ch // nrow
    deep = nrow // 2
    members = float(nrow * px * (ch // GROUPS))
    links = Links(nrow, nimg)
    links.greet()
    pairs = (
        (r_w2h, r_w2),
        (r_a2h, r_a2),
        (r_w1h, r_w1),
        (r_a1h, r_a1),
        (r_ench, r_enc),
        (r_ctxh, r_ctx),
    )
    loads = [pltpu.make_async_copy(a, b, r_lsem.at[i]) for i, (a, b) in enumerate(pairs)]
    for c in loads:
        c.start()
    load_w2, load_a2, load_w1, load_a1, load_enc, load_ctx = loads
    stats = Stats(links, r_st_src, r_st_dst, r_st_send, r_st_recv)
    halo = Halo(links, r_h_send, r_h_recv)
    ends = (pl.ds(0, wide), pl.ds(px - wide, wide))

    def edges(slot, block, land):
        return halo.start(slot, block.at[ends[0]], block.at[ends[1]], land)

    others = (
        links.img + 1 - 2 * lax.rem(links.img, 2),
        lax.rem(links.img + 2, nimg),
        nimg - 1 - links.img,
    )
    row_z, row_x = links.row // 2, lax.rem(links.row, 2)
    img_y, img_c = links.img // 2, lax.rem(links.img, 2)

    def par(i):
        return r_par[i : i + 1, :]

    def stat(i):
        return r_stats[i : i + 1, :]

    scale1, shift = r_ss[0:1], r_ss[1:2]

    def share(slot, src, dst):
        copies = [pltpu.make_async_copy(src(links.img), dst(links.img), r_osem.at[slot])]
        for k, at in enumerate(others):
            copies.append(
                links.to(
                    "img", at, src(at), dst(links.img), r_i_send.at[slot, k], r_i_recv.at[slot, k]
                )
            )
        for c in copies:
            c.start()
        return copies

    def wait(copies):
        for c in copies:
            c.wait()

    def columns(at, img):
        return pl.ds(pl.multiple_of(at + img * part, 128), part)

    def row_x_start(slot, src, land):
        c = links.to(
            "row", links.row + 1 - 2 * row_x, src.at[:, 1 - row_x], land,
            r_x_send.at[slot], r_x_recv.at[slot],
        )
        c.start()
        return c

    def row_z_start(slot, c, src, land, mid, last):
        c.wait()
        mid[...] = (src[:, row_x].astype(f32) + land[...].astype(f32)).astype(bf16)
        copies = []
        for k in range(1, deep):
            z = lax.rem(row_z + k, deep)
            copies.append(
                links.to(
                    "row", 2 * z + row_x, mid.at[z], last.at[k - 1],
                    r_z_send.at[slot, k - 1], r_z_recv.at[slot, k - 1],
                )
            )
        for d in copies:
            d.start()
        return copies

    def row_end(copies, mid, last):
        wait(copies)
        s = mid[row_z].astype(f32)
        for k in range(1, deep):
            s = s + last[k - 1].astype(f32)
        return s.astype(bf16)

    def back_means(gain, gain_sum, bias_sum):
        both = jnp.concatenate([gain * bias_sum, gain * gain_sum, jnp.zeros((6, ch), f32)], axis=0)
        return group_total(both) * (1.0 / members)

    def norm_back(u, normed, rstd, gain, means):
        return rstd * (u * gain - means[0:1] - normed * means[1:2])

    def conv_back(stage, grad, before, after, weights):
        buf = r_buf.at[stage]
        put_block(links, buf, grad, before, after, wide)
        copies = share(
            stage, lambda i: buf.at[:, columns(ch, i)], lambda i: r_gq.at[stage, i]
        )
        acc = None
        for ky in range(3):
            for kx in range(3):
                g = buf[pl.ds(ky * wide, px), pl.ds(kx * ch, ch)]
                w = weights[2 - ky, pl.ds((2 - kx) * ch, ch), :]
                d = nt_dot(g, w)
                acc = d if acc is None else acc + d
        return acc, copies

    def kernel_part(stage, acts, ky, images):
        tot = None
        for b in images:
            at = pl.ds(pl.multiple_of(b * px, 128), px)
            d = nn(acts[:, at], r_gs[b, ky * wide : ky * wide + px, :])
            tot = d if tot is None else tot + d
        return tot

    def kernel_grads(stage, acts, copies):
        near, far = (links.img, others[0]), others[1:]
        for group, first in ((near, True), (far, False)):
            for b, c in zip(group, copies[:2] if first else copies[2:]):
                c.wait()
                put_shifts(r_gs.at[b], 0, r_gq[stage, b].astype(f32), wide)
            if first:
                for ky in range(3):
                    r_kacc[ky] = kernel_part(stage, acts, ky, near)
        sent = []
        for ky in range(3):
            tot = r_kacc[ky] + kernel_part(stage, acts, ky, far)
            r_ks[stage, ky] = tot.astype(bf16).reshape(deep, 2, rows, 3 * part)
            sent.append(row_x_start(3 * stage + ky, r_ks.at[stage, ky], r_kx.at[stage, ky]))
        return sent

    def kernel_mid(stage, sent, ky):
        return row_z_start(
            3 * stage + ky, sent[ky], r_ks.at[stage, ky], r_kx.at[stage, ky],
            r_km.at[stage, ky], r_kz.at[stage, ky],
        )

    def kernel_end(stage, copies):
        out = []
        for ky in range(3):
            r_kf[stage, ky] = row_end(copies[ky], r_km.at[stage, ky], r_kz.at[stage, ky])
            out += share(
                2 + 3 * stage + ky,
                lambda i, ky=ky: r_kf.at[stage, ky],
                lambda i, ky=ky: r_kq.at[stage, ky, i],
            )
        return out

    tgt = r_tg[...].reshape(3 * ch, px)
    u3 = nn(tgt.T, r_wt[...])
    normed3 = (r_middle[...] - stat(4)) * stat(5)
    grad_out = r_oc[...].astype(f32) * par(10)
    r_mg[...] = u3
    sums = [total(u3 * normed3), total(u3), total(grad_out)]
    links.greeted()
    stats.start(0, sums)
    c_u = edges(0, r_mg, r_hu.at[0])
    load_enc.wait()
    c_encq = share(8, lambda i: r_enc.at[pl.ds(2 * i, 2)], lambda i: r_encq.at[i])
    a3 = r_a3[...]
    low = (r_oc[...].astype(f32) * par(10)).astype(bf16)
    pout = nn(r_att[...].reshape(ch, px), low).astype(bf16)
    for q in range(nimg):
        pin = nt_dot(a3, r_tg[2 * q : 2 * q + 2].reshape(6 * hd, px)).astype(bf16)
        r_os[q // 2, q % 2] = jnp.concatenate(
            [pin, pout[:, q * part : (q + 1) * part]], axis=1
        )
    c_ox = links.to(
        "img", links.img + 1 - 2 * img_c, r_os.at[:, 1 - img_c], r_ox,
        r_i_send.at[9, 0], r_i_recv.at[9, 0],
    )
    c_ox.start()
    sums3 = stats.finish(0)
    means3 = back_means(par(8), sums3[0:1], sums3[1:2])

    def middle_back(u, middle, oc):
        normed = (middle - stat(4)) * stat(5)
        return oc.astype(f32) * par(10) + norm_back(u, normed, stat(5), par(8), means3)

    halo.finish(c_u)
    middle_grad = middle_back(r_mg[...], r_middle[...], r_oc[...])
    r_mg[...] = middle_grad
    load_w2.wait()
    act_grad, c_g2 = conv_back(
        0,
        middle_grad,
        middle_back(r_hu[0, 0], r_hmid[0], r_hoc[0]),
        middle_back(r_hu[0, 1], r_hmid[1], r_hoc[1]),
        r_w2,
    )
    normed2 = (r_hidden[...] - stat(2)) * stat(3)
    ntg = act_grad * slope((normed2 * par(3) + par(4)) * scale1 + shift)
    r_ntg[...] = ntg
    stats.start(1, [total(ntg * normed2), total(ntg)])
    c_n = edges(1, r_ntg, r_hu.at[1])
    middle_sum = total(r_mg[...])
    load_a2.wait()
    c_k2 = kernel_grads(0, r_a2, c_g2)
    c_ox.wait()
    r_os[:, 0] = (
        r_os[:, img_c].astype(f32) + r_ox[...].astype(f32)
    ).astype(bf16)
    c_oy = links.to(
        "img", lax.rem(links.img + 2, nimg), r_os.at[1 - img_y, 0], r_oy,
        r_i_send.at[9, 1], r_i_recv.at[9, 1],
    )
    c_oy.start()
    sums2 = stats.finish(1)
    means2 = back_means(par(3), scale1 * sums2[0:1], scale1 * sums2[1:2])

    def hidden_back(u, hidden):
        normed = (hidden - stat(2)) * stat(3)
        return norm_back(u * scale1, normed, stat(3), par(3), means2)

    halo.finish(c_n)
    hidden_grad = hidden_back(r_ntg[...], r_hidden[...])
    hidden_sum = total(hidden_grad)
    load_w1.wait()
    act_grad, c_g1 = conv_back(
        1,
        hidden_grad,
        hidden_back(r_hu[1, 0], r_hhid[0]),
        hidden_back(r_hu[1, 1], r_hhid[1]),
        r_w1,
    )
    m_k2 = [kernel_mid(0, c_k2, 0), kernel_mid(0, c_k2, 1)]
    c_oy.wait()
    both = r_os[img_y, 0].astype(f32) + r_oy[...].astype(f32)
    r_of[...] = both.astype(bf16).reshape(deep, 2, rows, 6 * hd + part)
    c_o = row_x_start(6, r_of, r_oz.at[0])
    normed1 = (r_img[...].astype(f32) - stat(0)) * stat(1)
    n1g = act_grad * slope(normed1 * par(0) + par(1))
    r_ntg[...] = n1g
    stats.start(2, [total(n1g * normed1), total(n1g), hidden_sum, middle_sum])
    m_k2.append(kernel_mid(0, c_k2, 2))
    load_a1.wait()
    c_k1 = kernel_grads(1, r_a1, c_g1)
    c_o = row_z_start(6, c_o, r_of, r_oz.at[0], r_oz.at[1], r_oz.at[2, pl.ds(0, deep - 1)])
    sums1 = stats.finish(2)
    scale_grad = par(3) * sums2[0:1] + par(4) * sums2[1:2]
    r_vsrc[...] = jnp.concatenate(
        [
            sums1[0:3],
            scale1 * sums2[0:1],
            scale1 * sums2[1:2],
            sums1[3:4],
            sums3[0:3],
            scale_grad,
            sums2[1:2],
            jnp.zeros((5, ch), f32),
        ],
        axis=0,
    )
    out = share(10, lambda i: r_vsrc, lambda i: r_every.at[i])
    m_k1 = [kernel_mid(1, c_k1, 0)]
    normed1 = (r_img[...].astype(f32) - stat(0)) * stat(1)
    means1 = back_means(par(0), sums1[0:1], sums1[1:2])
    r_igrad[...] = r_mg[...] + norm_back(r_ntg[...], normed1, stat(1), par(0), means1)
    m_k1.append(kernel_mid(1, c_k1, 1))
    out += kernel_end(0, m_k2)
    m_k1.append(kernel_mid(1, c_k1, 2))
    wait(c_encq)
    load_ctx.wait()
    turned = r_ctx[...].reshape(nimg * padc, -1).T
    pairs = jnp.concatenate([r_encq[:, 0], r_encq[:, 1]], axis=2)
    r_cq[...] = nn(turned, pairs.reshape(nimg * padc, 4 * hd)).astype(bf16)
    out += share(11, lambda i: r_cq, lambda i: r_cr.at[i])
    r_oy[:rows] = row_end(c_o, r_oz.at[1], r_oz.at[2])
    out += share(12, lambda i: r_oy.at[pl.ds(0, rows)], lambda i: r_oq.at[i])
    out += kernel_end(1, m_k1)
    wait(out)


def backward(nrow, nimg, wide, *args):
    px, ch = args[0].shape
    hd = ch // HEADS
    ctx, enc = args[19], args[18]
    padc = enc.shape[1]
    cfg = (nrow, nimg, wide, ch, hd, padc)
    part, rows, deep = ch // nimg, ch // nrow, nrow // 2
    proj = 6 * hd + part
    V = pl.BlockSpec(memory_space=pltpu.VMEM)
    A = pl.BlockSpec(memory_space=pl.ANY)
    S = jax.ShapeDtypeStruct
    dma = pltpu.SemaphoreType.DMA
    M = pltpu.VMEM
    text = ctx.shape[2]
    return pl.pallas_call(
        functools.partial(back_kernel, cfg),
        out_shape=(
            S((px, ch), f32),
            S((2, 3, nimg, rows, 3 * part), bf16),
            S((nimg, rows, proj), bf16),
            S((nimg, text, 4 * hd), bf16),
            S((nimg, 16, ch), f32),
        ),
        in_specs=[V] * 14 + [A] * 6,
        out_specs=(V,) + (A,) * 4,
        scratch_shapes=[
            M((3, 3 * ch, ch), bf16),
            M((3, 3 * ch, ch), bf16),
            M((ch, nimg * px), bf16),
            M((ch, nimg * px), bf16),
            M(enc.shape, bf16),
            M(ctx.shape, bf16),
            M((px, ch), f32),
            M((px, ch), f32),
            M((2, px + 2 * wide, 3 * ch), bf16),
            M((2, nimg, px + 2 * wide, part), bf16),
            M((nimg, px + 2 * wide, 3 * part), bf16),
            M((2, 3, deep, 2, rows, 3 * part), bf16),
            M((2, 3, deep, rows, 3 * part), bf16),
            M((2, 3, deep, rows, 3 * part), bf16),
            M((2, 3, deep - 1, rows, 3 * part), bf16),
            M((2, 3, rows, 3 * part), bf16),
            M((2, 2, ch, proj), bf16),
            M((2, ch, proj), bf16),
            M((ch, proj), bf16),
            M((3, deep, rows, proj), bf16),
            M((deep, 2, rows, proj), bf16),
            M((nimg, 2, padc, 2 * hd), bf16),
            M((text, 4 * hd), bf16),
            M((16, ch), f32),
            M((3, 16, 128), f32),
            M((3, nrow, 16, 128), f32),
            M((2, 2, wide, ch), f32),
            M((3, ch, 3 * part), f32),
            dma((6,)),
            dma((3, nrow - 1)),
            dma((3, nrow - 1)),
            dma((2, 2)),
            dma((2, 2)),
            dma((13, nimg - 1)),
            dma((13, nimg - 1)),
            dma((1, nrow - 1)),
            dma((1, nrow - 1)),
            dma((7,)),
            dma((7,)),
            dma((7, deep - 1)),
            dma((7, deep - 1)),
            dma((13,)),
        ],
        compiler_params=pltpu.CompilerParams(
            collective_id=4, has_side_effects=True, vmem_limit_bytes=60 * 2**20
        ),
        name="back",
    )(*args)


def finish_kernel(cfg, *refs):
    nrow, nimg, ch, hd, nvec = cfg
    igh, kqh, oqh, crh, everyh, embh, middleh, atth, pouth, parh = refs[:10]
    resh, igouth, k1h, k2h, inh, outh, ctxgh, embgh = refs[10:18]
    vecs = refs[18 : 18 + nvec]
    kq, oq, cr, every, emb, middle, att, pout, par = refs[18 + nvec : 27 + nvec]
    res, k1g, k2g, ing, outg, ctxg, embg, isem, osem = refs[27 + nvec :]
    px = middle.shape[0]
    part = ch // nimg
    me = lax.axis_index("row")
    done = [pltpu.make_async_copy(igh, igouth, osem.at[0])]
    done[0].start()
    pairs = (
        (kqh.at[0], kq.at[0]),
        (kqh.at[1], kq.at[1]),
        (atth, att),
        (pouth, pout),
        (middleh, middle),
        (parh, par),
        (everyh, every),
        (embh, emb),
        (crh, cr),
        (oqh, oq),
    )
    loads = [pltpu.make_async_copy(a, b, isem.at[i]) for i, (a, b) in enumerate(pairs)]
    for c in loads:
        c.start()

    def put(slot, src, dst):
        c = pltpu.make_async_copy(src, dst, osem.at[slot])
        c.start()
        done.append(c)

    for stage, out, dst in ((0, k2g, k2h), (1, k1g, k1h)):
        loads[stage].wait()
        for ky in range(3):
            for b in range(nimg):
                v = kq[stage, ky, b].astype(f32)
                for kx in range(3):
                    out[2 - ky, 2 - kx, :, b * part : (b + 1) * part] = v[
                        :, kx * part : (kx + 1) * part
                    ]
        put(1 + stage, out, dst)
    for c in loads[2:6]:
        c.wait()
    branch = nn(att[...].reshape(ch, px).T, pout[...])
    res[...] = (middle[...] + branch + par[11:12, :]).astype(bf16)
    put(3, res, resh)
    loads[6].wait()
    loads[7].wait()
    acts = emb[:, 0, :].T
    for j in range(2):
        d = None
        for b in range(nimg):
            t = acts[:, b : b + 1] * every[b, 9 + j : 10 + j]
            d = t if d is None else d + t
        embg[:, j * ch : (j + 1) * ch] = d
    put(4, embg, embgh)
    loads[8].wait()
    for b in range(nimg):
        v = cr[b].astype(f32)
        p = [v[:, j * hd : (j + 1) * hd] for j in range(4)]
        ctxg[:, b * 2 * hd : (b + 1) * 2 * hd] = jnp.concatenate([p[0], p[2]], axis=1)
        ctxg[:, ch + b * 2 * hd : ch + (b + 1) * 2 * hd] = jnp.concatenate([p[1], p[3]], axis=1)
    put(5, ctxg, ctxgh)
    loads[9].wait()
    for b in range(nimg):
        v = oq[b].astype(f32)
        for j in range(3):
            ing[:, j * ch + b * 2 * hd : j * ch + (b + 1) * 2 * hd] = jnp.concatenate(
                [v[:, j * hd : (j + 1) * hd], v[:, (3 + j) * hd : (4 + j) * hd]], axis=1
            )
        outg[:, b * part : (b + 1) * part] = v[:, 6 * hd :]
    put(6, ing, inh)
    put(7, outg, outh)
    sums = jnp.sum(every[...], axis=0)
    size = ch // nrow
    turned = pltpu.roll(sums, lax.rem(ch - me * size, ch), 1)
    for i in range(nvec - 1):
        vecs[i][...] = turned[i, :size]
    both = jnp.concatenate([sums[9:10], sums[10:11]], axis=1)
    both = jnp.concatenate([both] * 8, axis=0)
    both = pltpu.roll(both, lax.rem(2 * ch - me * 2 * size, 2 * ch), 1)
    vecs[nvec - 1][...] = both[0, : 2 * size]
    for c in done:
        c.wait()


def finish(nrow, nimg, *args):
    px, ch = args[0].shape
    hd = ch // HEADS
    kq, oq, cr, every, emb = args[1:6]
    rows = ch // nrow
    nvec = 10
    V = pl.BlockSpec(memory_space=pltpu.VMEM)
    A = pl.BlockSpec(memory_space=pl.ANY)
    S = jax.ShapeDtypeStruct
    M = pltpu.VMEM
    dma = pltpu.SemaphoreType.DMA
    outs = (
        ((px, ch), bf16),
        ((3, 3, rows, ch), f32),
        ((3, 3, rows, ch), f32),
        ((rows, 3 * ch), f32),
        ((rows, ch), f32),
        ((cr.shape[1], 2 * ch), f32),
        ((emb.shape[2], 2 * ch), f32),
    )
    return pl.pallas_call(
        functools.partial(finish_kernel, (nrow, nimg, ch, hd, nvec)),
        out_shape=(S(*outs[0]), S((px, ch), f32))
        + tuple(S(*o) for o in outs[1:])
        + (S((rows,), f32),) * (nvec - 1)
        + (S((2 * rows,), f32),),
        in_specs=[A] * 10,
        out_specs=(A,) * 8 + (V,) * nvec,
        scratch_shapes=[M(a.shape, a.dtype) for a in args[1:]]
        + [M(*o) for o in outs]
        + [dma((10,)), dma((8,))],
        compiler_params=pltpu.CompilerParams(vmem_limit_bytes=62 * 2**20),
        name="finish",
    )(*args)


def local_fast(
    images,
    timesteps,
    clip_embed,
    context,
    out_cotangent,
    item_weight,
    first_gain,
    first_bias,
    first_kernel,
    first_offset,
    embed_weight,
    embed_bias,
    second_gain,
    second_bias,
    second_kernel,
    second_offset,
    third_gain,
    third_bias,
    project_in,
    context_weight,
    project_out,
    output_bias,
):
    _, tall, wide, ch = images.shape
    pixels = tall * wide
    nrow = lax.axis_size("row")
    nimg = lax.axis_size("img")
    me_row = lax.axis_index("row")
    nctx = context.shape[1]
    image = images.reshape(pixels, ch)
    cotangent = out_cotangent.reshape(pixels, ch)
    width = clip_embed.shape[1]
    at = jnp.arange(width, dtype=jnp.int32)[None, :]
    half = width // 2
    index = jnp.where(at < half, at, at - half).astype(f32)
    angles = timesteps.astype(f32)[:, None] * jnp.exp(-math.log(10000.0) * index / half)
    embedding = jnp.where(at < half, jnp.cos(angles), jnp.sin(angles)) + clip_embed.astype(f32)
    emb = jax.nn.silu(embedding)
    vectors = [
        v.reshape(1, -1)
        for v in (
            first_gain, first_bias, first_offset, second_gain, second_bias, second_offset,
            third_gain, third_bias, output_bias, embed_bias,
        )
    ]
    w1 = first_kernel.reshape(3, 3 * ch, ch)
    w2 = second_kernel.reshape(3, 3 * ch, ch)
    (
        par, hidden, middle, stats, ss, turned_in, act_three, halo_cot, halo_hidden, halo_middle,
        acts_one, acts_two, ctx_parts, emb_parts, grads, attended, enc_grads,
    ) = front(
        image, cotangent, project_out, context[0], emb, item_weight, vectors, w1, w2, project_in, context_weight,
        embed_weight, nrow, nimg, wide,
    )
    image_grad, kq, oq, cr, every = backward(
        nrow, nimg, wide,
        image, cotangent, par, ss, stats, hidden, middle, halo_cot, halo_hidden, halo_middle, act_three, grads, attended, turned_in,
        w2, w1, acts_two, acts_one, enc_grads, ctx_parts,
    )
    result, image_grad, k1g, k2g, ing, outg, ctxg, embg, *vecs = finish(
        nrow, nimg, image_grad, kq, oq, cr, every, emb_parts, middle, attended, project_out, par
    )
    return (
        result.reshape(images.shape),
        image_grad.reshape(images.shape),
        vecs[0],
        vecs[1],
        k1g,
        vecs[2],
        embg,
        vecs[9],
        vecs[3],
        vecs[4],
        k2g,
        vecs[5],
        vecs[6],
        vecs[7],
        ing,
        ctxg,
        outg,
        vecs[8],
    )


def solution(mesh):
    every = P()
    image = P("img", "row", None, None)
    placed = (image, P("img"), P("img", None), P("img", None, None), image, P("img")) + (every,) * 16
    vec = P("row")
    matrix = P("row", None)
    taps = P(None, None, "row", None)
    nimg, nrow = mesh.shape["img"], mesh.shape["row"]
    quick = nrow == HEADS and nimg == 4
    return jax.shard_map(
        local_fast if quick else local,
        mesh=mesh,
        in_specs=placed,
        out_specs=(
            image,
            image,
            vec,
            vec,
            taps,
            vec,
            matrix,
            vec,
            vec,
            vec,
            taps,
            vec,
            vec,
            vec,
            matrix,
            matrix,
            matrix,
            vec,
        ),
        check_vma=False,
    )
```

```python
import functools
import math

import jax
import jax.numpy as jnp
from jax import lax
from jax.experimental import pallas as pl
from jax.experimental.pallas import tpu as pltpu
from jax.sharding import PartitionSpec as P

HEADS = 8
GROUPS = 32
EPSILON = 1e-05
f32 = jnp.float32
bf16 = jnp.bfloat16
MESH = pl.DeviceIdType.MESH
LOG2E=math.log2(math.e)

def nt(a,b):
    return lax.dot_general(a,b,(((1,),(1,)),((),())),preferred_element_type=f32)
def nn(a,b):
    return jnp.dot(a,b,preferred_element_type=f32)

def attn_kernel(cfg, *refs):
    if cfg[0]:
        q_ref, ctx_ref, g_ref, out_ref, dq_ref, dctx_ref = refs[:6]
        kv_ref, dkv_ref = q_ref, dq_ref
        at_kv = cfg[-1]
    else:
        q_ref, kv_ref, ctx_ref, g_ref, out_ref, dq_ref, dkv_ref, dctx_ref = refs[:8]
        at_kv = 0
    (kx, vx, kt, vt, sbuf, pbuf, acc) = refs[-7:]
    joined, nqs, nsrc, width, bq, kc, nctx, padc, hd = cfg
    npix = nsrc*width
    nk = npix + padc
    ones_rows = jnp.where(lax.broadcasted_iota(jnp.int32,(hd,width),0)<2,1.0,0.0).astype(bf16)
    def fill(pair, at, w):
        k = pair[:hd].astype(f32)*(LOG2E*0.125)
        hi = k.astype(bf16)
        lo = (k-hi.astype(f32)).astype(bf16)
        kx[pl.ds(at,w),:] = jnp.concatenate([hi,lo],axis=0).T
        vfull = jnp.concatenate([pair[hd:], ones_rows[:, :w]],axis=0)
        vx[pl.ds(at,w),:] = vfull.T
        return vfull
    for s in range(nsrc):
        pair = kv_ref[s, at_kv:]
        vfull = fill(pair, s*width, width)
        kt[:, s*width:(s+1)*width] = pair[:hd]
        vt[:, s*width:(s+1)*width] = vfull[:hd+16]
    cpair = ctx_ref[...]
    vfull = fill(cpair, npix, padc)
    kt[:, npix:npix+padc] = cpair[:hd]
    vt[:, npix:npix+padc] = vfull[:hd+16]
    acc[...] = jnp.zeros_like(acc)

    nfull = npix//kc
    per = width//bq
    def block(j, _):
        s = j//per
        off = pl.multiple_of((j%per)*bq, bq)
        qt = q_ref[s,:hd,pl.ds(off,bq)]
        gt = g_ref[s,:,pl.ds(off,bq)]
        q2 = jnp.concatenate([qt,qt],axis=0)
        sc = nn(kx[pl.ds(npix,padc),:], q2)
        sc = jnp.where(lax.broadcasted_iota(jnp.int32,(padc,bq),0)<nctx, sc, -jnp.inf)
        sbuf[pl.ds(npix,padc),:] = sc
        m8 = jnp.max(sc.reshape(padc//8,8,bq),axis=0)
        def phase_a(c, m8):
            at = pl.multiple_of(c*kc,kc)
            sv = nn(kx[pl.ds(at,kc),:], q2)
            sbuf[pl.ds(at,kc),:] = sv
            return jnp.maximum(m8, jnp.max(sv.reshape(kc//8,8,bq),axis=0))
        m8 = lax.fori_loop(0,nfull,phase_a,m8,unroll=True)
        m = jnp.max(m8,axis=0,keepdims=True)
        pc = jnp.exp2(sbuf[pl.ds(npix,padc),:]-m).astype(bf16)
        pbuf[pl.ds(npix,padc),:] = pc
        o = nn(vt[:,npix:npix+padc], pc)
        def phase_b(c, o):
            at = pl.multiple_of(c*kc,kc)
            p = jnp.exp2(sbuf[pl.ds(at,kc),:]-m).astype(bf16)
            pbuf[pl.ds(at,kc),:] = p
            return o + nn(vt[:,pl.ds(at,kc)], p)
        o = lax.fori_loop(0,nfull,phase_b,o,unroll=True)
        inv = 1.0/o[hd:hd+1]
        att = o[:hd]*inv
        out_ref[s,:,pl.ds(off,bq)] = att.astype(bf16)
        gf = gt.astype(f32)
        delta = jnp.sum(gf*att,axis=0,keepdims=True)*inv
        gl = (gf*inv).astype(bf16)
        dhi = (-delta).astype(bf16)
        dlo = (-delta-dhi.astype(f32)).astype(bf16)
        gx = jnp.concatenate([gl,dhi,dlo,jnp.zeros((hd-2,bq),bf16)],axis=0)
        zero = jnp.zeros((hd,bq),bf16)
        rq = jnp.concatenate([qt,zero],axis=0).T
        rg = jnp.concatenate([zero,gl],axis=0).T
        rr = jnp.concatenate([rq,rg],axis=0)
        def piece(at, w, dq):
            p = pbuf[pl.ds(at,w),:]
            dp = nn(vx[pl.ds(at,w),:], gx)
            ds = (p.astype(f32)*dp).astype(bf16)
            acc[pl.ds(at,w),:] += nn(jnp.concatenate([ds,p],axis=1), rr)
            return dq + nn(kt[:,pl.ds(at,w)], ds)
        dq = piece(npix, padc, jnp.zeros((hd,bq),f32))
        def phase_d(c, dq):
            return piece(pl.multiple_of(c*kc,kc), kc, dq)
        dq = lax.fori_loop(0,nfull,phase_d,dq,unroll=True)
        dq_ref[s,:hd,pl.ds(off,bq)] = (dq*0.125).astype(bf16)
        return 0
    lax.fori_loop(0, nqs*per, block, 0)
    scale = jnp.where(lax.broadcasted_iota(jnp.int32,(1,2*hd),1)<hd,0.125,1.0)
    for s in range(nsrc):
        dkv_ref[s, at_kv:] = (acc[s*width:(s+1)*width,:]*scale).astype(bf16).T
    dctx_ref[...] = (acc[npix:npix+padc,:]*scale).astype(bf16)

def attention(q, kv, ctx, g, nctx, bq=512, kc=512):
    joined = kv is None
    nqs, _, width = q.shape
    hd = g.shape[1]
    nsrc = nqs if joined else kv.shape[0]
    padc = ctx.shape[1]
    nk = nsrc*width+padc
    cfg=(joined,nqs,nsrc,width,bq,kc,nctx,padc,hd)
    V=pl.BlockSpec(memory_space=pltpu.VMEM)
    S=jax.ShapeDtypeStruct
    grads=(S((nqs,3*hd,width),bf16),) if joined else (S((nqs,hd,width),bf16),S((nsrc,2*hd,width),bf16))
    args=(q,ctx,g) if joined else (q,kv,ctx,g)
    return pl.pallas_call(
        functools.partial(attn_kernel,cfg),
        out_shape=(S((nqs,hd,width),bf16),)+grads+(S((padc,2*hd),bf16),),
        in_specs=[V]*len(args), out_specs=(V,)*(2+len(grads)),
        scratch_shapes=[pltpu.VMEM((nk,2*hd),bf16),pltpu.VMEM((nk,2*hd),bf16),
                        pltpu.VMEM((hd,nk),bf16),pltpu.VMEM((hd+16,nk),bf16),
                        pltpu.VMEM((nk,bq),f32),pltpu.VMEM((nk,bq),bf16),
                        pltpu.VMEM((nk,2*hd),f32)],
        compiler_params=pltpu.CompilerParams(vmem_limit_bytes=48*2**20),
        cost_estimate=pl.CostEstimate(flops=6*2*64*4096*4228,bytes_accessed=8*2**20,transcendentals=4096*4228),
        name="attend",
    )(*args)

def exchange_kernel(axis, n, x_ref, out_ref, send_sem, recv_sem):
    me = lax.axis_index(axis)
    barrier = pltpu.get_barrier_semaphore()
    for k in range(1, n):
        pl.semaphore_signal(
            barrier, inc=1, device_id={axis: lax.rem(me + k, n)}, device_id_type=MESH
        )
    out_ref[me] = x_ref[...]
    pl.semaphore_wait(barrier, n - 1)
    copies = []
    for k in range(1, n):
        copy = pltpu.make_async_remote_copy(
            src_ref=x_ref,
            dst_ref=out_ref.at[me],
            send_sem=send_sem.at[k - 1],
            recv_sem=recv_sem.at[k - 1],
            device_id={axis: lax.rem(me + k, n)},
            device_id_type=MESH,
        )
        copy.start()
        copies.append(copy)
    for copy in copies:
        copy.wait()


def exchange(x, axis, cid):
    n = lax.axis_size(axis)
    V = pl.BlockSpec(memory_space=pltpu.VMEM)
    return pl.pallas_call(
        functools.partial(exchange_kernel, axis, n),
        out_shape=jax.ShapeDtypeStruct((n,) + x.shape, x.dtype),
        in_specs=[V],
        out_specs=V,
        scratch_shapes=[
            pltpu.SemaphoreType.DMA((n - 1,)),
            pltpu.SemaphoreType.DMA((n - 1,)),
        ],
        compiler_params=pltpu.CompilerParams(collective_id=cid, has_side_effects=True),
        name="exchange_" + axis,
    )(x)


def row_sum(rows):
    x = jnp.concatenate(
        [jnp.stack(rows), jnp.zeros((8 - len(rows), rows[0].shape[0]), f32)], axis=0
    )
    return jnp.sum(exchange(x, "row", 1), axis=0)


def sinusoid(steps, width):
    half_width = width // 2
    frequency = jnp.exp(-math.log(10000.0) * jnp.arange(half_width, dtype=f32) / half_width)
    angles = steps.astype(f32)[:, None] * frequency[None, :]
    return jnp.concatenate([jnp.cos(angles), jnp.sin(angles)], axis=1)


def swish_slope(values):
    sig_v = jax.nn.sigmoid(values)
    return sig_v * (1.0 + values * (1.0 - sig_v))


def per_group(vec, members):
    n = vec.shape[-1]
    g = jnp.sum(vec.reshape(vec.shape[0], GROUPS, n // GROUPS), axis=2) / members
    return jnp.repeat(g, n // GROUPS, axis=1)


def norm_stats(values, members):
    sums = row_sum([jnp.sum(values, axis=0), jnp.sum(values * values, axis=0)])
    means = per_group(sums[:2], members)
    return (means[0], lax.rsqrt(means[1] - means[0] * means[0] + EPSILON))


def halo(x):
    devices = lax.axis_size("row")
    up = [(i, i + 1) for i in range(devices - 1)]
    down = [(i + 1, i) for i in range(devices - 1)]
    before = lax.ppermute(x[-1:], "row", up)
    after = lax.ppermute(x[:1], "row", down)
    return jnp.concatenate([before, x, after], axis=0)


def conv(padded, kernel):
    x = jnp.pad(padded, ((0, 0), (1, 1), (0, 0)))[None]
    return lax.conv_general_dilated(
        x,
        kernel,
        (1, 1),
        "VALID",
        dimension_numbers=("NHWC", "HWIO", "NHWC"),
        preferred_element_type=f32,
    )[0]


def flip_kernel(kernel):
    return jnp.flip(kernel, (0, 1)).transpose(0, 1, 3, 2)


def tn(left, right):
    return lax.dot_general(left, right, (((0,), (0,)), ((), ())), preferred_element_type=f32)


def split_cols(x, n):
    rows, cols = x.shape
    return x.reshape(rows, n, cols // n).transpose(1, 0, 2)


def kernel_grad(acts, grad_padded, tall):
    n = lax.axis_size("img")
    rows, wide, ch = grad_padded.shape
    part = ch // n
    g = lax.all_to_all(
        split_cols(grad_padded.reshape(rows * wide, ch), n),
        "img",
        split_axis=0,
        concat_axis=0,
        tiled=True,
    ).reshape(n, rows, wide, part)
    g = jnp.pad(g, ((0, 0), (0, 0), (1, 1), (0, 0)))
    lines = []
    for ky in range(3):
        for kx in range(3):
            lines.append(
                g[:, 2 - ky : 2 - ky + tall, 2 - kx : 2 - kx + wide].reshape(-1, part)
            )
    return tn(acts, jnp.concatenate(lines, axis=1))


def local(
    images,
    timesteps,
    clip_embed,
    context,
    out_cotangent,
    item_weight,
    first_gain,
    first_bias,
    first_kernel,
    first_offset,
    embed_weight,
    embed_bias,
    second_gain,
    second_bias,
    second_kernel,
    second_offset,
    third_gain,
    third_bias,
    project_in,
    context_weight,
    project_out,
    output_bias,
):
    _, tall, wide, ch = images.shape
    pixels = tall * wide
    hd = ch // HEADS
    nrow = lax.axis_size("row")
    nimg = lax.axis_size("img")
    me_row = lax.axis_index("row")
    gq = nrow // HEADS
    head = me_row // gq
    text = context.shape[2]
    nctx = context.shape[1]
    members = float(nrow * pixels * (ch // GROUPS))

    def gather_img(x):
        return lax.all_gather(x, "img", axis=0, tiled=True)

    grad_out = out_cotangent.reshape(pixels, ch).astype(f32) * (item_weight.astype(f32) * 0.25)
    grad_low = grad_out.astype(bf16)
    attended_grad = (
        lax.dot_general(project_out, grad_low, (((1,), (1,)), ((), ())), preferred_element_type=f32)
        .astype(bf16)
        .reshape(HEADS, hd, pixels)
    )

    def queries_out(x):
        x = x.reshape(HEADS, hd, gq, pixels // gq).transpose(0, 2, 1, 3)
        x = x.reshape(nrow, hd, pixels // gq)
        return x

    def a2a(x):
        return lax.all_to_all(x, "row", split_axis=0, concat_axis=0, tiled=True)

    grad_heads = a2a(queries_out(attended_grad))

    image_f = images.reshape(pixels, ch).astype(f32)
    embedding = sinusoid(timesteps, clip_embed.shape[1]) + clip_embed.astype(f32)
    embed_act = jax.nn.silu(embedding).astype(bf16)
    scale_shift = (jnp.dot(embed_act, embed_weight, preferred_element_type=f32) + embed_bias)[0]
    scale1 = 1.0 + scale_shift[:ch]
    shift = scale_shift[ch:]
    pair_at = (head // 2) * (2 * hd)
    cw_k = lax.dynamic_slice_in_dim(context_weight, pair_at, 2 * hd, 1)
    cw_v = lax.dynamic_slice_in_dim(context_weight, ch + pair_at, 2 * hd, 1)
    cw = jnp.concatenate([cw_k, cw_v], axis=1)
    enc = lax.dot_general(
        cw, context[0], (((0,), (1,)), ((), ())), preferred_element_type=f32
    ).astype(bf16)
    enc = enc.reshape(2, 2, hd, nctx)
    enc = jnp.where(head % 2 == 0, enc[:, 0], enc[:, 1]).reshape(2 * hd, nctx)
    padc = -(-nctx // 16) * 16
    enc = jnp.pad(enc, ((0, 0), (0, padc - nctx)))

    mean1, rstd1 = norm_stats(image_f, members)
    normed1 = (image_f - mean1) * rstd1
    norm_one = normed1 * first_gain + first_bias
    act_one = jax.nn.silu(norm_one).astype(bf16)
    hidden = conv(halo(act_one.reshape(tall, wide, ch)), first_kernel).reshape(pixels, ch)
    hidden = hidden + first_offset
    acts_one = gather_img(act_one)
    mean2, rstd2 = norm_stats(hidden, members)
    normed2 = (hidden - mean2) * rstd2
    affine_two = normed2 * second_gain + second_bias
    norm_two = affine_two * scale1 + shift
    act_two = jax.nn.silu(norm_two).astype(bf16)
    acts_two = gather_img(act_two)
    middle = (
        image_f
        + conv(halo(act_two.reshape(tall, wide, ch)), second_kernel).reshape(pixels, ch)
        + second_offset
    )
    mean3, rstd3 = norm_stats(middle, members)
    normed3 = (middle - mean3) * rstd3
    act_three = (normed3 * third_gain + third_bias).astype(bf16)
    acts_three = gather_img(act_three)
    triple = (
        lax.dot_general(project_in, act_three, (((0,), (1,)), ((), ())), preferred_element_type=f32)
        .astype(bf16)
        .reshape(3, HEADS, hd, pixels)
    )
    if gq == 1:
        recv = a2a(triple.transpose(1, 0, 2, 3).reshape(nrow, 3 * hd, pixels))
        q_h, kv_h = recv[:, :hd], recv[:, hd:]
        grad_h = grad_heads
    else:
        pair = triple[1:].transpose(1, 0, 2, 3).reshape(HEADS, 1, 2 * hd, pixels)
        pair = jnp.broadcast_to(pair, (HEADS, gq, 2 * hd, pixels)).reshape(nrow, 2 * hd, pixels)
        q_h, kv_h = a2a(queries_out(triple[0])), a2a(pair)

        def regroup(x, rows):
            x = x.transpose(1, 0, 2).reshape(rows, -1, 512)
            return x.transpose(1, 0, 2)

        q_h, kv_h, grad_h = regroup(q_h, hd), regroup(kv_h, 2 * hd), regroup(grad_heads, hd)
    att_h, dq_h, dkv_h, dctx = attention(q_h, kv_h, enc, grad_h, nctx)
    if gq == 1:
        attended = a2a(att_h).reshape(ch, pixels)
        back = a2a(jnp.concatenate([dq_h, dkv_h], axis=1)).reshape(HEADS, 3, hd, pixels)
        back = back.transpose(1, 0, 2, 3).reshape(3 * ch, pixels)
    else:

        def ungroup(x, part):
            rows = x.shape[1]
            x = x.transpose(1, 0, 2).reshape(rows, nrow, part)
            return x.transpose(1, 0, 2)

        def from_queries(x):
            x = x.reshape(HEADS, gq, hd, pixels // gq).transpose(0, 2, 1, 3)
            return x.reshape(ch, pixels)

        attended = from_queries(a2a(ungroup(att_h, pixels // gq)))
        dq = from_queries(a2a(ungroup(dq_h, pixels // gq)))
        dkv = a2a(ungroup(dkv_h, pixels)).reshape(HEADS, gq, 2, hd, pixels)
        dkv = jnp.sum(dkv.astype(f32), axis=1).astype(bf16)
        dkv = dkv.transpose(1, 0, 2, 3).reshape(2 * ch, pixels)
        back = jnp.concatenate([dq, dkv], axis=0)
    branch = tn(attended, project_out)
    result_image = (middle + branch + output_bias).astype(bf16)

    part_text = text // nrow
    enc_all = lax.all_gather(dctx[:nctx].astype(bf16), ("img", "row"), axis=0)
    enc_all = enc_all.reshape(nimg, HEADS, gq, nctx, 2, hd)
    if gq > 1:
        enc_all = jnp.sum(enc_all.astype(f32), axis=2, keepdims=True).astype(bf16)
    enc_all = enc_all[:, :, 0].transpose(0, 2, 3, 1, 4).reshape(nimg * nctx, 2 * ch)
    ctx_rows = lax.dynamic_slice_in_dim(context[0], me_row * part_text, part_text, 1)
    ctx_rows = gather_img(ctx_rows)
    context_weight_grad = tn(ctx_rows, enc_all)

    triple_grad = back.T
    act_three_grad = lax.dot_general(
        triple_grad, project_in, (((1,), (1,)), ((), ())), preferred_element_type=f32
    )
    sums3 = row_sum(
        [
            jnp.sum(act_three_grad * normed3, axis=0),
            jnp.sum(act_three_grad, axis=0),
            jnp.sum(grad_out, axis=0),
        ]
    )

    def norm_back(u, normed, rstd, gain, gain_sum, bias_sum):
        means = per_group(jnp.stack([gain * bias_sum, gain * gain_sum]), members)
        return rstd * (u * gain - means[0] - normed * means[1])

    middle_grad = grad_out + norm_back(
        act_three_grad, normed3, rstd3, third_gain, sums3[0], sums3[1]
    )
    middle_low = halo(middle_grad.astype(bf16).reshape(tall, wide, ch))
    act_two_grad = conv(middle_low, flip_kernel(second_kernel)).reshape(pixels, ch)
    norm_two_grad = act_two_grad * swish_slope(norm_two)
    sums2 = row_sum(
        [
            jnp.sum(norm_two_grad * normed2, axis=0),
            jnp.sum(norm_two_grad, axis=0),
            jnp.sum(middle_grad, axis=0),
        ]
    )
    scale_grad = second_gain * sums2[0] + second_bias * sums2[1]
    shift_grad = sums2[1]
    gain2_sum, bias2_sum = scale1 * sums2[0], scale1 * sums2[1]
    hidden_grad = norm_back(
        norm_two_grad * scale1, normed2, rstd2, second_gain, gain2_sum, bias2_sum
    )
    hidden_low = halo(hidden_grad.astype(bf16).reshape(tall, wide, ch))
    act_one_grad = conv(hidden_low, flip_kernel(first_kernel)).reshape(pixels, ch)
    norm_one_grad = act_one_grad * swish_slope(norm_one)
    sums1 = row_sum(
        [
            jnp.sum(norm_one_grad * normed1, axis=0),
            jnp.sum(norm_one_grad, axis=0),
            jnp.sum(hidden_grad, axis=0),
        ]
    )
    image_grad = middle_grad + norm_back(
        norm_one_grad, normed1, rstd1, first_gain, sums1[0], sums1[1]
    )

    def swap_img(x):
        x = split_cols(x, nimg)
        x = lax.all_to_all(x, "img", split_axis=0, concat_axis=0, tiled=True)
        return x.reshape(-1, x.shape[2])

    kg2 = kernel_grad(acts_two, middle_low, tall)
    kg1 = kernel_grad(acts_one, hidden_low, tall)
    pin = tn(acts_three, swap_img(triple_grad))
    pout = tn(gather_img(attended.T), swap_img(grad_low))

    def finish(x):
        x = lax.psum_scatter(x.astype(bf16), "row", scatter_dimension=0, tiled=True)
        return lax.all_gather(x, "img", axis=0).astype(f32)

    c2 = finish(kg2)
    c1 = finish(kg1)
    c3 = finish(jnp.concatenate([pin, pout], axis=1))
    part = ch // nrow
    cols = ch // nimg

    def conv_out(x):
        return x.reshape(nimg, part, 3, 3, cols).transpose(2, 3, 1, 0, 4).reshape(3, 3, part, ch)

    wide_in = 3 * ch // nimg
    pin_out = c3[:, :, :wide_in].transpose(1, 0, 2).reshape(part, 3 * ch)
    pout_out = c3[:, :, wide_in:].transpose(1, 0, 2).reshape(part, ch)

    rows = jnp.stack(
        [
            sums1[0],
            sums1[1],
            sums1[2],
            gain2_sum,
            bias2_sum,
            sums2[2],
            sums3[0],
            sums3[1],
            sums3[2],
            scale_grad,
            shift_grad,
        ]
        + [jnp.zeros((ch,), f32)] * 5
    )
    every = exchange(rows, "img", 2)
    acts_embed = gather_img(embed_act)
    part_emb = embed_act.shape[1] // nrow
    acts_embed = lax.dynamic_slice_in_dim(acts_embed, me_row * part_emb, part_emb, 1).astype(f32)
    shift_scale = every[:, 9:11].reshape(nimg, 2 * ch)
    embed_weight_grad = jnp.sum(acts_embed[:, :, None] * shift_scale[:, None, :], axis=0)
    part_bias = 2 * ch // nrow
    embed_bias_grad = lax.dynamic_slice_in_dim(
        jnp.sum(shift_scale, axis=0), me_row * part_bias, part_bias, 0
    )
    vecs = lax.dynamic_slice_in_dim(jnp.sum(every[:, :9], axis=0), me_row * part, part, 1)
    return (
        result_image.reshape(images.shape),
        image_grad.reshape(images.shape),
        vecs[0],
        vecs[1],
        conv_out(c1),
        vecs[2],
        embed_weight_grad,
        embed_bias_grad,
        vecs[3],
        vecs[4],
        conv_out(c2),
        vecs[5],
        vecs[6],
        vecs[7],
        pin_out,
        context_weight_grad,
        pout_out,
        vecs[8],
    )


def nt_dot(a, b):
    return lax.dot_general(a, b, (((1,), (1,)), ((), ())), preferred_element_type=f32)


def group_total(x):
    per = x.shape[1] // GROUPS
    lane = lax.broadcasted_iota(jnp.int32, x.shape, 1)
    n = x.shape[1]
    step = 1
    while step < per:
        upper = (lane // step) % 2 == 1
        x = x + jnp.where(upper, pltpu.roll(x, step, 1), pltpu.roll(x, n - step, 1))
        step *= 2
    return x


def total(v):
    return jnp.sum(v, axis=0, keepdims=True)


def put_shifts(buf, at, v, wide):
    n, ch = v.shape
    col = lax.rem(lax.broadcasted_iota(jnp.int32, (n, 1), 0), wide)
    buf[pl.ds(at, n), pl.ds(ch, ch)] = v.astype(bf16)
    left = jnp.where(col == 0, 0.0, pltpu.roll(v, 1, 0))
    buf[pl.ds(at, n), pl.ds(0, ch)] = left.astype(bf16)
    right = jnp.where(col == wide - 1, 0.0, pltpu.roll(v, n - 1, 0))
    buf[pl.ds(at, n), pl.ds(2 * ch, ch)] = right.astype(bf16)


class Links:
    def __init__(self, nrow, nimg):
        self.nrow, self.nimg = nrow, nimg
        self.row, self.img = lax.axis_index("row"), lax.axis_index("img")

    def peer(self, axis, k):
        if axis == "row":
            return lax.rem(self.row + k, self.nrow)
        return lax.rem(self.img + k, self.nimg)

    def greet(self):
        barrier = pltpu.get_barrier_semaphore()
        for axis, n in (("row", self.nrow), ("img", self.nimg)):
            for k in range(1, n):
                pl.semaphore_signal(
                    barrier, inc=1, device_id={axis: self.peer(axis, k)}, device_id_type=MESH
                )

    def greeted(self):
        pl.semaphore_wait(pltpu.get_barrier_semaphore(), self.nrow + self.nimg - 2)

    def to(self, axis, at, src, dst, send, recv):
        return pltpu.make_async_remote_copy(
            src_ref=src,
            dst_ref=dst,
            send_sem=send,
            recv_sem=recv,
            device_id={axis: at},
            device_id_type=MESH,
        )

    def copy(self, axis, k, src, dst, send, recv):
        return self.to(axis, self.peer(axis, k), src, dst, send, recv)


class Stats:
    def __init__(self, links, src, dst, send, recv):
        self.links, self.src, self.dst, self.send, self.recv = links, src, dst, send, recv

    def start(self, stage, rows):
        links = self.links
        ch = rows[0].shape[1]
        blocks = [r[:, i * 128 : (i + 1) * 128] for r in rows for i in range(ch // 128)]
        height = self.src.shape[1]
        blocks = blocks + [jnp.zeros((1, 128), f32)] * (height - len(blocks))
        packed = jnp.concatenate(blocks, axis=0)
        self.src[stage] = packed
        self.dst[stage, links.row] = packed
        self.rows, self.per = len(rows), ch // 128
        self.copies = []
        for k in range(1, links.nrow):
            c = links.copy(
                "row",
                k,
                self.src.at[stage],
                self.dst.at[stage, links.row],
                self.send.at[stage, k - 1],
                self.recv.at[stage, k - 1],
            )
            c.start()
            self.copies.append(c)

    def finish(self, stage):
        for c in self.copies:
            c.wait()
        s = jnp.sum(self.dst[stage], axis=0)
        per = self.per
        rows = [
            jnp.concatenate([s[r * per + i : r * per + i + 1] for i in range(per)], axis=1)
            for r in range(self.rows)
        ]
        return jnp.concatenate(rows + [jnp.zeros((8 - self.rows, per * 128), f32)], axis=0)


class Halo:
    def __init__(self, links, send, recv):
        self.links, self.send, self.recv = links, send, recv

    def copies(self, slot, first, last, land):
        links = self.links
        down = links.copy(
            "row", links.nrow - 1, first, land.at[1],
            self.send.at[slot, 0], self.recv.at[slot, 1],
        )
        up = links.copy(
            "row", 1, last, land.at[0],
            self.send.at[slot, 1], self.recv.at[slot, 0],
        )
        return down, up

    def start(self, slot, first, last, land):
        links = self.links
        down, up = self.copies(slot, first, last, land)

        @pl.when(links.row > 0)
        def _():
            down.start()

        @pl.when(links.row < links.nrow - 1)
        def _():
            up.start()

        @pl.when(links.row == 0)
        def _():
            land[0] = jnp.zeros(land.shape[1:], land.dtype)

        @pl.when(links.row == links.nrow - 1)
        def _():
            land[1] = jnp.zeros(land.shape[1:], land.dtype)

        return down, up

    def finish(self, pair):
        links = self.links
        down, up = pair

        @pl.when(links.row > 0)
        def _():
            down.wait_send()
            up.wait_recv()

        @pl.when(links.row < links.nrow - 1)
        def _():
            up.wait_send()
            down.wait_recv()


def put_block(links, buf, mid, before, after, wide):
    put_shifts(buf, wide, mid, wide)
    put_shifts(buf, 0, jnp.where(links.row > 0, before, 0.0), wide)
    put_shifts(buf, buf.shape[0] - wide, jnp.where(links.row < links.nrow - 1, after, 0.0), wide)


def front_kernel(
    cfg,
    *refs,
):
    nvec = cfg[-1]
    _front(cfg[:-1], *refs[:6], refs[6 : 6 + nvec], *refs[6 + nvec :])


def _front(
    cfg,
    r_img,
    r_oc,
    r_pout,
    r_cxt,
    r_embv,
    r_weight,
    r_vecs,
    r_w1h,
    r_w2h,
    r_winh,
    r_cwh,
    r_ewh,
    r_par,
    r_hidden,
    r_middle,
    r_stats,
    r_ss,
    r_wt,
    r_a3,
    r_hoc,
    r_hhid,
    r_hmid,
    r_a1h,
    r_a2h,
    r_ctxh,
    r_embh,
    r_tgh,
    r_atth,
    r_ench,
    r_emb,
    r_himg,
    r_gx,
    r_dqa,
    r_cw,
    r_ctx,
    r_buf,
    r_at,
    r_gs,
    r_ts,
    r_qkv,
    r_g,
    r_kx,
    r_vx,
    r_kt,
    r_vt,
    r_sb,
    r_pb,
    r_acc,
    r_atb,
    r_dqb,
    r_dcb,
    r_st_src,
    r_st_dst,
    r_wsem,
    r_vsem,
    r_st_send,
    r_st_recv,
    r_h_send,
    r_h_recv,
    r_i_send,
    r_i_recv,
    r_r_send,
    r_r_recv,
    r_osem,
):
    nrow, nimg, wide, ch, hd, kc, joint = cfg
    px = r_img.shape[0]
    members = float(nrow * px * (ch // GROUPS))
    links = Links(nrow, nimg)
    links.greet()
    head = links.row
    me = links.row

    def pair_at(at):
        return pl.ds(pl.multiple_of(at + (head // 2) * (2 * hd), 128), 2 * hd)

    deep = 3 * ch
    at_ew, at_win, at_w1 = 0, 2 * r_embv.shape[1], 2 * r_embv.shape[1] + deep
    at_w2 = at_w1 + 3 * deep
    text_in = r_embv.shape[1]
    groups = (
        [(r_w1h.at[k], at_w1 + k * deep, deep) for k in range(3)],
        [(r_ewh.at[:, k * ch : (k + 1) * ch], at_ew + k * text_in, text_in) for k in range(2)],
        [(r_winh.at[:, k * ch : (k + 1) * ch], at_win + k * ch, ch) for k in range(3)],
        [(r_w2h.at[k], at_w2 + k * deep, deep) for k in range(3)],
    )
    count = 0
    loads = []
    for group in groups:
        loads.append([])
        for src, at, n in group:
            c = pltpu.make_async_copy(src, r_pb.at[pl.ds(at, n)], r_wsem.at[count])
            c.start()
            loads[-1].append(c)
            count += 1
    loads.append([])
    for src, dst in (
        (r_cwh.at[:, pair_at(0)], r_cw.at[:, : 2 * hd]),
        (r_cwh.at[:, pair_at(ch)], r_cw.at[:, 2 * hd :]),
    ):
        c = pltpu.make_async_copy(src, dst, r_wsem.at[count])
        c.start()
        loads[-1].append(c)
        count += 1
    load_w1, load_ew, load_win, load_w2, load_cw = loads

    def ready(copies):
        for c in copies:
            c.wait()

    places = (0, 1, 2, 3, 4, 7, 8, 9, 11, 12, 13)
    flat = [v for v in r_vecs[:-1]] + [r_vecs[-1].at[:, :ch], r_vecs[-1].at[:, ch:]]
    vec_loads = [
        pltpu.make_async_copy(v, r_par.at[pl.ds(at, 1)], r_vsem.at[i])
        for i, (v, at) in enumerate(zip(flat, places))
    ]
    for c in vec_loads:
        c.start()
    weight = r_weight[0].astype(f32) * 0.25
    for at in (5, 6, 14, 15):
        r_par[at : at + 1, :] = jnp.zeros((1, ch), f32)
    r_par[10:11, :] = jnp.full((1, ch), 1.0, f32) * weight
    stats = Stats(links, r_st_src, r_st_dst, r_st_send, r_st_recv)
    halo = Halo(links, r_h_send, r_h_recv)
    ends = (pl.ds(0, wide), pl.ds(px - wide, wide))

    def edges(slot, block, land):
        return halo.start(slot, block.at[ends[0]], block.at[ends[1]], land)

    pending = []

    def par(i):
        return r_par[i : i + 1, :]

    def share(slot, src, dst):
        copies = [pltpu.make_async_copy(src(links.img), dst(links.img), r_osem.at[slot])]
        for k in range(1, nimg):
            copies.append(
                links.copy(
                    "img", k, src(links.peer("img", k)), dst(links.img),
                    r_i_send.at[slot, k - 1], r_i_recv.at[slot, k - 1],
                )
            )
        for c in copies:
            c.start()
        pending.extend(copies)

    def scatter(slot, src, dst):
        copies = []
        for k in range(1, nrow):
            copies.append(
                links.copy(
                    "row", k, src(links.peer("row", k)), dst(me),
                    r_r_send.at[slot, k - 1], r_r_recv.at[slot, k - 1],
                )
            )
        for c in copies:
            c.start()
        return copies

    def lanes(img):
        return pl.ds(pl.multiple_of(img * px, 128), px)

    def moments(v):
        return [total(v), total(v * v)]

    def center(stage, sums):
        means = group_total(sums) * (1.0 / members)
        mean = means[0:1]
        rstd = lax.rsqrt(means[1:2] - mean * mean + EPSILON)
        r_stats[2 * stage : 2 * stage + 1, :] = mean
        r_stats[2 * stage + 1 : 2 * stage + 2, :] = rstd
        return mean, rstd

    r_stats[...] = jnp.zeros_like(r_stats)
    rows = moments(r_img[...].astype(f32))
    low = (r_oc[...].astype(f32) * weight).astype(bf16)
    r_gs[...] = nt_dot(r_pout[...], low).astype(bf16).reshape(r_gs.shape)
    r_emb[...] = jnp.broadcast_to(r_embv[...].astype(bf16).astype(f32), r_emb.shape)
    links.greeted()
    stats.start(0, rows)
    c_img = edges(0, r_img, r_himg)
    c_g = scatter(2, lambda r: r_gs.at[r], lambda r: r_g.at[r])
    for c in vec_loads:
        c.wait()
    ready(load_ew)
    emb = r_emb[...].astype(bf16)
    scale1 = 1.0 + (nn(emb, r_pb[at_ew : at_ew + text_in])[0:1] + par(12))
    shift = nn(emb, r_pb[at_ew + text_in : at_ew + 2 * text_in])[0:1] + par(13)
    r_ss[...] = jnp.concatenate([scale1, shift, jnp.zeros((6, ch), f32)], axis=0)
    mean, rstd = center(0, stats.finish(0))

    def conv_stage(stage, act, before, after, weights):
        buf = r_buf
        put_block(links, buf, act, before, after, wide)
        acc = None
        for ky in range(3):
            d = nn(
                buf[pl.ds(ky * wide, px), :],
                r_pb[weights + ky * deep : weights + (ky + 1) * deep, :],
            )
            acc = d if acc is None else acc + d
        r_at[stage] = act.astype(bf16).T
        return acc


    def act_one(v):
        return jax.nn.silu((v.astype(f32) - mean) * rstd * par(0) + par(1))

    halo.finish(c_img)
    ready(load_w1)
    hidden = conv_stage(
        0, act_one(r_img[...]), act_one(r_himg[0]), act_one(r_himg[1]), at_w1
    ) + par(2)
    r_hidden[...] = hidden
    stats.start(1, moments(hidden))
    c_hid = edges(1, r_hidden, r_hhid)
    ready(load_win)
    for j in range(3):
        turned = r_pb[at_win + j * ch : at_win + (j + 1) * ch, :].T
        for h in range(HEADS):
            r_wt[(3 * h + j) * hd : (3 * h + j + 1) * hd, :] = turned[h * hd : (h + 1) * hd]
    mean_two, rstd_two = center(1, stats.finish(1))

    def act_two(v):
        affine = (v - mean_two) * rstd_two * par(3) + par(4)
        return jax.nn.silu(affine * r_ss[0:1] + r_ss[1:2])

    halo.finish(c_hid)
    ready(load_w2)
    middle = conv_stage(1, act_two(r_hidden[...]), act_two(r_hhid[0]), act_two(r_hhid[1]), at_w2)
    middle = r_img[...].astype(f32) + middle + par(7)
    r_middle[...] = middle
    stats.start(2, moments(middle))
    c_mid = edges(2, r_middle, r_hmid)
    c_oc = edges(3, r_oc, r_hoc)
    nctx, text = r_cxt.shape
    padc = r_ctx.shape[0]
    r_ctx[...] = jnp.concatenate(
        [r_cxt[...], jnp.zeros((padc - nctx, text), bf16)], axis=0
    )
    ready(load_cw)
    enc = nn(r_ctx[...], r_cw[...]).T.astype(bf16)
    first = lax.rem(head, 2) == 0
    enc = jnp.concatenate(
        [
            jnp.where(first, enc[2 * j * hd : (2 * j + 1) * hd], enc[(2 * j + 1) * hd : (2 * j + 2) * hd])
            for j in range(2)
        ],
        axis=0,
    )
    mean, rstd = center(2, stats.finish(2))
    act3 = ((r_middle[...] - mean) * rstd * par(8) + par(9)).astype(bf16)
    r_a3[...] = act3.T
    ts, qkv, gs, g = r_ts, r_qkv, r_gs, r_g
    ts[...] = nn(r_wt[...], r_a3[...]).astype(bf16).reshape(ts.shape)
    tall = nrow // 2
    row_z, row_x = me // 2, lax.rem(me, 2)

    def source(i):
        z = lax.rem(row_z + lax.rem((i + 1) // 2, tall), tall)
        return 2 * z + lax.rem(row_x + i + 1, 2)

    def target(i):
        z = lax.rem(row_z + tall - lax.rem((i + 1) // 2, tall), tall)
        return 2 * z + lax.rem(row_x + i + 1, 2)

    def q_copy(i):
        to = target(i)
        return links.to(
            "row", to, ts.at[to, pl.ds(0, hd)], qkv.at[me, pl.ds(0, hd)],
            r_r_send.at[1, i], r_r_recv.at[1, i],
        )

    q_copy(0).start()
    c_kv = scatter(0, lambda r: ts.at[r, pl.ds(hd, 2 * hd)], lambda r: qkv.at[r, pl.ds(hd, 2 * hd)])
    npix = nrow * px
    ones_rows = jnp.where(lax.broadcasted_iota(jnp.int32, (hd, px), 0) < 2, 1.0, 0.0).astype(bf16)
    kx, vx, kt, vt, sb, pb, acc = (r_kx, r_vx, r_kt, r_vt, r_sb, r_pb, r_acc)

    def fill(pair, at, w):
        k = pair[:hd].astype(f32) * (LOG2E * 0.125)
        hi = k.astype(bf16)
        lo = (k - hi.astype(f32)).astype(bf16)
        kx[pl.ds(at, w), :] = jnp.concatenate([hi, lo], axis=0).T
        vfull = jnp.concatenate([pair[hd:], ones_rows[:, :w]], axis=0)
        vx[pl.ds(at, w), :] = vfull.T
        kt[:, pl.ds(at, w)] = pair[:hd]
        vt[:, pl.ds(at, w)] = vfull[: hd + 16]

    fill(enc, npix, padc)
    qkv[me] = ts[me]
    g[me] = gs[me]
    acc[...] = jnp.zeros_like(acc)

    def own(r):
        return pl.multiple_of(r * px, 128)

    fill(ts[me, hd:], own(me), px)
    for k in range(1, nrow):
        c_kv[k - 1].wait()
        frm = lax.rem(me + nrow - k, nrow)
        fill(qkv[frm, hd:], own(frm), px)


    q_copy(1).start()
    for i in range(2):
        share(i, lambda p, i=i: r_at.at[i], lambda p, i=i: (r_a1h, r_a2h)[i].at[:, lanes(p)])
    mine = text // nrow
    text_at = pl.ds(pl.multiple_of(me * mine, 128), mine)
    share(2, lambda p: r_ctx.at[:, text_at], lambda p: r_ctxh.at[p])
    wide_emb = r_emb.shape[1] // nrow
    emb_at = pl.ds(pl.multiple_of(me * wide_emb, 128), wide_emb)
    share(3, lambda p: r_emb.at[:, emb_at], lambda p: r_embh.at[p])
    halo.finish(c_mid)
    halo.finish(c_oc)

    bq = px
    nfull = npix // kc

    def att_copy(i):
        to = source(i)
        return links.to(
            "row", to, r_atb.at[to], r_atth.at[me], r_r_send.at[3, i], r_r_recv.at[3, i]
        )

    def dq_copy(i):
        to = source(i)
        return links.to(
            "row", to, r_dqb.at[to, pl.ds(0, hd)], r_tgh.at[me, pl.ds(0, hd)],
            r_r_send.at[4, i], r_r_recv.at[4, i],
        )

    nk = npix + padc

    def scores(i, slot):
        s = source(i)
        base = pl.multiple_of(slot * nk, 16)

        @pl.when(i + 2 < nrow - 1)
        def _():
            q_copy(i + 2).start()

        @pl.when(i < nrow - 1)
        def _():
            q_copy(i).wait_recv()
            k = lax.rem(me - s + nrow, nrow) - 1
            links.to("row", s, gs.at[s], g.at[s], r_r_send.at[2, k], r_r_recv.at[2, k]).wait_recv()

        qt = qkv[s, :hd]
        gt = g[s]
        q2 = jnp.concatenate([qt, qt], axis=0)
        sc = nn(kx[pl.ds(npix, padc), :], q2)
        sc = jnp.where(lax.broadcasted_iota(jnp.int32, (padc, bq), 0) < nctx, sc, -jnp.inf)
        sb[pl.ds(npix, padc), :] = sc
        m8 = jnp.max(sc.reshape(padc // 8, 8, bq), axis=0)

        def phase_a(c, m8):
            at = pl.multiple_of(c * kc, kc)
            sv = nn(kx[pl.ds(at, kc), :], q2)
            sb[pl.ds(at, kc), :] = sv
            return jnp.maximum(m8, jnp.max(sv.reshape(kc // 8, 8, bq), axis=0))

        m8 = lax.fori_loop(0, nfull, phase_a, m8, unroll=True)
        m = jnp.max(m8, axis=0, keepdims=True)
        pc = jnp.exp2(sb[pl.ds(npix, padc), :] - m).astype(bf16)
        pb[pl.ds(base + npix, padc), :] = pc
        o = nn(vt[:, npix : npix + padc], pc)

        def phase_b(c, o):
            at = pl.multiple_of(c * kc, kc)
            p = jnp.exp2(sb[pl.ds(at, kc), :] - m).astype(bf16)
            pb[pl.ds(pl.multiple_of(base + at, 16), kc), :] = p
            return o + nn(vt[:, pl.ds(at, kc)], p)

        o = lax.fori_loop(0, nfull, phase_b, o, unroll=True)
        inv = 1.0 / o[hd : hd + 1]
        att = o[:hd] * inv
        r_atb[s] = att.astype(bf16)

        @pl.when(i < nrow - 1)
        def _():
            att_copy(i).start()

        gf = gt.astype(f32)
        delta = total(gf * att) * inv
        gl = (gf * inv).astype(bf16)
        dhi = (-delta).astype(bf16)
        dlo = (-delta - dhi.astype(f32)).astype(bf16)
        r_gx[slot] = jnp.concatenate([gl, dhi, dlo, jnp.zeros((hd - 2, bq), bf16)], axis=0)
        r_dqa[slot] = piece(slot, qt, npix, padc, jnp.zeros((hd, bq), f32))

    def piece(slot, qt, at, w, dq):
        gx = r_gx[slot]
        p = pb[pl.ds(pl.multiple_of(slot * nk + at, 16), w), :]
        dp = nn(vx[pl.ds(at, w), :], gx)
        ds = (p.astype(f32) * dp).astype(bf16)
        acc[:hd, pl.ds(at, w)] += nt_dot(qt, ds)
        acc[hd:, pl.ds(at, w)] += nt_dot(gx[:hd], p)
        return dq + nn(kt[:, pl.ds(at, w)], ds)

    def block(i, _):
        s = source(i)
        scores(i, 0)
        qt = qkv[s, :hd]

        def phase_d(c, dq):
            return piece(0, qt, pl.multiple_of(c * kc, kc), kc, dq)

        dq = lax.fori_loop(0, nfull, phase_d, r_dqa[0], unroll=True)
        r_dqb[s, :hd] = (dq * 0.125).astype(bf16)
        dq_copy(i).start()
        return 0

    alone = nrow - joint
    lax.fori_loop(0, alone, block, 0)
    scale = jnp.where(lax.broadcasted_iota(jnp.int32, (2 * hd, 1), 0) < hd, 0.125, 1.0)

    def first(j, _):
        scores(alone + j, j)
        return 0

    lax.fori_loop(0, joint, first, 0)

    def key_home(c):
        z = lax.rem(row_z + 1 + c // 2, tall)
        return 2 * z + lax.rem(row_x + c + 1, 2)

    def kv_back(c):
        s = key_home(c)
        return links.to(
            "row", s, r_dqb.at[s, pl.ds(hd, 2 * hd)], r_tgh.at[me, pl.ds(hd, 2 * hd)],
            r_r_send.at[5, c], r_r_recv.at[5, c],
        )

    def keys_done(c, _):
        z = lax.rem(row_z + 1 + c, tall)
        at = pl.multiple_of(z * (2 * px), 128)
        for j in range(joint):
            qt = qkv[source(alone + j), :hd]
            r_dqa[j] = piece(j, qt, at, 2 * px, r_dqa[j])
        for h in range(2):
            s = key_home(2 * c + h)
            r_dqb[s, hd:] = (acc[:, pl.ds(own(s), px)] * scale).astype(bf16)

            @pl.when(2 * c + h < nrow - 1)
            def _():
                kv_back(2 * c + h).start()

        return 0

    lax.fori_loop(0, tall, keys_done, 0, unroll=True)
    copies = []
    for j in range(joint):
        r_dqb[source(alone + j), :hd] = (r_dqa[j] * 0.125).astype(bf16)
        if alone + j < nrow - 1:
            dq_copy(alone + j).start()
    r_dcb[...] = (acc[:, npix : npix + padc] * scale).astype(bf16).T
    copies += scatter(6, lambda r: r_dcb, lambda r: r_ench.at[r])
    for i, (a, b) in enumerate(
        (
            (r_dqb.at[me], r_tgh.at[me]),
            (r_atb.at[me], r_atth.at[me]),
            (r_dcb, r_ench.at[me]),
        )
    ):
        c = pltpu.make_async_copy(a, b, r_osem.at[4 + i])
        c.start()
        copies.append(c)
    for i in range(nrow - 1):
        q_copy(i).wait_send()
    for c in c_g:
        c.wait_send()
    for i in range(nrow - 1):
        att_copy(i).wait()
        dq_copy(i).wait()
        kv_back(i).wait()
    for c in copies + pending:
        c.wait()


def front(
    images, out_cot, project_out, context, emb, weight, vectors, w1, w2, win, cw, ew, nrow, nimg, wide
):
    px, ch = images.shape
    hd = ch // HEADS
    padc = -(-context.shape[0] // 16) * 16
    cfg = (nrow, nimg, wide, ch, hd, 1024, 3, len(vectors))
    nk = nrow * px + padc
    joint = cfg[6]
    V = pl.BlockSpec(memory_space=pltpu.VMEM)
    A = pl.BlockSpec(memory_space=pl.ANY)
    S = jax.ShapeDtypeStruct
    M = pltpu.VMEM
    dma = pltpu.SemaphoreType.DMA
    return pl.pallas_call(
        functools.partial(front_kernel, cfg),
        out_shape=(
            S((16, ch), f32),
            S((px, ch), f32),
            S((px, ch), f32),
            S((8, ch), f32),
            S((8, ch), f32),
            S((3 * ch, ch), bf16),
            S((ch, px), bf16),
            S((2, wide, ch), bf16),
            S((2, wide, ch), f32),
            S((2, wide, ch), f32),
            S((ch, nimg * px), bf16),
            S((ch, nimg * px), bf16),
            S((nimg, padc, context.shape[1] // nrow), bf16),
            S((nimg, 8, emb.shape[1] // nrow), f32),
            S((nrow, 3 * hd, px), bf16),
            S((nrow, hd, px), bf16),
            S((nrow, padc, 2 * hd), bf16),
        ),
        in_specs=[V] * 5
        + [pl.BlockSpec(memory_space=pltpu.SMEM)]
        + [A] * (len(vectors) + 5),
        out_specs=(V,) * 10 + (A,) * 7,
        scratch_shapes=[
            M((8, emb.shape[1]), f32),
            M((2, wide, ch), bf16),
            M((joint, 2 * hd, px), bf16),
            M((joint, hd, px), f32),
            M((cw.shape[0], 4 * hd), bf16),
            M((padc, cw.shape[0]), bf16),
            M((px + 2 * wide, 3 * ch), bf16),
            M((2, ch, px), bf16),
            M((nrow, hd, px), bf16),
            M((nrow, 3 * hd, px), bf16),
            M((nrow, 3 * hd, px), bf16),
            M((nrow, hd, px), bf16),
            M((nk, 2 * hd), bf16),
            M((nk, 2 * hd), bf16),
            M((hd, nk), bf16),
            M((hd + 16, nk), bf16),
            M((nk, px), f32),
            M((max(joint * nk, 2 * emb.shape[1] + 21 * ch), px), bf16),
            M((2 * hd, nk), f32),
            M((nrow, hd, px), bf16),
            M((nrow, 3 * hd, px), bf16),
            M((padc, 2 * hd), bf16),
            M((3, 8, 128), f32),
            M((3, nrow, 8, 128), f32),
            dma((13,)),
            dma((11,)),
            dma((3, nrow - 1)),
            dma((3, nrow - 1)),
            dma((4, 2)),
            dma((4, 2)),
            dma((4, nimg - 1)),
            dma((4, nimg - 1)),
            dma((7, nrow - 1)),
            dma((7, nrow - 1)),
            dma((8,)),
        ],
        compiler_params=pltpu.CompilerParams(
            collective_id=3, has_side_effects=True, vmem_limit_bytes=62 * 2**20
        ),
        name="front",
    )(images, out_cot, project_out, context, emb, weight, *vectors, w1, w2, win, cw, ew)
def slope(values):
    sig = jax.nn.sigmoid(values)
    return sig * (1.0 + values * (1.0 - sig))


def back_kernel(
    cfg,
    r_img,
    r_oc,
    r_par,
    r_ss,
    r_stats,
    r_hidden,
    r_middle,
    r_hoc,
    r_hhid,
    r_hmid,
    r_a3,
    r_tg,
    r_att,
    r_wt,
    r_w2h,
    r_w1h,
    r_a2h,
    r_a1h,
    r_ench,
    r_ctxh,
    r_igrad,
    r_kq,
    r_oq,
    r_cr,
    r_every,
    r_w2,
    r_w1,
    r_a2,
    r_a1,
    r_enc,
    r_ctx,
    r_mg,
    r_ntg,
    r_buf,
    r_gq,
    r_gs,
    r_ks,
    r_kx,
    r_km,
    r_kz,
    r_kf,
    r_os,
    r_ox,
    r_oy,
    r_oz,
    r_of,
    r_encq,
    r_cq,
    r_vsrc,
    r_st_src,
    r_st_dst,
    r_hu,
    r_kacc,
    r_lsem,
    r_st_send,
    r_st_recv,
    r_h_send,
    r_h_recv,
    r_i_send,
    r_i_recv,
    r_r_send,
    r_r_recv,
    r_x_send,
    r_x_recv,
    r_z_send,
    r_z_recv,
    r_osem,
):
    nrow, nimg, wide, ch, hd, padc = cfg
    px = r_img.shape[0]
    part = ch // nimg
    rows = ch // nrow
    deep = nrow // 2
    members = float(nrow * px * (ch // GROUPS))
    links = Links(nrow, nimg)
    links.greet()
    pairs = (
        (r_w2h, r_w2),
        (r_a2h, r_a2),
        (r_w1h, r_w1),
        (r_a1h, r_a1),
        (r_ench, r_enc),
        (r_ctxh, r_ctx),
    )
    loads = [pltpu.make_async_copy(a, b, r_lsem.at[i]) for i, (a, b) in enumerate(pairs)]
    for c in loads:
        c.start()
    load_w2, load_a2, load_w1, load_a1, load_enc, load_ctx = loads
    stats = Stats(links, r_st_src, r_st_dst, r_st_send, r_st_recv)
    halo = Halo(links, r_h_send, r_h_recv)
    ends = (pl.ds(0, wide), pl.ds(px - wide, wide))

    def edges(slot, block, land):
        return halo.start(slot, block.at[ends[0]], block.at[ends[1]], land)

    others = (
        links.img + 1 - 2 * lax.rem(links.img, 2),
        lax.rem(links.img + 2, nimg),
        nimg - 1 - links.img,
    )
    row_z, row_x = links.row // 2, lax.rem(links.row, 2)
    img_y, img_c = links.img // 2, lax.rem(links.img, 2)

    def par(i):
        return r_par[i : i + 1, :]

    def stat(i):
        return r_stats[i : i + 1, :]

    scale1, shift = r_ss[0:1], r_ss[1:2]

    def share(slot, src, dst):
        copies = [pltpu.make_async_copy(src(links.img), dst(links.img), r_osem.at[slot])]
        for k, at in enumerate(others):
            copies.append(
                links.to(
                    "img", at, src(at), dst(links.img), r_i_send.at[slot, k], r_i_recv.at[slot, k]
                )
            )
        for c in copies:
            c.start()
        return copies

    def wait(copies):
        for c in copies:
            c.wait()

    def columns(at, img):
        return pl.ds(pl.multiple_of(at + img * part, 128), part)

    def row_x_start(slot, src, land):
        c = links.to(
            "row", links.row + 1 - 2 * row_x, src.at[:, 1 - row_x], land,
            r_x_send.at[slot], r_x_recv.at[slot],
        )
        c.start()
        return c

    def row_z_start(slot, c, src, land, mid, last):
        c.wait()
        mid[...] = (src[:, row_x].astype(f32) + land[...].astype(f32)).astype(bf16)
        copies = []
        for k in range(1, deep):
            z = lax.rem(row_z + k, deep)
            copies.append(
                links.to(
                    "row", 2 * z + row_x, mid.at[z], last.at[k - 1],
                    r_z_send.at[slot, k - 1], r_z_recv.at[slot, k - 1],
                )
            )
        for d in copies:
            d.start()
        return copies

    def row_end(copies, mid, last):
        wait(copies)
        s = mid[row_z].astype(f32)
        for k in range(1, deep):
            s = s + last[k - 1].astype(f32)
        return s.astype(bf16)

    def back_means(gain, gain_sum, bias_sum):
        both = jnp.concatenate([gain * bias_sum, gain * gain_sum, jnp.zeros((6, ch), f32)], axis=0)
        return group_total(both) * (1.0 / members)

    def norm_back(u, normed, rstd, gain, means):
        return rstd * (u * gain - means[0:1] - normed * means[1:2])

    def conv_back(stage, grad, before, after, weights):
        buf = r_buf.at[stage]
        put_block(links, buf, grad, before, after, wide)
        copies = share(
            stage, lambda i: buf.at[:, columns(ch, i)], lambda i: r_gq.at[stage, i]
        )
        acc = None
        for ky in range(3):
            for kx in range(3):
                g = buf[pl.ds(ky * wide, px), pl.ds(kx * ch, ch)]
                w = weights[2 - ky, pl.ds((2 - kx) * ch, ch), :]
                d = nt_dot(g, w)
                acc = d if acc is None else acc + d
        return acc, copies

    def kernel_part(stage, acts, ky, images):
        tot = None
        for b in images:
            at = pl.ds(pl.multiple_of(b * px, 128), px)
            d = nn(acts[:, at], r_gs[b, ky * wide : ky * wide + px, :])
            tot = d if tot is None else tot + d
        return tot

    def kernel_grads(stage, acts, copies):
        near, far = (links.img, others[0]), others[1:]
        for group, first in ((near, True), (far, False)):
            for b, c in zip(group, copies[:2] if first else copies[2:]):
                c.wait()
                put_shifts(r_gs.at[b], 0, r_gq[stage, b].astype(f32), wide)
            if first:
                for ky in range(3):
                    r_kacc[ky] = kernel_part(stage, acts, ky, near)
        sent = []
        for ky in range(3):
            tot = r_kacc[ky] + kernel_part(stage, acts, ky, far)
            r_ks[stage, ky] = tot.astype(bf16).reshape(deep, 2, rows, 3 * part)
            sent.append(row_x_start(3 * stage + ky, r_ks.at[stage, ky], r_kx.at[stage, ky]))
        return sent

    def kernel_mid(stage, sent, ky):
        return row_z_start(
            3 * stage + ky, sent[ky], r_ks.at[stage, ky], r_kx.at[stage, ky],
            r_km.at[stage, ky], r_kz.at[stage, ky],
        )

    def kernel_end(stage, copies):
        out = []
        for ky in range(3):
            r_kf[stage, ky] = row_end(copies[ky], r_km.at[stage, ky], r_kz.at[stage, ky])
            out += share(
                2 + 3 * stage + ky,
                lambda i, ky=ky: r_kf.at[stage, ky],
                lambda i, ky=ky: r_kq.at[stage, ky, i],
            )
        return out

    tgt = r_tg[...].reshape(3 * ch, px)
    u3 = nn(tgt.T, r_wt[...])
    normed3 = (r_middle[...] - stat(4)) * stat(5)
    grad_out = r_oc[...].astype(f32) * par(10)
    r_mg[...] = u3
    sums = [total(u3 * normed3), total(u3), total(grad_out)]
    links.greeted()
    stats.start(0, sums)
    c_u = edges(0, r_mg, r_hu.at[0])
    load_enc.wait()
    c_encq = share(8, lambda i: r_enc.at[pl.ds(2 * i, 2)], lambda i: r_encq.at[i])
    a3 = r_a3[...]
    low = (r_oc[...].astype(f32) * par(10)).astype(bf16)
    pout = nn(r_att[...].reshape(ch, px), low).astype(bf16)
    for q in range(nimg):
        pin = nt_dot(a3, r_tg[2 * q : 2 * q + 2].reshape(6 * hd, px)).astype(bf16)
        r_os[q // 2, q % 2] = jnp.concatenate(
            [pin, pout[:, q * part : (q + 1) * part]], axis=1
        )
    c_ox = links.to(
        "img", links.img + 1 - 2 * img_c, r_os.at[:, 1 - img_c], r_ox,
        r_i_send.at[9, 0], r_i_recv.at[9, 0],
    )
    c_ox.start()
    sums3 = stats.finish(0)
    means3 = back_means(par(8), sums3[0:1], sums3[1:2])

    def middle_back(u, middle, oc):
        normed = (middle - stat(4)) * stat(5)
        return oc.astype(f32) * par(10) + norm_back(u, normed, stat(5), par(8), means3)

    halo.finish(c_u)
    middle_grad = middle_back(r_mg[...], r_middle[...], r_oc[...])
    r_mg[...] = middle_grad
    load_w2.wait()
    act_grad, c_g2 = conv_back(
        0,
        middle_grad,
        middle_back(r_hu[0, 0], r_hmid[0], r_hoc[0]),
        middle_back(r_hu[0, 1], r_hmid[1], r_hoc[1]),
        r_w2,
    )
    normed2 = (r_hidden[...] - stat(2)) * stat(3)
    ntg = act_grad * slope((normed2 * par(3) + par(4)) * scale1 + shift)
    r_ntg[...] = ntg
    stats.start(1, [total(ntg * normed2), total(ntg)])
    c_n = edges(1, r_ntg, r_hu.at[1])
    middle_sum = total(r_mg[...])
    load_a2.wait()
    c_k2 = kernel_grads(0, r_a2, c_g2)
    c_ox.wait()
    r_os[:, 0] = (
        r_os[:, img_c].astype(f32) + r_ox[...].astype(f32)
    ).astype(bf16)
    c_oy = links.to(
        "img", lax.rem(links.img + 2, nimg), r_os.at[1 - img_y, 0], r_oy,
        r_i_send.at[9, 1], r_i_recv.at[9, 1],
    )
    c_oy.start()
    sums2 = stats.finish(1)
    means2 = back_means(par(3), scale1 * sums2[0:1], scale1 * sums2[1:2])

    def hidden_back(u, hidden):
        normed = (hidden - stat(2)) * stat(3)
        return norm_back(u * scale1, normed, stat(3), par(3), means2)

    halo.finish(c_n)
    hidden_grad = hidden_back(r_ntg[...], r_hidden[...])
    hidden_sum = total(hidden_grad)
    load_w1.wait()
    act_grad, c_g1 = conv_back(
        1,
        hidden_grad,
        hidden_back(r_hu[1, 0], r_hhid[0]),
        hidden_back(r_hu[1, 1], r_hhid[1]),
        r_w1,
    )
    m_k2 = [kernel_mid(0, c_k2, 0), kernel_mid(0, c_k2, 1)]
    c_oy.wait()
    both = r_os[img_y, 0].astype(f32) + r_oy[...].astype(f32)
    r_of[...] = both.astype(bf16).reshape(deep, 2, rows, 6 * hd + part)
    c_o = row_x_start(6, r_of, r_oz.at[0])
    normed1 = (r_img[...].astype(f32) - stat(0)) * stat(1)
    n1g = act_grad * slope(normed1 * par(0) + par(1))
    r_ntg[...] = n1g
    stats.start(2, [total(n1g * normed1), total(n1g), hidden_sum, middle_sum])
    m_k2.append(kernel_mid(0, c_k2, 2))
    load_a1.wait()
    c_k1 = kernel_grads(1, r_a1, c_g1)
    c_o = row_z_start(6, c_o, r_of, r_oz.at[0], r_oz.at[1], r_oz.at[2, pl.ds(0, deep - 1)])
    sums1 = stats.finish(2)
    scale_grad = par(3) * sums2[0:1] + par(4) * sums2[1:2]
    r_vsrc[...] = jnp.concatenate(
        [
            sums1[0:3],
            scale1 * sums2[0:1],
            scale1 * sums2[1:2],
            sums1[3:4],
            sums3[0:3],
            scale_grad,
            sums2[1:2],
            jnp.zeros((5, ch), f32),
        ],
        axis=0,
    )
    out = share(10, lambda i: r_vsrc, lambda i: r_every.at[i])
    m_k1 = [kernel_mid(1, c_k1, 0)]
    normed1 = (r_img[...].astype(f32) - stat(0)) * stat(1)
    means1 = back_means(par(0), sums1[0:1], sums1[1:2])
    r_igrad[...] = r_mg[...] + norm_back(r_ntg[...], normed1, stat(1), par(0), means1)
    m_k1.append(kernel_mid(1, c_k1, 1))
    out += kernel_end(0, m_k2)
    m_k1.append(kernel_mid(1, c_k1, 2))
    wait(c_encq)
    load_ctx.wait()
    turned = r_ctx[...].reshape(nimg * padc, -1).T
    pairs = jnp.concatenate([r_encq[:, 0], r_encq[:, 1]], axis=2)
    r_cq[...] = nn(turned, pairs.reshape(nimg * padc, 4 * hd)).astype(bf16)
    out += share(11, lambda i: r_cq, lambda i: r_cr.at[i])
    r_oy[:rows] = row_end(c_o, r_oz.at[1], r_oz.at[2])
    out += share(12, lambda i: r_oy.at[pl.ds(0, rows)], lambda i: r_oq.at[i])
    out += kernel_end(1, m_k1)
    wait(out)


def backward(nrow, nimg, wide, *args):
    px, ch = args[0].shape
    hd = ch // HEADS
    ctx, enc = args[19], args[18]
    padc = enc.shape[1]
    cfg = (nrow, nimg, wide, ch, hd, padc)
    part, rows, deep = ch // nimg, ch // nrow, nrow // 2
    proj = 6 * hd + part
    V = pl.BlockSpec(memory_space=pltpu.VMEM)
    A = pl.BlockSpec(memory_space=pl.ANY)
    S = jax.ShapeDtypeStruct
    dma = pltpu.SemaphoreType.DMA
    M = pltpu.VMEM
    text = ctx.shape[2]
    return pl.pallas_call(
        functools.partial(back_kernel, cfg),
        out_shape=(
            S((px, ch), f32),
            S((2, 3, nimg, rows, 3 * part), bf16),
            S((nimg, rows, proj), bf16),
            S((nimg, text, 4 * hd), bf16),
            S((nimg, 16, ch), f32),
        ),
        in_specs=[V] * 14 + [A] * 6,
        out_specs=(V,) + (A,) * 4,
        scratch_shapes=[
            M((3, 3 * ch, ch), bf16),
            M((3, 3 * ch, ch), bf16),
            M((ch, nimg * px), bf16),
            M((ch, nimg * px), bf16),
            M(enc.shape, bf16),
            M(ctx.shape, bf16),
            M((px, ch), f32),
            M((px, ch), f32),
            M((2, px + 2 * wide, 3 * ch), bf16),
            M((2, nimg, px + 2 * wide, part), bf16),
            M((nimg, px + 2 * wide, 3 * part), bf16),
            M((2, 3, deep, 2, rows, 3 * part), bf16),
            M((2, 3, deep, rows, 3 * part), bf16),
            M((2, 3, deep, rows, 3 * part), bf16),
            M((2, 3, deep - 1, rows, 3 * part), bf16),
            M((2, 3, rows, 3 * part), bf16),
            M((2, 2, ch, proj), bf16),
            M((2, ch, proj), bf16),
            M((ch, proj), bf16),
            M((3, deep, rows, proj), bf16),
            M((deep, 2, rows, proj), bf16),
            M((nimg, 2, padc, 2 * hd), bf16),
            M((text, 4 * hd), bf16),
            M((16, ch), f32),
            M((3, 16, 128), f32),
            M((3, nrow, 16, 128), f32),
            M((2, 2, wide, ch), f32),
            M((3, ch, 3 * part), f32),
            dma((6,)),
            dma((3, nrow - 1)),
            dma((3, nrow - 1)),
            dma((2, 2)),
            dma((2, 2)),
            dma((13, nimg - 1)),
            dma((13, nimg - 1)),
            dma((1, nrow - 1)),
            dma((1, nrow - 1)),
            dma((7,)),
            dma((7,)),
            dma((7, deep - 1)),
            dma((7, deep - 1)),
            dma((13,)),
        ],
        compiler_params=pltpu.CompilerParams(
            collective_id=4, has_side_effects=True, vmem_limit_bytes=60 * 2**20
        ),
        name="back",
    )(*args)


def finish_kernel(cfg, *refs):
    nrow, nimg, ch, hd, nvec = cfg
    igh, kqh, oqh, crh, everyh, embh, middleh, atth, pouth, parh = refs[:10]
    resh, igouth, k1h, k2h, inh, outh, ctxgh, embgh = refs[10:18]
    vecs = refs[18 : 18 + nvec]
    ig, kq, oq, cr, every, emb, middle, att, pout, par = refs[18 + nvec : 28 + nvec]
    res, k1g, k2g, ing, outg, ctxg, embg, isem, osem = refs[28 + nvec :]
    px = middle.shape[0]
    part = ch // nimg
    me = lax.axis_index("row")
    done = []
    pairs = (
        (kqh.at[0], kq.at[0]),
        (kqh.at[1], kq.at[1]),
        (atth, att),
        (pouth, pout),
        (middleh, middle),
        (parh, par),
        (everyh, every),
        (embh, emb),
        (crh, cr),
        (oqh, oq),
        (igh, ig),
    )
    loads = [pltpu.make_async_copy(a, b, isem.at[i]) for i, (a, b) in enumerate(pairs)]
    for c in loads:
        c.start()

    def put(slot, src, dst):
        c = pltpu.make_async_copy(src, dst, osem.at[slot])
        c.start()
        done.append(c)

    loads[10].wait()
    put(0, ig, igouth)
    for stage, out, dst in ((0, k2g, k2h), (1, k1g, k1h)):
        loads[stage].wait()
        for ky in range(3):
            for b in range(nimg):
                v = kq[stage, ky, b].astype(f32)
                for kx in range(3):
                    out[2 - ky, 2 - kx, :, b * part : (b + 1) * part] = v[
                        :, kx * part : (kx + 1) * part
                    ]
        put(1 + stage, out, dst)
    for c in loads[2:6]:
        c.wait()
    branch = nn(att[...].reshape(ch, px).T, pout[...])
    res[...] = (middle[...] + branch + par[11:12, :]).astype(bf16)
    put(3, res, resh)
    loads[6].wait()
    loads[7].wait()
    acts = emb[:, 0, :].T
    for j in range(2):
        d = None
        for b in range(nimg):
            t = acts[:, b : b + 1] * every[b, 9 + j : 10 + j]
            d = t if d is None else d + t
        embg[:, j * ch : (j + 1) * ch] = d
    put(4, embg, embgh)
    loads[8].wait()
    for b in range(nimg):
        v = cr[b].astype(f32)
        p = [v[:, j * hd : (j + 1) * hd] for j in range(4)]
        ctxg[:, b * 2 * hd : (b + 1) * 2 * hd] = jnp.concatenate([p[0], p[2]], axis=1)
        ctxg[:, ch + b * 2 * hd : ch + (b + 1) * 2 * hd] = jnp.concatenate([p[1], p[3]], axis=1)
    put(5, ctxg, ctxgh)
    loads[9].wait()
    for b in range(nimg):
        v = oq[b].astype(f32)
        for j in range(3):
            ing[:, j * ch + b * 2 * hd : j * ch + (b + 1) * 2 * hd] = jnp.concatenate(
                [v[:, j * hd : (j + 1) * hd], v[:, (3 + j) * hd : (4 + j) * hd]], axis=1
            )
        outg[:, b * part : (b + 1) * part] = v[:, 6 * hd :]
    put(6, ing, inh)
    put(7, outg, outh)
    sums = jnp.sum(every[...], axis=0)
    size = ch // nrow
    turned = pltpu.roll(sums, lax.rem(ch - me * size, ch), 1)
    for i in range(nvec - 1):
        vecs[i][...] = turned[i, :size]
    both = jnp.concatenate([sums[9:10], sums[10:11]], axis=1)
    both = jnp.concatenate([both] * 8, axis=0)
    both = pltpu.roll(both, lax.rem(2 * ch - me * 2 * size, 2 * ch), 1)
    vecs[nvec - 1][...] = both[0, : 2 * size]
    for c in done:
        c.wait()


def finish(nrow, nimg, *args):
    px, ch = args[0].shape
    hd = ch // HEADS
    kq, oq, cr, every, emb = args[1:6]
    rows = ch // nrow
    nvec = 10
    V = pl.BlockSpec(memory_space=pltpu.VMEM)
    A = pl.BlockSpec(memory_space=pl.ANY)
    S = jax.ShapeDtypeStruct
    M = pltpu.VMEM
    dma = pltpu.SemaphoreType.DMA
    outs = (
        ((px, ch), bf16),
        ((3, 3, rows, ch), f32),
        ((3, 3, rows, ch), f32),
        ((rows, 3 * ch), f32),
        ((rows, ch), f32),
        ((cr.shape[1], 2 * ch), f32),
        ((emb.shape[2], 2 * ch), f32),
    )
    return pl.pallas_call(
        functools.partial(finish_kernel, (nrow, nimg, ch, hd, nvec)),
        out_shape=(S(*outs[0]), S((px, ch), f32))
        + tuple(S(*o) for o in outs[1:])
        + (S((rows,), f32),) * (nvec - 1)
        + (S((2 * rows,), f32),),
        in_specs=[A] * 10,
        out_specs=(A,) * 8 + (V,) * nvec,
        scratch_shapes=[M(a.shape, a.dtype) for a in args]
        + [M(*o) for o in outs]
        + [dma((11,)), dma((8,))],
        compiler_params=pltpu.CompilerParams(vmem_limit_bytes=62 * 2**20),
        name="finish",
    )(*args)


def local_fast(
    images,
    timesteps,
    clip_embed,
    context,
    out_cotangent,
    item_weight,
    first_gain,
    first_bias,
    first_kernel,
    first_offset,
    embed_weight,
    embed_bias,
    second_gain,
    second_bias,
    second_kernel,
    second_offset,
    third_gain,
    third_bias,
    project_in,
    context_weight,
    project_out,
    output_bias,
):
    _, tall, wide, ch = images.shape
    pixels = tall * wide
    nrow = lax.axis_size("row")
    nimg = lax.axis_size("img")
    me_row = lax.axis_index("row")
    nctx = context.shape[1]
    image = images.reshape(pixels, ch)
    cotangent = out_cotangent.reshape(pixels, ch)
    width = clip_embed.shape[1]
    at = jnp.arange(width, dtype=jnp.int32)[None, :]
    half = width // 2
    index = jnp.where(at < half, at, at - half).astype(f32)
    angles = timesteps.astype(f32)[:, None] * jnp.exp(-math.log(10000.0) * index / half)
    embedding = jnp.where(at < half, jnp.cos(angles), jnp.sin(angles)) + clip_embed.astype(f32)
    emb = jax.nn.silu(embedding)
    vectors = [
        v.reshape(1, -1)
        for v in (
            first_gain, first_bias, first_offset, second_gain, second_bias, second_offset,
            third_gain, third_bias, output_bias, embed_bias,
        )
    ]
    w1 = first_kernel.reshape(3, 3 * ch, ch)
    w2 = second_kernel.reshape(3, 3 * ch, ch)
    (
        par, hidden, middle, stats, ss, turned_in, act_three, halo_cot, halo_hidden, halo_middle,
        acts_one, acts_two, ctx_parts, emb_parts, grads, attended, enc_grads,
    ) = front(
        image, cotangent, project_out, context[0], emb, item_weight, vectors, w1, w2, project_in, context_weight,
        embed_weight, nrow, nimg, wide,
    )
    image_grad, kq, oq, cr, every = backward(
        nrow, nimg, wide,
        image, cotangent, par, ss, stats, hidden, middle, halo_cot, halo_hidden, halo_middle, act_three, grads, attended, turned_in,
        w2, w1, acts_two, acts_one, enc_grads, ctx_parts,
    )
    result, image_grad, k1g, k2g, ing, outg, ctxg, embg, *vecs = finish(
        nrow, nimg, image_grad, kq, oq, cr, every, emb_parts, middle, attended, project_out, par
    )
    return (
        result.reshape(images.shape),
        image_grad.reshape(images.shape),
        vecs[0],
        vecs[1],
        k1g,
        vecs[2],
        embg,
        vecs[9],
        vecs[3],
        vecs[4],
        k2g,
        vecs[5],
        vecs[6],
        vecs[7],
        ing,
        ctxg,
        outg,
        vecs[8],
    )


def solution(mesh):
    every = P()
    image = P("img", "row", None, None)
    placed = (image, P("img"), P("img", None), P("img", None, None), image, P("img")) + (every,) * 16
    vec = P("row")
    matrix = P("row", None)
    taps = P(None, None, "row", None)
    nimg, nrow = mesh.shape["img"], mesh.shape["row"]
    quick = nrow == HEADS and nimg == 4
    return jax.shard_map(
        local_fast if quick else local,
        mesh=mesh,
        in_specs=placed,
        out_specs=(
            image,
            image,
            vec,
            vec,
            taps,
            vec,
            matrix,
            vec,
            vec,
            vec,
            taps,
            vec,
            vec,
            vec,
            matrix,
            matrix,
            matrix,
            vec,
        ),
        check_vma=False,
    )
```

```python
import functools
import math

import jax
import jax.numpy as jnp
from jax import lax
from jax.experimental import pallas as pl
from jax.experimental.pallas import tpu as pltpu
from jax.sharding import PartitionSpec as P

HEADS = 8
GROUPS = 32
EPSILON = 1e-05
f32 = jnp.float32
bf16 = jnp.bfloat16
MESH = pl.DeviceIdType.MESH
LOG2E=math.log2(math.e)

def nt(a,b):
    return lax.dot_general(a,b,(((1,),(1,)),((),())),preferred_element_type=f32)
def nn(a,b):
    return jnp.dot(a,b,preferred_element_type=f32)

def attn_kernel(cfg, *refs):
    if cfg[0]:
        q_ref, ctx_ref, g_ref, out_ref, dq_ref, dctx_ref = refs[:6]
        kv_ref, dkv_ref = q_ref, dq_ref
        at_kv = cfg[-1]
    else:
        q_ref, kv_ref, ctx_ref, g_ref, out_ref, dq_ref, dkv_ref, dctx_ref = refs[:8]
        at_kv = 0
    (kx, vx, kt, vt, sbuf, pbuf, acc) = refs[-7:]
    joined, nqs, nsrc, width, bq, kc, nctx, padc, hd = cfg
    npix = nsrc*width
    nk = npix + padc
    ones_rows = jnp.where(lax.broadcasted_iota(jnp.int32,(hd,width),0)<2,1.0,0.0).astype(bf16)
    def fill(pair, at, w):
        k = pair[:hd].astype(f32)*(LOG2E*0.125)
        hi = k.astype(bf16)
        lo = (k-hi.astype(f32)).astype(bf16)
        kx[pl.ds(at,w),:] = jnp.concatenate([hi,lo],axis=0).T
        vfull = jnp.concatenate([pair[hd:], ones_rows[:, :w]],axis=0)
        vx[pl.ds(at,w),:] = vfull.T
        return vfull
    for s in range(nsrc):
        pair = kv_ref[s, at_kv:]
        vfull = fill(pair, s*width, width)
        kt[:, s*width:(s+1)*width] = pair[:hd]
        vt[:, s*width:(s+1)*width] = vfull[:hd+16]
    cpair = ctx_ref[...]
    vfull = fill(cpair, npix, padc)
    kt[:, npix:npix+padc] = cpair[:hd]
    vt[:, npix:npix+padc] = vfull[:hd+16]
    acc[...] = jnp.zeros_like(acc)

    nfull = npix//kc
    per = width//bq
    def block(j, _):
        s = j//per
        off = pl.multiple_of((j%per)*bq, bq)
        qt = q_ref[s,:hd,pl.ds(off,bq)]
        gt = g_ref[s,:,pl.ds(off,bq)]
        q2 = jnp.concatenate([qt,qt],axis=0)
        sc = nn(kx[pl.ds(npix,padc),:], q2)
        sc = jnp.where(lax.broadcasted_iota(jnp.int32,(padc,bq),0)<nctx, sc, -jnp.inf)
        sbuf[pl.ds(npix,padc),:] = sc
        m8 = jnp.max(sc.reshape(padc//8,8,bq),axis=0)
        def phase_a(c, m8):
            at = pl.multiple_of(c*kc,kc)
            sv = nn(kx[pl.ds(at,kc),:], q2)
            sbuf[pl.ds(at,kc),:] = sv
            return jnp.maximum(m8, jnp.max(sv.reshape(kc//8,8,bq),axis=0))
        m8 = lax.fori_loop(0,nfull,phase_a,m8,unroll=True)
        m = jnp.max(m8,axis=0,keepdims=True)
        pc = jnp.exp2(sbuf[pl.ds(npix,padc),:]-m).astype(bf16)
        pbuf[pl.ds(npix,padc),:] = pc
        o = nn(vt[:,npix:npix+padc], pc)
        def phase_b(c, o):
            at = pl.multiple_of(c*kc,kc)
            p = jnp.exp2(sbuf[pl.ds(at,kc),:]-m).astype(bf16)
            pbuf[pl.ds(at,kc),:] = p
            return o + nn(vt[:,pl.ds(at,kc)], p)
        o = lax.fori_loop(0,nfull,phase_b,o,unroll=True)
        inv = 1.0/o[hd:hd+1]
        att = o[:hd]*inv
        out_ref[s,:,pl.ds(off,bq)] = att.astype(bf16)
        gf = gt.astype(f32)
        delta = jnp.sum(gf*att,axis=0,keepdims=True)*inv
        gl = (gf*inv).astype(bf16)
        dhi = (-delta).astype(bf16)
        dlo = (-delta-dhi.astype(f32)).astype(bf16)
        gx = jnp.concatenate([gl,dhi,dlo,jnp.zeros((hd-2,bq),bf16)],axis=0)
        zero = jnp.zeros((hd,bq),bf16)
        rq = jnp.concatenate([qt,zero],axis=0).T
        rg = jnp.concatenate([zero,gl],axis=0).T
        rr = jnp.concatenate([rq,rg],axis=0)
        def piece(at, w, dq):
            p = pbuf[pl.ds(at,w),:]
            dp = nn(vx[pl.ds(at,w),:], gx)
            ds = (p.astype(f32)*dp).astype(bf16)
            acc[pl.ds(at,w),:] += nn(jnp.concatenate([ds,p],axis=1), rr)
            return dq + nn(kt[:,pl.ds(at,w)], ds)
        dq = piece(npix, padc, jnp.zeros((hd,bq),f32))
        def phase_d(c, dq):
            return piece(pl.multiple_of(c*kc,kc), kc, dq)
        dq = lax.fori_loop(0,nfull,phase_d,dq,unroll=True)
        dq_ref[s,:hd,pl.ds(off,bq)] = (dq*0.125).astype(bf16)
        return 0
    lax.fori_loop(0, nqs*per, block, 0)
    scale = jnp.where(lax.broadcasted_iota(jnp.int32,(1,2*hd),1)<hd,0.125,1.0)
    for s in range(nsrc):
        dkv_ref[s, at_kv:] = (acc[s*width:(s+1)*width,:]*scale).astype(bf16).T
    dctx_ref[...] = (acc[npix:npix+padc,:]*scale).astype(bf16)

def attention(q, kv, ctx, g, nctx, bq=512, kc=512):
    joined = kv is None
    nqs, _, width = q.shape
    hd = g.shape[1]
    nsrc = nqs if joined else kv.shape[0]
    padc = ctx.shape[1]
    nk = nsrc*width+padc
    cfg=(joined,nqs,nsrc,width,bq,kc,nctx,padc,hd)
    V=pl.BlockSpec(memory_space=pltpu.VMEM)
    S=jax.ShapeDtypeStruct
    grads=(S((nqs,3*hd,width),bf16),) if joined else (S((nqs,hd,width),bf16),S((nsrc,2*hd,width),bf16))
    args=(q,ctx,g) if joined else (q,kv,ctx,g)
    return pl.pallas_call(
        functools.partial(attn_kernel,cfg),
        out_shape=(S((nqs,hd,width),bf16),)+grads+(S((padc,2*hd),bf16),),
        in_specs=[V]*len(args), out_specs=(V,)*(2+len(grads)),
        scratch_shapes=[pltpu.VMEM((nk,2*hd),bf16),pltpu.VMEM((nk,2*hd),bf16),
                        pltpu.VMEM((hd,nk),bf16),pltpu.VMEM((hd+16,nk),bf16),
                        pltpu.VMEM((nk,bq),f32),pltpu.VMEM((nk,bq),bf16),
                        pltpu.VMEM((nk,2*hd),f32)],
        compiler_params=pltpu.CompilerParams(vmem_limit_bytes=48*2**20),
        cost_estimate=pl.CostEstimate(flops=6*2*64*4096*4228,bytes_accessed=8*2**20,transcendentals=4096*4228),
        name="attend",
    )(*args)

def exchange_kernel(axis, n, x_ref, out_ref, send_sem, recv_sem):
    me = lax.axis_index(axis)
    barrier = pltpu.get_barrier_semaphore()
    for k in range(1, n):
        pl.semaphore_signal(
            barrier, inc=1, device_id={axis: lax.rem(me + k, n)}, device_id_type=MESH
        )
    out_ref[me] = x_ref[...]
    pl.semaphore_wait(barrier, n - 1)
    copies = []
    for k in range(1, n):
        copy = pltpu.make_async_remote_copy(
            src_ref=x_ref,
            dst_ref=out_ref.at[me],
            send_sem=send_sem.at[k - 1],
            recv_sem=recv_sem.at[k - 1],
            device_id={axis: lax.rem(me + k, n)},
            device_id_type=MESH,
        )
        copy.start()
        copies.append(copy)
    for copy in copies:
        copy.wait()


def exchange(x, axis, cid):
    n = lax.axis_size(axis)
    V = pl.BlockSpec(memory_space=pltpu.VMEM)
    return pl.pallas_call(
        functools.partial(exchange_kernel, axis, n),
        out_shape=jax.ShapeDtypeStruct((n,) + x.shape, x.dtype),
        in_specs=[V],
        out_specs=V,
        scratch_shapes=[
            pltpu.SemaphoreType.DMA((n - 1,)),
            pltpu.SemaphoreType.DMA((n - 1,)),
        ],
        compiler_params=pltpu.CompilerParams(collective_id=cid, has_side_effects=True),
        name="exchange_" + axis,
    )(x)


def row_sum(rows):
    x = jnp.concatenate(
        [jnp.stack(rows), jnp.zeros((8 - len(rows), rows[0].shape[0]), f32)], axis=0
    )
    return jnp.sum(exchange(x, "row", 1), axis=0)


def sinusoid(steps, width):
    half_width = width // 2
    frequency = jnp.exp(-math.log(10000.0) * jnp.arange(half_width, dtype=f32) / half_width)
    angles = steps.astype(f32)[:, None] * frequency[None, :]
    return jnp.concatenate([jnp.cos(angles), jnp.sin(angles)], axis=1)


def swish_slope(values):
    sig_v = jax.nn.sigmoid(values)
    return sig_v * (1.0 + values * (1.0 - sig_v))


def per_group(vec, members):
    n = vec.shape[-1]
    g = jnp.sum(vec.reshape(vec.shape[0], GROUPS, n // GROUPS), axis=2) / members
    return jnp.repeat(g, n // GROUPS, axis=1)


def norm_stats(values, members):
    sums = row_sum([jnp.sum(values, axis=0), jnp.sum(values * values, axis=0)])
    means = per_group(sums[:2], members)
    return (means[0], lax.rsqrt(means[1] - means[0] * means[0] + EPSILON))


def halo(x):
    devices = lax.axis_size("row")
    up = [(i, i + 1) for i in range(devices - 1)]
    down = [(i + 1, i) for i in range(devices - 1)]
    before = lax.ppermute(x[-1:], "row", up)
    after = lax.ppermute(x[:1], "row", down)
    return jnp.concatenate([before, x, after], axis=0)


def conv(padded, kernel):
    x = jnp.pad(padded, ((0, 0), (1, 1), (0, 0)))[None]
    return lax.conv_general_dilated(
        x,
        kernel,
        (1, 1),
        "VALID",
        dimension_numbers=("NHWC", "HWIO", "NHWC"),
        preferred_element_type=f32,
    )[0]


def flip_kernel(kernel):
    return jnp.flip(kernel, (0, 1)).transpose(0, 1, 3, 2)


def tn(left, right):
    return lax.dot_general(left, right, (((0,), (0,)), ((), ())), preferred_element_type=f32)


def split_cols(x, n):
    rows, cols = x.shape
    return x.reshape(rows, n, cols // n).transpose(1, 0, 2)


def kernel_grad(acts, grad_padded, tall):
    n = lax.axis_size("img")
    rows, wide, ch = grad_padded.shape
    part = ch // n
    g = lax.all_to_all(
        split_cols(grad_padded.reshape(rows * wide, ch), n),
        "img",
        split_axis=0,
        concat_axis=0,
        tiled=True,
    ).reshape(n, rows, wide, part)
    g = jnp.pad(g, ((0, 0), (0, 0), (1, 1), (0, 0)))
    lines = []
    for ky in range(3):
        for kx in range(3):
            lines.append(
                g[:, 2 - ky : 2 - ky + tall, 2 - kx : 2 - kx + wide].reshape(-1, part)
            )
    return tn(acts, jnp.concatenate(lines, axis=1))


def local(
    images,
    timesteps,
    clip_embed,
    context,
    out_cotangent,
    item_weight,
    first_gain,
    first_bias,
    first_kernel,
    first_offset,
    embed_weight,
    embed_bias,
    second_gain,
    second_bias,
    second_kernel,
    second_offset,
    third_gain,
    third_bias,
    project_in,
    context_weight,
    project_out,
    output_bias,
):
    _, tall, wide, ch = images.shape
    pixels = tall * wide
    hd = ch // HEADS
    nrow = lax.axis_size("row")
    nimg = lax.axis_size("img")
    me_row = lax.axis_index("row")
    gq = nrow // HEADS
    head = me_row // gq
    text = context.shape[2]
    nctx = context.shape[1]
    members = float(nrow * pixels * (ch // GROUPS))

    def gather_img(x):
        return lax.all_gather(x, "img", axis=0, tiled=True)

    grad_out = out_cotangent.reshape(pixels, ch).astype(f32) * (item_weight.astype(f32) * 0.25)
    grad_low = grad_out.astype(bf16)
    attended_grad = (
        lax.dot_general(project_out, grad_low, (((1,), (1,)), ((), ())), preferred_element_type=f32)
        .astype(bf16)
        .reshape(HEADS, hd, pixels)
    )

    def queries_out(x):
        x = x.reshape(HEADS, hd, gq, pixels // gq).transpose(0, 2, 1, 3)
        x = x.reshape(nrow, hd, pixels // gq)
        return x

    def a2a(x):
        return lax.all_to_all(x, "row", split_axis=0, concat_axis=0, tiled=True)

    grad_heads = a2a(queries_out(attended_grad))

    image_f = images.reshape(pixels, ch).astype(f32)
    embedding = sinusoid(timesteps, clip_embed.shape[1]) + clip_embed.astype(f32)
    embed_act = jax.nn.silu(embedding).astype(bf16)
    scale_shift = (jnp.dot(embed_act, embed_weight, preferred_element_type=f32) + embed_bias)[0]
    scale1 = 1.0 + scale_shift[:ch]
    shift = scale_shift[ch:]
    pair_at = (head // 2) * (2 * hd)
    cw_k = lax.dynamic_slice_in_dim(context_weight, pair_at, 2 * hd, 1)
    cw_v = lax.dynamic_slice_in_dim(context_weight, ch + pair_at, 2 * hd, 1)
    cw = jnp.concatenate([cw_k, cw_v], axis=1)
    enc = lax.dot_general(
        cw, context[0], (((0,), (1,)), ((), ())), preferred_element_type=f32
    ).astype(bf16)
    enc = enc.reshape(2, 2, hd, nctx)
    enc = jnp.where(head % 2 == 0, enc[:, 0], enc[:, 1]).reshape(2 * hd, nctx)
    padc = -(-nctx // 16) * 16
    enc = jnp.pad(enc, ((0, 0), (0, padc - nctx)))

    mean1, rstd1 = norm_stats(image_f, members)
    normed1 = (image_f - mean1) * rstd1
    norm_one = normed1 * first_gain + first_bias
    act_one = jax.nn.silu(norm_one).astype(bf16)
    hidden = conv(halo(act_one.reshape(tall, wide, ch)), first_kernel).reshape(pixels, ch)
    hidden = hidden + first_offset
    acts_one = gather_img(act_one)
    mean2, rstd2 = norm_stats(hidden, members)
    normed2 = (hidden - mean2) * rstd2
    affine_two = normed2 * second_gain + second_bias
    norm_two = affine_two * scale1 + shift
    act_two = jax.nn.silu(norm_two).astype(bf16)
    acts_two = gather_img(act_two)
    middle = (
        image_f
        + conv(halo(act_two.reshape(tall, wide, ch)), second_kernel).reshape(pixels, ch)
        + second_offset
    )
    mean3, rstd3 = norm_stats(middle, members)
    normed3 = (middle - mean3) * rstd3
    act_three = (normed3 * third_gain + third_bias).astype(bf16)
    acts_three = gather_img(act_three)
    triple = (
        lax.dot_general(project_in, act_three, (((0,), (1,)), ((), ())), preferred_element_type=f32)
        .astype(bf16)
        .reshape(3, HEADS, hd, pixels)
    )
    if gq == 1:
        recv = a2a(triple.transpose(1, 0, 2, 3).reshape(nrow, 3 * hd, pixels))
        q_h, kv_h = recv[:, :hd], recv[:, hd:]
        grad_h = grad_heads
    else:
        pair = triple[1:].transpose(1, 0, 2, 3).reshape(HEADS, 1, 2 * hd, pixels)
        pair = jnp.broadcast_to(pair, (HEADS, gq, 2 * hd, pixels)).reshape(nrow, 2 * hd, pixels)
        q_h, kv_h = a2a(queries_out(triple[0])), a2a(pair)

        def regroup(x, rows):
            x = x.transpose(1, 0, 2).reshape(rows, -1, 512)
            return x.transpose(1, 0, 2)

        q_h, kv_h, grad_h = regroup(q_h, hd), regroup(kv_h, 2 * hd), regroup(grad_heads, hd)
    att_h, dq_h, dkv_h, dctx = attention(q_h, kv_h, enc, grad_h, nctx)
    if gq == 1:
        attended = a2a(att_h).reshape(ch, pixels)
        back = a2a(jnp.concatenate([dq_h, dkv_h], axis=1)).reshape(HEADS, 3, hd, pixels)
        back = back.transpose(1, 0, 2, 3).reshape(3 * ch, pixels)
    else:

        def ungroup(x, part):
            rows = x.shape[1]
            x = x.transpose(1, 0, 2).reshape(rows, nrow, part)
            return x.transpose(1, 0, 2)

        def from_queries(x):
            x = x.reshape(HEADS, gq, hd, pixels // gq).transpose(0, 2, 1, 3)
            return x.reshape(ch, pixels)

        attended = from_queries(a2a(ungroup(att_h, pixels // gq)))
        dq = from_queries(a2a(ungroup(dq_h, pixels // gq)))
        dkv = a2a(ungroup(dkv_h, pixels)).reshape(HEADS, gq, 2, hd, pixels)
        dkv = jnp.sum(dkv.astype(f32), axis=1).astype(bf16)
        dkv = dkv.transpose(1, 0, 2, 3).reshape(2 * ch, pixels)
        back = jnp.concatenate([dq, dkv], axis=0)
    branch = tn(attended, project_out)
    result_image = (middle + branch + output_bias).astype(bf16)

    part_text = text // nrow
    enc_all = lax.all_gather(dctx[:nctx].astype(bf16), ("img", "row"), axis=0)
    enc_all = enc_all.reshape(nimg, HEADS, gq, nctx, 2, hd)
    if gq > 1:
        enc_all = jnp.sum(enc_all.astype(f32), axis=2, keepdims=True).astype(bf16)
    enc_all = enc_all[:, :, 0].transpose(0, 2, 3, 1, 4).reshape(nimg * nctx, 2 * ch)
    ctx_rows = lax.dynamic_slice_in_dim(context[0], me_row * part_text, part_text, 1)
    ctx_rows = gather_img(ctx_rows)
    context_weight_grad = tn(ctx_rows, enc_all)

    triple_grad = back.T
    act_three_grad = lax.dot_general(
        triple_grad, project_in, (((1,), (1,)), ((), ())), preferred_element_type=f32
    )
    sums3 = row_sum(
        [
            jnp.sum(act_three_grad * normed3, axis=0),
            jnp.sum(act_three_grad, axis=0),
            jnp.sum(grad_out, axis=0),
        ]
    )

    def norm_back(u, normed, rstd, gain, gain_sum, bias_sum):
        means = per_group(jnp.stack([gain * bias_sum, gain * gain_sum]), members)
        return rstd * (u * gain - means[0] - normed * means[1])

    middle_grad = grad_out + norm_back(
        act_three_grad, normed3, rstd3, third_gain, sums3[0], sums3[1]
    )
    middle_low = halo(middle_grad.astype(bf16).reshape(tall, wide, ch))
    act_two_grad = conv(middle_low, flip_kernel(second_kernel)).reshape(pixels, ch)
    norm_two_grad = act_two_grad * swish_slope(norm_two)
    sums2 = row_sum(
        [
            jnp.sum(norm_two_grad * normed2, axis=0),
            jnp.sum(norm_two_grad, axis=0),
            jnp.sum(middle_grad, axis=0),
        ]
    )
    scale_grad = second_gain * sums2[0] + second_bias * sums2[1]
    shift_grad = sums2[1]
    gain2_sum, bias2_sum = scale1 * sums2[0], scale1 * sums2[1]
    hidden_grad = norm_back(
        norm_two_grad * scale1, normed2, rstd2, second_gain, gain2_sum, bias2_sum
    )
    hidden_low = halo(hidden_grad.astype(bf16).reshape(tall, wide, ch))
    act_one_grad = conv(hidden_low, flip_kernel(first_kernel)).reshape(pixels, ch)
    norm_one_grad = act_one_grad * swish_slope(norm_one)
    sums1 = row_sum(
        [
            jnp.sum(norm_one_grad * normed1, axis=0),
            jnp.sum(norm_one_grad, axis=0),
            jnp.sum(hidden_grad, axis=0),
        ]
    )
    image_grad = middle_grad + norm_back(
        norm_one_grad, normed1, rstd1, first_gain, sums1[0], sums1[1]
    )

    def swap_img(x):
        x = split_cols(x, nimg)
        x = lax.all_to_all(x, "img", split_axis=0, concat_axis=0, tiled=True)
        return x.reshape(-1, x.shape[2])

    kg2 = kernel_grad(acts_two, middle_low, tall)
    kg1 = kernel_grad(acts_one, hidden_low, tall)
    pin = tn(acts_three, swap_img(triple_grad))
    pout = tn(gather_img(attended.T), swap_img(grad_low))

    def finish(x):
        x = lax.psum_scatter(x.astype(bf16), "row", scatter_dimension=0, tiled=True)
        return lax.all_gather(x, "img", axis=0).astype(f32)

    c2 = finish(kg2)
    c1 = finish(kg1)
    c3 = finish(jnp.concatenate([pin, pout], axis=1))
    part = ch // nrow
    cols = ch // nimg

    def conv_out(x):
        return x.reshape(nimg, part, 3, 3, cols).transpose(2, 3, 1, 0, 4).reshape(3, 3, part, ch)

    wide_in = 3 * ch // nimg
    pin_out = c3[:, :, :wide_in].transpose(1, 0, 2).reshape(part, 3 * ch)
    pout_out = c3[:, :, wide_in:].transpose(1, 0, 2).reshape(part, ch)

    rows = jnp.stack(
        [
            sums1[0],
            sums1[1],
            sums1[2],
            gain2_sum,
            bias2_sum,
            sums2[2],
            sums3[0],
            sums3[1],
            sums3[2],
            scale_grad,
            shift_grad,
        ]
        + [jnp.zeros((ch,), f32)] * 5
    )
    every = exchange(rows, "img", 2)
    acts_embed = gather_img(embed_act)
    part_emb = embed_act.shape[1] // nrow
    acts_embed = lax.dynamic_slice_in_dim(acts_embed, me_row * part_emb, part_emb, 1).astype(f32)
    shift_scale = every[:, 9:11].reshape(nimg, 2 * ch)
    embed_weight_grad = jnp.sum(acts_embed[:, :, None] * shift_scale[:, None, :], axis=0)
    part_bias = 2 * ch // nrow
    embed_bias_grad = lax.dynamic_slice_in_dim(
        jnp.sum(shift_scale, axis=0), me_row * part_bias, part_bias, 0
    )
    vecs = lax.dynamic_slice_in_dim(jnp.sum(every[:, :9], axis=0), me_row * part, part, 1)
    return (
        result_image.reshape(images.shape),
        image_grad.reshape(images.shape),
        vecs[0],
        vecs[1],
        conv_out(c1),
        vecs[2],
        embed_weight_grad,
        embed_bias_grad,
        vecs[3],
        vecs[4],
        conv_out(c2),
        vecs[5],
        vecs[6],
        vecs[7],
        pin_out,
        context_weight_grad,
        pout_out,
        vecs[8],
    )


def nt_dot(a, b):
    return lax.dot_general(a, b, (((1,), (1,)), ((), ())), preferred_element_type=f32)


def group_total(x):
    per = x.shape[1] // GROUPS
    lane = lax.broadcasted_iota(jnp.int32, x.shape, 1)
    n = x.shape[1]
    step = 1
    while step < per:
        upper = (lane // step) % 2 == 1
        x = x + jnp.where(upper, pltpu.roll(x, step, 1), pltpu.roll(x, n - step, 1))
        step *= 2
    return x


def total(v):
    return jnp.sum(v, axis=0, keepdims=True)


def put_shifts(buf, at, v, wide):
    n, ch = v.shape
    col = lax.rem(lax.broadcasted_iota(jnp.int32, (n, 1), 0), wide)
    buf[pl.ds(at, n), pl.ds(ch, ch)] = v.astype(bf16)
    left = jnp.where(col == 0, 0.0, pltpu.roll(v, 1, 0))
    buf[pl.ds(at, n), pl.ds(0, ch)] = left.astype(bf16)
    right = jnp.where(col == wide - 1, 0.0, pltpu.roll(v, n - 1, 0))
    buf[pl.ds(at, n), pl.ds(2 * ch, ch)] = right.astype(bf16)


class Links:
    def __init__(self, nrow, nimg):
        self.nrow, self.nimg = nrow, nimg
        self.row, self.img = lax.axis_index("row"), lax.axis_index("img")

    def peer(self, axis, k):
        if axis == "row":
            return lax.rem(self.row + k, self.nrow)
        return lax.rem(self.img + k, self.nimg)

    def greet(self):
        barrier = pltpu.get_barrier_semaphore()
        for axis, n in (("row", self.nrow), ("img", self.nimg)):
            for k in range(1, n):
                pl.semaphore_signal(
                    barrier, inc=1, device_id={axis: self.peer(axis, k)}, device_id_type=MESH
                )

    def greeted(self):
        pl.semaphore_wait(pltpu.get_barrier_semaphore(), self.nrow + self.nimg - 2)

    def to(self, axis, at, src, dst, send, recv):
        return pltpu.make_async_remote_copy(
            src_ref=src,
            dst_ref=dst,
            send_sem=send,
            recv_sem=recv,
            device_id={axis: at},
            device_id_type=MESH,
        )

    def copy(self, axis, k, src, dst, send, recv):
        return self.to(axis, self.peer(axis, k), src, dst, send, recv)


class Stats:
    def __init__(self, links, src, dst, send, recv):
        self.links, self.src, self.dst, self.send, self.recv = links, src, dst, send, recv

    def start(self, stage, rows):
        links = self.links
        ch = rows[0].shape[1]
        blocks = [r[:, i * 128 : (i + 1) * 128] for r in rows for i in range(ch // 128)]
        height = self.src.shape[1]
        blocks = blocks + [jnp.zeros((1, 128), f32)] * (height - len(blocks))
        packed = jnp.concatenate(blocks, axis=0)
        self.src[stage] = packed
        self.dst[stage, links.row] = packed
        self.rows, self.per = len(rows), ch // 128
        self.copies = []
        for k in range(1, links.nrow):
            c = links.copy(
                "row",
                k,
                self.src.at[stage],
                self.dst.at[stage, links.row],
                self.send.at[stage, k - 1],
                self.recv.at[stage, k - 1],
            )
            c.start()
            self.copies.append(c)

    def finish(self, stage):
        for c in self.copies:
            c.wait()
        s = jnp.sum(self.dst[stage], axis=0)
        per = self.per
        rows = [
            jnp.concatenate([s[r * per + i : r * per + i + 1] for i in range(per)], axis=1)
            for r in range(self.rows)
        ]
        return jnp.concatenate(rows + [jnp.zeros((8 - self.rows, per * 128), f32)], axis=0)


class Halo:
    def __init__(self, links, send, recv):
        self.links, self.send, self.recv = links, send, recv

    def copies(self, slot, first, last, land):
        links = self.links
        down = links.copy(
            "row", links.nrow - 1, first, land.at[1],
            self.send.at[slot, 0], self.recv.at[slot, 1],
        )
        up = links.copy(
            "row", 1, last, land.at[0],
            self.send.at[slot, 1], self.recv.at[slot, 0],
        )
        return down, up

    def start(self, slot, first, last, land):
        links = self.links
        down, up = self.copies(slot, first, last, land)

        @pl.when(links.row > 0)
        def _():
            down.start()

        @pl.when(links.row < links.nrow - 1)
        def _():
            up.start()

        @pl.when(links.row == 0)
        def _():
            land[0] = jnp.zeros(land.shape[1:], land.dtype)

        @pl.when(links.row == links.nrow - 1)
        def _():
            land[1] = jnp.zeros(land.shape[1:], land.dtype)

        return down, up

    def finish(self, pair):
        links = self.links
        down, up = pair

        @pl.when(links.row > 0)
        def _():
            down.wait_send()
            up.wait_recv()

        @pl.when(links.row < links.nrow - 1)
        def _():
            up.wait_send()
            down.wait_recv()


def put_block(links, buf, mid, before, after, wide):
    put_shifts(buf, wide, mid, wide)
    put_shifts(buf, 0, jnp.where(links.row > 0, before, 0.0), wide)
    put_shifts(buf, buf.shape[0] - wide, jnp.where(links.row < links.nrow - 1, after, 0.0), wide)


def front_kernel(
    cfg,
    *refs,
):
    nvec = cfg[-1]
    _front(cfg[:-1], *refs[:6], refs[6 : 6 + nvec], *refs[6 + nvec :])


def _front(
    cfg,
    r_img,
    r_oc,
    r_pout,
    r_cxt,
    r_embv,
    r_weight,
    r_vecs,
    r_w1h,
    r_w2h,
    r_winh,
    r_cwh,
    r_ewh,
    r_par,
    r_stats,
    r_ss,
    r_hiddenh,
    r_middleh,
    r_wth,
    r_a3h,
    r_hoch,
    r_hhidh,
    r_hmidh,
    r_a1h,
    r_a2h,
    r_ctxh,
    r_embh,
    r_tgh,
    r_atth,
    r_ench,
    r_hidden,
    r_middle,
    r_wt,
    r_a3,
    r_hoc,
    r_hhid,
    r_hmid,
    r_emb,
    r_himg,
    r_gx,
    r_dqa,
    r_cw,
    r_ctx,
    r_buf,
    r_at,
    r_gs,
    r_ts,
    r_qkv,
    r_g,
    r_kx,
    r_vx,
    r_kt,
    r_vt,
    r_sb,
    r_pb,
    r_acc,
    r_atb,
    r_dqb,
    r_dcb,
    r_st_src,
    r_st_dst,
    r_wsem,
    r_vsem,
    r_st_send,
    r_st_recv,
    r_h_send,
    r_h_recv,
    r_i_send,
    r_i_recv,
    r_r_send,
    r_r_recv,
    r_osem,
    r_bsem,
):
    nrow, nimg, wide, ch, hd, kc, joint = cfg
    px = r_img.shape[0]
    members = float(nrow * px * (ch // GROUPS))
    links = Links(nrow, nimg)
    links.greet()
    head = links.row
    me = links.row

    def pair_at(at):
        return pl.ds(pl.multiple_of(at + (head // 2) * (2 * hd), 128), 2 * hd)

    deep = 3 * ch
    at_ew, at_win, at_w1 = 0, 2 * r_embv.shape[1], 2 * r_embv.shape[1] + deep
    at_w2 = at_w1 + 3 * deep
    text_in = r_embv.shape[1]
    groups = (
        [(r_w1h.at[k], at_w1 + k * deep, deep) for k in range(3)],
        [(r_ewh.at[:, k * ch : (k + 1) * ch], at_ew + k * text_in, text_in) for k in range(2)],
        [(r_winh.at[:, k * ch : (k + 1) * ch], at_win + k * ch, ch) for k in range(3)],
        [(r_w2h.at[k], at_w2 + k * deep, deep) for k in range(3)],
    )
    count = 0
    loads = []
    for group in groups:
        loads.append([])
        for src, at, n in group:
            c = pltpu.make_async_copy(src, r_pb.at[pl.ds(at, n)], r_wsem.at[count])
            c.start()
            loads[-1].append(c)
            count += 1
    loads.append([])
    for src, dst in (
        (r_cwh.at[:, pair_at(0)], r_cw.at[:, : 2 * hd]),
        (r_cwh.at[:, pair_at(ch)], r_cw.at[:, 2 * hd :]),
    ):
        c = pltpu.make_async_copy(src, dst, r_wsem.at[count])
        c.start()
        loads[-1].append(c)
        count += 1
    load_w1, load_ew, load_win, load_w2, load_cw = loads

    def ready(copies):
        for c in copies:
            c.wait()

    places = (0, 1, 2, 3, 4, 7, 8, 9, 11, 12, 13)
    flat = [v for v in r_vecs[:-1]] + [r_vecs[-1].at[:, :ch], r_vecs[-1].at[:, ch:]]
    vec_loads = [
        pltpu.make_async_copy(v, r_par.at[pl.ds(at, 1)], r_vsem.at[i])
        for i, (v, at) in enumerate(zip(flat, places))
    ]
    for c in vec_loads:
        c.start()
    weight = r_weight[0].astype(f32) * 0.25
    for at in (5, 6, 14, 15):
        r_par[at : at + 1, :] = jnp.zeros((1, ch), f32)
    r_par[10:11, :] = jnp.full((1, ch), 1.0, f32) * weight
    stats = Stats(links, r_st_src, r_st_dst, r_st_send, r_st_recv)
    halo = Halo(links, r_h_send, r_h_recv)
    ends = (pl.ds(0, wide), pl.ds(px - wide, wide))

    def edges(slot, block, land):
        return halo.start(slot, block.at[ends[0]], block.at[ends[1]], land)

    pending = []

    def par(i):
        return r_par[i : i + 1, :]

    def share(slot, src, dst):
        copies = [pltpu.make_async_copy(src(links.img), dst(links.img), r_osem.at[slot])]
        for k in range(1, nimg):
            copies.append(
                links.copy(
                    "img", k, src(links.peer("img", k)), dst(links.img),
                    r_i_send.at[slot, k - 1], r_i_recv.at[slot, k - 1],
                )
            )
        for c in copies:
            c.start()
        pending.extend(copies)

    def scatter(slot, src, dst):
        copies = []
        for k in range(1, nrow):
            copies.append(
                links.copy(
                    "row", k, src(links.peer("row", k)), dst(me),
                    r_r_send.at[slot, k - 1], r_r_recv.at[slot, k - 1],
                )
            )
        for c in copies:
            c.start()
        return copies

    def lanes(img):
        return pl.ds(pl.multiple_of(img * px, 128), px)

    def moments(v):
        return [total(v), total(v * v)]

    def center(stage, sums):
        means = group_total(sums) * (1.0 / members)
        mean = means[0:1]
        rstd = lax.rsqrt(means[1:2] - mean * mean + EPSILON)
        r_stats[2 * stage : 2 * stage + 1, :] = mean
        r_stats[2 * stage + 1 : 2 * stage + 2, :] = rstd
        return mean, rstd

    r_stats[...] = jnp.zeros_like(r_stats)
    rows = moments(r_img[...].astype(f32))
    low = (r_oc[...].astype(f32) * weight).astype(bf16)
    r_gs[...] = nt_dot(r_pout[...], low).astype(bf16).reshape(r_gs.shape)
    r_emb[...] = jnp.broadcast_to(r_embv[...].astype(bf16).astype(f32), r_emb.shape)
    links.greeted()
    stats.start(0, rows)
    c_img = edges(0, r_img, r_himg)
    c_g = scatter(2, lambda r: r_gs.at[r], lambda r: r_g.at[r])
    for c in vec_loads:
        c.wait()
    ready(load_ew)
    emb = r_emb[...].astype(bf16)
    scale1 = 1.0 + (nn(emb, r_pb[at_ew : at_ew + text_in])[0:1] + par(12))
    shift = nn(emb, r_pb[at_ew + text_in : at_ew + 2 * text_in])[0:1] + par(13)
    r_ss[...] = jnp.concatenate([scale1, shift, jnp.zeros((6, ch), f32)], axis=0)
    mean, rstd = center(0, stats.finish(0))

    def conv_stage(stage, act, before, after, weights):
        buf = r_buf
        put_block(links, buf, act, before, after, wide)
        acc = None
        for ky in range(3):
            d = nn(
                buf[pl.ds(ky * wide, px), :],
                r_pb[weights + ky * deep : weights + (ky + 1) * deep, :],
            )
            acc = d if acc is None else acc + d
        r_at[stage] = act.astype(bf16).T
        return acc


    def act_one(v):
        return jax.nn.silu((v.astype(f32) - mean) * rstd * par(0) + par(1))

    halo.finish(c_img)
    ready(load_w1)
    hidden = conv_stage(
        0, act_one(r_img[...]), act_one(r_himg[0]), act_one(r_himg[1]), at_w1
    ) + par(2)
    r_hidden[...] = hidden
    stats.start(1, moments(hidden))
    c_hid = edges(1, r_hidden, r_hhid)
    ready(load_win)
    for j in range(3):
        turned = r_pb[at_win + j * ch : at_win + (j + 1) * ch, :].T
        for h in range(HEADS):
            r_wt[(3 * h + j) * hd : (3 * h + j + 1) * hd, :] = turned[h * hd : (h + 1) * hd]
    mean_two, rstd_two = center(1, stats.finish(1))

    def act_two(v):
        affine = (v - mean_two) * rstd_two * par(3) + par(4)
        return jax.nn.silu(affine * r_ss[0:1] + r_ss[1:2])

    halo.finish(c_hid)
    ready(load_w2)
    middle = conv_stage(1, act_two(r_hidden[...]), act_two(r_hhid[0]), act_two(r_hhid[1]), at_w2)
    middle = r_img[...].astype(f32) + middle + par(7)
    r_middle[...] = middle
    stats.start(2, moments(middle))
    c_mid = edges(2, r_middle, r_hmid)
    c_oc = edges(3, r_oc, r_hoc)
    nctx, text = r_cxt.shape
    padc = r_ctx.shape[0]
    r_ctx[...] = jnp.concatenate(
        [r_cxt[...], jnp.zeros((padc - nctx, text), bf16)], axis=0
    )
    ready(load_cw)
    enc = nn(r_ctx[...], r_cw[...]).T.astype(bf16)
    first = lax.rem(head, 2) == 0
    enc = jnp.concatenate(
        [
            jnp.where(first, enc[2 * j * hd : (2 * j + 1) * hd], enc[(2 * j + 1) * hd : (2 * j + 2) * hd])
            for j in range(2)
        ],
        axis=0,
    )
    mean, rstd = center(2, stats.finish(2))
    act3 = ((r_middle[...] - mean) * rstd * par(8) + par(9)).astype(bf16)
    r_a3[...] = act3.T
    ts, qkv, gs, g = r_ts, r_qkv, r_gs, r_g
    ts[...] = nn(r_wt[...], r_a3[...]).astype(bf16).reshape(ts.shape)
    tall = nrow // 2
    row_z, row_x = me // 2, lax.rem(me, 2)

    def source(i):
        z = lax.rem(row_z + lax.rem((i + 1) // 2, tall), tall)
        return 2 * z + lax.rem(row_x + i + 1, 2)

    def target(i):
        z = lax.rem(row_z + tall - lax.rem((i + 1) // 2, tall), tall)
        return 2 * z + lax.rem(row_x + i + 1, 2)

    def q_copy(i):
        to = target(i)
        return links.to(
            "row", to, ts.at[to, pl.ds(0, hd)], qkv.at[me, pl.ds(0, hd)],
            r_r_send.at[1, i], r_r_recv.at[1, i],
        )

    q_copy(0).start()
    c_kv = scatter(0, lambda r: ts.at[r, pl.ds(hd, 2 * hd)], lambda r: qkv.at[r, pl.ds(hd, 2 * hd)])
    npix = nrow * px
    ones_rows = jnp.where(lax.broadcasted_iota(jnp.int32, (hd, px), 0) < 2, 1.0, 0.0).astype(bf16)
    kx, vx, kt, vt, sb, pb, acc = (r_kx, r_vx, r_kt, r_vt, r_sb, r_pb, r_acc)

    def fill(pair, at, w):
        k = pair[:hd].astype(f32) * (LOG2E * 0.125)
        hi = k.astype(bf16)
        lo = (k - hi.astype(f32)).astype(bf16)
        kx[pl.ds(at, w), :] = jnp.concatenate([hi, lo], axis=0).T
        vfull = jnp.concatenate([pair[hd:], ones_rows[:, :w]], axis=0)
        vx[pl.ds(at, w), :] = vfull.T
        kt[:, pl.ds(at, w)] = pair[:hd]
        vt[:, pl.ds(at, w)] = vfull[: hd + 16]

    fill(enc, npix, padc)
    qkv[me] = ts[me]
    g[me] = gs[me]
    acc[...] = jnp.zeros_like(acc)

    def own(r):
        return pl.multiple_of(r * px, 128)

    fill(ts[me, hd:], own(me), px)
    for k in range(1, nrow):
        c_kv[k - 1].wait()
        frm = lax.rem(me + nrow - k, nrow)
        fill(qkv[frm, hd:], own(frm), px)


    q_copy(1).start()
    for i in range(2):
        share(i, lambda p, i=i: r_at.at[i], lambda p, i=i: (r_a1h, r_a2h)[i].at[:, lanes(p)])
    mine = text // nrow
    text_at = pl.ds(pl.multiple_of(me * mine, 128), mine)
    share(2, lambda p: r_ctx.at[:, text_at], lambda p: r_ctxh.at[p])
    wide_emb = r_emb.shape[1] // nrow
    emb_at = pl.ds(pl.multiple_of(me * wide_emb, 128), wide_emb)
    share(3, lambda p: r_emb.at[:, emb_at], lambda p: r_embh.at[p])
    halo.finish(c_mid)
    halo.finish(c_oc)
    kept = (
        (r_hidden, r_hiddenh),
        (r_middle, r_middleh),
        (r_wt, r_wth),
        (r_a3, r_a3h),
        (r_hoc, r_hoch),
        (r_hhid, r_hhidh),
        (r_hmid, r_hmidh),
    )
    for i, (a, b) in enumerate(kept):
        c = pltpu.make_async_copy(a, b, r_bsem.at[i])
        c.start()
        pending.append(c)

    bq = px
    nfull = npix // kc

    def att_copy(i):
        to = source(i)
        return links.to(
            "row", to, r_atb.at[to], r_atth.at[me], r_r_send.at[3, i], r_r_recv.at[3, i]
        )

    def dq_copy(i):
        to = source(i)
        return links.to(
            "row", to, r_dqb.at[to, pl.ds(0, hd)], r_tgh.at[me, pl.ds(0, hd)],
            r_r_send.at[4, i], r_r_recv.at[4, i],
        )

    nk = npix + padc

    def scores(i, slot):
        s = source(i)
        base = pl.multiple_of(slot * nk, 16)

        @pl.when(i + 2 < nrow - 1)
        def _():
            q_copy(i + 2).start()

        @pl.when(i < nrow - 1)
        def _():
            q_copy(i).wait_recv()
            k = lax.rem(me - s + nrow, nrow) - 1
            links.to("row", s, gs.at[s], g.at[s], r_r_send.at[2, k], r_r_recv.at[2, k]).wait_recv()

        qt = qkv[s, :hd]
        gt = g[s]
        q2 = jnp.concatenate([qt, qt], axis=0)
        sc = nn(kx[pl.ds(npix, padc), :], q2)
        sc = jnp.where(lax.broadcasted_iota(jnp.int32, (padc, bq), 0) < nctx, sc, -jnp.inf)
        sb[pl.ds(npix, padc), :] = sc
        m8 = jnp.max(sc.reshape(padc // 8, 8, bq), axis=0)

        def phase_a(c, m8):
            at = pl.multiple_of(c * kc, kc)
            sv = nn(kx[pl.ds(at, kc), :], q2)
            sb[pl.ds(at, kc), :] = sv
            return jnp.maximum(m8, jnp.max(sv.reshape(kc // 8, 8, bq), axis=0))

        m8 = lax.fori_loop(0, nfull, phase_a, m8, unroll=True)
        m = jnp.max(m8, axis=0, keepdims=True)
        pc = jnp.exp2(sb[pl.ds(npix, padc), :] - m).astype(bf16)
        pb[pl.ds(base + npix, padc), :] = pc
        o = nn(vt[:, npix : npix + padc], pc)

        def phase_b(c, o):
            at = pl.multiple_of(c * kc, kc)
            p = jnp.exp2(sb[pl.ds(at, kc), :] - m).astype(bf16)
            pb[pl.ds(pl.multiple_of(base + at, 16), kc), :] = p
            return o + nn(vt[:, pl.ds(at, kc)], p)

        o = lax.fori_loop(0, nfull, phase_b, o, unroll=True)
        inv = 1.0 / o[hd : hd + 1]
        att = o[:hd] * inv
        r_atb[s] = att.astype(bf16)

        @pl.when(i < nrow - 1)
        def _():
            att_copy(i).start()

        gf = gt.astype(f32)
        delta = total(gf * att) * inv
        gl = (gf * inv).astype(bf16)
        dhi = (-delta).astype(bf16)
        dlo = (-delta - dhi.astype(f32)).astype(bf16)
        r_gx[slot] = jnp.concatenate([gl, dhi, dlo, jnp.zeros((hd - 2, bq), bf16)], axis=0)
        r_dqa[slot] = piece(slot, qt, npix, padc, jnp.zeros((hd, bq), f32))

    def piece(slot, qt, at, w, dq):
        gx = r_gx[slot]
        p = pb[pl.ds(pl.multiple_of(slot * nk + at, 16), w), :]
        dp = nn(vx[pl.ds(at, w), :], gx)
        ds = (p.astype(f32) * dp).astype(bf16)
        acc[:hd, pl.ds(at, w)] += nt_dot(qt, ds)
        acc[hd:, pl.ds(at, w)] += nt_dot(gx[:hd], p)
        return dq + nn(kt[:, pl.ds(at, w)], ds)

    def block(i, _):
        s = source(i)
        scores(i, 0)
        qt = qkv[s, :hd]

        def phase_d(c, dq):
            return piece(0, qt, pl.multiple_of(c * kc, kc), kc, dq)

        dq = lax.fori_loop(0, nfull, phase_d, r_dqa[0], unroll=True)
        r_dqb[s, :hd] = (dq * 0.125).astype(bf16)
        dq_copy(i).start()
        return 0

    alone = nrow - joint
    lax.fori_loop(0, alone, block, 0)
    scale = jnp.where(lax.broadcasted_iota(jnp.int32, (2 * hd, 1), 0) < hd, 0.125, 1.0)

    def first(j, _):
        scores(alone + j, j)
        return 0

    lax.fori_loop(0, joint, first, 0)

    def key_home(c):
        z = lax.rem(row_z + 1 + c // 2, tall)
        return 2 * z + lax.rem(row_x + c + 1, 2)

    def kv_back(c):
        s = key_home(c)
        return links.to(
            "row", s, r_dqb.at[s, pl.ds(hd, 2 * hd)], r_tgh.at[me, pl.ds(hd, 2 * hd)],
            r_r_send.at[5, c], r_r_recv.at[5, c],
        )

    def keys_done(c, _):
        z = lax.rem(row_z + 1 + c, tall)
        at = pl.multiple_of(z * (2 * px), 128)
        for j in range(joint):
            qt = qkv[source(alone + j), :hd]
            r_dqa[j] = piece(j, qt, at, 2 * px, r_dqa[j])
        for h in range(2):
            s = key_home(2 * c + h)
            r_dqb[s, hd:] = (acc[:, pl.ds(own(s), px)] * scale).astype(bf16)

            @pl.when(2 * c + h < nrow - 1)
            def _():
                kv_back(2 * c + h).start()

        return 0

    lax.fori_loop(0, tall, keys_done, 0, unroll=True)
    copies = []
    for j in range(joint):
        r_dqb[source(alone + j), :hd] = (r_dqa[j] * 0.125).astype(bf16)
        if alone + j < nrow - 1:
            dq_copy(alone + j).start()
    r_dcb[...] = (acc[:, npix : npix + padc] * scale).astype(bf16).T
    copies += scatter(6, lambda r: r_dcb, lambda r: r_ench.at[r])
    for i, (a, b) in enumerate(
        (
            (r_dqb.at[me], r_tgh.at[me]),
            (r_atb.at[me], r_atth.at[me]),
            (r_dcb, r_ench.at[me]),
        )
    ):
        c = pltpu.make_async_copy(a, b, r_osem.at[4 + i])
        c.start()
        copies.append(c)
    for i in range(nrow - 1):
        q_copy(i).wait_send()
    for c in c_g:
        c.wait_send()
    for i in range(nrow - 1):
        att_copy(i).wait()
        dq_copy(i).wait()
        kv_back(i).wait()
    for c in copies + pending:
        c.wait()


def front(
    images, out_cot, project_out, context, emb, weight, vectors, w1, w2, win, cw, ew, nrow, nimg, wide
):
    px, ch = images.shape
    hd = ch // HEADS
    padc = -(-context.shape[0] // 16) * 16
    cfg = (nrow, nimg, wide, ch, hd, 1024, 3, len(vectors))
    nk = nrow * px + padc
    joint = cfg[6]
    V = pl.BlockSpec(memory_space=pltpu.VMEM)
    A = pl.BlockSpec(memory_space=pl.ANY)
    S = jax.ShapeDtypeStruct
    M = pltpu.VMEM
    dma = pltpu.SemaphoreType.DMA
    return pl.pallas_call(
        functools.partial(front_kernel, cfg),
        out_shape=(
            S((16, ch), f32),
            S((8, ch), f32),
            S((8, ch), f32),
            S((px, ch), f32),
            S((px, ch), f32),
            S((3 * ch, ch), bf16),
            S((ch, px), bf16),
            S((2, wide, ch), bf16),
            S((2, wide, ch), f32),
            S((2, wide, ch), f32),
            S((ch, nimg * px), bf16),
            S((ch, nimg * px), bf16),
            S((nimg, padc, context.shape[1] // nrow), bf16),
            S((nimg, 8, emb.shape[1] // nrow), f32),
            S((nrow, 3 * hd, px), bf16),
            S((nrow, hd, px), bf16),
            S((nrow, padc, 2 * hd), bf16),
        ),
        in_specs=[V] * 5
        + [pl.BlockSpec(memory_space=pltpu.SMEM)]
        + [A] * (len(vectors) + 5),
        out_specs=(V,) * 3 + (A,) * 14,
        scratch_shapes=[
            M((px, ch), f32),
            M((px, ch), f32),
            M((3 * ch, ch), bf16),
            M((ch, px), bf16),
            M((2, wide, ch), bf16),
            M((2, wide, ch), f32),
            M((2, wide, ch), f32),
            M((8, emb.shape[1]), f32),
            M((2, wide, ch), bf16),
            M((joint, 2 * hd, px), bf16),
            M((joint, hd, px), f32),
            M((cw.shape[0], 4 * hd), bf16),
            M((padc, cw.shape[0]), bf16),
            M((px + 2 * wide, 3 * ch), bf16),
            M((2, ch, px), bf16),
            M((nrow, hd, px), bf16),
            M((nrow, 3 * hd, px), bf16),
            M((nrow, 3 * hd, px), bf16),
            M((nrow, hd, px), bf16),
            M((nk, 2 * hd), bf16),
            M((nk, 2 * hd), bf16),
            M((hd, nk), bf16),
            M((hd + 16, nk), bf16),
            M((nk, px), f32),
            M((max(joint * nk, 2 * emb.shape[1] + 21 * ch), px), bf16),
            M((2 * hd, nk), f32),
            M((nrow, hd, px), bf16),
            M((nrow, 3 * hd, px), bf16),
            M((padc, 2 * hd), bf16),
            M((3, 8, 128), f32),
            M((3, nrow, 8, 128), f32),
            dma((13,)),
            dma((11,)),
            dma((3, nrow - 1)),
            dma((3, nrow - 1)),
            dma((4, 2)),
            dma((4, 2)),
            dma((4, nimg - 1)),
            dma((4, nimg - 1)),
            dma((7, nrow - 1)),
            dma((7, nrow - 1)),
            dma((8,)),
            dma((7,)),
        ],
        compiler_params=pltpu.CompilerParams(
            collective_id=3, has_side_effects=True, vmem_limit_bytes=62 * 2**20
        ),
        name="front",
    )(images, out_cot, project_out, context, emb, weight, *vectors, w1, w2, win, cw, ew)
def slope(values):
    sig = jax.nn.sigmoid(values)
    return sig * (1.0 + values * (1.0 - sig))


def back_kernel(
    cfg,
    r_imgh,
    r_och,
    r_par,
    r_ss,
    r_stats,
    r_hiddenh,
    r_middleh,
    r_hoch,
    r_hhidh,
    r_hmidh,
    r_a3h,
    r_tgh,
    r_atth,
    r_wth,
    r_w2h,
    r_w1h,
    r_a2h,
    r_a1h,
    r_ench,
    r_ctxh,
    r_igrad,
    r_kq,
    r_oq,
    r_cr,
    r_every,
    r_img,
    r_oc,
    r_hidden,
    r_middle,
    r_hoc,
    r_hhid,
    r_hmid,
    r_a3,
    r_tg,
    r_att,
    r_wt,
    r_w2,
    r_w1,
    r_a2,
    r_a1,
    r_enc,
    r_ctx,
    r_mg,
    r_ntg,
    r_buf,
    r_gq,
    r_gs,
    r_ks,
    r_kx,
    r_km,
    r_kz,
    r_kf,
    r_os,
    r_ox,
    r_oy,
    r_oz,
    r_of,
    r_encq,
    r_cq,
    r_vsrc,
    r_st_src,
    r_st_dst,
    r_hu,
    r_kacc,
    r_lsem,
    r_st_send,
    r_st_recv,
    r_h_send,
    r_h_recv,
    r_i_send,
    r_i_recv,
    r_r_send,
    r_r_recv,
    r_x_send,
    r_x_recv,
    r_z_send,
    r_z_recv,
    r_osem,
):
    nrow, nimg, wide, ch, hd, padc = cfg
    px = r_img.shape[0]
    part = ch // nimg
    rows = ch // nrow
    deep = nrow // 2
    members = float(nrow * px * (ch // GROUPS))
    links = Links(nrow, nimg)
    links.greet()
    pairs = (
        (r_tgh, r_tg),
        (r_wth, r_wt),
        (r_middleh, r_middle),
        (r_och, r_oc),
        (r_a3h, r_a3),
        (r_atth, r_att),
        (r_hiddenh, r_hidden),
        (r_imgh, r_img),
        (r_hmidh, r_hmid),
        (r_hoch, r_hoc),
        (r_hhidh, r_hhid),
        (r_w2h, r_w2),
        (r_a2h, r_a2),
        (r_w1h, r_w1),
        (r_a1h, r_a1),
        (r_ench, r_enc),
        (r_ctxh, r_ctx),
    )
    loads = [pltpu.make_async_copy(a, b, r_lsem.at[i]) for i, (a, b) in enumerate(pairs)]
    for c in loads:
        c.start()
    load_w2, load_a2, load_w1, load_a1, load_enc, load_ctx = loads[11:]
    stats = Stats(links, r_st_src, r_st_dst, r_st_send, r_st_recv)
    halo = Halo(links, r_h_send, r_h_recv)
    ends = (pl.ds(0, wide), pl.ds(px - wide, wide))

    def edges(slot, block, land):
        return halo.start(slot, block.at[ends[0]], block.at[ends[1]], land)

    others = (
        links.img + 1 - 2 * lax.rem(links.img, 2),
        lax.rem(links.img + 2, nimg),
        nimg - 1 - links.img,
    )
    row_z, row_x = links.row // 2, lax.rem(links.row, 2)
    img_y, img_c = links.img // 2, lax.rem(links.img, 2)

    def par(i):
        return r_par[i : i + 1, :]

    def stat(i):
        return r_stats[i : i + 1, :]

    scale1, shift = r_ss[0:1], r_ss[1:2]

    def share(slot, src, dst):
        copies = [pltpu.make_async_copy(src(links.img), dst(links.img), r_osem.at[slot])]
        for k, at in enumerate(others):
            copies.append(
                links.to(
                    "img", at, src(at), dst(links.img), r_i_send.at[slot, k], r_i_recv.at[slot, k]
                )
            )
        for c in copies:
            c.start()
        return copies

    def wait(copies):
        for c in copies:
            c.wait()

    def columns(at, img):
        return pl.ds(pl.multiple_of(at + img * part, 128), part)

    def row_x_start(slot, src, land):
        c = links.to(
            "row", links.row + 1 - 2 * row_x, src.at[:, 1 - row_x], land,
            r_x_send.at[slot], r_x_recv.at[slot],
        )
        c.start()
        return c

    def row_z_start(slot, c, src, land, mid, last):
        c.wait()
        mid[...] = (src[:, row_x].astype(f32) + land[...].astype(f32)).astype(bf16)
        copies = []
        for k in range(1, deep):
            z = lax.rem(row_z + k, deep)
            copies.append(
                links.to(
                    "row", 2 * z + row_x, mid.at[z], last.at[k - 1],
                    r_z_send.at[slot, k - 1], r_z_recv.at[slot, k - 1],
                )
            )
        for d in copies:
            d.start()
        return copies

    def row_end(copies, mid, last):
        wait(copies)
        s = mid[row_z].astype(f32)
        for k in range(1, deep):
            s = s + last[k - 1].astype(f32)
        return s.astype(bf16)

    def back_means(gain, gain_sum, bias_sum):
        both = jnp.concatenate([gain * bias_sum, gain * gain_sum, jnp.zeros((6, ch), f32)], axis=0)
        return group_total(both) * (1.0 / members)

    def norm_back(u, normed, rstd, gain, means):
        return rstd * (u * gain - means[0:1] - normed * means[1:2])

    def conv_back(stage, grad, before, after, weights):
        buf = r_buf.at[stage]
        put_block(links, buf, grad, before, after, wide)
        copies = share(
            stage, lambda i: buf.at[:, columns(ch, i)], lambda i: r_gq.at[stage, i]
        )
        acc = None
        for ky in range(3):
            for kx in range(3):
                g = buf[pl.ds(ky * wide, px), pl.ds(kx * ch, ch)]
                w = weights[2 - ky, pl.ds((2 - kx) * ch, ch), :]
                d = nt_dot(g, w)
                acc = d if acc is None else acc + d
        return acc, copies

    def kernel_part(stage, acts, ky, images):
        tot = None
        for b in images:
            at = pl.ds(pl.multiple_of(b * px, 128), px)
            d = nn(acts[:, at], r_gs[b, ky * wide : ky * wide + px, :])
            tot = d if tot is None else tot + d
        return tot

    def kernel_grads(stage, acts, copies):
        near, far = (links.img, others[0]), others[1:]
        for group, first in ((near, True), (far, False)):
            for b, c in zip(group, copies[:2] if first else copies[2:]):
                c.wait()
                put_shifts(r_gs.at[b], 0, r_gq[stage, b].astype(f32), wide)
            if first:
                for ky in range(3):
                    r_kacc[ky] = kernel_part(stage, acts, ky, near)
        sent = []
        for ky in range(3):
            tot = r_kacc[ky] + kernel_part(stage, acts, ky, far)
            r_ks[stage, ky] = tot.astype(bf16).reshape(deep, 2, rows, 3 * part)
            sent.append(row_x_start(3 * stage + ky, r_ks.at[stage, ky], r_kx.at[stage, ky]))
        return sent

    def kernel_mid(stage, sent, ky):
        return row_z_start(
            3 * stage + ky, sent[ky], r_ks.at[stage, ky], r_kx.at[stage, ky],
            r_km.at[stage, ky], r_kz.at[stage, ky],
        )

    def kernel_end(stage, copies):
        out = []
        for ky in range(3):
            r_kf[stage, ky] = row_end(copies[ky], r_km.at[stage, ky], r_kz.at[stage, ky])
            out += share(
                2 + 3 * stage + ky,
                lambda i, ky=ky: r_kf.at[stage, ky],
                lambda i, ky=ky: r_kq.at[stage, ky, i],
            )
        return out

    for c in loads[:11]:
        c.wait()
    tgt = r_tg[...].reshape(3 * ch, px)
    u3 = nn(tgt.T, r_wt[...])
    normed3 = (r_middle[...] - stat(4)) * stat(5)
    grad_out = r_oc[...].astype(f32) * par(10)
    r_mg[...] = u3
    sums = [total(u3 * normed3), total(u3), total(grad_out)]
    links.greeted()
    stats.start(0, sums)
    c_u = edges(0, r_mg, r_hu.at[0])
    load_enc.wait()
    c_encq = share(8, lambda i: r_enc.at[pl.ds(2 * i, 2)], lambda i: r_encq.at[i])
    a3 = r_a3[...]
    low = (r_oc[...].astype(f32) * par(10)).astype(bf16)
    pout = nn(r_att[...].reshape(ch, px), low).astype(bf16)
    for q in range(nimg):
        pin = nt_dot(a3, r_tg[2 * q : 2 * q + 2].reshape(6 * hd, px)).astype(bf16)
        r_os[q // 2, q % 2] = jnp.concatenate(
            [pin, pout[:, q * part : (q + 1) * part]], axis=1
        )
    c_ox = links.to(
        "img", links.img + 1 - 2 * img_c, r_os.at[:, 1 - img_c], r_ox,
        r_i_send.at[9, 0], r_i_recv.at[9, 0],
    )
    c_ox.start()
    sums3 = stats.finish(0)
    means3 = back_means(par(8), sums3[0:1], sums3[1:2])

    def middle_back(u, middle, oc):
        normed = (middle - stat(4)) * stat(5)
        return oc.astype(f32) * par(10) + norm_back(u, normed, stat(5), par(8), means3)

    halo.finish(c_u)
    middle_grad = middle_back(r_mg[...], r_middle[...], r_oc[...])
    r_mg[...] = middle_grad
    load_w2.wait()
    act_grad, c_g2 = conv_back(
        0,
        middle_grad,
        middle_back(r_hu[0, 0], r_hmid[0], r_hoc[0]),
        middle_back(r_hu[0, 1], r_hmid[1], r_hoc[1]),
        r_w2,
    )
    normed2 = (r_hidden[...] - stat(2)) * stat(3)
    ntg = act_grad * slope((normed2 * par(3) + par(4)) * scale1 + shift)
    r_ntg[...] = ntg
    stats.start(1, [total(ntg * normed2), total(ntg)])
    c_n = edges(1, r_ntg, r_hu.at[1])
    middle_sum = total(r_mg[...])
    load_a2.wait()
    c_k2 = kernel_grads(0, r_a2, c_g2)
    c_ox.wait()
    r_os[:, 0] = (
        r_os[:, img_c].astype(f32) + r_ox[...].astype(f32)
    ).astype(bf16)
    c_oy = links.to(
        "img", lax.rem(links.img + 2, nimg), r_os.at[1 - img_y, 0], r_oy,
        r_i_send.at[9, 1], r_i_recv.at[9, 1],
    )
    c_oy.start()
    sums2 = stats.finish(1)
    means2 = back_means(par(3), scale1 * sums2[0:1], scale1 * sums2[1:2])

    def hidden_back(u, hidden):
        normed = (hidden - stat(2)) * stat(3)
        return norm_back(u * scale1, normed, stat(3), par(3), means2)

    halo.finish(c_n)
    hidden_grad = hidden_back(r_ntg[...], r_hidden[...])
    hidden_sum = total(hidden_grad)
    load_w1.wait()
    act_grad, c_g1 = conv_back(
        1,
        hidden_grad,
        hidden_back(r_hu[1, 0], r_hhid[0]),
        hidden_back(r_hu[1, 1], r_hhid[1]),
        r_w1,
    )
    m_k2 = [kernel_mid(0, c_k2, 0), kernel_mid(0, c_k2, 1)]
    c_oy.wait()
    both = r_os[img_y, 0].astype(f32) + r_oy[...].astype(f32)
    r_of[...] = both.astype(bf16).reshape(deep, 2, rows, 6 * hd + part)
    c_o = row_x_start(6, r_of, r_oz.at[0])
    normed1 = (r_img[...].astype(f32) - stat(0)) * stat(1)
    n1g = act_grad * slope(normed1 * par(0) + par(1))
    r_ntg[...] = n1g
    stats.start(2, [total(n1g * normed1), total(n1g), hidden_sum, middle_sum])
    m_k2.append(kernel_mid(0, c_k2, 2))
    load_a1.wait()
    c_k1 = kernel_grads(1, r_a1, c_g1)
    c_o = row_z_start(6, c_o, r_of, r_oz.at[0], r_oz.at[1], r_oz.at[2, pl.ds(0, deep - 1)])
    wait(c_encq)
    load_ctx.wait()
    turned = r_ctx[...].reshape(nimg * padc, -1).T
    pairs = jnp.concatenate([r_encq[:, 0], r_encq[:, 1]], axis=2)
    r_cq[...] = nn(turned, pairs.reshape(nimg * padc, 4 * hd)).astype(bf16)
    out = share(11, lambda i: r_cq, lambda i: r_cr.at[i])
    sums1 = stats.finish(2)
    scale_grad = par(3) * sums2[0:1] + par(4) * sums2[1:2]
    r_vsrc[...] = jnp.concatenate(
        [
            sums1[0:3],
            scale1 * sums2[0:1],
            scale1 * sums2[1:2],
            sums1[3:4],
            sums3[0:3],
            scale_grad,
            sums2[1:2],
            jnp.zeros((5, ch), f32),
        ],
        axis=0,
    )
    out += share(10, lambda i: r_vsrc, lambda i: r_every.at[i])
    m_k1 = [kernel_mid(1, c_k1, 0)]
    normed1 = (r_img[...].astype(f32) - stat(0)) * stat(1)
    means1 = back_means(par(0), sums1[0:1], sums1[1:2])
    r_igrad[...] = r_mg[...] + norm_back(r_ntg[...], normed1, stat(1), par(0), means1)
    m_k1.append(kernel_mid(1, c_k1, 1))
    out += kernel_end(0, m_k2)
    m_k1.append(kernel_mid(1, c_k1, 2))
    r_oy[:rows] = row_end(c_o, r_oz.at[1], r_oz.at[2])
    out += share(12, lambda i: r_oy.at[pl.ds(0, rows)], lambda i: r_oq.at[i])
    out += kernel_end(1, m_k1)
    wait(out)


def backward(nrow, nimg, wide, *args):
    px, ch = args[0].shape
    hd = ch // HEADS
    ctx, enc = args[19], args[18]
    padc = enc.shape[1]
    cfg = (nrow, nimg, wide, ch, hd, padc)
    part, rows, deep = ch // nimg, ch // nrow, nrow // 2
    proj = 6 * hd + part
    V = pl.BlockSpec(memory_space=pltpu.VMEM)
    A = pl.BlockSpec(memory_space=pl.ANY)
    S = jax.ShapeDtypeStruct
    dma = pltpu.SemaphoreType.DMA
    M = pltpu.VMEM
    text = ctx.shape[2]
    return pl.pallas_call(
        functools.partial(back_kernel, cfg),
        out_shape=(
            S((px, ch), f32),
            S((2, 3, nimg, rows, 3 * part), bf16),
            S((nimg, rows, proj), bf16),
            S((nimg, text, 4 * hd), bf16),
            S((nimg, 16, ch), f32),
        ),
        in_specs=[A, A, V, V, V, A, A, A, A, A, A, A, A, A] + [A] * 6,
        out_specs=(V,) + (A,) * 4,
        scratch_shapes=[M(args[i].shape, args[i].dtype) for i in (0, 1, 5, 6, 7, 8, 9, 10, 11, 12, 13)]
        + [
            M((3, 3 * ch, ch), bf16),
            M((3, 3 * ch, ch), bf16),
            M((ch, nimg * px), bf16),
            M((ch, nimg * px), bf16),
            M(enc.shape, bf16),
            M(ctx.shape, bf16),
            M((px, ch), f32),
            M((px, ch), f32),
            M((2, px + 2 * wide, 3 * ch), bf16),
            M((2, nimg, px + 2 * wide, part), bf16),
            M((nimg, px + 2 * wide, 3 * part), bf16),
            M((2, 3, deep, 2, rows, 3 * part), bf16),
            M((2, 3, deep, rows, 3 * part), bf16),
            M((2, 3, deep, rows, 3 * part), bf16),
            M((2, 3, deep - 1, rows, 3 * part), bf16),
            M((2, 3, rows, 3 * part), bf16),
            M((2, 2, ch, proj), bf16),
            M((2, ch, proj), bf16),
            M((ch, proj), bf16),
            M((3, deep, rows, proj), bf16),
            M((deep, 2, rows, proj), bf16),
            M((nimg, 2, padc, 2 * hd), bf16),
            M((text, 4 * hd), bf16),
            M((16, ch), f32),
            M((3, 16, 128), f32),
            M((3, nrow, 16, 128), f32),
            M((2, 2, wide, ch), f32),
            M((3, ch, 3 * part), f32),
            dma((17,)),
            dma((3, nrow - 1)),
            dma((3, nrow - 1)),
            dma((2, 2)),
            dma((2, 2)),
            dma((13, nimg - 1)),
            dma((13, nimg - 1)),
            dma((1, nrow - 1)),
            dma((1, nrow - 1)),
            dma((7,)),
            dma((7,)),
            dma((7, deep - 1)),
            dma((7, deep - 1)),
            dma((13,)),
        ],
        compiler_params=pltpu.CompilerParams(
            collective_id=4, has_side_effects=True, vmem_limit_bytes=60 * 2**20
        ),
        name="back",
    )(*args)


def finish_kernel(cfg, *refs):
    nrow, nimg, ch, hd, nvec = cfg
    igh, kqh, oqh, crh, everyh, embh, middleh, atth, pouth, parh = refs[:10]
    resh, igouth, k1h, k2h, inh, outh, ctxgh, embgh = refs[10:18]
    vecs = refs[18 : 18 + nvec]
    ig, kq, oq, cr, every, emb, middle, att, pout, par = refs[18 + nvec : 28 + nvec]
    res, k1g, k2g, ing, outg, ctxg, embg, isem, osem = refs[28 + nvec :]
    px = middle.shape[0]
    part = ch // nimg
    me = lax.axis_index("row")
    done = []
    pairs = (
        (kqh.at[0], kq.at[0]),
        (kqh.at[1], kq.at[1]),
        (atth, att),
        (pouth, pout),
        (middleh, middle),
        (parh, par),
        (everyh, every),
        (embh, emb),
        (crh, cr),
        (oqh, oq),
        (igh, ig),
    )
    loads = [pltpu.make_async_copy(a, b, isem.at[i]) for i, (a, b) in enumerate(pairs)]
    for c in loads:
        c.start()

    def put(slot, src, dst):
        c = pltpu.make_async_copy(src, dst, osem.at[slot])
        c.start()
        done.append(c)

    loads[10].wait()
    put(0, ig, igouth)
    for stage, out, dst in ((0, k2g, k2h), (1, k1g, k1h)):
        loads[stage].wait()
        for ky in range(3):
            for b in range(nimg):
                v = kq[stage, ky, b].astype(f32)
                for kx in range(3):
                    out[2 - ky, 2 - kx, :, b * part : (b + 1) * part] = v[
                        :, kx * part : (kx + 1) * part
                    ]
        put(1 + stage, out, dst)
    for c in loads[2:6]:
        c.wait()
    branch = nn(att[...].reshape(ch, px).T, pout[...])
    res[...] = (middle[...] + branch + par[11:12, :]).astype(bf16)
    put(3, res, resh)
    loads[6].wait()
    loads[7].wait()
    acts = emb[:, 0, :].T
    for j in range(2):
        d = None
        for b in range(nimg):
            t = acts[:, b : b + 1] * every[b, 9 + j : 10 + j]
            d = t if d is None else d + t
        embg[:, j * ch : (j + 1) * ch] = d
    put(4, embg, embgh)
    loads[8].wait()
    for b in range(nimg):
        v = cr[b].astype(f32)
        p = [v[:, j * hd : (j + 1) * hd] for j in range(4)]
        ctxg[:, b * 2 * hd : (b + 1) * 2 * hd] = jnp.concatenate([p[0], p[2]], axis=1)
        ctxg[:, ch + b * 2 * hd : ch + (b + 1) * 2 * hd] = jnp.concatenate([p[1], p[3]], axis=1)
    put(5, ctxg, ctxgh)
    loads[9].wait()
    for b in range(nimg):
        v = oq[b].astype(f32)
        for j in range(3):
            ing[:, j * ch + b * 2 * hd : j * ch + (b + 1) * 2 * hd] = jnp.concatenate(
                [v[:, j * hd : (j + 1) * hd], v[:, (3 + j) * hd : (4 + j) * hd]], axis=1
            )
        outg[:, b * part : (b + 1) * part] = v[:, 6 * hd :]
    put(6, ing, inh)
    put(7, outg, outh)
    sums = jnp.sum(every[...], axis=0)
    size = ch // nrow
    turned = pltpu.roll(sums, lax.rem(ch - me * size, ch), 1)
    for i in range(nvec - 1):
        vecs[i][...] = turned[i, :size]
    both = jnp.concatenate([sums[9:10], sums[10:11]], axis=1)
    both = jnp.concatenate([both] * 8, axis=0)
    both = pltpu.roll(both, lax.rem(2 * ch - me * 2 * size, 2 * ch), 1)
    vecs[nvec - 1][...] = both[0, : 2 * size]
    for c in done:
        c.wait()


def finish(nrow, nimg, *args):
    px, ch = args[0].shape
    hd = ch // HEADS
    kq, oq, cr, every, emb = args[1:6]
    rows = ch // nrow
    nvec = 10
    V = pl.BlockSpec(memory_space=pltpu.VMEM)
    A = pl.BlockSpec(memory_space=pl.ANY)
    S = jax.ShapeDtypeStruct
    M = pltpu.VMEM
    dma = pltpu.SemaphoreType.DMA
    outs = (
        ((px, ch), bf16),
        ((3, 3, rows, ch), f32),
        ((3, 3, rows, ch), f32),
        ((rows, 3 * ch), f32),
        ((rows, ch), f32),
        ((cr.shape[1], 2 * ch), f32),
        ((emb.shape[2], 2 * ch), f32),
    )
    return pl.pallas_call(
        functools.partial(finish_kernel, (nrow, nimg, ch, hd, nvec)),
        out_shape=(S(*outs[0]), S((px, ch), f32))
        + tuple(S(*o) for o in outs[1:])
        + (S((rows,), f32),) * (nvec - 1)
        + (S((2 * rows,), f32),),
        in_specs=[A] * 10,
        out_specs=(A,) * 8 + (V,) * nvec,
        scratch_shapes=[M(a.shape, a.dtype) for a in args]
        + [M(*o) for o in outs]
        + [dma((11,)), dma((8,))],
        compiler_params=pltpu.CompilerParams(vmem_limit_bytes=62 * 2**20),
        name="finish",
    )(*args)


def local_fast(
    images,
    timesteps,
    clip_embed,
    context,
    out_cotangent,
    item_weight,
    first_gain,
    first_bias,
    first_kernel,
    first_offset,
    embed_weight,
    embed_bias,
    second_gain,
    second_bias,
    second_kernel,
    second_offset,
    third_gain,
    third_bias,
    project_in,
    context_weight,
    project_out,
    output_bias,
):
    _, tall, wide, ch = images.shape
    pixels = tall * wide
    nrow = lax.axis_size("row")
    nimg = lax.axis_size("img")
    me_row = lax.axis_index("row")
    nctx = context.shape[1]
    image = images.reshape(pixels, ch)
    cotangent = out_cotangent.reshape(pixels, ch)
    width = clip_embed.shape[1]
    at = jnp.arange(width, dtype=jnp.int32)[None, :]
    half = width // 2
    index = jnp.where(at < half, at, at - half).astype(f32)
    angles = timesteps.astype(f32)[:, None] * jnp.exp(-math.log(10000.0) * index / half)
    embedding = jnp.where(at < half, jnp.cos(angles), jnp.sin(angles)) + clip_embed.astype(f32)
    emb = jax.nn.silu(embedding)
    vectors = [
        v.reshape(1, -1)
        for v in (
            first_gain, first_bias, first_offset, second_gain, second_bias, second_offset,
            third_gain, third_bias, output_bias, embed_bias,
        )
    ]
    w1 = first_kernel.reshape(3, 3 * ch, ch)
    w2 = second_kernel.reshape(3, 3 * ch, ch)
    (
        par, stats, ss, hidden, middle, turned_in, act_three, halo_cot, halo_hidden, halo_middle,
        acts_one, acts_two, ctx_parts, emb_parts, grads, attended, enc_grads,
    ) = front(
        image, cotangent, project_out, context[0], emb, item_weight, vectors, w1, w2, project_in, context_weight,
        embed_weight, nrow, nimg, wide,
    )
    image_grad, kq, oq, cr, every = backward(
        nrow, nimg, wide,
        image, cotangent, par, ss, stats, hidden, middle, halo_cot, halo_hidden, halo_middle, act_three, grads, attended, turned_in,
        w2, w1, acts_two, acts_one, enc_grads, ctx_parts,
    )
    result, image_grad, k1g, k2g, ing, outg, ctxg, embg, *vecs = finish(
        nrow, nimg, image_grad, kq, oq, cr, every, emb_parts, middle, attended, project_out, par
    )
    return (
        result.reshape(images.shape),
        image_grad.reshape(images.shape),
        vecs[0],
        vecs[1],
        k1g,
        vecs[2],
        embg,
        vecs[9],
        vecs[3],
        vecs[4],
        k2g,
        vecs[5],
        vecs[6],
        vecs[7],
        ing,
        ctxg,
        outg,
        vecs[8],
    )


def solution(mesh):
    every = P()
    image = P("img", "row", None, None)
    placed = (image, P("img"), P("img", None), P("img", None, None), image, P("img")) + (every,) * 16
    vec = P("row")
    matrix = P("row", None)
    taps = P(None, None, "row", None)
    nimg, nrow = mesh.shape["img"], mesh.shape["row"]
    quick = nrow == HEADS and nimg == 4
    return jax.shard_map(
        local_fast if quick else local,
        mesh=mesh,
        in_specs=placed,
        out_specs=(
            image,
            image,
            vec,
            vec,
            taps,
            vec,
            matrix,
            vec,
            vec,
            vec,
            taps,
            vec,
            vec,
            vec,
            matrix,
            matrix,
            matrix,
            vec,
        ),
        check_vma=False,
    )
```

```python
import functools
import math

import jax
import jax.numpy as jnp
from jax import lax
from jax.experimental import pallas as pl
from jax.experimental.pallas import tpu as pltpu
from jax.sharding import PartitionSpec as P

HEADS = 8
GROUPS = 32
EPSILON = 1e-05
f32 = jnp.float32
bf16 = jnp.bfloat16
MESH = pl.DeviceIdType.MESH
LOG2E=math.log2(math.e)

def nt(a,b):
    return lax.dot_general(a,b,(((1,),(1,)),((),())),preferred_element_type=f32)
def nn(a,b):
    return jnp.dot(a,b,preferred_element_type=f32)

def attn_kernel(cfg, *refs):
    if cfg[0]:
        q_ref, ctx_ref, g_ref, out_ref, dq_ref, dctx_ref = refs[:6]
        kv_ref, dkv_ref = q_ref, dq_ref
        at_kv = cfg[-1]
    else:
        q_ref, kv_ref, ctx_ref, g_ref, out_ref, dq_ref, dkv_ref, dctx_ref = refs[:8]
        at_kv = 0
    (kx, vx, kt, vt, sbuf, pbuf, acc) = refs[-7:]
    joined, nqs, nsrc, width, bq, kc, nctx, padc, hd = cfg
    npix = nsrc*width
    nk = npix + padc
    ones_rows = jnp.where(lax.broadcasted_iota(jnp.int32,(hd,width),0)<2,1.0,0.0).astype(bf16)
    def fill(pair, at, w):
        k = pair[:hd].astype(f32)*(LOG2E*0.125)
        hi = k.astype(bf16)
        lo = (k-hi.astype(f32)).astype(bf16)
        kx[pl.ds(at,w),:] = jnp.concatenate([hi,lo],axis=0).T
        vfull = jnp.concatenate([pair[hd:], ones_rows[:, :w]],axis=0)
        vx[pl.ds(at,w),:] = vfull.T
        return vfull
    for s in range(nsrc):
        pair = kv_ref[s, at_kv:]
        vfull = fill(pair, s*width, width)
        kt[:, s*width:(s+1)*width] = pair[:hd]
        vt[:, s*width:(s+1)*width] = vfull[:hd+16]
    cpair = ctx_ref[...]
    vfull = fill(cpair, npix, padc)
    kt[:, npix:npix+padc] = cpair[:hd]
    vt[:, npix:npix+padc] = vfull[:hd+16]
    acc[...] = jnp.zeros_like(acc)

    nfull = npix//kc
    per = width//bq
    def block(j, _):
        s = j//per
        off = pl.multiple_of((j%per)*bq, bq)
        qt = q_ref[s,:hd,pl.ds(off,bq)]
        gt = g_ref[s,:,pl.ds(off,bq)]
        q2 = jnp.concatenate([qt,qt],axis=0)
        sc = nn(kx[pl.ds(npix,padc),:], q2)
        sc = jnp.where(lax.broadcasted_iota(jnp.int32,(padc,bq),0)<nctx, sc, -jnp.inf)
        sbuf[pl.ds(npix,padc),:] = sc
        m8 = jnp.max(sc.reshape(padc//8,8,bq),axis=0)
        def phase_a(c, m8):
            at = pl.multiple_of(c*kc,kc)
            sv = nn(kx[pl.ds(at,kc),:], q2)
            sbuf[pl.ds(at,kc),:] = sv
            return jnp.maximum(m8, jnp.max(sv.reshape(kc//8,8,bq),axis=0))
        m8 = lax.fori_loop(0,nfull,phase_a,m8,unroll=True)
        m = jnp.max(m8,axis=0,keepdims=True)
        pc = jnp.exp2(sbuf[pl.ds(npix,padc),:]-m).astype(bf16)
        pbuf[pl.ds(npix,padc),:] = pc
        o = nn(vt[:,npix:npix+padc], pc)
        def phase_b(c, o):
            at = pl.multiple_of(c*kc,kc)
            p = jnp.exp2(sbuf[pl.ds(at,kc),:]-m).astype(bf16)
            pbuf[pl.ds(at,kc),:] = p
            return o + nn(vt[:,pl.ds(at,kc)], p)
        o = lax.fori_loop(0,nfull,phase_b,o,unroll=True)
        inv = 1.0/o[hd:hd+1]
        att = o[:hd]*inv
        out_ref[s,:,pl.ds(off,bq)] = att.astype(bf16)
        gf = gt.astype(f32)
        delta = jnp.sum(gf*att,axis=0,keepdims=True)*inv
        gl = (gf*inv).astype(bf16)
        dhi = (-delta).astype(bf16)
        dlo = (-delta-dhi.astype(f32)).astype(bf16)
        gx = jnp.concatenate([gl,dhi,dlo,jnp.zeros((hd-2,bq),bf16)],axis=0)
        zero = jnp.zeros((hd,bq),bf16)
        rq = jnp.concatenate([qt,zero],axis=0).T
        rg = jnp.concatenate([zero,gl],axis=0).T
        rr = jnp.concatenate([rq,rg],axis=0)
        def piece(at, w, dq):
            p = pbuf[pl.ds(at,w),:]
            dp = nn(vx[pl.ds(at,w),:], gx)
            ds = (p.astype(f32)*dp).astype(bf16)
            acc[pl.ds(at,w),:] += nn(jnp.concatenate([ds,p],axis=1), rr)
            return dq + nn(kt[:,pl.ds(at,w)], ds)
        dq = piece(npix, padc, jnp.zeros((hd,bq),f32))
        def phase_d(c, dq):
            return piece(pl.multiple_of(c*kc,kc), kc, dq)
        dq = lax.fori_loop(0,nfull,phase_d,dq,unroll=True)
        dq_ref[s,:hd,pl.ds(off,bq)] = (dq*0.125).astype(bf16)
        return 0
    lax.fori_loop(0, nqs*per, block, 0)
    scale = jnp.where(lax.broadcasted_iota(jnp.int32,(1,2*hd),1)<hd,0.125,1.0)
    for s in range(nsrc):
        dkv_ref[s, at_kv:] = (acc[s*width:(s+1)*width,:]*scale).astype(bf16).T
    dctx_ref[...] = (acc[npix:npix+padc,:]*scale).astype(bf16)

def attention(q, kv, ctx, g, nctx, bq=512, kc=512):
    joined = kv is None
    nqs, _, width = q.shape
    hd = g.shape[1]
    nsrc = nqs if joined else kv.shape[0]
    padc = ctx.shape[1]
    nk = nsrc*width+padc
    cfg=(joined,nqs,nsrc,width,bq,kc,nctx,padc,hd)
    V=pl.BlockSpec(memory_space=pltpu.VMEM)
    S=jax.ShapeDtypeStruct
    grads=(S((nqs,3*hd,width),bf16),) if joined else (S((nqs,hd,width),bf16),S((nsrc,2*hd,width),bf16))
    args=(q,ctx,g) if joined else (q,kv,ctx,g)
    return pl.pallas_call(
        functools.partial(attn_kernel,cfg),
        out_shape=(S((nqs,hd,width),bf16),)+grads+(S((padc,2*hd),bf16),),
        in_specs=[V]*len(args), out_specs=(V,)*(2+len(grads)),
        scratch_shapes=[pltpu.VMEM((nk,2*hd),bf16),pltpu.VMEM((nk,2*hd),bf16),
                        pltpu.VMEM((hd,nk),bf16),pltpu.VMEM((hd+16,nk),bf16),
                        pltpu.VMEM((nk,bq),f32),pltpu.VMEM((nk,bq),bf16),
                        pltpu.VMEM((nk,2*hd),f32)],
        compiler_params=pltpu.CompilerParams(vmem_limit_bytes=48*2**20),
        cost_estimate=pl.CostEstimate(flops=6*2*64*4096*4228,bytes_accessed=8*2**20,transcendentals=4096*4228),
        name="attend",
    )(*args)

def exchange_kernel(axis, n, x_ref, out_ref, send_sem, recv_sem):
    me = lax.axis_index(axis)
    barrier = pltpu.get_barrier_semaphore()
    for k in range(1, n):
        pl.semaphore_signal(
            barrier, inc=1, device_id={axis: lax.rem(me + k, n)}, device_id_type=MESH
        )
    out_ref[me] = x_ref[...]
    pl.semaphore_wait(barrier, n - 1)
    copies = []
    for k in range(1, n):
        copy = pltpu.make_async_remote_copy(
            src_ref=x_ref,
            dst_ref=out_ref.at[me],
            send_sem=send_sem.at[k - 1],
            recv_sem=recv_sem.at[k - 1],
            device_id={axis: lax.rem(me + k, n)},
            device_id_type=MESH,
        )
        copy.start()
        copies.append(copy)
    for copy in copies:
        copy.wait()


def exchange(x, axis, cid):
    n = lax.axis_size(axis)
    V = pl.BlockSpec(memory_space=pltpu.VMEM)
    return pl.pallas_call(
        functools.partial(exchange_kernel, axis, n),
        out_shape=jax.ShapeDtypeStruct((n,) + x.shape, x.dtype),
        in_specs=[V],
        out_specs=V,
        scratch_shapes=[
            pltpu.SemaphoreType.DMA((n - 1,)),
            pltpu.SemaphoreType.DMA((n - 1,)),
        ],
        compiler_params=pltpu.CompilerParams(collective_id=cid, has_side_effects=True),
        name="exchange_" + axis,
    )(x)


def row_sum(rows):
    x = jnp.concatenate(
        [jnp.stack(rows), jnp.zeros((8 - len(rows), rows[0].shape[0]), f32)], axis=0
    )
    return jnp.sum(exchange(x, "row", 1), axis=0)


def sinusoid(steps, width):
    half_width = width // 2
    frequency = jnp.exp(-math.log(10000.0) * jnp.arange(half_width, dtype=f32) / half_width)
    angles = steps.astype(f32)[:, None] * frequency[None, :]
    return jnp.concatenate([jnp.cos(angles), jnp.sin(angles)], axis=1)


def swish_slope(values):
    sig_v = jax.nn.sigmoid(values)
    return sig_v * (1.0 + values * (1.0 - sig_v))


def per_group(vec, members):
    n = vec.shape[-1]
    g = jnp.sum(vec.reshape(vec.shape[0], GROUPS, n // GROUPS), axis=2) / members
    return jnp.repeat(g, n // GROUPS, axis=1)


def norm_stats(values, members):
    sums = row_sum([jnp.sum(values, axis=0), jnp.sum(values * values, axis=0)])
    means = per_group(sums[:2], members)
    return (means[0], lax.rsqrt(means[1] - means[0] * means[0] + EPSILON))


def halo(x):
    devices = lax.axis_size("row")
    up = [(i, i + 1) for i in range(devices - 1)]
    down = [(i + 1, i) for i in range(devices - 1)]
    before = lax.ppermute(x[-1:], "row", up)
    after = lax.ppermute(x[:1], "row", down)
    return jnp.concatenate([before, x, after], axis=0)


def conv(padded, kernel):
    x = jnp.pad(padded, ((0, 0), (1, 1), (0, 0)))[None]
    return lax.conv_general_dilated(
        x,
        kernel,
        (1, 1),
        "VALID",
        dimension_numbers=("NHWC", "HWIO", "NHWC"),
        preferred_element_type=f32,
    )[0]


def flip_kernel(kernel):
    return jnp.flip(kernel, (0, 1)).transpose(0, 1, 3, 2)


def tn(left, right):
    return lax.dot_general(left, right, (((0,), (0,)), ((), ())), preferred_element_type=f32)


def split_cols(x, n):
    rows, cols = x.shape
    return x.reshape(rows, n, cols // n).transpose(1, 0, 2)


def kernel_grad(acts, grad_padded, tall):
    n = lax.axis_size("img")
    rows, wide, ch = grad_padded.shape
    part = ch // n
    g = lax.all_to_all(
        split_cols(grad_padded.reshape(rows * wide, ch), n),
        "img",
        split_axis=0,
        concat_axis=0,
        tiled=True,
    ).reshape(n, rows, wide, part)
    g = jnp.pad(g, ((0, 0), (0, 0), (1, 1), (0, 0)))
    lines = []
    for ky in range(3):
        for kx in range(3):
            lines.append(
                g[:, 2 - ky : 2 - ky + tall, 2 - kx : 2 - kx + wide].reshape(-1, part)
            )
    return tn(acts, jnp.concatenate(lines, axis=1))


def local(
    images,
    timesteps,
    clip_embed,
    context,
    out_cotangent,
    item_weight,
    first_gain,
    first_bias,
    first_kernel,
    first_offset,
    embed_weight,
    embed_bias,
    second_gain,
    second_bias,
    second_kernel,
    second_offset,
    third_gain,
    third_bias,
    project_in,
    context_weight,
    project_out,
    output_bias,
):
    _, tall, wide, ch = images.shape
    pixels = tall * wide
    hd = ch // HEADS
    nrow = lax.axis_size("row")
    nimg = lax.axis_size("img")
    me_row = lax.axis_index("row")
    gq = nrow // HEADS
    head = me_row // gq
    text = context.shape[2]
    nctx = context.shape[1]
    members = float(nrow * pixels * (ch // GROUPS))

    def gather_img(x):
        return lax.all_gather(x, "img", axis=0, tiled=True)

    grad_out = out_cotangent.reshape(pixels, ch).astype(f32) * (item_weight.astype(f32) * 0.25)
    grad_low = grad_out.astype(bf16)
    attended_grad = (
        lax.dot_general(project_out, grad_low, (((1,), (1,)), ((), ())), preferred_element_type=f32)
        .astype(bf16)
        .reshape(HEADS, hd, pixels)
    )

    def queries_out(x):
        x = x.reshape(HEADS, hd, gq, pixels // gq).transpose(0, 2, 1, 3)
        x = x.reshape(nrow, hd, pixels // gq)
        return x

    def a2a(x):
        return lax.all_to_all(x, "row", split_axis=0, concat_axis=0, tiled=True)

    grad_heads = a2a(queries_out(attended_grad))

    image_f = images.reshape(pixels, ch).astype(f32)
    embedding = sinusoid(timesteps, clip_embed.shape[1]) + clip_embed.astype(f32)
    embed_act = jax.nn.silu(embedding).astype(bf16)
    scale_shift = (jnp.dot(embed_act, embed_weight, preferred_element_type=f32) + embed_bias)[0]
    scale1 = 1.0 + scale_shift[:ch]
    shift = scale_shift[ch:]
    pair_at = (head // 2) * (2 * hd)
    cw_k = lax.dynamic_slice_in_dim(context_weight, pair_at, 2 * hd, 1)
    cw_v = lax.dynamic_slice_in_dim(context_weight, ch + pair_at, 2 * hd, 1)
    cw = jnp.concatenate([cw_k, cw_v], axis=1)
    enc = lax.dot_general(
        cw, context[0], (((0,), (1,)), ((), ())), preferred_element_type=f32
    ).astype(bf16)
    enc = enc.reshape(2, 2, hd, nctx)
    enc = jnp.where(head % 2 == 0, enc[:, 0], enc[:, 1]).reshape(2 * hd, nctx)
    padc = -(-nctx // 16) * 16
    enc = jnp.pad(enc, ((0, 0), (0, padc - nctx)))

    mean1, rstd1 = norm_stats(image_f, members)
    normed1 = (image_f - mean1) * rstd1
    norm_one = normed1 * first_gain + first_bias
    act_one = jax.nn.silu(norm_one).astype(bf16)
    hidden = conv(halo(act_one.reshape(tall, wide, ch)), first_kernel).reshape(pixels, ch)
    hidden = hidden + first_offset
    acts_one = gather_img(act_one)
    mean2, rstd2 = norm_stats(hidden, members)
    normed2 = (hidden - mean2) * rstd2
    affine_two = normed2 * second_gain + second_bias
    norm_two = affine_two * scale1 + shift
    act_two = jax.nn.silu(norm_two).astype(bf16)
    acts_two = gather_img(act_two)
    middle = (
        image_f
        + conv(halo(act_two.reshape(tall, wide, ch)), second_kernel).reshape(pixels, ch)
        + second_offset
    )
    mean3, rstd3 = norm_stats(middle, members)
    normed3 = (middle - mean3) * rstd3
    act_three = (normed3 * third_gain + third_bias).astype(bf16)
    acts_three = gather_img(act_three)
    triple = (
        lax.dot_general(project_in, act_three, (((0,), (1,)), ((), ())), preferred_element_type=f32)
        .astype(bf16)
        .reshape(3, HEADS, hd, pixels)
    )
    if gq == 1:
        recv = a2a(triple.transpose(1, 0, 2, 3).reshape(nrow, 3 * hd, pixels))
        q_h, kv_h = recv[:, :hd], recv[:, hd:]
        grad_h = grad_heads
    else:
        pair = triple[1:].transpose(1, 0, 2, 3).reshape(HEADS, 1, 2 * hd, pixels)
        pair = jnp.broadcast_to(pair, (HEADS, gq, 2 * hd, pixels)).reshape(nrow, 2 * hd, pixels)
        q_h, kv_h = a2a(queries_out(triple[0])), a2a(pair)

        def regroup(x, rows):
            x = x.transpose(1, 0, 2).reshape(rows, -1, 512)
            return x.transpose(1, 0, 2)

        q_h, kv_h, grad_h = regroup(q_h, hd), regroup(kv_h, 2 * hd), regroup(grad_heads, hd)
    att_h, dq_h, dkv_h, dctx = attention(q_h, kv_h, enc, grad_h, nctx)
    if gq == 1:
        attended = a2a(att_h).reshape(ch, pixels)
        back = a2a(jnp.concatenate([dq_h, dkv_h], axis=1)).reshape(HEADS, 3, hd, pixels)
        back = back.transpose(1, 0, 2, 3).reshape(3 * ch, pixels)
    else:

        def ungroup(x, part):
            rows = x.shape[1]
            x = x.transpose(1, 0, 2).reshape(rows, nrow, part)
            return x.transpose(1, 0, 2)

        def from_queries(x):
            x = x.reshape(HEADS, gq, hd, pixels // gq).transpose(0, 2, 1, 3)
            return x.reshape(ch, pixels)

        attended = from_queries(a2a(ungroup(att_h, pixels // gq)))
        dq = from_queries(a2a(ungroup(dq_h, pixels // gq)))
        dkv = a2a(ungroup(dkv_h, pixels)).reshape(HEADS, gq, 2, hd, pixels)
        dkv = jnp.sum(dkv.astype(f32), axis=1).astype(bf16)
        dkv = dkv.transpose(1, 0, 2, 3).reshape(2 * ch, pixels)
        back = jnp.concatenate([dq, dkv], axis=0)
    branch = tn(attended, project_out)
    result_image = (middle + branch + output_bias).astype(bf16)

    part_text = text // nrow
    enc_all = lax.all_gather(dctx[:nctx].astype(bf16), ("img", "row"), axis=0)
    enc_all = enc_all.reshape(nimg, HEADS, gq, nctx, 2, hd)
    if gq > 1:
        enc_all = jnp.sum(enc_all.astype(f32), axis=2, keepdims=True).astype(bf16)
    enc_all = enc_all[:, :, 0].transpose(0, 2, 3, 1, 4).reshape(nimg * nctx, 2 * ch)
    ctx_rows = lax.dynamic_slice_in_dim(context[0], me_row * part_text, part_text, 1)
    ctx_rows = gather_img(ctx_rows)
    context_weight_grad = tn(ctx_rows, enc_all)

    triple_grad = back.T
    act_three_grad = lax.dot_general(
        triple_grad, project_in, (((1,), (1,)), ((), ())), preferred_element_type=f32
    )
    sums3 = row_sum(
        [
            jnp.sum(act_three_grad * normed3, axis=0),
            jnp.sum(act_three_grad, axis=0),
            jnp.sum(grad_out, axis=0),
        ]
    )

    def norm_back(u, normed, rstd, gain, gain_sum, bias_sum):
        means = per_group(jnp.stack([gain * bias_sum, gain * gain_sum]), members)
        return rstd * (u * gain - means[0] - normed * means[1])

    middle_grad = grad_out + norm_back(
        act_three_grad, normed3, rstd3, third_gain, sums3[0], sums3[1]
    )
    middle_low = halo(middle_grad.astype(bf16).reshape(tall, wide, ch))
    act_two_grad = conv(middle_low, flip_kernel(second_kernel)).reshape(pixels, ch)
    norm_two_grad = act_two_grad * swish_slope(norm_two)
    sums2 = row_sum(
        [
            jnp.sum(norm_two_grad * normed2, axis=0),
            jnp.sum(norm_two_grad, axis=0),
            jnp.sum(middle_grad, axis=0),
        ]
    )
    scale_grad = second_gain * sums2[0] + second_bias * sums2[1]
    shift_grad = sums2[1]
    gain2_sum, bias2_sum = scale1 * sums2[0], scale1 * sums2[1]
    hidden_grad = norm_back(
        norm_two_grad * scale1, normed2, rstd2, second_gain, gain2_sum, bias2_sum
    )
    hidden_low = halo(hidden_grad.astype(bf16).reshape(tall, wide, ch))
    act_one_grad = conv(hidden_low, flip_kernel(first_kernel)).reshape(pixels, ch)
    norm_one_grad = act_one_grad * swish_slope(norm_one)
    sums1 = row_sum(
        [
            jnp.sum(norm_one_grad * normed1, axis=0),
            jnp.sum(norm_one_grad, axis=0),
            jnp.sum(hidden_grad, axis=0),
        ]
    )
    image_grad = middle_grad + norm_back(
        norm_one_grad, normed1, rstd1, first_gain, sums1[0], sums1[1]
    )

    def swap_img(x):
        x = split_cols(x, nimg)
        x = lax.all_to_all(x, "img", split_axis=0, concat_axis=0, tiled=True)
        return x.reshape(-1, x.shape[2])

    kg2 = kernel_grad(acts_two, middle_low, tall)
    kg1 = kernel_grad(acts_one, hidden_low, tall)
    pin = tn(acts_three, swap_img(triple_grad))
    pout = tn(gather_img(attended.T), swap_img(grad_low))

    def finish(x):
        x = lax.psum_scatter(x.astype(bf16), "row", scatter_dimension=0, tiled=True)
        return lax.all_gather(x, "img", axis=0).astype(f32)

    c2 = finish(kg2)
    c1 = finish(kg1)
    c3 = finish(jnp.concatenate([pin, pout], axis=1))
    part = ch // nrow
    cols = ch // nimg

    def conv_out(x):
        return x.reshape(nimg, part, 3, 3, cols).transpose(2, 3, 1, 0, 4).reshape(3, 3, part, ch)

    wide_in = 3 * ch // nimg
    pin_out = c3[:, :, :wide_in].transpose(1, 0, 2).reshape(part, 3 * ch)
    pout_out = c3[:, :, wide_in:].transpose(1, 0, 2).reshape(part, ch)

    rows = jnp.stack(
        [
            sums1[0],
            sums1[1],
            sums1[2],
            gain2_sum,
            bias2_sum,
            sums2[2],
            sums3[0],
            sums3[1],
            sums3[2],
            scale_grad,
            shift_grad,
        ]
        + [jnp.zeros((ch,), f32)] * 5
    )
    every = exchange(rows, "img", 2)
    acts_embed = gather_img(embed_act)
    part_emb = embed_act.shape[1] // nrow
    acts_embed = lax.dynamic_slice_in_dim(acts_embed, me_row * part_emb, part_emb, 1).astype(f32)
    shift_scale = every[:, 9:11].reshape(nimg, 2 * ch)
    embed_weight_grad = jnp.sum(acts_embed[:, :, None] * shift_scale[:, None, :], axis=0)
    part_bias = 2 * ch // nrow
    embed_bias_grad = lax.dynamic_slice_in_dim(
        jnp.sum(shift_scale, axis=0), me_row * part_bias, part_bias, 0
    )
    vecs = lax.dynamic_slice_in_dim(jnp.sum(every[:, :9], axis=0), me_row * part, part, 1)
    return (
        result_image.reshape(images.shape),
        image_grad.reshape(images.shape),
        vecs[0],
        vecs[1],
        conv_out(c1),
        vecs[2],
        embed_weight_grad,
        embed_bias_grad,
        vecs[3],
        vecs[4],
        conv_out(c2),
        vecs[5],
        vecs[6],
        vecs[7],
        pin_out,
        context_weight_grad,
        pout_out,
        vecs[8],
    )


def nt_dot(a, b):
    return lax.dot_general(a, b, (((1,), (1,)), ((), ())), preferred_element_type=f32)


def group_total(x):
    per = x.shape[1] // GROUPS
    lane = lax.broadcasted_iota(jnp.int32, x.shape, 1)
    n = x.shape[1]
    step = 1
    while step < per:
        upper = (lane // step) % 2 == 1
        x = x + jnp.where(upper, pltpu.roll(x, step, 1), pltpu.roll(x, n - step, 1))
        step *= 2
    return x


def total(v):
    return jnp.sum(v, axis=0, keepdims=True)


def put_shifts(buf, at, v, wide):
    n, ch = v.shape
    col = lax.rem(lax.broadcasted_iota(jnp.int32, (n, 1), 0), wide)
    buf[pl.ds(at, n), pl.ds(ch, ch)] = v.astype(bf16)
    left = jnp.where(col == 0, 0.0, pltpu.roll(v, 1, 0))
    buf[pl.ds(at, n), pl.ds(0, ch)] = left.astype(bf16)
    right = jnp.where(col == wide - 1, 0.0, pltpu.roll(v, n - 1, 0))
    buf[pl.ds(at, n), pl.ds(2 * ch, ch)] = right.astype(bf16)


class Links:
    def __init__(self, nrow, nimg):
        self.nrow, self.nimg = nrow, nimg
        self.row, self.img = lax.axis_index("row"), lax.axis_index("img")

    def peer(self, axis, k):
        if axis == "row":
            return lax.rem(self.row + k, self.nrow)
        return lax.rem(self.img + k, self.nimg)

    def greet(self):
        barrier = pltpu.get_barrier_semaphore()
        for axis, n in (("row", self.nrow), ("img", self.nimg)):
            for k in range(1, n):
                pl.semaphore_signal(
                    barrier, inc=1, device_id={axis: self.peer(axis, k)}, device_id_type=MESH
                )

    def greeted(self):
        pl.semaphore_wait(pltpu.get_barrier_semaphore(), self.nrow + self.nimg - 2)

    def to(self, axis, at, src, dst, send, recv):
        return pltpu.make_async_remote_copy(
            src_ref=src,
            dst_ref=dst,
            send_sem=send,
            recv_sem=recv,
            device_id={axis: at},
            device_id_type=MESH,
        )

    def copy(self, axis, k, src, dst, send, recv):
        return self.to(axis, self.peer(axis, k), src, dst, send, recv)


class Stats:
    def __init__(self, links, src, dst, send, recv):
        self.links, self.src, self.dst, self.send, self.recv = links, src, dst, send, recv

    def start(self, stage, rows):
        links = self.links
        ch = rows[0].shape[1]
        blocks = [r[:, i * 128 : (i + 1) * 128] for r in rows for i in range(ch // 128)]
        height = self.src.shape[1]
        blocks = blocks + [jnp.zeros((1, 128), f32)] * (height - len(blocks))
        packed = jnp.concatenate(blocks, axis=0)
        self.src[stage] = packed
        self.dst[stage, links.row] = packed
        self.rows, self.per = len(rows), ch // 128
        self.copies = []
        for k in range(1, links.nrow):
            c = links.copy(
                "row",
                k,
                self.src.at[stage],
                self.dst.at[stage, links.row],
                self.send.at[stage, k - 1],
                self.recv.at[stage, k - 1],
            )
            c.start()
            self.copies.append(c)

    def finish(self, stage):
        for c in self.copies:
            c.wait()
        s = jnp.sum(self.dst[stage], axis=0)
        per = self.per
        rows = [
            jnp.concatenate([s[r * per + i : r * per + i + 1] for i in range(per)], axis=1)
            for r in range(self.rows)
        ]
        return jnp.concatenate(rows + [jnp.zeros((8 - self.rows, per * 128), f32)], axis=0)


class Halo:
    def __init__(self, links, send, recv):
        self.links, self.send, self.recv = links, send, recv

    def copies(self, slot, first, last, land):
        links = self.links
        down = links.copy(
            "row", links.nrow - 1, first, land.at[1],
            self.send.at[slot, 0], self.recv.at[slot, 1],
        )
        up = links.copy(
            "row", 1, last, land.at[0],
            self.send.at[slot, 1], self.recv.at[slot, 0],
        )
        return down, up

    def start(self, slot, first, last, land):
        links = self.links
        down, up = self.copies(slot, first, last, land)

        @pl.when(links.row > 0)
        def _():
            down.start()

        @pl.when(links.row < links.nrow - 1)
        def _():
            up.start()

        @pl.when(links.row == 0)
        def _():
            land[0] = jnp.zeros(land.shape[1:], land.dtype)

        @pl.when(links.row == links.nrow - 1)
        def _():
            land[1] = jnp.zeros(land.shape[1:], land.dtype)

        return down, up

    def finish(self, pair):
        links = self.links
        down, up = pair

        @pl.when(links.row > 0)
        def _():
            down.wait_send()
            up.wait_recv()

        @pl.when(links.row < links.nrow - 1)
        def _():
            up.wait_send()
            down.wait_recv()


def put_block(links, buf, mid, before, after, wide):
    put_shifts(buf, wide, mid, wide)
    put_shifts(buf, 0, jnp.where(links.row > 0, before, 0.0), wide)
    put_shifts(buf, buf.shape[0] - wide, jnp.where(links.row < links.nrow - 1, after, 0.0), wide)


def front_kernel(
    cfg,
    *refs,
):
    nvec = cfg[-1]
    _front(cfg[:-1], *refs[:6], refs[6 : 6 + nvec], *refs[6 + nvec :])


def _front(
    cfg,
    r_img,
    r_oc,
    r_pout,
    r_cxt,
    r_embv,
    r_weight,
    r_vecs,
    r_w1h,
    r_w2h,
    r_winh,
    r_cwh,
    r_ewh,
    r_par,
    r_stats,
    r_ss,
    r_hiddenh,
    r_middleh,
    r_wth,
    r_a3h,
    r_hoch,
    r_hhidh,
    r_hmidh,
    r_a1h,
    r_a2h,
    r_ctxh,
    r_embh,
    r_tgh,
    r_atth,
    r_ench,
    r_hidden,
    r_middle,
    r_wt,
    r_a3,
    r_hoc,
    r_hhid,
    r_hmid,
    r_emb,
    r_himg,
    r_gx,
    r_dqa,
    r_cw,
    r_ctx,
    r_buf,
    r_at,
    r_gs,
    r_ts,
    r_qkv,
    r_g,
    r_kx,
    r_vx,
    r_kt,
    r_vt,
    r_sb,
    r_pb,
    r_acc,
    r_atb,
    r_dqb,
    r_dcb,
    r_st_src,
    r_st_dst,
    r_wsem,
    r_vsem,
    r_st_send,
    r_st_recv,
    r_h_send,
    r_h_recv,
    r_i_send,
    r_i_recv,
    r_r_send,
    r_r_recv,
    r_osem,
    r_bsem,
):
    nrow, nimg, wide, ch, hd, kc, joint = cfg
    px = r_img.shape[0]
    members = float(nrow * px * (ch // GROUPS))
    links = Links(nrow, nimg)
    links.greet()
    head = links.row
    me = links.row

    def pair_at(at):
        return pl.ds(pl.multiple_of(at + (head // 2) * (2 * hd), 128), 2 * hd)

    deep = 3 * ch
    at_ew, at_win, at_w1 = 0, 2 * r_embv.shape[1], 2 * r_embv.shape[1] + deep
    at_w2 = at_w1 + 3 * deep
    text_in = r_embv.shape[1]
    groups = (
        [(r_w1h.at[k], at_w1 + k * deep, deep) for k in range(3)],
        [(r_ewh.at[:, k * ch : (k + 1) * ch], at_ew + k * text_in, text_in) for k in range(2)],
        [(r_winh.at[:, k * ch : (k + 1) * ch], at_win + k * ch, ch) for k in range(3)],
        [(r_w2h.at[k], at_w2 + k * deep, deep) for k in range(3)],
    )
    count = 0
    loads = []
    for group in groups:
        loads.append([])
        for src, at, n in group:
            c = pltpu.make_async_copy(src, r_pb.at[pl.ds(at, n)], r_wsem.at[count])
            c.start()
            loads[-1].append(c)
            count += 1
    loads.append([])
    for src, dst in (
        (r_cwh.at[:, pair_at(0)], r_cw.at[:, : 2 * hd]),
        (r_cwh.at[:, pair_at(ch)], r_cw.at[:, 2 * hd :]),
    ):
        c = pltpu.make_async_copy(src, dst, r_wsem.at[count])
        c.start()
        loads[-1].append(c)
        count += 1
    load_w1, load_ew, load_win, load_w2, load_cw = loads

    def ready(copies):
        for c in copies:
            c.wait()

    places = (0, 1, 2, 3, 4, 7, 8, 9, 11, 12, 13)
    flat = [v for v in r_vecs[:-1]] + [r_vecs[-1].at[:, :ch], r_vecs[-1].at[:, ch:]]
    vec_loads = [
        pltpu.make_async_copy(v, r_par.at[pl.ds(at, 1)], r_vsem.at[i])
        for i, (v, at) in enumerate(zip(flat, places))
    ]
    for c in vec_loads:
        c.start()
    weight = r_weight[0].astype(f32) * 0.25
    for at in (5, 6, 14, 15):
        r_par[at : at + 1, :] = jnp.zeros((1, ch), f32)
    r_par[10:11, :] = jnp.full((1, ch), 1.0, f32) * weight
    stats = Stats(links, r_st_src, r_st_dst, r_st_send, r_st_recv)
    halo = Halo(links, r_h_send, r_h_recv)
    ends = (pl.ds(0, wide), pl.ds(px - wide, wide))

    def edges(slot, block, land):
        return halo.start(slot, block.at[ends[0]], block.at[ends[1]], land)

    pending = []

    def par(i):
        return r_par[i : i + 1, :]

    def share(slot, src, dst):
        copies = [pltpu.make_async_copy(src(links.img), dst(links.img), r_osem.at[slot])]
        for k in range(1, nimg):
            copies.append(
                links.copy(
                    "img", k, src(links.peer("img", k)), dst(links.img),
                    r_i_send.at[slot, k - 1], r_i_recv.at[slot, k - 1],
                )
            )
        for c in copies:
            c.start()
        pending.extend(copies)

    def scatter(slot, src, dst):
        copies = []
        for k in range(1, nrow):
            copies.append(
                links.copy(
                    "row", k, src(links.peer("row", k)), dst(me),
                    r_r_send.at[slot, k - 1], r_r_recv.at[slot, k - 1],
                )
            )
        for c in copies:
            c.start()
        return copies

    def lanes(img):
        return pl.ds(pl.multiple_of(img * px, 128), px)

    def moments(v):
        return [total(v), total(v * v)]

    def center(stage, sums):
        means = group_total(sums) * (1.0 / members)
        mean = means[0:1]
        rstd = lax.rsqrt(means[1:2] - mean * mean + EPSILON)
        r_stats[2 * stage : 2 * stage + 1, :] = mean
        r_stats[2 * stage + 1 : 2 * stage + 2, :] = rstd
        return mean, rstd

    r_stats[...] = jnp.zeros_like(r_stats)
    rows = moments(r_img[...].astype(f32))
    low = (r_oc[...].astype(f32) * weight).astype(bf16)
    r_gs[...] = nt_dot(r_pout[...], low).astype(bf16).reshape(r_gs.shape)
    r_emb[...] = jnp.broadcast_to(r_embv[...].astype(bf16).astype(f32), r_emb.shape)
    links.greeted()
    stats.start(0, rows)
    c_img = edges(0, r_img, r_himg)
    c_g = scatter(2, lambda r: r_gs.at[r], lambda r: r_g.at[r])
    for c in vec_loads:
        c.wait()
    ready(load_ew)
    emb = r_emb[...].astype(bf16)
    scale1 = 1.0 + (nn(emb, r_pb[at_ew : at_ew + text_in])[0:1] + par(12))
    shift = nn(emb, r_pb[at_ew + text_in : at_ew + 2 * text_in])[0:1] + par(13)
    r_ss[...] = jnp.concatenate([scale1, shift, jnp.zeros((6, ch), f32)], axis=0)
    mean, rstd = center(0, stats.finish(0))

    def conv_stage(stage, act, before, after, weights):
        buf = r_buf
        put_block(links, buf, act, before, after, wide)
        acc = None
        for ky in range(3):
            d = nn(
                buf[pl.ds(ky * wide, px), :],
                r_pb[weights + ky * deep : weights + (ky + 1) * deep, :],
            )
            acc = d if acc is None else acc + d
        r_at[stage] = act.astype(bf16).T
        return acc


    def act_one(v):
        return jax.nn.silu((v.astype(f32) - mean) * rstd * par(0) + par(1))

    halo.finish(c_img)
    ready(load_w1)
    hidden = conv_stage(
        0, act_one(r_img[...]), act_one(r_himg[0]), act_one(r_himg[1]), at_w1
    ) + par(2)
    r_hidden[...] = hidden
    stats.start(1, moments(hidden))
    c_hid = edges(1, r_hidden, r_hhid)
    ready(load_win)
    for j in range(3):
        turned = r_pb[at_win + j * ch : at_win + (j + 1) * ch, :].T
        for h in range(HEADS):
            r_wt[(3 * h + j) * hd : (3 * h + j + 1) * hd, :] = turned[h * hd : (h + 1) * hd]
    mean_two, rstd_two = center(1, stats.finish(1))

    def act_two(v):
        affine = (v - mean_two) * rstd_two * par(3) + par(4)
        return jax.nn.silu(affine * r_ss[0:1] + r_ss[1:2])

    halo.finish(c_hid)
    ready(load_w2)
    middle = conv_stage(1, act_two(r_hidden[...]), act_two(r_hhid[0]), act_two(r_hhid[1]), at_w2)
    middle = r_img[...].astype(f32) + middle + par(7)
    r_middle[...] = middle
    stats.start(2, moments(middle))
    c_mid = edges(2, r_middle, r_hmid)
    c_oc = edges(3, r_oc, r_hoc)
    nctx, text = r_cxt.shape
    padc = r_ctx.shape[0]
    r_ctx[...] = jnp.concatenate(
        [r_cxt[...], jnp.zeros((padc - nctx, text), bf16)], axis=0
    )
    ready(load_cw)
    enc = nn(r_ctx[...], r_cw[...]).T.astype(bf16)
    first = lax.rem(head, 2) == 0
    enc = jnp.concatenate(
        [
            jnp.where(first, enc[2 * j * hd : (2 * j + 1) * hd], enc[(2 * j + 1) * hd : (2 * j + 2) * hd])
            for j in range(2)
        ],
        axis=0,
    )
    mean, rstd = center(2, stats.finish(2))
    act3 = ((r_middle[...] - mean) * rstd * par(8) + par(9)).astype(bf16)
    r_a3[...] = act3.T
    ts, qkv, gs, g = r_ts, r_qkv, r_gs, r_g
    tall = nrow // 2
    row_z, row_x = me // 2, lax.rem(me, 2)

    def source(i):
        z = lax.rem(row_z + lax.rem((i + 1) // 2, tall), tall)
        return 2 * z + lax.rem(row_x + i + 1, 2)

    def target(i):
        z = lax.rem(row_z + tall - lax.rem((i + 1) // 2, tall), tall)
        return 2 * z + lax.rem(row_x + i + 1, 2)

    def q_copy(i):
        to = target(i)
        return links.to(
            "row", to, ts.at[to, pl.ds(0, hd)], qkv.at[me, pl.ds(0, hd)],
            r_r_send.at[1, i], r_r_recv.at[1, i],
        )

    def kv_copy(k):
        to = lax.rem(me + k, nrow)
        return links.to(
            "row", to, ts.at[to, pl.ds(hd, 2 * hd)], qkv.at[me, pl.ds(hd, 2 * hd)],
            r_r_send.at[0, k - 1], r_r_recv.at[0, k - 1],
        )

    for dz in (2, 1, 3, 0):
        pair = 2 * lax.rem(row_z + dz, tall)
        here = pl.ds(pl.multiple_of(pair * (3 * hd), 16), 6 * hd)
        made = nn(r_wt[here, :], r_a3[...]).astype(bf16)
        ts[pl.ds(pair, 2)] = made.reshape(2, 3 * hd, px)
        if dz:
            for h in range(2):
                kv_copy(lax.rem(pair + h - me + nrow, nrow)).start()
        else:
            kv_copy(lax.rem(pair + 1 - row_x - me + nrow, nrow)).start()
    q_copy(0).start()
    npix = nrow * px
    ones_rows = jnp.where(lax.broadcasted_iota(jnp.int32, (hd, px), 0) < 2, 1.0, 0.0).astype(bf16)
    kx, vx, kt, vt, sb, pb, acc = (r_kx, r_vx, r_kt, r_vt, r_sb, r_pb, r_acc)

    def fill(pair, at, w):
        k = pair[:hd].astype(f32) * (LOG2E * 0.125)
        hi = k.astype(bf16)
        lo = (k - hi.astype(f32)).astype(bf16)
        kx[pl.ds(at, w), :] = jnp.concatenate([hi, lo], axis=0).T
        vfull = jnp.concatenate([pair[hd:], ones_rows[:, :w]], axis=0)
        vx[pl.ds(at, w), :] = vfull.T
        kt[:, pl.ds(at, w)] = pair[:hd]
        vt[:, pl.ds(at, w)] = vfull[: hd + 16]

    fill(enc, npix, padc)
    qkv[me] = ts[me]
    g[me] = gs[me]
    acc[...] = jnp.zeros_like(acc)

    def own(r):
        return pl.multiple_of(r * px, 128)

    fill(ts[me, hd:], own(me), px)
    for k in range(1, nrow):
        kv_copy(k).wait()
        frm = lax.rem(me + nrow - k, nrow)
        fill(qkv[frm, hd:], own(frm), px)


    q_copy(1).start()
    for i in range(2):
        share(i, lambda p, i=i: r_at.at[i], lambda p, i=i: (r_a1h, r_a2h)[i].at[:, lanes(p)])
    mine = text // nrow
    text_at = pl.ds(pl.multiple_of(me * mine, 128), mine)
    share(2, lambda p: r_ctx.at[:, text_at], lambda p: r_ctxh.at[p])
    wide_emb = r_emb.shape[1] // nrow
    emb_at = pl.ds(pl.multiple_of(me * wide_emb, 128), wide_emb)
    share(3, lambda p: r_emb.at[:, emb_at], lambda p: r_embh.at[p])
    halo.finish(c_mid)
    halo.finish(c_oc)
    kept = (
        (r_hidden, r_hiddenh),
        (r_middle, r_middleh),
        (r_wt, r_wth),
        (r_a3, r_a3h),
        (r_hoc, r_hoch),
        (r_hhid, r_hhidh),
        (r_hmid, r_hmidh),
    )
    for i, (a, b) in enumerate(kept):
        c = pltpu.make_async_copy(a, b, r_bsem.at[i])
        c.start()
        pending.append(c)

    bq = px
    nfull = npix // kc

    def att_copy(i):
        to = source(i)
        return links.to(
            "row", to, r_atb.at[to], r_atth.at[me], r_r_send.at[3, i], r_r_recv.at[3, i]
        )

    def dq_copy(i):
        to = source(i)
        return links.to(
            "row", to, r_dqb.at[to, pl.ds(0, hd)], r_tgh.at[me, pl.ds(0, hd)],
            r_r_send.at[4, i], r_r_recv.at[4, i],
        )

    nk = npix + padc

    def scores(i, slot):
        s = source(i)
        base = pl.multiple_of(slot * nk, 16)

        @pl.when(i + 2 < nrow - 1)
        def _():
            q_copy(i + 2).start()

        @pl.when(i < nrow - 1)
        def _():
            q_copy(i).wait_recv()
            k = lax.rem(me - s + nrow, nrow) - 1
            links.to("row", s, gs.at[s], g.at[s], r_r_send.at[2, k], r_r_recv.at[2, k]).wait_recv()

        qt = qkv[s, :hd]
        gt = g[s]
        q2 = jnp.concatenate([qt, qt], axis=0)
        sc = nn(kx[pl.ds(npix, padc), :], q2)
        sc = jnp.where(lax.broadcasted_iota(jnp.int32, (padc, bq), 0) < nctx, sc, -jnp.inf)
        sb[pl.ds(npix, padc), :] = sc
        m8 = jnp.max(sc.reshape(padc // 8, 8, bq), axis=0)

        def phase_a(c, m8):
            at = pl.multiple_of(c * kc, kc)
            sv = nn(kx[pl.ds(at, kc), :], q2)
            sb[pl.ds(at, kc), :] = sv
            return jnp.maximum(m8, jnp.max(sv.reshape(kc // 8, 8, bq), axis=0))

        m8 = lax.fori_loop(0, nfull, phase_a, m8, unroll=True)
        m = jnp.max(m8, axis=0, keepdims=True)
        pc = jnp.exp2(sb[pl.ds(npix, padc), :] - m).astype(bf16)
        pb[pl.ds(base + npix, padc), :] = pc
        o = nn(vt[:, npix : npix + padc], pc)

        def phase_b(c, o):
            at = pl.multiple_of(c * kc, kc)
            p = jnp.exp2(sb[pl.ds(at, kc), :] - m).astype(bf16)
            pb[pl.ds(pl.multiple_of(base + at, 16), kc), :] = p
            return o + nn(vt[:, pl.ds(at, kc)], p)

        o = lax.fori_loop(0, nfull, phase_b, o, unroll=True)
        inv = 1.0 / o[hd : hd + 1]
        att = o[:hd] * inv
        r_atb[s] = att.astype(bf16)

        @pl.when(i < nrow - 1)
        def _():
            att_copy(i).start()

        gf = gt.astype(f32)
        delta = total(gf * att) * inv
        gl = (gf * inv).astype(bf16)
        dhi = (-delta).astype(bf16)
        dlo = (-delta - dhi.astype(f32)).astype(bf16)
        r_gx[slot] = jnp.concatenate([gl, dhi, dlo, jnp.zeros((hd - 2, bq), bf16)], axis=0)
        r_dqa[slot] = piece(slot, qt, npix, padc, jnp.zeros((hd, bq), f32))

    def piece(slot, qt, at, w, dq):
        gx = r_gx[slot]
        p = pb[pl.ds(pl.multiple_of(slot * nk + at, 16), w), :]
        dp = nn(vx[pl.ds(at, w), :], gx)
        ds = (p.astype(f32) * dp).astype(bf16)
        acc[:hd, pl.ds(at, w)] += nt_dot(qt, ds)
        acc[hd:, pl.ds(at, w)] += nt_dot(gx[:hd], p)
        return dq + nn(kt[:, pl.ds(at, w)], ds)

    def block(i, _):
        s = source(i)
        scores(i, 0)
        qt = qkv[s, :hd]

        def phase_d(c, dq):
            return piece(0, qt, pl.multiple_of(c * kc, kc), kc, dq)

        dq = lax.fori_loop(0, nfull, phase_d, r_dqa[0], unroll=True)
        r_dqb[s, :hd] = (dq * 0.125).astype(bf16)
        dq_copy(i).start()
        return 0

    alone = nrow - joint
    lax.fori_loop(0, alone, block, 0)
    scale = jnp.where(lax.broadcasted_iota(jnp.int32, (2 * hd, 1), 0) < hd, 0.125, 1.0)

    def first(j, _):
        scores(alone + j, j)
        return 0

    lax.fori_loop(0, joint, first, 0)

    def key_home(c):
        z = lax.rem(row_z + 1 + c // 2, tall)
        return 2 * z + lax.rem(row_x + c + 1, 2)

    def kv_back(c):
        s = key_home(c)
        return links.to(
            "row", s, r_dqb.at[s, pl.ds(hd, 2 * hd)], r_tgh.at[me, pl.ds(hd, 2 * hd)],
            r_r_send.at[5, c], r_r_recv.at[5, c],
        )

    def keys_done(c, _):
        z = lax.rem(row_z + 1 + c, tall)
        at = pl.multiple_of(z * (2 * px), 128)
        for j in range(joint):
            qt = qkv[source(alone + j), :hd]
            r_dqa[j] = piece(j, qt, at, 2 * px, r_dqa[j])
        for h in range(2):
            s = key_home(2 * c + h)
            r_dqb[s, hd:] = (acc[:, pl.ds(own(s), px)] * scale).astype(bf16)

            @pl.when(2 * c + h < nrow - 1)
            def _():
                kv_back(2 * c + h).start()

        return 0

    lax.fori_loop(0, tall, keys_done, 0, unroll=True)
    copies = []
    for j in range(joint):
        r_dqb[source(alone + j), :hd] = (r_dqa[j] * 0.125).astype(bf16)
        if alone + j < nrow - 1:
            dq_copy(alone + j).start()
    r_dcb[...] = (acc[:, npix : npix + padc] * scale).astype(bf16).T
    copies += scatter(6, lambda r: r_dcb, lambda r: r_ench.at[r])
    for i, (a, b) in enumerate(
        (
            (r_dqb.at[me], r_tgh.at[me]),
            (r_atb.at[me], r_atth.at[me]),
            (r_dcb, r_ench.at[me]),
        )
    ):
        c = pltpu.make_async_copy(a, b, r_osem.at[4 + i])
        c.start()
        copies.append(c)
    for i in range(nrow - 1):
        q_copy(i).wait_send()
    for c in c_g:
        c.wait_send()
    for i in range(nrow - 1):
        att_copy(i).wait()
        dq_copy(i).wait()
        kv_back(i).wait()
    for c in copies + pending:
        c.wait()


def front(
    images, out_cot, project_out, context, emb, weight, vectors, w1, w2, win, cw, ew, nrow, nimg, wide
):
    px, ch = images.shape
    hd = ch // HEADS
    padc = -(-context.shape[0] // 16) * 16
    cfg = (nrow, nimg, wide, ch, hd, 1024, 3, len(vectors))
    nk = nrow * px + padc
    joint = cfg[6]
    V = pl.BlockSpec(memory_space=pltpu.VMEM)
    A = pl.BlockSpec(memory_space=pl.ANY)
    S = jax.ShapeDtypeStruct
    M = pltpu.VMEM
    dma = pltpu.SemaphoreType.DMA
    return pl.pallas_call(
        functools.partial(front_kernel, cfg),
        out_shape=(
            S((16, ch), f32),
            S((8, ch), f32),
            S((8, ch), f32),
            S((px, ch), f32),
            S((px, ch), f32),
            S((3 * ch, ch), bf16),
            S((ch, px), bf16),
            S((2, wide, ch), bf16),
            S((2, wide, ch), f32),
            S((2, wide, ch), f32),
            S((ch, nimg * px), bf16),
            S((ch, nimg * px), bf16),
            S((nimg, padc, context.shape[1] // nrow), bf16),
            S((nimg, 8, emb.shape[1] // nrow), f32),
            S((nrow, 3 * hd, px), bf16),
            S((nrow, hd, px), bf16),
            S((nrow, padc, 2 * hd), bf16),
        ),
        in_specs=[V] * 5
        + [pl.BlockSpec(memory_space=pltpu.SMEM)]
        + [A] * (len(vectors) + 5),
        out_specs=(V,) * 3 + (A,) * 14,
        scratch_shapes=[
            M((px, ch), f32),
            M((px, ch), f32),
            M((3 * ch, ch), bf16),
            M((ch, px), bf16),
            M((2, wide, ch), bf16),
            M((2, wide, ch), f32),
            M((2, wide, ch), f32),
            M((8, emb.shape[1]), f32),
            M((2, wide, ch), bf16),
            M((joint, 2 * hd, px), bf16),
            M((joint, hd, px), f32),
            M((cw.shape[0], 4 * hd), bf16),
            M((padc, cw.shape[0]), bf16),
            M((px + 2 * wide, 3 * ch), bf16),
            M((2, ch, px), bf16),
            M((nrow, hd, px), bf16),
            M((nrow, 3 * hd, px), bf16),
            M((nrow, 3 * hd, px), bf16),
            M((nrow, hd, px), bf16),
            M((nk, 2 * hd), bf16),
            M((nk, 2 * hd), bf16),
            M((hd, nk), bf16),
            M((hd + 16, nk), bf16),
            M((nk, px), f32),
            M((max(joint * nk, 2 * emb.shape[1] + 21 * ch), px), bf16),
            M((2 * hd, nk), f32),
            M((nrow, hd, px), bf16),
            M((nrow, 3 * hd, px), bf16),
            M((padc, 2 * hd), bf16),
            M((3, 8, 128), f32),
            M((3, nrow, 8, 128), f32),
            dma((13,)),
            dma((11,)),
            dma((3, nrow - 1)),
            dma((3, nrow - 1)),
            dma((4, 2)),
            dma((4, 2)),
            dma((4, nimg - 1)),
            dma((4, nimg - 1)),
            dma((7, nrow - 1)),
            dma((7, nrow - 1)),
            dma((8,)),
            dma((7,)),
        ],
        compiler_params=pltpu.CompilerParams(
            collective_id=3, has_side_effects=True, vmem_limit_bytes=62 * 2**20
        ),
        name="front",
    )(images, out_cot, project_out, context, emb, weight, *vectors, w1, w2, win, cw, ew)
def slope(values):
    sig = jax.nn.sigmoid(values)
    return sig * (1.0 + values * (1.0 - sig))


def back_kernel(
    cfg,
    r_imgh,
    r_och,
    r_par,
    r_ss,
    r_stats,
    r_hiddenh,
    r_middleh,
    r_hoch,
    r_hhidh,
    r_hmidh,
    r_a3h,
    r_tgh,
    r_atth,
    r_wth,
    r_w2h,
    r_w1h,
    r_a2h,
    r_a1h,
    r_ench,
    r_ctxh,
    r_igrad,
    r_kq,
    r_oq,
    r_cr,
    r_every,
    r_img,
    r_oc,
    r_hidden,
    r_middle,
    r_hoc,
    r_hhid,
    r_hmid,
    r_a3,
    r_tg,
    r_att,
    r_wt,
    r_w2,
    r_w1,
    r_a2,
    r_a1,
    r_enc,
    r_ctx,
    r_mg,
    r_ntg,
    r_buf,
    r_gq,
    r_gs,
    r_ks,
    r_kx,
    r_km,
    r_kz,
    r_kf,
    r_os,
    r_ox,
    r_oy,
    r_oz,
    r_of,
    r_encq,
    r_cq,
    r_vsrc,
    r_st_src,
    r_st_dst,
    r_hu,
    r_kacc,
    r_lsem,
    r_st_send,
    r_st_recv,
    r_h_send,
    r_h_recv,
    r_i_send,
    r_i_recv,
    r_r_send,
    r_r_recv,
    r_x_send,
    r_x_recv,
    r_z_send,
    r_z_recv,
    r_osem,
):
    nrow, nimg, wide, ch, hd, padc = cfg
    px = r_img.shape[0]
    part = ch // nimg
    rows = ch // nrow
    deep = nrow // 2
    members = float(nrow * px * (ch // GROUPS))
    links = Links(nrow, nimg)
    links.greet()
    pairs = (
        (r_tgh, r_tg),
        (r_wth, r_wt),
        (r_middleh, r_middle),
        (r_och, r_oc),
        (r_a3h, r_a3),
        (r_atth, r_att),
        (r_hiddenh, r_hidden),
        (r_imgh, r_img),
        (r_hmidh, r_hmid),
        (r_hoch, r_hoc),
        (r_hhidh, r_hhid),
        (r_w2h, r_w2),
        (r_a2h, r_a2),
        (r_w1h, r_w1),
        (r_a1h, r_a1),
        (r_ench, r_enc),
        (r_ctxh, r_ctx),
    )
    loads = [pltpu.make_async_copy(a, b, r_lsem.at[i]) for i, (a, b) in enumerate(pairs)]
    for c in loads:
        c.start()
    load_w2, load_a2, load_w1, load_a1, load_enc, load_ctx = loads[11:]
    stats = Stats(links, r_st_src, r_st_dst, r_st_send, r_st_recv)
    halo = Halo(links, r_h_send, r_h_recv)
    ends = (pl.ds(0, wide), pl.ds(px - wide, wide))

    def edges(slot, block, land):
        return halo.start(slot, block.at[ends[0]], block.at[ends[1]], land)

    others = (
        links.img + 1 - 2 * lax.rem(links.img, 2),
        lax.rem(links.img + 2, nimg),
        nimg - 1 - links.img,
    )
    row_z, row_x = links.row // 2, lax.rem(links.row, 2)
    img_y, img_c = links.img // 2, lax.rem(links.img, 2)

    def par(i):
        return r_par[i : i + 1, :]

    def stat(i):
        return r_stats[i : i + 1, :]

    scale1, shift = r_ss[0:1], r_ss[1:2]

    def share(slot, src, dst):
        copies = [pltpu.make_async_copy(src(links.img), dst(links.img), r_osem.at[slot])]
        for k, at in enumerate(others):
            copies.append(
                links.to(
                    "img", at, src(at), dst(links.img), r_i_send.at[slot, k], r_i_recv.at[slot, k]
                )
            )
        for c in copies:
            c.start()
        return copies

    def wait(copies):
        for c in copies:
            c.wait()

    def columns(at, img):
        return pl.ds(pl.multiple_of(at + img * part, 128), part)

    def row_x_start(slot, src, land):
        c = links.to(
            "row", links.row + 1 - 2 * row_x, src.at[:, 1 - row_x], land,
            r_x_send.at[slot], r_x_recv.at[slot],
        )
        c.start()
        return c

    def row_z_start(slot, c, src, land, mid, last):
        c.wait()
        mid[...] = (src[:, row_x].astype(f32) + land[...].astype(f32)).astype(bf16)
        copies = []
        for k in range(1, deep):
            z = lax.rem(row_z + k, deep)
            copies.append(
                links.to(
                    "row", 2 * z + row_x, mid.at[z], last.at[k - 1],
                    r_z_send.at[slot, k - 1], r_z_recv.at[slot, k - 1],
                )
            )
        for d in copies:
            d.start()
        return copies

    def row_end(copies, mid, last):
        wait(copies)
        s = mid[row_z].astype(f32)
        for k in range(1, deep):
            s = s + last[k - 1].astype(f32)
        return s.astype(bf16)

    def back_means(gain, gain_sum, bias_sum):
        both = jnp.concatenate([gain * bias_sum, gain * gain_sum, jnp.zeros((6, ch), f32)], axis=0)
        return group_total(both) * (1.0 / members)

    def norm_back(u, normed, rstd, gain, means):
        return rstd * (u * gain - means[0:1] - normed * means[1:2])

    def conv_back(stage, grad, before, after, weights):
        buf = r_buf.at[stage]
        put_block(links, buf, grad, before, after, wide)
        copies = share(
            stage, lambda i: buf.at[:, columns(ch, i)], lambda i: r_gq.at[stage, i]
        )
        acc = None
        for ky in range(3):
            for kx in range(3):
                g = buf[pl.ds(ky * wide, px), pl.ds(kx * ch, ch)]
                w = weights[2 - ky, pl.ds((2 - kx) * ch, ch), :]
                d = nt_dot(g, w)
                acc = d if acc is None else acc + d
        return acc, copies

    def kernel_part(stage, acts, ky, images):
        tot = None
        for b in images:
            at = pl.ds(pl.multiple_of(b * px, 128), px)
            d = nn(acts[:, at], r_gs[b, ky * wide : ky * wide + px, :])
            tot = d if tot is None else tot + d
        return tot

    def kernel_grads(stage, acts, copies):
        near, far = (links.img, others[0]), others[1:]
        for group, first in ((near, True), (far, False)):
            for b, c in zip(group, copies[:2] if first else copies[2:]):
                c.wait()
                put_shifts(r_gs.at[b], 0, r_gq[stage, b].astype(f32), wide)
            if first:
                for ky in range(3):
                    r_kacc[ky] = kernel_part(stage, acts, ky, near)
        sent = []
        for ky in range(3):
            tot = r_kacc[ky] + kernel_part(stage, acts, ky, far)
            r_ks[stage, ky] = tot.astype(bf16).reshape(deep, 2, rows, 3 * part)
            sent.append(row_x_start(3 * stage + ky, r_ks.at[stage, ky], r_kx.at[stage, ky]))
        return sent

    def kernel_mid(stage, sent, ky):
        return row_z_start(
            3 * stage + ky, sent[ky], r_ks.at[stage, ky], r_kx.at[stage, ky],
            r_km.at[stage, ky], r_kz.at[stage, ky],
        )

    def kernel_end(stage, copies):
        out = []
        for ky in range(3):
            r_kf[stage, ky] = row_end(copies[ky], r_km.at[stage, ky], r_kz.at[stage, ky])
            out += share(
                2 + 3 * stage + ky,
                lambda i, ky=ky: r_kf.at[stage, ky],
                lambda i, ky=ky: r_kq.at[stage, ky, i],
            )
        return out

    for c in loads[:11]:
        c.wait()
    tgt = r_tg[...].reshape(3 * ch, px)
    u3 = nn(tgt.T, r_wt[...])
    normed3 = (r_middle[...] - stat(4)) * stat(5)
    grad_out = r_oc[...].astype(f32) * par(10)
    r_mg[...] = u3
    sums = [total(u3 * normed3), total(u3), total(grad_out)]
    links.greeted()
    stats.start(0, sums)
    c_u = edges(0, r_mg, r_hu.at[0])
    load_enc.wait()
    c_encq = share(8, lambda i: r_enc.at[pl.ds(2 * i, 2)], lambda i: r_encq.at[i])
    a3 = r_a3[...]
    low = (r_oc[...].astype(f32) * par(10)).astype(bf16)
    pout = nn(r_att[...].reshape(ch, px), low).astype(bf16)
    for q in range(nimg):
        pin = nt_dot(a3, r_tg[2 * q : 2 * q + 2].reshape(6 * hd, px)).astype(bf16)
        r_os[q // 2, q % 2] = jnp.concatenate(
            [pin, pout[:, q * part : (q + 1) * part]], axis=1
        )
    c_ox = links.to(
        "img", links.img + 1 - 2 * img_c, r_os.at[:, 1 - img_c], r_ox,
        r_i_send.at[9, 0], r_i_recv.at[9, 0],
    )
    c_ox.start()
    sums3 = stats.finish(0)
    means3 = back_means(par(8), sums3[0:1], sums3[1:2])

    def middle_back(u, middle, oc):
        normed = (middle - stat(4)) * stat(5)
        return oc.astype(f32) * par(10) + norm_back(u, normed, stat(5), par(8), means3)

    halo.finish(c_u)
    middle_grad = middle_back(r_mg[...], r_middle[...], r_oc[...])
    r_mg[...] = middle_grad
    load_w2.wait()
    act_grad, c_g2 = conv_back(
        0,
        middle_grad,
        middle_back(r_hu[0, 0], r_hmid[0], r_hoc[0]),
        middle_back(r_hu[0, 1], r_hmid[1], r_hoc[1]),
        r_w2,
    )
    normed2 = (r_hidden[...] - stat(2)) * stat(3)
    ntg = act_grad * slope((normed2 * par(3) + par(4)) * scale1 + shift)
    r_ntg[...] = ntg
    stats.start(1, [total(ntg * normed2), total(ntg)])
    c_n = edges(1, r_ntg, r_hu.at[1])
    middle_sum = total(r_mg[...])
    load_a2.wait()
    c_k2 = kernel_grads(0, r_a2, c_g2)
    c_ox.wait()
    r_os[:, 0] = (
        r_os[:, img_c].astype(f32) + r_ox[...].astype(f32)
    ).astype(bf16)
    c_oy = links.to(
        "img", lax.rem(links.img + 2, nimg), r_os.at[1 - img_y, 0], r_oy,
        r_i_send.at[9, 1], r_i_recv.at[9, 1],
    )
    c_oy.start()
    sums2 = stats.finish(1)
    means2 = back_means(par(3), scale1 * sums2[0:1], scale1 * sums2[1:2])

    def hidden_back(u, hidden):
        normed = (hidden - stat(2)) * stat(3)
        return norm_back(u * scale1, normed, stat(3), par(3), means2)

    halo.finish(c_n)
    hidden_grad = hidden_back(r_ntg[...], r_hidden[...])
    hidden_sum = total(hidden_grad)
    load_w1.wait()
    act_grad, c_g1 = conv_back(
        1,
        hidden_grad,
        hidden_back(r_hu[1, 0], r_hhid[0]),
        hidden_back(r_hu[1, 1], r_hhid[1]),
        r_w1,
    )
    m_k2 = [kernel_mid(0, c_k2, 0), kernel_mid(0, c_k2, 1)]
    c_oy.wait()
    both = r_os[img_y, 0].astype(f32) + r_oy[...].astype(f32)
    r_of[...] = both.astype(bf16).reshape(deep, 2, rows, 6 * hd + part)
    c_o = row_x_start(6, r_of, r_oz.at[0])
    normed1 = (r_img[...].astype(f32) - stat(0)) * stat(1)
    n1g = act_grad * slope(normed1 * par(0) + par(1))
    r_ntg[...] = n1g
    stats.start(2, [total(n1g * normed1), total(n1g), hidden_sum, middle_sum])
    m_k2.append(kernel_mid(0, c_k2, 2))
    load_a1.wait()
    c_k1 = kernel_grads(1, r_a1, c_g1)
    c_o = row_z_start(6, c_o, r_of, r_oz.at[0], r_oz.at[1], r_oz.at[2, pl.ds(0, deep - 1)])
    wait(c_encq)
    load_ctx.wait()
    turned = r_ctx[...].reshape(nimg * padc, -1).T
    pairs = jnp.concatenate([r_encq[:, 0], r_encq[:, 1]], axis=2)
    r_cq[...] = nn(turned, pairs.reshape(nimg * padc, 4 * hd)).astype(bf16)
    out = share(11, lambda i: r_cq, lambda i: r_cr.at[i])
    sums1 = stats.finish(2)
    scale_grad = par(3) * sums2[0:1] + par(4) * sums2[1:2]
    r_vsrc[...] = jnp.concatenate(
        [
            sums1[0:3],
            scale1 * sums2[0:1],
            scale1 * sums2[1:2],
            sums1[3:4],
            sums3[0:3],
            scale_grad,
            sums2[1:2],
            jnp.zeros((5, ch), f32),
        ],
        axis=0,
    )
    out += share(10, lambda i: r_vsrc, lambda i: r_every.at[i])
    m_k1 = [kernel_mid(1, c_k1, 0)]
    out += kernel_end(0, m_k2)
    normed1 = (r_img[...].astype(f32) - stat(0)) * stat(1)
    means1 = back_means(par(0), sums1[0:1], sums1[1:2])
    r_igrad[...] = r_mg[...] + norm_back(r_ntg[...], normed1, stat(1), par(0), means1)
    m_k1.append(kernel_mid(1, c_k1, 1))
    m_k1.append(kernel_mid(1, c_k1, 2))
    r_oy[:rows] = row_end(c_o, r_oz.at[1], r_oz.at[2])
    out += share(12, lambda i: r_oy.at[pl.ds(0, rows)], lambda i: r_oq.at[i])
    out += kernel_end(1, m_k1)
    wait(out)


def backward(nrow, nimg, wide, *args):
    px, ch = args[0].shape
    hd = ch // HEADS
    ctx, enc = args[19], args[18]
    padc = enc.shape[1]
    cfg = (nrow, nimg, wide, ch, hd, padc)
    part, rows, deep = ch // nimg, ch // nrow, nrow // 2
    proj = 6 * hd + part
    V = pl.BlockSpec(memory_space=pltpu.VMEM)
    A = pl.BlockSpec(memory_space=pl.ANY)
    S = jax.ShapeDtypeStruct
    dma = pltpu.SemaphoreType.DMA
    M = pltpu.VMEM
    text = ctx.shape[2]
    return pl.pallas_call(
        functools.partial(back_kernel, cfg),
        out_shape=(
            S((px, ch), f32),
            S((2, 3, nimg, rows, 3 * part), bf16),
            S((nimg, rows, proj), bf16),
            S((nimg, text, 4 * hd), bf16),
            S((nimg, 16, ch), f32),
        ),
        in_specs=[A, A, V, V, V, A, A, A, A, A, A, A, A, A] + [A] * 6,
        out_specs=(V,) + (A,) * 4,
        scratch_shapes=[M(args[i].shape, args[i].dtype) for i in (0, 1, 5, 6, 7, 8, 9, 10, 11, 12, 13)]
        + [
            M((3, 3 * ch, ch), bf16),
            M((3, 3 * ch, ch), bf16),
            M((ch, nimg * px), bf16),
            M((ch, nimg * px), bf16),
            M(enc.shape, bf16),
            M(ctx.shape, bf16),
            M((px, ch), f32),
            M((px, ch), f32),
            M((2, px + 2 * wide, 3 * ch), bf16),
            M((2, nimg, px + 2 * wide, part), bf16),
            M((nimg, px + 2 * wide, 3 * part), bf16),
            M((2, 3, deep, 2, rows, 3 * part), bf16),
            M((2, 3, deep, rows, 3 * part), bf16),
            M((2, 3, deep, rows, 3 * part), bf16),
            M((2, 3, deep - 1, rows, 3 * part), bf16),
            M((2, 3, rows, 3 * part), bf16),
            M((2, 2, ch, proj), bf16),
            M((2, ch, proj), bf16),
            M((ch, proj), bf16),
            M((3, deep, rows, proj), bf16),
            M((deep, 2, rows, proj), bf16),
            M((nimg, 2, padc, 2 * hd), bf16),
            M((text, 4 * hd), bf16),
            M((16, ch), f32),
            M((3, 16, 128), f32),
            M((3, nrow, 16, 128), f32),
            M((2, 2, wide, ch), f32),
            M((3, ch, 3 * part), f32),
            dma((17,)),
            dma((3, nrow - 1)),
            dma((3, nrow - 1)),
            dma((2, 2)),
            dma((2, 2)),
            dma((13, nimg - 1)),
            dma((13, nimg - 1)),
            dma((1, nrow - 1)),
            dma((1, nrow - 1)),
            dma((7,)),
            dma((7,)),
            dma((7, deep - 1)),
            dma((7, deep - 1)),
            dma((13,)),
        ],
        compiler_params=pltpu.CompilerParams(
            collective_id=4, has_side_effects=True, vmem_limit_bytes=60 * 2**20
        ),
        name="back",
    )(*args)


def finish_kernel(cfg, *refs):
    nrow, nimg, ch, hd, nvec = cfg
    igh, kqh, oqh, crh, everyh, embh, middleh, atth, pouth, parh = refs[:10]
    resh, igouth, k1h, k2h, inh, outh, ctxgh, embgh = refs[10:18]
    vecs = refs[18 : 18 + nvec]
    ig, kq, oq, cr, every, emb, middle, att, pout, par = refs[18 + nvec : 28 + nvec]
    res, k1g, k2g, ing, outg, ctxg, embg, isem, osem = refs[28 + nvec :]
    px = middle.shape[0]
    part = ch // nimg
    me = lax.axis_index("row")
    done = []
    pairs = (
        (kqh.at[0], kq.at[0]),
        (kqh.at[1], kq.at[1]),
        (atth, att),
        (pouth, pout),
        (middleh, middle),
        (parh, par),
        (everyh, every),
        (embh, emb),
        (crh, cr),
        (oqh, oq),
        (igh, ig),
    )
    loads = [pltpu.make_async_copy(a, b, isem.at[i]) for i, (a, b) in enumerate(pairs)]
    for c in loads:
        c.start()

    def put(slot, src, dst):
        c = pltpu.make_async_copy(src, dst, osem.at[slot])
        c.start()
        done.append(c)

    loads[10].wait()
    put(0, ig, igouth)
    for stage, out, dst in ((0, k2g, k2h), (1, k1g, k1h)):
        loads[stage].wait()
        for ky in range(3):
            for b in range(nimg):
                v = kq[stage, ky, b].astype(f32)
                for kx in range(3):
                    out[2 - ky, 2 - kx, :, b * part : (b + 1) * part] = v[
                        :, kx * part : (kx + 1) * part
                    ]
        put(1 + stage, out, dst)
    for c in loads[2:6]:
        c.wait()
    branch = nn(att[...].reshape(ch, px).T, pout[...])
    res[...] = (middle[...] + branch + par[11:12, :]).astype(bf16)
    put(3, res, resh)
    loads[6].wait()
    loads[7].wait()
    acts = emb[:, 0, :].T
    for j in range(2):
        d = None
        for b in range(nimg):
            t = acts[:, b : b + 1] * every[b, 9 + j : 10 + j]
            d = t if d is None else d + t
        embg[:, j * ch : (j + 1) * ch] = d
    put(4, embg, embgh)
    loads[8].wait()
    for b in range(nimg):
        v = cr[b].astype(f32)
        p = [v[:, j * hd : (j + 1) * hd] for j in range(4)]
        ctxg[:, b * 2 * hd : (b + 1) * 2 * hd] = jnp.concatenate([p[0], p[2]], axis=1)
        ctxg[:, ch + b * 2 * hd : ch + (b + 1) * 2 * hd] = jnp.concatenate([p[1], p[3]], axis=1)
    put(5, ctxg, ctxgh)
    loads[9].wait()
    for b in range(nimg):
        v = oq[b].astype(f32)
        for j in range(3):
            ing[:, j * ch + b * 2 * hd : j * ch + (b + 1) * 2 * hd] = jnp.concatenate(
                [v[:, j * hd : (j + 1) * hd], v[:, (3 + j) * hd : (4 + j) * hd]], axis=1
            )
        outg[:, b * part : (b + 1) * part] = v[:, 6 * hd :]
    put(6, ing, inh)
    put(7, outg, outh)
    sums = jnp.sum(every[...], axis=0)
    size = ch // nrow
    turned = pltpu.roll(sums, lax.rem(ch - me * size, ch), 1)
    for i in range(nvec - 1):
        vecs[i][...] = turned[i, :size]
    both = jnp.concatenate([sums[9:10], sums[10:11]], axis=1)
    both = jnp.concatenate([both] * 8, axis=0)
    both = pltpu.roll(both, lax.rem(2 * ch - me * 2 * size, 2 * ch), 1)
    vecs[nvec - 1][...] = both[0, : 2 * size]
    for c in done:
        c.wait()


def finish(nrow, nimg, *args):
    px, ch = args[0].shape
    hd = ch // HEADS
    kq, oq, cr, every, emb = args[1:6]
    rows = ch // nrow
    nvec = 10
    V = pl.BlockSpec(memory_space=pltpu.VMEM)
    A = pl.BlockSpec(memory_space=pl.ANY)
    S = jax.ShapeDtypeStruct
    M = pltpu.VMEM
    dma = pltpu.SemaphoreType.DMA
    outs = (
        ((px, ch), bf16),
        ((3, 3, rows, ch), f32),
        ((3, 3, rows, ch), f32),
        ((rows, 3 * ch), f32),
        ((rows, ch), f32),
        ((cr.shape[1], 2 * ch), f32),
        ((emb.shape[2], 2 * ch), f32),
    )
    return pl.pallas_call(
        functools.partial(finish_kernel, (nrow, nimg, ch, hd, nvec)),
        out_shape=(S(*outs[0]), S((px, ch), f32))
        + tuple(S(*o) for o in outs[1:])
        + (S((rows,), f32),) * (nvec - 1)
        + (S((2 * rows,), f32),),
        in_specs=[A] * 10,
        out_specs=(A,) * 8 + (V,) * nvec,
        scratch_shapes=[M(a.shape, a.dtype) for a in args]
        + [M(*o) for o in outs]
        + [dma((11,)), dma((8,))],
        compiler_params=pltpu.CompilerParams(vmem_limit_bytes=62 * 2**20),
        name="finish",
    )(*args)


def local_fast(
    images,
    timesteps,
    clip_embed,
    context,
    out_cotangent,
    item_weight,
    first_gain,
    first_bias,
    first_kernel,
    first_offset,
    embed_weight,
    embed_bias,
    second_gain,
    second_bias,
    second_kernel,
    second_offset,
    third_gain,
    third_bias,
    project_in,
    context_weight,
    project_out,
    output_bias,
):
    _, tall, wide, ch = images.shape
    pixels = tall * wide
    nrow = lax.axis_size("row")
    nimg = lax.axis_size("img")
    me_row = lax.axis_index("row")
    nctx = context.shape[1]
    image = images.reshape(pixels, ch)
    cotangent = out_cotangent.reshape(pixels, ch)
    width = clip_embed.shape[1]
    at = jnp.arange(width, dtype=jnp.int32)[None, :]
    half = width // 2
    index = jnp.where(at < half, at, at - half).astype(f32)
    angles = timesteps.astype(f32)[:, None] * jnp.exp(-math.log(10000.0) * index / half)
    embedding = jnp.where(at < half, jnp.cos(angles), jnp.sin(angles)) + clip_embed.astype(f32)
    emb = jax.nn.silu(embedding)
    vectors = [
        v.reshape(1, -1)
        for v in (
            first_gain, first_bias, first_offset, second_gain, second_bias, second_offset,
            third_gain, third_bias, output_bias, embed_bias,
        )
    ]
    w1 = first_kernel.reshape(3, 3 * ch, ch)
    w2 = second_kernel.reshape(3, 3 * ch, ch)
    (
        par, stats, ss, hidden, middle, turned_in, act_three, halo_cot, halo_hidden, halo_middle,
        acts_one, acts_two, ctx_parts, emb_parts, grads, attended, enc_grads,
    ) = front(
        image, cotangent, project_out, context[0], emb, item_weight, vectors, w1, w2, project_in, context_weight,
        embed_weight, nrow, nimg, wide,
    )
    image_grad, kq, oq, cr, every = backward(
        nrow, nimg, wide,
        image, cotangent, par, ss, stats, hidden, middle, halo_cot, halo_hidden, halo_middle, act_three, grads, attended, turned_in,
        w2, w1, acts_two, acts_one, enc_grads, ctx_parts,
    )
    result, image_grad, k1g, k2g, ing, outg, ctxg, embg, *vecs = finish(
        nrow, nimg, image_grad, kq, oq, cr, every, emb_parts, middle, attended, project_out, par
    )
    return (
        result.reshape(images.shape),
        image_grad.reshape(images.shape),
        vecs[0],
        vecs[1],
        k1g,
        vecs[2],
        embg,
        vecs[9],
        vecs[3],
        vecs[4],
        k2g,
        vecs[5],
        vecs[6],
        vecs[7],
        ing,
        ctxg,
        outg,
        vecs[8],
    )


def solution(mesh):
    every = P()
    image = P("img", "row", None, None)
    placed = (image, P("img"), P("img", None), P("img", None, None), image, P("img")) + (every,) * 16
    vec = P("row")
    matrix = P("row", None)
    taps = P(None, None, "row", None)
    nimg, nrow = mesh.shape["img"], mesh.shape["row"]
    quick = nrow == HEADS and nimg == 4
    return jax.shard_map(
        local_fast if quick else local,
        mesh=mesh,
        in_specs=placed,
        out_specs=(
            image,
            image,
            vec,
            vec,
            taps,
            vec,
            matrix,
            vec,
            vec,
            vec,
            taps,
            vec,
            vec,
            vec,
            matrix,
            matrix,
            matrix,
            vec,
        ),
        check_vma=False,
    )
```

```python
import functools
import math

import jax
import jax.numpy as jnp
from jax import lax
from jax.experimental import pallas as pl
from jax.experimental.pallas import tpu as pltpu
from jax.sharding import PartitionSpec as P

HEADS = 8
GROUPS = 32
EPSILON = 1e-05
f32 = jnp.float32
bf16 = jnp.bfloat16
MESH = pl.DeviceIdType.MESH
LOG2E=math.log2(math.e)

def nt(a,b):
    return lax.dot_general(a,b,(((1,),(1,)),((),())),preferred_element_type=f32)
def nn(a,b):
    return jnp.dot(a,b,preferred_element_type=f32)

def attn_kernel(cfg, *refs):
    if cfg[0]:
        q_ref, ctx_ref, g_ref, out_ref, dq_ref, dctx_ref = refs[:6]
        kv_ref, dkv_ref = q_ref, dq_ref
        at_kv = cfg[-1]
    else:
        q_ref, kv_ref, ctx_ref, g_ref, out_ref, dq_ref, dkv_ref, dctx_ref = refs[:8]
        at_kv = 0
    (kx, vx, kt, vt, sbuf, pbuf, acc) = refs[-7:]
    joined, nqs, nsrc, width, bq, kc, nctx, padc, hd = cfg
    npix = nsrc*width
    nk = npix + padc
    ones_rows = jnp.where(lax.broadcasted_iota(jnp.int32,(hd,width),0)<2,1.0,0.0).astype(bf16)
    def fill(pair, at, w):
        k = pair[:hd].astype(f32)*(LOG2E*0.125)
        hi = k.astype(bf16)
        lo = (k-hi.astype(f32)).astype(bf16)
        kx[pl.ds(at,w),:] = jnp.concatenate([hi,lo],axis=0).T
        vfull = jnp.concatenate([pair[hd:], ones_rows[:, :w]],axis=0)
        vx[pl.ds(at,w),:] = vfull.T
        return vfull
    for s in range(nsrc):
        pair = kv_ref[s, at_kv:]
        vfull = fill(pair, s*width, width)
        kt[:, s*width:(s+1)*width] = pair[:hd]
        vt[:, s*width:(s+1)*width] = vfull[:hd+16]
    cpair = ctx_ref[...]
    vfull = fill(cpair, npix, padc)
    kt[:, npix:npix+padc] = cpair[:hd]
    vt[:, npix:npix+padc] = vfull[:hd+16]
    acc[...] = jnp.zeros_like(acc)

    nfull = npix//kc
    per = width//bq
    def block(j, _):
        s = j//per
        off = pl.multiple_of((j%per)*bq, bq)
        qt = q_ref[s,:hd,pl.ds(off,bq)]
        gt = g_ref[s,:,pl.ds(off,bq)]
        q2 = jnp.concatenate([qt,qt],axis=0)
        sc = nn(kx[pl.ds(npix,padc),:], q2)
        sc = jnp.where(lax.broadcasted_iota(jnp.int32,(padc,bq),0)<nctx, sc, -jnp.inf)
        sbuf[pl.ds(npix,padc),:] = sc
        m8 = jnp.max(sc.reshape(padc//8,8,bq),axis=0)
        def phase_a(c, m8):
            at = pl.multiple_of(c*kc,kc)
            sv = nn(kx[pl.ds(at,kc),:], q2)
            sbuf[pl.ds(at,kc),:] = sv
            return jnp.maximum(m8, jnp.max(sv.reshape(kc//8,8,bq),axis=0))
        m8 = lax.fori_loop(0,nfull,phase_a,m8,unroll=True)
        m = jnp.max(m8,axis=0,keepdims=True)
        pc = jnp.exp2(sbuf[pl.ds(npix,padc),:]-m).astype(bf16)
        pbuf[pl.ds(npix,padc),:] = pc
        o = nn(vt[:,npix:npix+padc], pc)
        def phase_b(c, o):
            at = pl.multiple_of(c*kc,kc)
            p = jnp.exp2(sbuf[pl.ds(at,kc),:]-m).astype(bf16)
            pbuf[pl.ds(at,kc),:] = p
            return o + nn(vt[:,pl.ds(at,kc)], p)
        o = lax.fori_loop(0,nfull,phase_b,o,unroll=True)
        inv = 1.0/o[hd:hd+1]
        att = o[:hd]*inv
        out_ref[s,:,pl.ds(off,bq)] = att.astype(bf16)
        gf = gt.astype(f32)
        delta = jnp.sum(gf*att,axis=0,keepdims=True)*inv
        gl = (gf*inv).astype(bf16)
        dhi = (-delta).astype(bf16)
        dlo = (-delta-dhi.astype(f32)).astype(bf16)
        gx = jnp.concatenate([gl,dhi,dlo,jnp.zeros((hd-2,bq),bf16)],axis=0)
        zero = jnp.zeros((hd,bq),bf16)
        rq = jnp.concatenate([qt,zero],axis=0).T
        rg = jnp.concatenate([zero,gl],axis=0).T
        rr = jnp.concatenate([rq,rg],axis=0)
        def piece(at, w, dq):
            p = pbuf[pl.ds(at,w),:]
            dp = nn(vx[pl.ds(at,w),:], gx)
            ds = (p.astype(f32)*dp).astype(bf16)
            acc[pl.ds(at,w),:] += nn(jnp.concatenate([ds,p],axis=1), rr)
            return dq + nn(kt[:,pl.ds(at,w)], ds)
        dq = piece(npix, padc, jnp.zeros((hd,bq),f32))
        def phase_d(c, dq):
            return piece(pl.multiple_of(c*kc,kc), kc, dq)
        dq = lax.fori_loop(0,nfull,phase_d,dq,unroll=True)
        dq_ref[s,:hd,pl.ds(off,bq)] = (dq*0.125).astype(bf16)
        return 0
    lax.fori_loop(0, nqs*per, block, 0)
    scale = jnp.where(lax.broadcasted_iota(jnp.int32,(1,2*hd),1)<hd,0.125,1.0)
    for s in range(nsrc):
        dkv_ref[s, at_kv:] = (acc[s*width:(s+1)*width,:]*scale).astype(bf16).T
    dctx_ref[...] = (acc[npix:npix+padc,:]*scale).astype(bf16)

def attention(q, kv, ctx, g, nctx, bq=512, kc=512):
    joined = kv is None
    nqs, _, width = q.shape
    hd = g.shape[1]
    nsrc = nqs if joined else kv.shape[0]
    padc = ctx.shape[1]
    nk = nsrc*width+padc
    cfg=(joined,nqs,nsrc,width,bq,kc,nctx,padc,hd)
    V=pl.BlockSpec(memory_space=pltpu.VMEM)
    S=jax.ShapeDtypeStruct
    grads=(S((nqs,3*hd,width),bf16),) if joined else (S((nqs,hd,width),bf16),S((nsrc,2*hd,width),bf16))
    args=(q,ctx,g) if joined else (q,kv,ctx,g)
    return pl.pallas_call(
        functools.partial(attn_kernel,cfg),
        out_shape=(S((nqs,hd,width),bf16),)+grads+(S((padc,2*hd),bf16),),
        in_specs=[V]*len(args), out_specs=(V,)*(2+len(grads)),
        scratch_shapes=[pltpu.VMEM((nk,2*hd),bf16),pltpu.VMEM((nk,2*hd),bf16),
                        pltpu.VMEM((hd,nk),bf16),pltpu.VMEM((hd+16,nk),bf16),
                        pltpu.VMEM((nk,bq),f32),pltpu.VMEM((nk,bq),bf16),
                        pltpu.VMEM((nk,2*hd),f32)],
        compiler_params=pltpu.CompilerParams(vmem_limit_bytes=48*2**20),
        cost_estimate=pl.CostEstimate(flops=6*2*64*4096*4228,bytes_accessed=8*2**20,transcendentals=4096*4228),
        name="attend",
    )(*args)

def exchange_kernel(axis, n, x_ref, out_ref, send_sem, recv_sem):
    me = lax.axis_index(axis)
    barrier = pltpu.get_barrier_semaphore()
    for k in range(1, n):
        pl.semaphore_signal(
            barrier, inc=1, device_id={axis: lax.rem(me + k, n)}, device_id_type=MESH
        )
    out_ref[me] = x_ref[...]
    pl.semaphore_wait(barrier, n - 1)
    copies = []
    for k in range(1, n):
        copy = pltpu.make_async_remote_copy(
            src_ref=x_ref,
            dst_ref=out_ref.at[me],
            send_sem=send_sem.at[k - 1],
            recv_sem=recv_sem.at[k - 1],
            device_id={axis: lax.rem(me + k, n)},
            device_id_type=MESH,
        )
        copy.start()
        copies.append(copy)
    for copy in copies:
        copy.wait()


def exchange(x, axis, cid):
    n = lax.axis_size(axis)
    V = pl.BlockSpec(memory_space=pltpu.VMEM)
    return pl.pallas_call(
        functools.partial(exchange_kernel, axis, n),
        out_shape=jax.ShapeDtypeStruct((n,) + x.shape, x.dtype),
        in_specs=[V],
        out_specs=V,
        scratch_shapes=[
            pltpu.SemaphoreType.DMA((n - 1,)),
            pltpu.SemaphoreType.DMA((n - 1,)),
        ],
        compiler_params=pltpu.CompilerParams(collective_id=cid, has_side_effects=True),
        name="exchange_" + axis,
    )(x)


def row_sum(rows):
    x = jnp.concatenate(
        [jnp.stack(rows), jnp.zeros((8 - len(rows), rows[0].shape[0]), f32)], axis=0
    )
    return jnp.sum(exchange(x, "row", 1), axis=0)


def sinusoid(steps, width):
    half_width = width // 2
    frequency = jnp.exp(-math.log(10000.0) * jnp.arange(half_width, dtype=f32) / half_width)
    angles = steps.astype(f32)[:, None] * frequency[None, :]
    return jnp.concatenate([jnp.cos(angles), jnp.sin(angles)], axis=1)


def swish_slope(values):
    sig_v = jax.nn.sigmoid(values)
    return sig_v * (1.0 + values * (1.0 - sig_v))


def per_group(vec, members):
    n = vec.shape[-1]
    g = jnp.sum(vec.reshape(vec.shape[0], GROUPS, n // GROUPS), axis=2) / members
    return jnp.repeat(g, n // GROUPS, axis=1)


def norm_stats(values, members):
    sums = row_sum([jnp.sum(values, axis=0), jnp.sum(values * values, axis=0)])
    means = per_group(sums[:2], members)
    return (means[0], lax.rsqrt(means[1] - means[0] * means[0] + EPSILON))


def halo(x):
    devices = lax.axis_size("row")
    up = [(i, i + 1) for i in range(devices - 1)]
    down = [(i + 1, i) for i in range(devices - 1)]
    before = lax.ppermute(x[-1:], "row", up)
    after = lax.ppermute(x[:1], "row", down)
    return jnp.concatenate([before, x, after], axis=0)


def conv(padded, kernel):
    x = jnp.pad(padded, ((0, 0), (1, 1), (0, 0)))[None]
    return lax.conv_general_dilated(
        x,
        kernel,
        (1, 1),
        "VALID",
        dimension_numbers=("NHWC", "HWIO", "NHWC"),
        preferred_element_type=f32,
    )[0]


def flip_kernel(kernel):
    return jnp.flip(kernel, (0, 1)).transpose(0, 1, 3, 2)


def tn(left, right):
    return lax.dot_general(left, right, (((0,), (0,)), ((), ())), preferred_element_type=f32)


def split_cols(x, n):
    rows, cols = x.shape
    return x.reshape(rows, n, cols // n).transpose(1, 0, 2)


def kernel_grad(acts, grad_padded, tall):
    n = lax.axis_size("img")
    rows, wide, ch = grad_padded.shape
    part = ch // n
    g = lax.all_to_all(
        split_cols(grad_padded.reshape(rows * wide, ch), n),
        "img",
        split_axis=0,
        concat_axis=0,
        tiled=True,
    ).reshape(n, rows, wide, part)
    g = jnp.pad(g, ((0, 0), (0, 0), (1, 1), (0, 0)))
    lines = []
    for ky in range(3):
        for kx in range(3):
            lines.append(
                g[:, 2 - ky : 2 - ky + tall, 2 - kx : 2 - kx + wide].reshape(-1, part)
            )
    return tn(acts, jnp.concatenate(lines, axis=1))


def local(
    images,
    timesteps,
    clip_embed,
    context,
    out_cotangent,
    item_weight,
    first_gain,
    first_bias,
    first_kernel,
    first_offset,
    embed_weight,
    embed_bias,
    second_gain,
    second_bias,
    second_kernel,
    second_offset,
    third_gain,
    third_bias,
    project_in,
    context_weight,
    project_out,
    output_bias,
):
    _, tall, wide, ch = images.shape
    pixels = tall * wide
    hd = ch // HEADS
    nrow = lax.axis_size("row")
    nimg = lax.axis_size("img")
    me_row = lax.axis_index("row")
    gq = nrow // HEADS
    head = me_row // gq
    text = context.shape[2]
    nctx = context.shape[1]
    members = float(nrow * pixels * (ch // GROUPS))

    def gather_img(x):
        return lax.all_gather(x, "img", axis=0, tiled=True)

    grad_out = out_cotangent.reshape(pixels, ch).astype(f32) * (item_weight.astype(f32) * 0.25)
    grad_low = grad_out.astype(bf16)
    attended_grad = (
        lax.dot_general(project_out, grad_low, (((1,), (1,)), ((), ())), preferred_element_type=f32)
        .astype(bf16)
        .reshape(HEADS, hd, pixels)
    )

    def queries_out(x):
        x = x.reshape(HEADS, hd, gq, pixels // gq).transpose(0, 2, 1, 3)
        x = x.reshape(nrow, hd, pixels // gq)
        return x

    def a2a(x):
        return lax.all_to_all(x, "row", split_axis=0, concat_axis=0, tiled=True)

    grad_heads = a2a(queries_out(attended_grad))

    image_f = images.reshape(pixels, ch).astype(f32)
    embedding = sinusoid(timesteps, clip_embed.shape[1]) + clip_embed.astype(f32)
    embed_act = jax.nn.silu(embedding).astype(bf16)
    scale_shift = (jnp.dot(embed_act, embed_weight, preferred_element_type=f32) + embed_bias)[0]
    scale1 = 1.0 + scale_shift[:ch]
    shift = scale_shift[ch:]
    pair_at = (head // 2) * (2 * hd)
    cw_k = lax.dynamic_slice_in_dim(context_weight, pair_at, 2 * hd, 1)
    cw_v = lax.dynamic_slice_in_dim(context_weight, ch + pair_at, 2 * hd, 1)
    cw = jnp.concatenate([cw_k, cw_v], axis=1)
    enc = lax.dot_general(
        cw, context[0], (((0,), (1,)), ((), ())), preferred_element_type=f32
    ).astype(bf16)
    enc = enc.reshape(2, 2, hd, nctx)
    enc = jnp.where(head % 2 == 0, enc[:, 0], enc[:, 1]).reshape(2 * hd, nctx)
    padc = -(-nctx // 16) * 16
    enc = jnp.pad(enc, ((0, 0), (0, padc - nctx)))

    mean1, rstd1 = norm_stats(image_f, members)
    normed1 = (image_f - mean1) * rstd1
    norm_one = normed1 * first_gain + first_bias
    act_one = jax.nn.silu(norm_one).astype(bf16)
    hidden = conv(halo(act_one.reshape(tall, wide, ch)), first_kernel).reshape(pixels, ch)
    hidden = hidden + first_offset
    acts_one = gather_img(act_one)
    mean2, rstd2 = norm_stats(hidden, members)
    normed2 = (hidden - mean2) * rstd2
    affine_two = normed2 * second_gain + second_bias
    norm_two = affine_two * scale1 + shift
    act_two = jax.nn.silu(norm_two).astype(bf16)
    acts_two = gather_img(act_two)
    middle = (
        image_f
        + conv(halo(act_two.reshape(tall, wide, ch)), second_kernel).reshape(pixels, ch)
        + second_offset
    )
    mean3, rstd3 = norm_stats(middle, members)
    normed3 = (middle - mean3) * rstd3
    act_three = (normed3 * third_gain + third_bias).astype(bf16)
    acts_three = gather_img(act_three)
    triple = (
        lax.dot_general(project_in, act_three, (((0,), (1,)), ((), ())), preferred_element_type=f32)
        .astype(bf16)
        .reshape(3, HEADS, hd, pixels)
    )
    if gq == 1:
        recv = a2a(triple.transpose(1, 0, 2, 3).reshape(nrow, 3 * hd, pixels))
        q_h, kv_h = recv[:, :hd], recv[:, hd:]
        grad_h = grad_heads
    else:
        pair = triple[1:].transpose(1, 0, 2, 3).reshape(HEADS, 1, 2 * hd, pixels)
        pair = jnp.broadcast_to(pair, (HEADS, gq, 2 * hd, pixels)).reshape(nrow, 2 * hd, pixels)
        q_h, kv_h = a2a(queries_out(triple[0])), a2a(pair)

        def regroup(x, rows):
            x = x.transpose(1, 0, 2).reshape(rows, -1, 512)
            return x.transpose(1, 0, 2)

        q_h, kv_h, grad_h = regroup(q_h, hd), regroup(kv_h, 2 * hd), regroup(grad_heads, hd)
    att_h, dq_h, dkv_h, dctx = attention(q_h, kv_h, enc, grad_h, nctx)
    if gq == 1:
        attended = a2a(att_h).reshape(ch, pixels)
        back = a2a(jnp.concatenate([dq_h, dkv_h], axis=1)).reshape(HEADS, 3, hd, pixels)
        back = back.transpose(1, 0, 2, 3).reshape(3 * ch, pixels)
    else:

        def ungroup(x, part):
            rows = x.shape[1]
            x = x.transpose(1, 0, 2).reshape(rows, nrow, part)
            return x.transpose(1, 0, 2)

        def from_queries(x):
            x = x.reshape(HEADS, gq, hd, pixels // gq).transpose(0, 2, 1, 3)
            return x.reshape(ch, pixels)

        attended = from_queries(a2a(ungroup(att_h, pixels // gq)))
        dq = from_queries(a2a(ungroup(dq_h, pixels // gq)))
        dkv = a2a(ungroup(dkv_h, pixels)).reshape(HEADS, gq, 2, hd, pixels)
        dkv = jnp.sum(dkv.astype(f32), axis=1).astype(bf16)
        dkv = dkv.transpose(1, 0, 2, 3).reshape(2 * ch, pixels)
        back = jnp.concatenate([dq, dkv], axis=0)
    branch = tn(attended, project_out)
    result_image = (middle + branch + output_bias).astype(bf16)

    part_text = text // nrow
    enc_all = lax.all_gather(dctx[:nctx].astype(bf16), ("img", "row"), axis=0)
    enc_all = enc_all.reshape(nimg, HEADS, gq, nctx, 2, hd)
    if gq > 1:
        enc_all = jnp.sum(enc_all.astype(f32), axis=2, keepdims=True).astype(bf16)
    enc_all = enc_all[:, :, 0].transpose(0, 2, 3, 1, 4).reshape(nimg * nctx, 2 * ch)
    ctx_rows = lax.dynamic_slice_in_dim(context[0], me_row * part_text, part_text, 1)
    ctx_rows = gather_img(ctx_rows)
    context_weight_grad = tn(ctx_rows, enc_all)

    triple_grad = back.T
    act_three_grad = lax.dot_general(
        triple_grad, project_in, (((1,), (1,)), ((), ())), preferred_element_type=f32
    )
    sums3 = row_sum(
        [
            jnp.sum(act_three_grad * normed3, axis=0),
            jnp.sum(act_three_grad, axis=0),
            jnp.sum(grad_out, axis=0),
        ]
    )

    def norm_back(u, normed, rstd, gain, gain_sum, bias_sum):
        means = per_group(jnp.stack([gain * bias_sum, gain * gain_sum]), members)
        return rstd * (u * gain - means[0] - normed * means[1])

    middle_grad = grad_out + norm_back(
        act_three_grad, normed3, rstd3, third_gain, sums3[0], sums3[1]
    )
    middle_low = halo(middle_grad.astype(bf16).reshape(tall, wide, ch))
    act_two_grad = conv(middle_low, flip_kernel(second_kernel)).reshape(pixels, ch)
    norm_two_grad = act_two_grad * swish_slope(norm_two)
    sums2 = row_sum(
        [
            jnp.sum(norm_two_grad * normed2, axis=0),
            jnp.sum(norm_two_grad, axis=0),
            jnp.sum(middle_grad, axis=0),
        ]
    )
    scale_grad = second_gain * sums2[0] + second_bias * sums2[1]
    shift_grad = sums2[1]
    gain2_sum, bias2_sum = scale1 * sums2[0], scale1 * sums2[1]
    hidden_grad = norm_back(
        norm_two_grad * scale1, normed2, rstd2, second_gain, gain2_sum, bias2_sum
    )
    hidden_low = halo(hidden_grad.astype(bf16).reshape(tall, wide, ch))
    act_one_grad = conv(hidden_low, flip_kernel(first_kernel)).reshape(pixels, ch)
    norm_one_grad = act_one_grad * swish_slope(norm_one)
    sums1 = row_sum(
        [
            jnp.sum(norm_one_grad * normed1, axis=0),
            jnp.sum(norm_one_grad, axis=0),
            jnp.sum(hidden_grad, axis=0),
        ]
    )
    image_grad = middle_grad + norm_back(
        norm_one_grad, normed1, rstd1, first_gain, sums1[0], sums1[1]
    )

    def swap_img(x):
        x = split_cols(x, nimg)
        x = lax.all_to_all(x, "img", split_axis=0, concat_axis=0, tiled=True)
        return x.reshape(-1, x.shape[2])

    kg2 = kernel_grad(acts_two, middle_low, tall)
    kg1 = kernel_grad(acts_one, hidden_low, tall)
    pin = tn(acts_three, swap_img(triple_grad))
    pout = tn(gather_img(attended.T), swap_img(grad_low))

    def finish(x):
        x = lax.psum_scatter(x.astype(bf16), "row", scatter_dimension=0, tiled=True)
        return lax.all_gather(x, "img", axis=0).astype(f32)

    c2 = finish(kg2)
    c1 = finish(kg1)
    c3 = finish(jnp.concatenate([pin, pout], axis=1))
    part = ch // nrow
    cols = ch // nimg

    def conv_out(x):
        return x.reshape(nimg, part, 3, 3, cols).transpose(2, 3, 1, 0, 4).reshape(3, 3, part, ch)

    wide_in = 3 * ch // nimg
    pin_out = c3[:, :, :wide_in].transpose(1, 0, 2).reshape(part, 3 * ch)
    pout_out = c3[:, :, wide_in:].transpose(1, 0, 2).reshape(part, ch)

    rows = jnp.stack(
        [
            sums1[0],
            sums1[1],
            sums1[2],
            gain2_sum,
            bias2_sum,
            sums2[2],
            sums3[0],
            sums3[1],
            sums3[2],
            scale_grad,
            shift_grad,
        ]
        + [jnp.zeros((ch,), f32)] * 5
    )
    every = exchange(rows, "img", 2)
    acts_embed = gather_img(embed_act)
    part_emb = embed_act.shape[1] // nrow
    acts_embed = lax.dynamic_slice_in_dim(acts_embed, me_row * part_emb, part_emb, 1).astype(f32)
    shift_scale = every[:, 9:11].reshape(nimg, 2 * ch)
    embed_weight_grad = jnp.sum(acts_embed[:, :, None] * shift_scale[:, None, :], axis=0)
    part_bias = 2 * ch // nrow
    embed_bias_grad = lax.dynamic_slice_in_dim(
        jnp.sum(shift_scale, axis=0), me_row * part_bias, part_bias, 0
    )
    vecs = lax.dynamic_slice_in_dim(jnp.sum(every[:, :9], axis=0), me_row * part, part, 1)
    return (
        result_image.reshape(images.shape),
        image_grad.reshape(images.shape),
        vecs[0],
        vecs[1],
        conv_out(c1),
        vecs[2],
        embed_weight_grad,
        embed_bias_grad,
        vecs[3],
        vecs[4],
        conv_out(c2),
        vecs[5],
        vecs[6],
        vecs[7],
        pin_out,
        context_weight_grad,
        pout_out,
        vecs[8],
    )


def nt_dot(a, b):
    return lax.dot_general(a, b, (((1,), (1,)), ((), ())), preferred_element_type=f32)


def group_total(x):
    per = x.shape[1] // GROUPS
    lane = lax.broadcasted_iota(jnp.int32, x.shape, 1)
    n = x.shape[1]
    step = 1
    while step < per:
        upper = (lane // step) % 2 == 1
        x = x + jnp.where(upper, pltpu.roll(x, step, 1), pltpu.roll(x, n - step, 1))
        step *= 2
    return x


def total(v):
    return jnp.sum(v, axis=0, keepdims=True)


def put_shifts(buf, at, v, wide):
    n, ch = v.shape
    col = lax.rem(lax.broadcasted_iota(jnp.int32, (n, 1), 0), wide)
    buf[pl.ds(at, n), pl.ds(ch, ch)] = v.astype(bf16)
    left = jnp.where(col == 0, 0.0, pltpu.roll(v, 1, 0))
    buf[pl.ds(at, n), pl.ds(0, ch)] = left.astype(bf16)
    right = jnp.where(col == wide - 1, 0.0, pltpu.roll(v, n - 1, 0))
    buf[pl.ds(at, n), pl.ds(2 * ch, ch)] = right.astype(bf16)


class Links:
    def __init__(self, nrow, nimg):
        self.nrow, self.nimg = nrow, nimg
        self.row, self.img = lax.axis_index("row"), lax.axis_index("img")

    def peer(self, axis, k):
        if axis == "row":
            return lax.rem(self.row + k, self.nrow)
        return lax.rem(self.img + k, self.nimg)

    def greet(self):
        barrier = pltpu.get_barrier_semaphore()
        for axis, n in (("row", self.nrow), ("img", self.nimg)):
            for k in range(1, n):
                pl.semaphore_signal(
                    barrier, inc=1, device_id={axis: self.peer(axis, k)}, device_id_type=MESH
                )

    def greeted(self):
        pl.semaphore_wait(pltpu.get_barrier_semaphore(), self.nrow + self.nimg - 2)

    def to(self, axis, at, src, dst, send, recv):
        return pltpu.make_async_remote_copy(
            src_ref=src,
            dst_ref=dst,
            send_sem=send,
            recv_sem=recv,
            device_id={axis: at},
            device_id_type=MESH,
        )

    def copy(self, axis, k, src, dst, send, recv):
        return self.to(axis, self.peer(axis, k), src, dst, send, recv)


class Stats:
    def __init__(self, links, src, dst, send, recv):
        self.links, self.src, self.dst, self.send, self.recv = links, src, dst, send, recv

    def start(self, stage, rows):
        links = self.links
        ch = rows[0].shape[1]
        blocks = [r[:, i * 128 : (i + 1) * 128] for r in rows for i in range(ch // 128)]
        height = self.src.shape[1]
        blocks = blocks + [jnp.zeros((1, 128), f32)] * (height - len(blocks))
        packed = jnp.concatenate(blocks, axis=0)
        self.src[stage] = packed
        self.dst[stage, links.row] = packed
        self.rows, self.per = len(rows), ch // 128
        self.copies = []
        for k in range(1, links.nrow):
            c = links.copy(
                "row",
                k,
                self.src.at[stage],
                self.dst.at[stage, links.row],
                self.send.at[stage, k - 1],
                self.recv.at[stage, k - 1],
            )
            c.start()
            self.copies.append(c)

    def finish(self, stage):
        for c in self.copies:
            c.wait()
        s = jnp.sum(self.dst[stage], axis=0)
        per = self.per
        rows = [
            jnp.concatenate([s[r * per + i : r * per + i + 1] for i in range(per)], axis=1)
            for r in range(self.rows)
        ]
        return jnp.concatenate(rows + [jnp.zeros((8 - self.rows, per * 128), f32)], axis=0)


class Halo:
    def __init__(self, links, send, recv):
        self.links, self.send, self.recv = links, send, recv

    def copies(self, slot, first, last, land):
        links = self.links
        down = links.copy(
            "row", links.nrow - 1, first, land.at[1],
            self.send.at[slot, 0], self.recv.at[slot, 1],
        )
        up = links.copy(
            "row", 1, last, land.at[0],
            self.send.at[slot, 1], self.recv.at[slot, 0],
        )
        return down, up

    def start(self, slot, first, last, land):
        links = self.links
        down, up = self.copies(slot, first, last, land)

        @pl.when(links.row > 0)
        def _():
            down.start()

        @pl.when(links.row < links.nrow - 1)
        def _():
            up.start()

        @pl.when(links.row == 0)
        def _():
            land[0] = jnp.zeros(land.shape[1:], land.dtype)

        @pl.when(links.row == links.nrow - 1)
        def _():
            land[1] = jnp.zeros(land.shape[1:], land.dtype)

        return down, up

    def finish(self, pair):
        links = self.links
        down, up = pair

        @pl.when(links.row > 0)
        def _():
            down.wait_send()
            up.wait_recv()

        @pl.when(links.row < links.nrow - 1)
        def _():
            up.wait_send()
            down.wait_recv()


def put_block(links, buf, mid, before, after, wide):
    put_shifts(buf, wide, mid, wide)
    put_shifts(buf, 0, jnp.where(links.row > 0, before, 0.0), wide)
    put_shifts(buf, buf.shape[0] - wide, jnp.where(links.row < links.nrow - 1, after, 0.0), wide)


def front_kernel(
    cfg,
    *refs,
):
    nvec = cfg[-1]
    _front(cfg[:-1], *refs[:6], refs[6 : 6 + nvec], *refs[6 + nvec :])


def _front(
    cfg,
    r_img,
    r_oc,
    r_pout,
    r_cxt,
    r_embv,
    r_weight,
    r_vecs,
    r_w1h,
    r_w2h,
    r_winh,
    r_cwh,
    r_ewh,
    r_par,
    r_stats,
    r_ss,
    r_hiddenh,
    r_middleh,
    r_wth,
    r_a3h,
    r_hoch,
    r_hhidh,
    r_hmidh,
    r_a1h,
    r_a2h,
    r_ctxh,
    r_embh,
    r_tgh,
    r_atth,
    r_ench,
    r_hidden,
    r_middle,
    r_wt,
    r_a3,
    r_hoc,
    r_hhid,
    r_hmid,
    r_emb,
    r_himg,
    r_gx,
    r_dqa,
    r_cw,
    r_ctx,
    r_buf,
    r_at,
    r_gs,
    r_ts,
    r_qkv,
    r_g,
    r_kx,
    r_vx,
    r_kt,
    r_vt,
    r_sb,
    r_pb,
    r_acc,
    r_atb,
    r_dqb,
    r_dcb,
    r_st_src,
    r_st_dst,
    r_wsem,
    r_vsem,
    r_st_send,
    r_st_recv,
    r_h_send,
    r_h_recv,
    r_i_send,
    r_i_recv,
    r_r_send,
    r_r_recv,
    r_osem,
    r_bsem,
):
    nrow, nimg, wide, ch, hd, kc, joint = cfg
    px = r_img.shape[0]
    members = float(nrow * px * (ch // GROUPS))
    links = Links(nrow, nimg)
    links.greet()
    head = links.row
    me = links.row

    def pair_at(at):
        return pl.ds(pl.multiple_of(at + (head // 2) * (2 * hd), 128), 2 * hd)

    deep = 3 * ch
    at_ew, at_win, at_w1 = 0, 2 * r_embv.shape[1], 2 * r_embv.shape[1] + deep
    at_w2 = at_w1 + 3 * deep
    text_in = r_embv.shape[1]
    groups = (
        [(r_w1h.at[k], at_w1 + k * deep, deep) for k in range(3)],
        [(r_ewh.at[:, k * ch : (k + 1) * ch], at_ew + k * text_in, text_in) for k in range(2)],
        [(r_winh.at[:, k * ch : (k + 1) * ch], at_win + k * ch, ch) for k in range(3)],
        [(r_w2h.at[k], at_w2 + k * deep, deep) for k in range(3)],
    )
    count = 0
    loads = []
    for group in groups:
        loads.append([])
        for src, at, n in group:
            c = pltpu.make_async_copy(src, r_pb.at[pl.ds(at, n)], r_wsem.at[count])
            c.start()
            loads[-1].append(c)
            count += 1
    loads.append([])
    for src, dst in (
        (r_cwh.at[:, pair_at(0)], r_cw.at[:, : 2 * hd]),
        (r_cwh.at[:, pair_at(ch)], r_cw.at[:, 2 * hd :]),
    ):
        c = pltpu.make_async_copy(src, dst, r_wsem.at[count])
        c.start()
        loads[-1].append(c)
        count += 1
    load_w1, load_ew, load_win, load_w2, load_cw = loads

    def ready(copies):
        for c in copies:
            c.wait()

    places = (0, 1, 2, 3, 4, 7, 8, 9, 11, 12, 13)
    flat = [v for v in r_vecs[:-1]] + [r_vecs[-1].at[:, :ch], r_vecs[-1].at[:, ch:]]
    vec_loads = [
        pltpu.make_async_copy(v, r_par.at[pl.ds(at, 1)], r_vsem.at[i])
        for i, (v, at) in enumerate(zip(flat, places))
    ]
    for c in vec_loads:
        c.start()
    weight = r_weight[0].astype(f32) * 0.25
    for at in (5, 6, 14, 15):
        r_par[at : at + 1, :] = jnp.zeros((1, ch), f32)
    r_par[10:11, :] = jnp.full((1, ch), 1.0, f32) * weight
    stats = Stats(links, r_st_src, r_st_dst, r_st_send, r_st_recv)
    halo = Halo(links, r_h_send, r_h_recv)
    ends = (pl.ds(0, wide), pl.ds(px - wide, wide))

    def edges(slot, block, land):
        return halo.start(slot, block.at[ends[0]], block.at[ends[1]], land)

    pending = []

    def par(i):
        return r_par[i : i + 1, :]

    def share(slot, src, dst):
        copies = [pltpu.make_async_copy(src(links.img), dst(links.img), r_osem.at[slot])]
        for k in range(1, nimg):
            copies.append(
                links.copy(
                    "img", k, src(links.peer("img", k)), dst(links.img),
                    r_i_send.at[slot, k - 1], r_i_recv.at[slot, k - 1],
                )
            )
        for c in copies:
            c.start()
        pending.extend(copies)

    def scatter(slot, src, dst):
        copies = []
        for k in range(1, nrow):
            copies.append(
                links.copy(
                    "row", k, src(links.peer("row", k)), dst(me),
                    r_r_send.at[slot, k - 1], r_r_recv.at[slot, k - 1],
                )
            )
        for c in copies:
            c.start()
        return copies

    def lanes(img):
        return pl.ds(pl.multiple_of(img * px, 128), px)

    def moments(v):
        return [total(v), total(v * v)]

    def center(stage, sums):
        means = group_total(sums) * (1.0 / members)
        mean = means[0:1]
        rstd = lax.rsqrt(means[1:2] - mean * mean + EPSILON)
        r_stats[2 * stage : 2 * stage + 1, :] = mean
        r_stats[2 * stage + 1 : 2 * stage + 2, :] = rstd
        return mean, rstd

    r_stats[...] = jnp.zeros_like(r_stats)
    rows = moments(r_img[...].astype(f32))
    low = (r_oc[...].astype(f32) * weight).astype(bf16)
    r_gs[...] = nt_dot(r_pout[...], low).astype(bf16).reshape(r_gs.shape)
    r_emb[...] = jnp.broadcast_to(r_embv[...].astype(bf16).astype(f32), r_emb.shape)
    links.greeted()
    stats.start(0, rows)
    c_img = edges(0, r_img, r_himg)
    c_g = scatter(2, lambda r: r_gs.at[r], lambda r: r_g.at[r])
    for c in vec_loads:
        c.wait()
    ready(load_ew)
    emb = r_emb[...].astype(bf16)
    scale1 = 1.0 + (nn(emb, r_pb[at_ew : at_ew + text_in])[0:1] + par(12))
    shift = nn(emb, r_pb[at_ew + text_in : at_ew + 2 * text_in])[0:1] + par(13)
    r_ss[...] = jnp.concatenate([scale1, shift, jnp.zeros((6, ch), f32)], axis=0)
    mean, rstd = center(0, stats.finish(0))

    def conv_stage(stage, act, before, after, weights):
        buf = r_buf
        put_block(links, buf, act, before, after, wide)
        acc = None
        for ky in range(3):
            d = nn(
                buf[pl.ds(ky * wide, px), :],
                r_pb[weights + ky * deep : weights + (ky + 1) * deep, :],
            )
            acc = d if acc is None else acc + d
        r_at[stage] = act.astype(bf16).T
        return acc


    def act_one(v):
        return jax.nn.silu((v.astype(f32) - mean) * rstd * par(0) + par(1))

    halo.finish(c_img)
    ready(load_w1)
    hidden = conv_stage(
        0, act_one(r_img[...]), act_one(r_himg[0]), act_one(r_himg[1]), at_w1
    ) + par(2)
    r_hidden[...] = hidden
    stats.start(1, moments(hidden))
    c_hid = edges(1, r_hidden, r_hhid)
    ready(load_win)
    for j in range(3):
        turned = r_pb[at_win + j * ch : at_win + (j + 1) * ch, :].T
        for h in range(HEADS):
            r_wt[(3 * h + j) * hd : (3 * h + j + 1) * hd, :] = turned[h * hd : (h + 1) * hd]
    mean_two, rstd_two = center(1, stats.finish(1))

    def act_two(v):
        affine = (v - mean_two) * rstd_two * par(3) + par(4)
        return jax.nn.silu(affine * r_ss[0:1] + r_ss[1:2])

    halo.finish(c_hid)
    ready(load_w2)
    middle = conv_stage(1, act_two(r_hidden[...]), act_two(r_hhid[0]), act_two(r_hhid[1]), at_w2)
    middle = r_img[...].astype(f32) + middle + par(7)
    r_middle[...] = middle
    stats.start(2, moments(middle))
    c_mid = edges(2, r_middle, r_hmid)
    c_oc = edges(3, r_oc, r_hoc)
    nctx, text = r_cxt.shape
    padc = r_ctx.shape[0]
    r_ctx[...] = jnp.concatenate(
        [r_cxt[...], jnp.zeros((padc - nctx, text), bf16)], axis=0
    )
    ready(load_cw)
    enc = nn(r_ctx[...], r_cw[...]).T.astype(bf16)
    first = lax.rem(head, 2) == 0
    enc = jnp.concatenate(
        [
            jnp.where(first, enc[2 * j * hd : (2 * j + 1) * hd], enc[(2 * j + 1) * hd : (2 * j + 2) * hd])
            for j in range(2)
        ],
        axis=0,
    )
    mean, rstd = center(2, stats.finish(2))
    act3 = ((r_middle[...] - mean) * rstd * par(8) + par(9)).astype(bf16)
    r_a3[...] = act3.T
    ts, qkv, gs, g = r_ts, r_qkv, r_gs, r_g
    ts[...] = nn(r_wt[...], r_a3[...]).astype(bf16).reshape(ts.shape)
    tall = nrow // 2
    row_z, row_x = me // 2, lax.rem(me, 2)

    def source(i):
        z = lax.rem(row_z + lax.rem((i + 1) // 2, tall), tall)
        return 2 * z + lax.rem(row_x + i + 1, 2)

    def target(i):
        z = lax.rem(row_z + tall - lax.rem((i + 1) // 2, tall), tall)
        return 2 * z + lax.rem(row_x + i + 1, 2)

    def q_copy(i):
        to = target(i)
        return links.to(
            "row", to, ts.at[to, pl.ds(0, hd)], qkv.at[me, pl.ds(0, hd)],
            r_r_send.at[1, i], r_r_recv.at[1, i],
        )

    q_copy(0).start()
    c_kv = scatter(0, lambda r: ts.at[r, pl.ds(hd, 2 * hd)], lambda r: qkv.at[r, pl.ds(hd, 2 * hd)])
    npix = nrow * px
    ones_rows = jnp.where(lax.broadcasted_iota(jnp.int32, (hd, px), 0) < 2, 1.0, 0.0).astype(bf16)
    kx, vx, kt, vt, sb, pb, acc = (r_kx, r_vx, r_kt, r_vt, r_sb, r_pb, r_acc)

    def fill(pair, at, w):
        k = pair[:hd].astype(f32) * (LOG2E * 0.125)
        hi = k.astype(bf16)
        lo = (k - hi.astype(f32)).astype(bf16)
        kx[pl.ds(at, w), :] = jnp.concatenate([hi, lo], axis=0).T
        vfull = jnp.concatenate([pair[hd:], ones_rows[:, :w]], axis=0)
        vx[pl.ds(at, w), :] = vfull.T
        kt[:, pl.ds(at, w)] = pair[:hd]
        vt[:, pl.ds(at, w)] = vfull[: hd + 16]

    fill(enc, npix, padc)
    qkv[me] = ts[me]
    g[me] = gs[me]
    acc[...] = jnp.zeros_like(acc)

    def own(r):
        return pl.multiple_of(r * px, 128)

    fill(ts[me, hd:], own(me), px)
    for k in range(1, nrow):
        c_kv[k - 1].wait()
        frm = lax.rem(me + nrow - k, nrow)
        fill(qkv[frm, hd:], own(frm), px)


    q_copy(1).start()
    for i in range(2):
        share(i, lambda p, i=i: r_at.at[i], lambda p, i=i: (r_a1h, r_a2h)[i].at[:, lanes(p)])
    mine = text // nrow
    text_at = pl.ds(pl.multiple_of(me * mine, 128), mine)
    share(2, lambda p: r_ctx.at[:, text_at], lambda p: r_ctxh.at[p])
    wide_emb = r_emb.shape[1] // nrow
    emb_at = pl.ds(pl.multiple_of(me * wide_emb, 128), wide_emb)
    share(3, lambda p: r_emb.at[:, emb_at], lambda p: r_embh.at[p])
    halo.finish(c_mid)
    halo.finish(c_oc)
    kept = (
        (r_hidden, r_hiddenh),
        (r_middle, r_middleh),
        (r_wt, r_wth),
        (r_a3, r_a3h),
        (r_hoc, r_hoch),
        (r_hhid, r_hhidh),
        (r_hmid, r_hmidh),
    )
    for i, (a, b) in enumerate(kept):
        c = pltpu.make_async_copy(a, b, r_bsem.at[i])
        c.start()
        pending.append(c)

    bq = px
    nfull = npix // kc

    def att_copy(i):
        to = source(i)
        return links.to(
            "row", to, r_atb.at[to], r_atth.at[me], r_r_send.at[3, i], r_r_recv.at[3, i]
        )

    def dq_copy(i):
        to = source(i)
        return links.to(
            "row", to, r_dqb.at[to, pl.ds(0, hd)], r_tgh.at[me, pl.ds(0, hd)],
            r_r_send.at[4, i], r_r_recv.at[4, i],
        )

    nk = npix + padc

    def scores(i, slot):
        s = source(i)
        base = pl.multiple_of(slot * nk, 16)

        @pl.when(i + 2 < nrow - 1)
        def _():
            q_copy(i + 2).start()

        @pl.when(i < nrow - 1)
        def _():
            q_copy(i).wait_recv()
            k = lax.rem(me - s + nrow, nrow) - 1
            links.to("row", s, gs.at[s], g.at[s], r_r_send.at[2, k], r_r_recv.at[2, k]).wait_recv()

        qt = qkv[s, :hd]
        gt = g[s]
        q2 = jnp.concatenate([qt, qt], axis=0)
        sc = nn(kx[pl.ds(npix, padc), :], q2)
        sc = jnp.where(lax.broadcasted_iota(jnp.int32, (padc, bq), 0) < nctx, sc, -jnp.inf)
        sb[pl.ds(npix, padc), :] = sc
        m8 = jnp.max(sc.reshape(padc // 8, 8, bq), axis=0)

        def phase_a(c, m8):
            at = pl.multiple_of(c * kc, kc)
            sv = nn(kx[pl.ds(at, kc), :], q2)
            sb[pl.ds(at, kc), :] = sv
            return jnp.maximum(m8, jnp.max(sv.reshape(kc // 8, 8, bq), axis=0))

        m8 = lax.fori_loop(0, nfull, phase_a, m8, unroll=True)
        m = jnp.max(m8, axis=0, keepdims=True)
        pc = jnp.exp2(sb[pl.ds(npix, padc), :] - m).astype(bf16)
        pb[pl.ds(base + npix, padc), :] = pc
        o = nn(vt[:, npix : npix + padc], pc)

        def phase_b(c, o):
            at = pl.multiple_of(c * kc, kc)
            p = jnp.exp2(sb[pl.ds(at, kc), :] - m).astype(bf16)
            pb[pl.ds(pl.multiple_of(base + at, 16), kc), :] = p
            return o + nn(vt[:, pl.ds(at, kc)], p)

        o = lax.fori_loop(0, nfull, phase_b, o, unroll=True)
        inv = 1.0 / o[hd : hd + 1]
        att = o[:hd] * inv
        r_atb[s] = att.astype(bf16)

        @pl.when(i < nrow - 1)
        def _():
            att_copy(i).start()

        gf = gt.astype(f32)
        delta = total(gf * att) * inv
        gl = (gf * inv).astype(bf16)
        dhi = (-delta).astype(bf16)
        dlo = (-delta - dhi.astype(f32)).astype(bf16)
        r_gx[slot] = jnp.concatenate([gl, dhi, dlo, jnp.zeros((hd - 2, bq), bf16)], axis=0)
        r_dqa[slot] = piece(slot, qt, npix, padc, jnp.zeros((hd, bq), f32))

    def piece(slot, qt, at, w, dq):
        gx = r_gx[slot]
        p = pb[pl.ds(pl.multiple_of(slot * nk + at, 16), w), :]
        dp = nn(vx[pl.ds(at, w), :], gx)
        ds = (p.astype(f32) * dp).astype(bf16)
        acc[:hd, pl.ds(at, w)] += nt_dot(qt, ds)
        acc[hd:, pl.ds(at, w)] += nt_dot(gx[:hd], p)
        return dq + nn(kt[:, pl.ds(at, w)], ds)

    def block(i, _):
        s = source(i)
        scores(i, 0)
        qt = qkv[s, :hd]

        def phase_d(c, dq):
            return piece(0, qt, pl.multiple_of(c * kc, kc), kc, dq)

        dq = lax.fori_loop(0, nfull, phase_d, r_dqa[0], unroll=True)
        r_dqb[s, :hd] = (dq * 0.125).astype(bf16)
        dq_copy(i).start()
        return 0

    alone = nrow - joint
    lax.fori_loop(0, alone, block, 0)
    scale = jnp.where(lax.broadcasted_iota(jnp.int32, (2 * hd, 1), 0) < hd, 0.125, 1.0)

    def first(j, _):
        scores(alone + j, j)
        return 0

    lax.fori_loop(0, joint, first, 0)

    def key_home(c):
        z = lax.rem(row_z + 1 + c // 2, tall)
        return 2 * z + lax.rem(row_x + c + 1, 2)

    def kv_back(c):
        s = key_home(c)
        return links.to(
            "row", s, r_dqb.at[s, pl.ds(hd, 2 * hd)], r_tgh.at[me, pl.ds(hd, 2 * hd)],
            r_r_send.at[5, c], r_r_recv.at[5, c],
        )

    def keys_done(c, _):
        z = lax.rem(row_z + 1 + c, tall)
        at = pl.multiple_of(z * (2 * px), 128)
        for j in range(joint):
            qt = qkv[source(alone + j), :hd]
            r_dqa[j] = piece(j, qt, at, 2 * px, r_dqa[j])
        for h in range(2):
            s = key_home(2 * c + h)
            r_dqb[s, hd:] = (acc[:, pl.ds(own(s), px)] * scale).astype(bf16)

            @pl.when(2 * c + h < nrow - 1)
            def _():
                kv_back(2 * c + h).start()

        return 0

    lax.fori_loop(0, tall, keys_done, 0, unroll=True)
    copies = []
    for j in range(joint):
        r_dqb[source(alone + j), :hd] = (r_dqa[j] * 0.125).astype(bf16)
        if alone + j < nrow - 1:
            dq_copy(alone + j).start()
    r_dcb[...] = (acc[:, npix : npix + padc] * scale).astype(bf16).T
    copies += scatter(6, lambda r: r_dcb, lambda r: r_ench.at[r])
    for i, (a, b) in enumerate(
        (
            (r_dqb.at[me], r_tgh.at[me]),
            (r_atb.at[me], r_atth.at[me]),
            (r_dcb, r_ench.at[me]),
        )
    ):
        c = pltpu.make_async_copy(a, b, r_osem.at[4 + i])
        c.start()
        copies.append(c)
    for i in range(nrow - 1):
        q_copy(i).wait_send()
    for c in c_g:
        c.wait_send()
    for i in range(nrow - 1):
        att_copy(i).wait()
        dq_copy(i).wait()
        kv_back(i).wait()
    for c in copies + pending:
        c.wait()


def front(
    images, out_cot, project_out, context, emb, weight, vectors, w1, w2, win, cw, ew, nrow, nimg, wide
):
    px, ch = images.shape
    hd = ch // HEADS
    padc = -(-context.shape[0] // 16) * 16
    cfg = (nrow, nimg, wide, ch, hd, 1024, 3, len(vectors))
    nk = nrow * px + padc
    joint = cfg[6]
    V = pl.BlockSpec(memory_space=pltpu.VMEM)
    A = pl.BlockSpec(memory_space=pl.ANY)
    S = jax.ShapeDtypeStruct
    M = pltpu.VMEM
    dma = pltpu.SemaphoreType.DMA
    return pl.pallas_call(
        functools.partial(front_kernel, cfg),
        out_shape=(
            S((16, ch), f32),
            S((8, ch), f32),
            S((8, ch), f32),
            S((px, ch), f32),
            S((px, ch), f32),
            S((3 * ch, ch), bf16),
            S((ch, px), bf16),
            S((2, wide, ch), bf16),
            S((2, wide, ch), f32),
            S((2, wide, ch), f32),
            S((ch, nimg * px), bf16),
            S((ch, nimg * px), bf16),
            S((nimg, padc, context.shape[1] // nrow), bf16),
            S((nimg, 8, emb.shape[1] // nrow), f32),
            S((nrow, 3 * hd, px), bf16),
            S((nrow, hd, px), bf16),
            S((nrow, padc, 2 * hd), bf16),
        ),
        in_specs=[V] * 5
        + [pl.BlockSpec(memory_space=pltpu.SMEM)]
        + [A] * (len(vectors) + 5),
        out_specs=(V,) * 3 + (A,) * 14,
        scratch_shapes=[
            M((px, ch), f32),
            M((px, ch), f32),
            M((3 * ch, ch), bf16),
            M((ch, px), bf16),
            M((2, wide, ch), bf16),
            M((2, wide, ch), f32),
            M((2, wide, ch), f32),
            M((8, emb.shape[1]), f32),
            M((2, wide, ch), bf16),
            M((joint, 2 * hd, px), bf16),
            M((joint, hd, px), f32),
            M((cw.shape[0], 4 * hd), bf16),
            M((padc, cw.shape[0]), bf16),
            M((px + 2 * wide, 3 * ch), bf16),
            M((2, ch, px), bf16),
            M((nrow, hd, px), bf16),
            M((nrow, 3 * hd, px), bf16),
            M((nrow, 3 * hd, px), bf16),
            M((nrow, hd, px), bf16),
            M((nk, 2 * hd), bf16),
            M((nk, 2 * hd), bf16),
            M((hd, nk), bf16),
            M((hd + 16, nk), bf16),
            M((nk, px), f32),
            M((max(joint * nk, 2 * emb.shape[1] + 21 * ch), px), bf16),
            M((2 * hd, nk), f32),
            M((nrow, hd, px), bf16),
            M((nrow, 3 * hd, px), bf16),
            M((padc, 2 * hd), bf16),
            M((3, 8, 128), f32),
            M((3, nrow, 8, 128), f32),
            dma((13,)),
            dma((11,)),
            dma((3, nrow - 1)),
            dma((3, nrow - 1)),
            dma((4, 2)),
            dma((4, 2)),
            dma((4, nimg - 1)),
            dma((4, nimg - 1)),
            dma((7, nrow - 1)),
            dma((7, nrow - 1)),
            dma((8,)),
            dma((7,)),
        ],
        compiler_params=pltpu.CompilerParams(
            collective_id=3, has_side_effects=True, vmem_limit_bytes=62 * 2**20
        ),
        name="front",
    )(images, out_cot, project_out, context, emb, weight, *vectors, w1, w2, win, cw, ew)
def slope(values):
    sig = jax.nn.sigmoid(values)
    return sig * (1.0 + values * (1.0 - sig))


def back_kernel(
    cfg,
    r_imgh,
    r_och,
    r_par,
    r_ss,
    r_stats,
    r_hiddenh,
    r_middleh,
    r_hoch,
    r_hhidh,
    r_hmidh,
    r_a3h,
    r_tgh,
    r_atth,
    r_wth,
    r_w2h,
    r_w1h,
    r_a2h,
    r_a1h,
    r_ench,
    r_ctxh,
    r_igrad,
    r_kq,
    r_oq,
    r_cr,
    r_every,
    r_img,
    r_oc,
    r_hidden,
    r_middle,
    r_hoc,
    r_hhid,
    r_hmid,
    r_a3,
    r_tg,
    r_att,
    r_wt,
    r_w2,
    r_w1,
    r_a2,
    r_a1,
    r_enc,
    r_ctx,
    r_mg,
    r_ntg,
    r_buf,
    r_gq,
    r_gs,
    r_ks,
    r_kx,
    r_km,
    r_kz,
    r_kf,
    r_os,
    r_ox,
    r_oy,
    r_oz,
    r_of,
    r_encq,
    r_cq,
    r_vsrc,
    r_st_src,
    r_st_dst,
    r_hu,
    r_kacc,
    r_lsem,
    r_st_send,
    r_st_recv,
    r_h_send,
    r_h_recv,
    r_i_send,
    r_i_recv,
    r_r_send,
    r_r_recv,
    r_x_send,
    r_x_recv,
    r_z_send,
    r_z_recv,
    r_osem,
):
    nrow, nimg, wide, ch, hd, padc = cfg
    px = r_img.shape[0]
    part = ch // nimg
    rows = ch // nrow
    deep = nrow // 2
    members = float(nrow * px * (ch // GROUPS))
    links = Links(nrow, nimg)
    links.greet()
    pairs = (
        (r_tgh, r_tg),
        (r_wth, r_wt),
        (r_middleh, r_middle),
        (r_och, r_oc),
        (r_a3h, r_a3),
        (r_atth, r_att),
        (r_hiddenh, r_hidden),
        (r_imgh, r_img),
        (r_hmidh, r_hmid),
        (r_hoch, r_hoc),
        (r_hhidh, r_hhid),
        (r_w2h, r_w2),
        (r_a2h, r_a2),
        (r_w1h, r_w1),
        (r_a1h, r_a1),
        (r_ench, r_enc),
        (r_ctxh, r_ctx),
    )
    loads = [pltpu.make_async_copy(a, b, r_lsem.at[i]) for i, (a, b) in enumerate(pairs)]
    for c in loads:
        c.start()
    load_w2, load_a2, load_w1, load_a1, load_enc, load_ctx = loads[11:]
    stats = Stats(links, r_st_src, r_st_dst, r_st_send, r_st_recv)
    halo = Halo(links, r_h_send, r_h_recv)
    ends = (pl.ds(0, wide), pl.ds(px - wide, wide))

    def edges(slot, block, land):
        return halo.start(slot, block.at[ends[0]], block.at[ends[1]], land)

    others = (
        links.img + 1 - 2 * lax.rem(links.img, 2),
        lax.rem(links.img + 2, nimg),
        nimg - 1 - links.img,
    )
    row_z, row_x = links.row // 2, lax.rem(links.row, 2)
    img_y, img_c = links.img // 2, lax.rem(links.img, 2)

    def par(i):
        return r_par[i : i + 1, :]

    def stat(i):
        return r_stats[i : i + 1, :]

    scale1, shift = r_ss[0:1], r_ss[1:2]

    def share(slot, src, dst):
        copies = [pltpu.make_async_copy(src(links.img), dst(links.img), r_osem.at[slot])]
        for k, at in enumerate(others):
            copies.append(
                links.to(
                    "img", at, src(at), dst(links.img), r_i_send.at[slot, k], r_i_recv.at[slot, k]
                )
            )
        for c in copies:
            c.start()
        return copies

    def wait(copies):
        for c in copies:
            c.wait()

    def columns(at, img):
        return pl.ds(pl.multiple_of(at + img * part, 128), part)

    def row_x_start(slot, src, land):
        c = links.to(
            "row", links.row + 1 - 2 * row_x, src.at[:, 1 - row_x], land,
            r_x_send.at[slot], r_x_recv.at[slot],
        )
        c.start()
        return c

    def row_z_start(slot, c, src, land, mid, last):
        c.wait()
        mid[...] = (src[:, row_x].astype(f32) + land[...].astype(f32)).astype(bf16)
        copies = []
        for k in range(1, deep):
            z = lax.rem(row_z + k, deep)
            copies.append(
                links.to(
                    "row", 2 * z + row_x, mid.at[z], last.at[k - 1],
                    r_z_send.at[slot, k - 1], r_z_recv.at[slot, k - 1],
                )
            )
        for d in copies:
            d.start()
        return copies

    def row_end(copies, mid, last):
        wait(copies)
        s = mid[row_z].astype(f32)
        for k in range(1, deep):
            s = s + last[k - 1].astype(f32)
        return s.astype(bf16)

    def back_means(gain, gain_sum, bias_sum):
        both = jnp.concatenate([gain * bias_sum, gain * gain_sum, jnp.zeros((6, ch), f32)], axis=0)
        return group_total(both) * (1.0 / members)

    def norm_back(u, normed, rstd, gain, means):
        return rstd * (u * gain - means[0:1] - normed * means[1:2])

    def conv_back(stage, grad, before, after, weights):
        buf = r_buf.at[stage]
        put_block(links, buf, grad, before, after, wide)
        copies = share(
            stage, lambda i: buf.at[:, columns(ch, i)], lambda i: r_gq.at[stage, i]
        )
        acc = None
        for ky in range(3):
            for kx in range(3):
                g = buf[pl.ds(ky * wide, px), pl.ds(kx * ch, ch)]
                w = weights[2 - ky, pl.ds((2 - kx) * ch, ch), :]
                d = nt_dot(g, w)
                acc = d if acc is None else acc + d
        return acc, copies

    def kernel_part(stage, acts, ky, images):
        tot = None
        for b in images:
            at = pl.ds(pl.multiple_of(b * px, 128), px)
            d = nn(acts[:, at], r_gs[b, ky * wide : ky * wide + px, :])
            tot = d if tot is None else tot + d
        return tot

    def kernel_grads(stage, acts, copies):
        near, far = (links.img, others[0]), others[1:]
        for group, first in ((near, True), (far, False)):
            for b, c in zip(group, copies[:2] if first else copies[2:]):
                c.wait()
                put_shifts(r_gs.at[b], 0, r_gq[stage, b].astype(f32), wide)
            if first:
                for ky in range(3):
                    r_kacc[ky] = kernel_part(stage, acts, ky, near)
        sent = []
        for ky in range(3):
            tot = r_kacc[ky] + kernel_part(stage, acts, ky, far)
            r_ks[stage, ky] = tot.astype(bf16).reshape(deep, 2, rows, 3 * part)
            sent.append(row_x_start(3 * stage + ky, r_ks.at[stage, ky], r_kx.at[stage, ky]))
        return sent

    def kernel_mid(stage, sent, ky):
        return row_z_start(
            3 * stage + ky, sent[ky], r_ks.at[stage, ky], r_kx.at[stage, ky],
            r_km.at[stage, ky], r_kz.at[stage, ky],
        )

    def kernel_end(stage, copies):
        out = []
        for ky in range(3):
            r_kf[stage, ky] = row_end(copies[ky], r_km.at[stage, ky], r_kz.at[stage, ky])
            out += share(
                2 + 3 * stage + ky,
                lambda i, ky=ky: r_kf.at[stage, ky],
                lambda i, ky=ky: r_kq.at[stage, ky, i],
            )
        return out

    for c in loads[:11]:
        c.wait()
    tgt = r_tg[...].reshape(3 * ch, px)
    u3 = nn(tgt.T, r_wt[...])
    normed3 = (r_middle[...] - stat(4)) * stat(5)
    grad_out = r_oc[...].astype(f32) * par(10)
    r_mg[...] = u3
    sums = [total(u3 * normed3), total(u3), total(grad_out)]
    links.greeted()
    stats.start(0, sums)
    c_u = edges(0, r_mg, r_hu.at[0])
    load_enc.wait()
    c_encq = share(8, lambda i: r_enc.at[pl.ds(2 * i, 2)], lambda i: r_encq.at[i])
    a3 = r_a3[...]
    low = (r_oc[...].astype(f32) * par(10)).astype(bf16)
    pout = nn(r_att[...].reshape(ch, px), low).astype(bf16)
    for q in range(nimg):
        pin = nt_dot(a3, r_tg[2 * q : 2 * q + 2].reshape(6 * hd, px)).astype(bf16)
        r_os[q // 2, q % 2] = jnp.concatenate(
            [pin, pout[:, q * part : (q + 1) * part]], axis=1
        )
    c_ox = links.to(
        "img", links.img + 1 - 2 * img_c, r_os.at[:, 1 - img_c], r_ox,
        r_i_send.at[9, 0], r_i_recv.at[9, 0],
    )
    c_ox.start()
    sums3 = stats.finish(0)
    means3 = back_means(par(8), sums3[0:1], sums3[1:2])

    def middle_back(u, middle, oc):
        normed = (middle - stat(4)) * stat(5)
        return oc.astype(f32) * par(10) + norm_back(u, normed, stat(5), par(8), means3)

    halo.finish(c_u)
    middle_grad = middle_back(r_mg[...], r_middle[...], r_oc[...])
    r_mg[...] = middle_grad
    load_w2.wait()
    act_grad, c_g2 = conv_back(
        0,
        middle_grad,
        middle_back(r_hu[0, 0], r_hmid[0], r_hoc[0]),
        middle_back(r_hu[0, 1], r_hmid[1], r_hoc[1]),
        r_w2,
    )
    normed2 = (r_hidden[...] - stat(2)) * stat(3)
    ntg = act_grad * slope((normed2 * par(3) + par(4)) * scale1 + shift)
    r_ntg[...] = ntg
    stats.start(1, [total(ntg * normed2), total(ntg)])
    c_n = edges(1, r_ntg, r_hu.at[1])
    middle_sum = total(r_mg[...])
    load_a2.wait()
    c_k2 = kernel_grads(0, r_a2, c_g2)
    c_ox.wait()
    r_os[:, 0] = (
        r_os[:, img_c].astype(f32) + r_ox[...].astype(f32)
    ).astype(bf16)
    c_oy = links.to(
        "img", lax.rem(links.img + 2, nimg), r_os.at[1 - img_y, 0], r_oy,
        r_i_send.at[9, 1], r_i_recv.at[9, 1],
    )
    c_oy.start()
    sums2 = stats.finish(1)
    means2 = back_means(par(3), scale1 * sums2[0:1], scale1 * sums2[1:2])

    def hidden_back(u, hidden):
        normed = (hidden - stat(2)) * stat(3)
        return norm_back(u * scale1, normed, stat(3), par(3), means2)

    halo.finish(c_n)
    hidden_grad = hidden_back(r_ntg[...], r_hidden[...])
    hidden_sum = total(hidden_grad)
    load_w1.wait()
    act_grad, c_g1 = conv_back(
        1,
        hidden_grad,
        hidden_back(r_hu[1, 0], r_hhid[0]),
        hidden_back(r_hu[1, 1], r_hhid[1]),
        r_w1,
    )
    m_k2 = [kernel_mid(0, c_k2, 0), kernel_mid(0, c_k2, 1)]
    c_oy.wait()
    both = r_os[img_y, 0].astype(f32) + r_oy[...].astype(f32)
    r_of[...] = both.astype(bf16).reshape(deep, 2, rows, 6 * hd + part)
    c_o = row_x_start(6, r_of, r_oz.at[0])
    normed1 = (r_img[...].astype(f32) - stat(0)) * stat(1)
    n1g = act_grad * slope(normed1 * par(0) + par(1))
    r_ntg[...] = n1g
    stats.start(2, [total(n1g * normed1), total(n1g), hidden_sum, middle_sum])
    m_k2.append(kernel_mid(0, c_k2, 2))
    load_a1.wait()
    c_k1 = kernel_grads(1, r_a1, c_g1)
    c_o = row_z_start(6, c_o, r_of, r_oz.at[0], r_oz.at[1], r_oz.at[2, pl.ds(0, deep - 1)])
    wait(c_encq)
    load_ctx.wait()
    turned = r_ctx[...].reshape(nimg * padc, -1).T
    pairs = jnp.concatenate([r_encq[:, 0], r_encq[:, 1]], axis=2)
    r_cq[...] = nn(turned, pairs.reshape(nimg * padc, 4 * hd)).astype(bf16)
    out = share(11, lambda i: r_cq, lambda i: r_cr.at[i])
    sums1 = stats.finish(2)
    scale_grad = par(3) * sums2[0:1] + par(4) * sums2[1:2]
    r_vsrc[...] = jnp.concatenate(
        [
            sums1[0:3],
            scale1 * sums2[0:1],
            scale1 * sums2[1:2],
            sums1[3:4],
            sums3[0:3],
            scale_grad,
            sums2[1:2],
            jnp.zeros((5, ch), f32),
        ],
        axis=0,
    )
    out += share(10, lambda i: r_vsrc, lambda i: r_every.at[i])
    m_k1 = [kernel_mid(1, c_k1, 0)]
    out += kernel_end(0, m_k2)
    normed1 = (r_img[...].astype(f32) - stat(0)) * stat(1)
    means1 = back_means(par(0), sums1[0:1], sums1[1:2])
    r_igrad[...] = r_mg[...] + norm_back(r_ntg[...], normed1, stat(1), par(0), means1)
    m_k1.append(kernel_mid(1, c_k1, 1))
    m_k1.append(kernel_mid(1, c_k1, 2))
    r_oy[:rows] = row_end(c_o, r_oz.at[1], r_oz.at[2])
    out += share(12, lambda i: r_oy.at[pl.ds(0, rows)], lambda i: r_oq.at[i])
    out += kernel_end(1, m_k1)
    wait(out)


def backward(nrow, nimg, wide, *args):
    px, ch = args[0].shape
    hd = ch // HEADS
    ctx, enc = args[19], args[18]
    padc = enc.shape[1]
    cfg = (nrow, nimg, wide, ch, hd, padc)
    part, rows, deep = ch // nimg, ch // nrow, nrow // 2
    proj = 6 * hd + part
    V = pl.BlockSpec(memory_space=pltpu.VMEM)
    A = pl.BlockSpec(memory_space=pl.ANY)
    S = jax.ShapeDtypeStruct
    dma = pltpu.SemaphoreType.DMA
    M = pltpu.VMEM
    text = ctx.shape[2]
    return pl.pallas_call(
        functools.partial(back_kernel, cfg),
        out_shape=(
            S((px, ch), f32),
            S((2, 3, nimg, rows, 3 * part), bf16),
            S((nimg, rows, proj), bf16),
            S((nimg, text, 4 * hd), bf16),
            S((nimg, 16, ch), f32),
        ),
        in_specs=[A, A, V, V, V, A, A, A, A, A, A, A, A, A] + [A] * 6,
        out_specs=(V,) + (A,) * 4,
        scratch_shapes=[M(args[i].shape, args[i].dtype) for i in (0, 1, 5, 6, 7, 8, 9, 10, 11, 12, 13)]
        + [
            M((3, 3 * ch, ch), bf16),
            M((3, 3 * ch, ch), bf16),
            M((ch, nimg * px), bf16),
            M((ch, nimg * px), bf16),
            M(enc.shape, bf16),
            M(ctx.shape, bf16),
            M((px, ch), f32),
            M((px, ch), f32),
            M((2, px + 2 * wide, 3 * ch), bf16),
            M((2, nimg, px + 2 * wide, part), bf16),
            M((nimg, px + 2 * wide, 3 * part), bf16),
            M((2, 3, deep, 2, rows, 3 * part), bf16),
            M((2, 3, deep, rows, 3 * part), bf16),
            M((2, 3, deep, rows, 3 * part), bf16),
            M((2, 3, deep - 1, rows, 3 * part), bf16),
            M((2, 3, rows, 3 * part), bf16),
            M((2, 2, ch, proj), bf16),
            M((2, ch, proj), bf16),
            M((ch, proj), bf16),
            M((3, deep, rows, proj), bf16),
            M((deep, 2, rows, proj), bf16),
            M((nimg, 2, padc, 2 * hd), bf16),
            M((text, 4 * hd), bf16),
            M((16, ch), f32),
            M((3, 16, 128), f32),
            M((3, nrow, 16, 128), f32),
            M((2, 2, wide, ch), f32),
            M((3, ch, 3 * part), f32),
            dma((17,)),
            dma((3, nrow - 1)),
            dma((3, nrow - 1)),
            dma((2, 2)),
            dma((2, 2)),
            dma((13, nimg - 1)),
            dma((13, nimg - 1)),
            dma((1, nrow - 1)),
            dma((1, nrow - 1)),
            dma((7,)),
            dma((7,)),
            dma((7, deep - 1)),
            dma((7, deep - 1)),
            dma((13,)),
        ],
        compiler_params=pltpu.CompilerParams(
            collective_id=4, has_side_effects=True, vmem_limit_bytes=60 * 2**20
        ),
        name="back",
    )(*args)


def finish_kernel(cfg, *refs):
    nrow, nimg, ch, hd, nvec = cfg
    igh, kqh, oqh, crh, everyh, embh, middleh, atth, pouth, parh = refs[:10]
    resh, igouth, k1h, k2h, inh, outh, ctxgh, embgh = refs[10:18]
    vecs = refs[18 : 18 + nvec]
    ig, kq, oq, cr, every, emb, middle, att, pout, par = refs[18 + nvec : 28 + nvec]
    res, k1g, k2g, ing, outg, ctxg, embg, isem, osem = refs[28 + nvec :]
    px = middle.shape[0]
    part = ch // nimg
    me = lax.axis_index("row")
    done = []
    pairs = (
        (kqh.at[0], kq.at[0]),
        (kqh.at[1], kq.at[1]),
        (atth, att),
        (pouth, pout),
        (middleh, middle),
        (parh, par),
        (everyh, every),
        (embh, emb),
        (crh, cr),
        (oqh, oq),
        (igh, ig),
    )
    loads = [pltpu.make_async_copy(a, b, isem.at[i]) for i, (a, b) in enumerate(pairs)]
    for c in loads:
        c.start()

    def put(slot, src, dst):
        c = pltpu.make_async_copy(src, dst, osem.at[slot])
        c.start()
        done.append(c)

    loads[10].wait()
    put(0, ig, igouth)
    for stage, out, dst in ((0, k2g, k2h), (1, k1g, k1h)):
        loads[stage].wait()
        for ky in range(3):
            for b in range(nimg):
                v = kq[stage, ky, b].astype(f32)
                for kx in range(3):
                    out[2 - ky, 2 - kx, :, b * part : (b + 1) * part] = v[
                        :, kx * part : (kx + 1) * part
                    ]
        put(1 + stage, out, dst)
    for c in loads[2:6]:
        c.wait()
    branch = nn(att[...].reshape(ch, px).T, pout[...])
    res[...] = (middle[...] + branch + par[11:12, :]).astype(bf16)
    put(3, res, resh)
    loads[6].wait()
    loads[7].wait()
    acts = emb[:, 0, :].T
    for j in range(2):
        d = None
        for b in range(nimg):
            t = acts[:, b : b + 1] * every[b, 9 + j : 10 + j]
            d = t if d is None else d + t
        embg[:, j * ch : (j + 1) * ch] = d
    put(4, embg, embgh)
    loads[8].wait()
    for b in range(nimg):
        v = cr[b].astype(f32)
        p = [v[:, j * hd : (j + 1) * hd] for j in range(4)]
        ctxg[:, b * 2 * hd : (b + 1) * 2 * hd] = jnp.concatenate([p[0], p[2]], axis=1)
        ctxg[:, ch + b * 2 * hd : ch + (b + 1) * 2 * hd] = jnp.concatenate([p[1], p[3]], axis=1)
    put(5, ctxg, ctxgh)
    loads[9].wait()
    for b in range(nimg):
        v = oq[b].astype(f32)
        for j in range(3):
            ing[:, j * ch + b * 2 * hd : j * ch + (b + 1) * 2 * hd] = jnp.concatenate(
                [v[:, j * hd : (j + 1) * hd], v[:, (3 + j) * hd : (4 + j) * hd]], axis=1
            )
        outg[:, b * part : (b + 1) * part] = v[:, 6 * hd :]
    put(6, ing, inh)
    put(7, outg, outh)
    sums = jnp.sum(every[...], axis=0)
    size = ch // nrow
    turned = pltpu.roll(sums, lax.rem(ch - me * size, ch), 1)
    for i in range(nvec - 1):
        vecs[i][...] = turned[i, :size]
    both = jnp.concatenate([sums[9:10], sums[10:11]], axis=1)
    both = jnp.concatenate([both] * 8, axis=0)
    both = pltpu.roll(both, lax.rem(2 * ch - me * 2 * size, 2 * ch), 1)
    vecs[nvec - 1][...] = both[0, : 2 * size]
    for c in done:
        c.wait()


def finish(nrow, nimg, *args):
    px, ch = args[0].shape
    hd = ch // HEADS
    kq, oq, cr, every, emb = args[1:6]
    rows = ch // nrow
    nvec = 10
    V = pl.BlockSpec(memory_space=pltpu.VMEM)
    A = pl.BlockSpec(memory_space=pl.ANY)
    S = jax.ShapeDtypeStruct
    M = pltpu.VMEM
    dma = pltpu.SemaphoreType.DMA
    outs = (
        ((px, ch), bf16),
        ((3, 3, rows, ch), f32),
        ((3, 3, rows, ch), f32),
        ((rows, 3 * ch), f32),
        ((rows, ch), f32),
        ((cr.shape[1], 2 * ch), f32),
        ((emb.shape[2], 2 * ch), f32),
    )
    return pl.pallas_call(
        functools.partial(finish_kernel, (nrow, nimg, ch, hd, nvec)),
        out_shape=(S(*outs[0]), S((px, ch), f32))
        + tuple(S(*o) for o in outs[1:])
        + (S((rows,), f32),) * (nvec - 1)
        + (S((2 * rows,), f32),),
        in_specs=[A] * 10,
        out_specs=(A,) * 8 + (V,) * nvec,
        scratch_shapes=[M(a.shape, a.dtype) for a in args]
        + [M(*o) for o in outs]
        + [dma((11,)), dma((8,))],
        compiler_params=pltpu.CompilerParams(vmem_limit_bytes=62 * 2**20),
        name="finish",
    )(*args)


def local_fast(
    images,
    timesteps,
    clip_embed,
    context,
    out_cotangent,
    item_weight,
    first_gain,
    first_bias,
    first_kernel,
    first_offset,
    embed_weight,
    embed_bias,
    second_gain,
    second_bias,
    second_kernel,
    second_offset,
    third_gain,
    third_bias,
    project_in,
    context_weight,
    project_out,
    output_bias,
):
    _, tall, wide, ch = images.shape
    pixels = tall * wide
    nrow = lax.axis_size("row")
    nimg = lax.axis_size("img")
    me_row = lax.axis_index("row")
    nctx = context.shape[1]
    image = images.reshape(pixels, ch)
    cotangent = out_cotangent.reshape(pixels, ch)
    width = clip_embed.shape[1]
    at = jnp.arange(width, dtype=jnp.int32)[None, :]
    half = width // 2
    index = jnp.where(at < half, at, at - half).astype(f32)
    angles = timesteps.astype(f32)[:, None] * jnp.exp(-math.log(10000.0) * index / half)
    embedding = jnp.where(at < half, jnp.cos(angles), jnp.sin(angles)) + clip_embed.astype(f32)
    emb = jax.nn.silu(embedding)
    vectors = [
        v.reshape(1, -1)
        for v in (
            first_gain, first_bias, first_offset, second_gain, second_bias, second_offset,
            third_gain, third_bias, output_bias, embed_bias,
        )
    ]
    w1 = first_kernel.reshape(3, 3 * ch, ch)
    w2 = second_kernel.reshape(3, 3 * ch, ch)
    (
        par, stats, ss, hidden, middle, turned_in, act_three, halo_cot, halo_hidden, halo_middle,
        acts_one, acts_two, ctx_parts, emb_parts, grads, attended, enc_grads,
    ) = front(
        image, cotangent, project_out, context[0], emb, item_weight, vectors, w1, w2, project_in, context_weight,
        embed_weight, nrow, nimg, wide,
    )
    image_grad, kq, oq, cr, every = backward(
        nrow, nimg, wide,
        image, cotangent, par, ss, stats, hidden, middle, halo_cot, halo_hidden, halo_middle, act_three, grads, attended, turned_in,
        w2, w1, acts_two, acts_one, enc_grads, ctx_parts,
    )
    result, image_grad, k1g, k2g, ing, outg, ctxg, embg, *vecs = finish(
        nrow, nimg, image_grad, kq, oq, cr, every, emb_parts, middle, attended, project_out, par
    )
    return (
        result.reshape(images.shape),
        image_grad.reshape(images.shape),
        vecs[0],
        vecs[1],
        k1g,
        vecs[2],
        embg,
        vecs[9],
        vecs[3],
        vecs[4],
        k2g,
        vecs[5],
        vecs[6],
        vecs[7],
        ing,
        ctxg,
        outg,
        vecs[8],
    )


def solution(mesh):
    every = P()
    image = P("img", "row", None, None)
    placed = (image, P("img"), P("img", None), P("img", None, None), image, P("img")) + (every,) * 16
    vec = P("row")
    matrix = P("row", None)
    taps = P(None, None, "row", None)
    nimg, nrow = mesh.shape["img"], mesh.shape["row"]
    quick = nrow == HEADS and nimg == 4
    return jax.shard_map(
        local_fast if quick else local,
        mesh=mesh,
        in_specs=placed,
        out_specs=(
            image,
            image,
            vec,
            vec,
            taps,
            vec,
            matrix,
            vec,
            vec,
            vec,
            taps,
            vec,
            vec,
            vec,
            matrix,
            matrix,
            matrix,
            vec,
        ),
        check_vma=False,
    )
```
